32 devices in a mesh: group: 4 (over y, x), dev: 8 (over z, core).
Axes of the slice: x: 2, y: 2, z: 4, core: 2. Of those that a mesh axis runs over, the one named last changes fastest.
Arguments:
- level_set: float32 [512, 8192], P(None, ('group', 'dev')), may hold values from -8 to 8
- speed: float32 [512, 8192], P(None, ('group', 'dev')), may hold values from 0.25 to 1
- peer_slabs: int32 [256, 40], P(('group', 'dev')), may hold values from -1 to 1535, as said below
- region_slabs: int32 [64, 16], P(('group', 'dev')), may hold values from 0 to 511, as said below
- halo_source: int32 [6, 8192], P(None, ('group', 'dev')), may hold values from 0 to 1887, as said below
Outputs:
- offset: float32 [512, 8192], P(None, ('group', 'dev'))
The draws below stay inside these ranges and needn't reach their ends.
Inputs may be any that keep to these rules, and one draw needn't show every extreme that they name: `peer_slabs`: row (device, e) lists the local slab ids that the device sends to device e of its region, -1 in empty slots. Every device fills all 40 slots of at least one row, and receives 40 slabs from at least one device. `region_slabs`: local slab ids of the leaf faces that border the previous region (row 0) and the next region (row 1). `halo_source`: an entry of the halo table of the column's device; only slots that the sender fills are named.
All inputs are finite; a program needn't handle non-finite values.
Results may differ from the reference program's by a relative error of at most 0.0003.
Values sent between devices are 32-bit elements; how exact they have to be, the bound alone decides.
No kernel may reach another device: no remote copies, remote signals or barrier semaphores. Data moves between devices by JAX's collectives and lax.ppermute only.
A program may use at most 64 MiB of HBM per device.

```python
import math
import jax
import jax.numpy as jnp
from jax import lax

LEAF_VOXELS = 512
BRICK_X = 16
BRICK_Y = 4
BRICK_Z = 4
OFFSET_STEPS = 2
REDIST_PASSES = 2
REGIONS = 4
GROUP_DEVS = 8
LEAVES_DEV = 256
LEAVES = 8192
FACES_PEER = 128
FACES_REGION = 16
HALF_SLOTS = 20
PEER_SLOTS = 40


def brick_layout(key):
    regions = REGIONS
    peer_count = GROUP_DEVS
    count = LEAVES_DEV
    keys = jax.random.split(jax.random.fold_in(key, 7001), 4)
    slot_of = jax.vmap(lambda subkey: jax.random.permutation(subkey, count))(jax.random.split(keys[0], regions * peer_count))
    slot_of = slot_of.astype(jnp.int32).reshape(regions, peer_count, count)
    leaf_at = jnp.argsort(slot_of, axis=2).astype(jnp.int32)
    ranking = jax.vmap(lambda subkey: jax.random.permutation(subkey, peer_count))(jax.random.split(keys[1], regions)).astype(jnp.int32)
    inverse = jnp.argsort(ranking, axis=1).astype(jnp.int32)
    classes = peer_count - 1
    grid_size = classes * HALF_SLOTS
    score = jax.random.permutation(keys[2], grid_size).astype(jnp.int32)
    cells = jnp.arange(grid_size, dtype=jnp.int32)
    forced = cells // HALF_SLOTS == peer_count // 2 - 1
    score = jnp.where(forced, score - grid_size, score)
    chosen = jnp.argsort(score).astype(jnp.int32)[:FACES_PEER]
    chosen = chosen[jax.random.permutation(keys[3], FACES_PEER)]
    shift_of = (chosen // HALF_SLOTS + 1).astype(jnp.int32)
    slot_in = (chosen % HALF_SLOTS).astype(jnp.int32)
    return (slot_of, leaf_at, ranking, inverse, shift_of, slot_in)


def peer_faces():
    places = jnp.arange(FACES_PEER, dtype=jnp.int32)
    y_count = BRICK_X * BRICK_Z
    on_y = places < y_count
    first = jnp.minimum(places, y_count - 1)
    second = jnp.maximum(places - y_count, 0)
    x_of_y = first // BRICK_Z
    z_of_y = first % BRICK_Z
    x_of_z = second // BRICK_Y
    y_of_z = second % BRICK_Y
    high_leaf = jnp.where(on_y, (x_of_y * BRICK_Y + BRICK_Y - 1) * BRICK_Z + z_of_y, (x_of_z * BRICK_Y + y_of_z) * BRICK_Z + BRICK_Z - 1)
    low_leaf = jnp.where(on_y, x_of_y * BRICK_Y * BRICK_Z + z_of_y, (x_of_z * BRICK_Y + y_of_z) * BRICK_Z)
    high_side = jnp.where(on_y, 3, 5).astype(jnp.int32)
    return (high_leaf.astype(jnp.int32), low_leaf.astype(jnp.int32), high_side)


def draw_peer_slabs(key, part):
    slot_of, leaf_at, ranking, inverse, shift_of, slot_in = brick_layout(key)
    high_leaf, low_leaf, high_side = peer_faces()
    regions = REGIONS
    peer_count = GROUP_DEVS
    count = LEAVES_DEV
    region_idx = jnp.arange(regions, dtype=jnp.int32)[:, None, None]
    device_idx = jnp.arange(peer_count, dtype=jnp.int32)[None, :, None]
    rank = ranking[:, :, None]
    up_target = inverse[region_idx, (rank + shift_of) % peer_count]
    down_target = inverse[region_idx, (rank - shift_of + peer_count) % peer_count]
    high_ids = high_side * count + slot_of[:, :, high_leaf]
    low_ids = (high_side - 1) * count + slot_of[:, :, low_leaf]
    listing = jnp.full((regions, peer_count, peer_count, PEER_SLOTS), -1, jnp.int32)
    listing = listing.at[region_idx, device_idx, up_target, slot_in].set(high_ids)
    listing = listing.at[region_idx, device_idx, down_target, HALF_SLOTS + slot_in].set(low_ids)
    return listing.reshape(regions * peer_count * peer_count, PEER_SLOTS)


def draw_region_slabs(key, part):
    slot_of, leaf_at, ranking, inverse, shift_of, slot_in = brick_layout(key)
    count = LEAVES_DEV
    places = jnp.arange(FACES_REGION, dtype=jnp.int32)
    y_place = places // BRICK_Z
    z_place = places % BRICK_Z
    low_leaf = y_place * BRICK_Z + z_place
    high_leaf = ((BRICK_X - 1) * BRICK_Y + y_place) * BRICK_Z + z_place
    stacked = jnp.stack([slot_of[:, :, low_leaf], count + slot_of[:, :, high_leaf]], axis=2)
    return stacked.reshape(REGIONS * GROUP_DEVS * 2, FACES_REGION).astype(jnp.int32)


def draw_halo_source(key, part):
    slot_of, leaf_at, ranking, inverse, shift_of, slot_in = brick_layout(key)
    regions = REGIONS
    peer_count = GROUP_DEVS
    count = LEAVES_DEV
    plane = BRICK_Y * BRICK_Z
    lattice = leaf_at
    x_pos = lattice // plane
    y_pos = lattice // BRICK_Z % BRICK_Y
    z_pos = lattice % BRICK_Z

    def slot_at(place):
        return jnp.take_along_axis(slot_of, jnp.clip(place, 0, count - 1), axis=2)
    local_total = 6 * count
    region_base = local_total + peer_count * PEER_SLOTS
    rank = ranking[:, :, None]
    region_idx = jnp.arange(regions, dtype=jnp.int32)[:, None, None]
    y_face = x_pos * BRICK_Z + z_pos
    z_face = BRICK_X * BRICK_Z + x_pos * BRICK_Y + y_pos

    def from_below(face):
        source = inverse[region_idx, (rank - shift_of[face] + peer_count) % peer_count]
        return local_total + source * PEER_SLOTS + slot_in[face]

    def from_above(face):
        source = inverse[region_idx, (rank + shift_of[face]) % peer_count]
        return local_total + source * PEER_SLOTS + HALF_SLOTS + slot_in[face]
    cross_place = y_pos * BRICK_Z + z_pos
    side_zero = jnp.where(x_pos > 0, count + slot_at(lattice - plane), region_base + cross_place)
    side_one = jnp.where(x_pos < BRICK_X - 1, slot_at(lattice + plane), region_base + FACES_REGION + cross_place)
    side_two = jnp.where(y_pos > 0, 3 * count + slot_at(lattice - BRICK_Z), from_below(y_face))
    side_three = jnp.where(y_pos < BRICK_Y - 1, 2 * count + slot_at(lattice + BRICK_Z), from_above(y_face))
    side_four = jnp.where(z_pos > 0, 5 * count + slot_at(lattice - 1), from_below(z_face))
    side_five = jnp.where(z_pos < BRICK_Z - 1, 4 * count + slot_at(lattice + 1), from_above(z_face))
    stacked = jnp.stack([side_zero, side_one, side_two, side_three, side_four, side_five], axis=0)
    return stacked.reshape(6, regions * peer_count * count).astype(jnp.int32)


def steps_of(own_key, shape, cuts, smallest, top_value):
    def one(dim, blocks):
        steps = jax.random.uniform(jax.random.fold_in(jax.random.fold_in(own_key, 6), dim), (blocks,), jnp.float32, smallest / len(cuts), top_value / len(cuts))
        return jnp.repeat(jnp.exp(steps), shape[dim] // blocks).reshape((-1,) + (1,) * (len(shape) - dim - 1))

    gain = one(*cuts[0])
    for cut in cuts[1:]:
        gain = gain * one(*cut)
    return gain


def noise(key, shape, deviation, bound, cuts=(), kind=jnp.bfloat16):
    values = jax.random.normal(key, shape, jnp.float32) * deviation
    if len(cuts) > 0:
        values = steps_of(key, shape, cuts, -0.22, 0.18) * values
    return jnp.clip(values, min=-bound, max=bound).astype(kind)


def setup_inputs(seed: int = 0) -> dict:
    seeds = jax.random.split(jax.random.key(seed), 6)
    return {
        "level_set": noise(seeds[0], (LEAF_VOXELS, LEAVES), 2.0, 8.0, ((1, 32),), jnp.float32),
        "speed": jnp.clip(jnp.exp(math.log(1.0) - 1.3862944 * jax.random.uniform(seeds[1], (LEAF_VOXELS, LEAVES), jnp.float32) ** steps_of(seeds[1], (LEAF_VOXELS, LEAVES), ((1, 32),), -0.2, 0.2)), 0.25, 1.0),
        "peer_slabs": draw_peer_slabs(jax.random.fold_in(seeds[5], 71), 0),
        "region_slabs": draw_region_slabs(jax.random.fold_in(seeds[5], 71), 0),
        "halo_source": draw_halo_source(jax.random.fold_in(seeds[5], 71), 0),
    }


advect_scale = 0.3
relax_scale = 0.3
weno_floor = 1e-06

def face_slabs(voxels, layers):
    count = voxels.shape[3]
    pieces = [voxels[:layers], voxels[8 - layers:], voxels[:, :layers], voxels[:, 8 - layers:], voxels[:, :, :layers], voxels[:, :, 8 - layers:]]
    return jnp.concatenate([piece.reshape(64 * layers, count) for piece in pieces], axis=1)

def weno_side(first, second, third, fourth, fifth):
    guess_a = first / 3.0 - 7.0 * second / 6.0 + 11.0 * third / 6.0
    guess_b = -second / 6.0 + 5.0 * third / 6.0 + fourth / 3.0
    guess_c = third / 3.0 + 5.0 * fourth / 6.0 - fifth / 6.0
    bend_a = first - 2.0 * second + third
    tilt_a = first - 4.0 * second + 3.0 * third
    bend_b = second - 2.0 * third + fourth
    tilt_b = second - fourth
    bend_c = third - 2.0 * fourth + fifth
    tilt_c = 3.0 * third - 4.0 * fourth + fifth
    smooth_a = weno_floor + 13.0 / 12.0 * bend_a * bend_a + 0.25 * tilt_a * tilt_a
    smooth_b = weno_floor + 13.0 / 12.0 * bend_b * bend_b + 0.25 * tilt_b * tilt_b
    smooth_c = weno_floor + 13.0 / 12.0 * bend_c * bend_c + 0.25 * tilt_c * tilt_c
    weight_a = 0.1 / (smooth_a * smooth_a)
    weight_b = 0.6 / (smooth_b * smooth_b)
    weight_c = 0.3 / (smooth_c * smooth_c)
    return (weight_a * guess_a + weight_b * guess_b + weight_c * guess_c) / (weight_a + weight_b + weight_c)

def one_sided(padded, along):
    differences = jnp.diff(padded, axis=along)

    def window(lowest):
        return lax.slice_in_dim(differences, lowest, lowest + 8, axis=along)
    backward = weno_side(window(0), window(1), window(2), window(3), window(4))
    forward = weno_side(window(5), window(4), window(3), window(2), window(1))
    return (backward, forward)

def widen(voxels, picked, layers):
    count = voxels.shape[3]

    def face_part(side, extent):
        return picked[:, side, :].reshape(extent + (count,))
    along_x = jnp.concatenate([face_part(0, (layers, 8, 8)), voxels, face_part(1, (layers, 8, 8))], axis=0)
    along_y = jnp.concatenate([face_part(2, (8, layers, 8)), voxels, face_part(3, (8, layers, 8))], axis=1)
    along_z = jnp.concatenate([face_part(4, (8, 8, layers)), voxels, face_part(5, (8, 8, layers))], axis=2)
    return (along_x, along_y, along_z)

def advect_leaves(voxels, speeds, picked):
    squared = jnp.zeros_like(voxels)
    for along, padded in enumerate(widen(voxels, picked, 3)):
        backward, forward = one_sided(padded, along)
        squared = squared + jnp.maximum(jnp.square(jnp.maximum(backward, 0.0)), jnp.square(jnp.minimum(forward, 0.0)))
    return voxels - advect_scale * speeds * jnp.sqrt(squared)

def relax_leaves(voxels, sign_field, picked):
    squared = jnp.zeros_like(voxels)
    for along, padded in enumerate(widen(voxels, picked, 1)):
        centre = lax.slice_in_dim(padded, 1, 9, axis=along)
        backward = centre - lax.slice_in_dim(padded, 0, 8, axis=along)
        forward = lax.slice_in_dim(padded, 2, 10, axis=along) - centre
        rising = jnp.maximum(jnp.square(jnp.maximum(backward, 0.0)), jnp.square(jnp.minimum(forward, 0.0)))
        falling = jnp.maximum(jnp.square(jnp.minimum(backward, 0.0)), jnp.square(jnp.maximum(forward, 0.0)))
        squared = squared + jnp.where(sign_field > 0.0, rising, falling)
    return voxels - relax_scale * sign_field * (jnp.sqrt(squared) - 1.0)

def pick_columns(entries, indices):
    return jnp.take(entries, indices, axis=1)

def halo_pass(voxels, layers, peer_slabs, region_slabs, sources):
    regions = voxels.shape[0]
    peer_count = voxels.shape[1]
    slab_rows = 64 * layers
    tables = jax.vmap(jax.vmap(lambda block: face_slabs(block, layers)))(voxels)
    pick = jax.vmap(jax.vmap(pick_columns))
    sends = jnp.maximum(peer_slabs.reshape(regions, peer_count, peer_count * PEER_SLOTS), 0)
    outgoing = pick(tables, sends).reshape(regions, peer_count, slab_rows, peer_count, PEER_SLOTS)
    arrived = jnp.transpose(outgoing, (0, 3, 2, 1, 4)).reshape(regions, peer_count, slab_rows, peer_count * PEER_SLOTS)
    border = pick(tables, region_slabs.reshape(regions, peer_count, 2 * FACES_REGION))
    border = border.reshape(regions, peer_count, slab_rows, 2, FACES_REGION)
    preceding = jnp.roll(border[:, :, :, 1], 1, axis=0)
    following = jnp.roll(border[:, :, :, 0], -1, axis=0)
    combined = jnp.concatenate([tables, arrived, preceding, following], axis=3)
    return pick(combined, sources)

def map_devices(update, first, second, third):
    leading = first.shape[:2]
    flattened = tuple((array.reshape((-1,) + array.shape[2:]) for array in (first, second, third)))
    updated = lax.map(lambda items: update(items[0], items[1], items[2]), flattened)
    return updated.reshape(leading + updated.shape[1:])

def reference(level_set, speed, peer_slabs, region_slabs, halo_source):
    regions = REGIONS
    peer_count = GROUP_DEVS
    count = LEAVES_DEV

    def per_device(values):
        return values.reshape(512, regions, peer_count, count).transpose(1, 2, 0, 3).reshape(regions, peer_count, 8, 8, 8, count)
    voxels = per_device(level_set)
    speeds = per_device(speed)
    sources = halo_source.reshape(6, regions, peer_count, count).transpose(1, 2, 0, 3)
    for offset_step in range(OFFSET_STEPS):
        picked = halo_pass(voxels, 3, peer_slabs, region_slabs, sources)
        voxels = map_devices(advect_leaves, voxels, speeds, picked)
        sign_field = voxels / jnp.sqrt(voxels * voxels + 1.0)
        for redist_pass in range(REDIST_PASSES):
            picked = halo_pass(voxels, 1, peer_slabs, region_slabs, sources)
            voxels = map_devices(relax_leaves, voxels, sign_field, picked)
    return voxels.reshape(regions, peer_count, 512, count).transpose(2, 0, 1, 3).reshape(512, regions * peer_count * count)
```

```python
import functools

import jax
import jax.numpy as jnp
from jax import lax
from jax.experimental import pallas as pl
from jax.experimental.pallas import tpu as pltpu
from jax.sharding import PartitionSpec as P

OFFSET_STEPS = 2
REDIST_PASSES = 2

advect_scale = 0.3
relax_scale = 0.3
weno_floor = 1e-06

LANES = 128


class Plan:
    def __init__(self, count, peers, slots, border, layers):
        self.count = count
        self.peers = peers
        self.slots = slots
        self.border = border
        self.layers = layers
        self.halves = count // LANES
        self.local_tiles = 6 * self.halves
        self.groups = 8 * layers
        self.per_tile = LANES // slots
        self.peer_tiles = -(-peers // self.per_tile)
        used = (peers - (self.peer_tiles - 1) * self.per_tile) * slots
        if used + 2 * border <= LANES:
            self.border_tile = self.peer_tiles - 1
            self.border_lane = used
        else:
            self.border_tile = self.peer_tiles
            self.border_lane = 0
        self.far_tiles = self.border_tile + 1
        self.pieces = min(LANES // slots, self.groups)
        self.piece_groups = -(-self.groups // self.pieces)
        self.border_pieces = min(LANES // border, self.groups)
        self.border_groups = -(-self.groups // self.border_pieces)

    def message(self):
        return (self.peers, 8 * self.piece_groups, LANES)

    def border_message(self):
        return (8 * self.border_groups, LANES)


def lane_ids():
    return lax.broadcasted_iota(jnp.int32, (8, LANES), 1)


def turn(block, shift):
    shift = shift % LANES
    return block if shift == 0 else pltpu.roll(block, shift, 1)


def in_block(lanes, start, size):
    return jnp.logical_and(lanes >= start, lanes < start + size)


def half(h):
    return pl.ds(h * LANES, LANES)


def rows8(start):
    return pl.ds(pl.multiple_of(start, 8), 8)


def bits_of(tile, tiles):
    return [(tile & (1 << b)) != 0 for b in range(max(tiles - 1, 1).bit_length())]


def pick_tile(values, masks):
    def pick(lowest, bit):
        if bit < 0:
            return values(lowest)
        first = pick(lowest, bit - 1)
        if lowest + (1 << bit) >= values.count:
            return first
        return jnp.where(masks[bit], pick(lowest + (1 << bit), bit - 1), first)

    return pick(0, len(masks) - 1)


class Taken:
    def __init__(self, sources, lane):
        self.sources = sources
        self.lane = lane
        self.count = len(sources)

    def __call__(self, tile):
        return jnp.take_along_axis(
            self.sources[tile], self.lane, axis=1, mode="promise_in_bounds"
        )


def gather(sources, code):
    return pick_tile(Taken(sources, code & (LANES - 1)), bits_of(code >> 7, len(sources)))


def local_sources(plan, phi, ends, g):
    w = plan.layers
    if w == 1:
        along_y = g * 64
    else:
        along_y = (g // w) * 64 + lax.rem(g, w) * 8
    starts = [g * 8, (8 - w) * 64 + g * 8, along_y, along_y + (8 - w) * 8]
    found = []
    for start in starts:
        for h in range(plan.halves):
            found.append(phi[h, rows8(start), :])
    for end in range(2):
        for h in range(plan.halves):
            if w == 1:
                found.append(phi[h, pl.ds(g * 64 + 7 * end, 8, stride=8), :])
            else:
                found.append(ends[end, h, rows8(g * 8), :])
    return found


def fill_ends(plan, phi, ends):
    w = plan.layers
    if w == 1:
        return

    @pl.loop(0, 8)
    def _(i):
        for end in range(2):
            for l in range(w):
                k = l + end * (8 - w)
                for h in range(plan.halves):
                    ends[end, h, pl.ds(i * 8 * w + l, 8, stride=w), :] = phi[
                        h, pl.ds(i * 64 + k, 8, stride=8), :
                    ]


def pack_sends(plan, phi, ends, send_code, table, outgoing, low, high):
    lanes = lane_ids()
    w = plan.layers

    @pl.loop(0, plan.groups)
    def _(g):
        sources = local_sources(plan, phi, ends, g)
        for t in range(plan.far_tiles):
            code = jnp.broadcast_to(send_code[pl.ds(t, 1), :], (8, LANES))
            table[t, rows8(g * 8), :] = gather(sources, code)

    for e in range(plan.peers):
        t, eq = divmod(e, plan.per_tile)
        for gi in range(plan.piece_groups):
            block = None
            for p in range(plan.pieces):
                g = p * plan.piece_groups + gi
                if g >= plan.groups:
                    continue
                part = turn(table[t, pl.ds(g * 8, 8), :], (p - eq) * plan.slots)
                if block is None:
                    block = part
                else:
                    block = jnp.where(lanes >= p * plan.slots, part, block)
            outgoing[e, pl.ds(gi * 8, 8), :] = block
    for side, target in enumerate((low, high)):
        for gi in range(plan.border_groups):
            block = None
            for p in range(plan.border_pieces):
                g = p * plan.border_groups + gi
                if g >= plan.groups:
                    continue
                part = turn(
                    table[plan.border_tile, pl.ds(g * 8, 8), :],
                    (p - side) * plan.border - plan.border_lane,
                )
                if block is None:
                    block = part
                else:
                    block = jnp.where(lanes >= p * plan.border, part, block)
            target[pl.ds(gi * 8, 8), :] = block


def unpack_far(plan, arrived, before, after, table):
    lanes = lane_ids()
    for g in range(plan.groups):
        p, gi = divmod(g, plan.piece_groups)
        bp, bgi = divmod(g, plan.border_groups)
        for t in range(plan.far_tiles):
            block = None
            if t < plan.peer_tiles:
                for eq in range(min(plan.per_tile, plan.peers - t * plan.per_tile)):
                    e = t * plan.per_tile + eq
                    part = turn(arrived[e, pl.ds(gi * 8, 8), :], (eq - p) * plan.slots)
                    if block is None:
                        block = part
                    else:
                        block = jnp.where(lanes >= eq * plan.slots, part, block)
            if t == plan.border_tile:
                for q, source in enumerate((before, after)):
                    start = plan.border_lane + q * plan.border
                    part = turn(source[pl.ds(bgi * 8, 8), :], start - bp * plan.border)
                    if block is None:
                        block = part
                    else:
                        block = jnp.where(lanes >= start, part, block)
            table[t, pl.ds(g * 8, 8), :] = block


def pull_halos(plan, phi, ends, table, halo_code, halos):
    @pl.loop(0, plan.groups)
    def _(g):
        sources = local_sources(plan, phi, ends, g)
        sources += [table[t, rows8(g * 8), :] for t in range(plan.far_tiles)]
        for s in range(6):
            for h in range(plan.halves):
                code = jnp.broadcast_to(halo_code[pl.ds(s, 1), half(h)], (8, LANES))
                halos[s, h, rows8(g * 8), :] = gather(sources, code)


def weno_line(q):
    first = [q[m + 1] - q[m] for m in range(13)]
    second = [first[m + 1] - first[m] for m in range(12)]
    third = [second[m + 1] - second[m] for m in range(11)]
    fourth = [(third[m] - third[m + 1]) * (1.0 / 3.0) for m in range(10)]
    bend = [t * t * (4.0 / 3.0) + weno_floor for t in third]
    backward, negated = [], []
    for m in range(9):
        s1, s2 = second[m + 1], second[m + 2]
        a = bend[m] + s1 * (s1 + third[m])
        b = bend[m + 1] + s1 * s2
        c = bend[m + 2] + s2 * (s2 - third[m + 2])
        a, b, c = a * a, b * b, c * c
        x = b * c
        z = a * b
        total = x + z + 6.0 * (a * c)
        xu = x * fourth[m]
        zu = z * fourth[m + 1]
        slope = s1 + s2
        middle = first[m + 2] + third[m + 1] * (1.0 / 12.0)
        if m < 8:
            fix = (xu + 1.5 * zu) * pl.reciprocal(total + 2.0 * z, approx=True)
            backward.append(middle + 0.25 * slope + fix)
        if m > 0:
            fix = (zu + 1.5 * xu) * pl.reciprocal(total + 2.0 * x, approx=True)
            negated.append(fix + 0.25 * slope - middle)
    found = []
    for n in range(8):
        steep = jnp.maximum(jnp.maximum(backward[n], negated[n]), 0.0)
        found.append(steep * steep)
    return found


def advect(plan, phi, speed, halos, squares, moved, sign):
    w = plan.layers
    for h in range(plan.halves):
        at = half(h)

        @pl.loop(0, 8)
        def _(i):
            line = [halos[4, h, pl.ds(i * 8 * w + l, 8, stride=w), :] for l in range(w)]
            line += [phi[h, pl.ds(i * 64 + k, 8, stride=8), :] for k in range(8)]
            line += [halos[5, h, pl.ds(i * 8 * w + l, 8, stride=w), :] for l in range(w)]
            for k, value in enumerate(weno_line(line)):
                squares[pl.ds(i * 64 + k, 8, stride=8), :] = value
            line = [halos[2, h, rows8((i * w + l) * 8), :] for l in range(w)]
            line += [phi[h, rows8(i * 64 + j * 8), :] for j in range(8)]
            line += [halos[3, h, rows8((i * w + l) * 8), :] for l in range(w)]
            for j, value in enumerate(weno_line(line)):
                squares[rows8(i * 64 + j * 8), :] += value

        @pl.loop(0, 8)
        def _(j):
            line = [halos[0, h, rows8((l * 8 + j) * 8), :] for l in range(w)]
            line += [phi[h, rows8(i * 64 + j * 8), :] for i in range(8)]
            line += [halos[1, h, rows8((l * 8 + j) * 8), :] for l in range(w)]
            for i, value in enumerate(weno_line(line)):
                here = rows8(i * 64 + j * 8)
                total = squares[here, :] + value
                value = line[w + i] - advect_scale * speed[here, at] * jnp.sqrt(total)
                moved[h, here, :] = value
                sign[h, here, :] = value * lax.rsqrt(value * value + 1.0)


def relax(plan, phi, sign, halos, moved, joined):
    row = lax.broadcasted_iota(jnp.int32, (8, LANES), 0)
    for h in range(plan.halves):
        at = half(h)

        def plane(i, previous, following):
            centre = [phi[h, rows8(i * 64 + j * 8), :] for j in range(8)]
            along_y = [halos[2, h, rows8(i * 8), :]] + centre + [halos[3, h, rows8(i * 8), :]]
            for j in range(8):
                here = rows8(i * 64 + j * 8)
                value = centre[j]
                sense = sign[h, here, :]
                facing = jnp.where(sense > 0.0, 1.0, -1.0)
                first = jnp.broadcast_to(halos[4, h, pl.ds(i * 8 + j, 1), :], (8, LANES))
                last = jnp.broadcast_to(halos[5, h, pl.ds(i * 8 + j, 1), :], (8, LANES))
                low_z = jnp.where(row == 0, first, pltpu.roll(value, 1, 0))
                high_z = jnp.where(row == 7, last, pltpu.roll(value, 7, 0))
                pairs = (
                    (previous(j), following(j)),
                    (along_y[j], along_y[j + 2]),
                    (low_z, high_z),
                )
                total = None
                for low, high in pairs:
                    steep = jnp.maximum((value - low) * facing, (value - high) * facing)
                    steep = jnp.maximum(steep, 0.0)
                    steep = steep * steep
                    total = steep if total is None else total + steep
                value = value - relax_scale * sense * (jnp.sqrt(total) - 1.0)
                if joined:
                    moved[here, at] = value
                else:
                    moved[h, here, :] = value

        def inner(i, j):
            return phi[h, rows8(i * 64 + j * 8), :]

        plane(0, lambda j: halos[0, h, pl.ds(j * 8, 8), :], lambda j: inner(1, j))

        @pl.loop(1, 7)
        def _(i):
            plane(i, lambda j: inner(i - 1, j), lambda j: inner(i + 1, j))

        plane(7, lambda j: inner(6, j), lambda j: halos[1, h, pl.ds(j * 8, 8), :])


def first_kernel(
    plan, level_set, peer_slabs, region_slabs, halo_source,
    phi, outgoing, low, high, send_code, halo_code, ends, table, padded,
):
    lanes = lane_ids()
    for h in range(plan.halves):
        phi[h] = level_set[:, half(h)]
    padded[...] = jnp.zeros_like(padded)
    padded[pl.ds(0, plan.peers), pl.ds(0, plan.slots)] = jnp.maximum(peer_slabs[...], 0)
    padded[pl.ds(plan.peers, 2), pl.ds(0, plan.border)] = region_slabs[...]

    def wide(row):
        return jnp.broadcast_to(padded[pl.ds(row, 1), :], (8, LANES))

    send_code[...] = jnp.zeros_like(send_code)
    for t in range(plan.far_tiles):
        block = jnp.zeros((8, LANES), jnp.int32)
        if t < plan.peer_tiles:
            for eq in range(min(plan.per_tile, plan.peers - t * plan.per_tile)):
                part = turn(wide(t * plan.per_tile + eq), eq * plan.slots)
                block = jnp.where(in_block(lanes, eq * plan.slots, plan.slots), part, block)
        if t == plan.border_tile:
            for side in range(2):
                start = plan.border_lane + side * plan.border
                part = turn(wide(plan.peers + side), start)
                block = jnp.where(in_block(lanes, start, plan.border), part, block)
        send_code[pl.ds(t, 1), :] = block[0:1]

    entry = halo_source[...]
    far = entry - plan.local_tiles * LANES
    tile_span = plan.per_tile * plan.slots
    tile = jnp.zeros_like(entry)
    for k in range(1, plan.peer_tiles):
        tile += (far >= k * tile_span).astype(jnp.int32)
    code = (plan.local_tiles + tile) * LANES + far - tile * tile_span
    edge = far - plan.peers * plan.slots
    edge_code = (plan.local_tiles + plan.border_tile) * LANES + plan.border_lane + edge
    code = jnp.where(edge >= 0, edge_code, code)
    halo_code[...] = jnp.where(far >= 0, code, entry)

    fill_ends(plan, phi, ends)
    pack_sends(plan, phi, ends, send_code, table, outgoing, low, high)


def advect_kernel(
    plan, sends, phi, speed, arrived, before, after, send_code, halo_code,
    moved, sign, outgoing, low, high, ends, table, halos, squares,
):
    fill_ends(plan, phi, ends)
    unpack_far(plan, arrived, before, after, table)
    pull_halos(plan, phi, ends, table, halo_code, halos)
    advect(plan, phi, speed, halos, squares, moved, sign)
    pack_sends(sends, moved, ends, send_code, table, outgoing, low, high)


def relax_kernel(plan, sends, phi, sign, arrived, before, after, send_code, halo_code, *rest):
    if sends is None:
        (moved, ends, table, halos) = rest
    else:
        (moved, outgoing, low, high, ends, table, halos) = rest
    unpack_far(plan, arrived, before, after, table)
    pull_halos(plan, phi, ends, table, halo_code, halos)
    relax(plan, phi, sign, halos, moved, sends is None)
    if sends is not None:
        fill_ends(sends, moved, ends)
        pack_sends(sends, moved, ends, send_code, table, outgoing, low, high)


def f32(shape):
    return jax.ShapeDtypeStruct(shape, jnp.float32)


def call(kernel, out_shape, scratch, flops, *operands):
    whole = pl.BlockSpec(memory_space=pltpu.VMEM)
    size = sum(x.size * 4 for x in operands) + sum(x.size * 4 for x in out_shape)
    return pl.pallas_call(
        kernel,
        out_shape=out_shape,
        in_specs=[whole] * len(operands),
        out_specs=[whole] * len(out_shape),
        scratch_shapes=scratch,
        cost_estimate=pl.CostEstimate(flops=flops, bytes_accessed=size, transcendentals=0),
        compiler_params=pltpu.CompilerParams(vmem_limit_bytes=24 * 1024 * 1024),
    )(*operands)


def exchange(outgoing, low, high):
    count = lax.axis_size("group")
    up = [(i, (i + 1) % count) for i in range(count)]
    down = [(target, source) for source, target in up]
    arrived = lax.all_to_all(outgoing, "dev", split_axis=0, concat_axis=0, tiled=True)
    before = lax.ppermute(high, "group", up)
    after = lax.ppermute(low, "group", down)
    return arrived, before, after


def per_device(level_set, speed, peer_slabs, region_slabs, halo_source):
    rows, count = level_set.shape
    peers, slots = peer_slabs.shape
    border = region_slabs.shape[1]
    wide = Plan(count, peers, slots, border, 3)
    thin = Plan(count, peers, slots, border, 1)
    code_rows = -(-wide.far_tiles // 8) * 8

    def ends(plan):
        return pltpu.VMEM((2, wide.halves, 64 * plan.layers, LANES), jnp.float32)

    def table(plan):
        return pltpu.VMEM((plan.far_tiles, 64 * plan.layers, LANES), jnp.float32)

    def halos(plan):
        return pltpu.VMEM((6, wide.halves, 64 * plan.layers, LANES), jnp.float32)

    def sent(plan):
        return [f32(plan.message()), f32(plan.border_message()), f32(plan.border_message())]

    field = f32((wide.halves, rows, LANES))
    pad_rows = -(-(peers + 2) // 8) * 8
    phi, *message, send_code, halo_code = call(
        functools.partial(first_kernel, wide),
        [field]
        + sent(wide)
        + [
            jax.ShapeDtypeStruct((code_rows, LANES), jnp.int32),
            jax.ShapeDtypeStruct(halo_source.shape, jnp.int32),
        ],
        [ends(wide), table(wide), pltpu.VMEM((pad_rows, LANES), jnp.int32)],
        1000000,
        level_set, peer_slabs, region_slabs, halo_source,
    )
    for offset_step in range(OFFSET_STEPS):
        phi, sign, *message = call(
            functools.partial(advect_kernel, wide, thin),
            [field, field] + sent(thin),
            [ends(wide), table(wide), halos(wide), pltpu.VMEM((rows, LANES), jnp.float32)],
            rows * count * 300,
            phi, speed, *exchange(*message), send_code, halo_code,
        )
        for redist_pass in range(REDIST_PASSES):
            if redist_pass < REDIST_PASSES - 1:
                sends = thin
            elif offset_step < OFFSET_STEPS - 1:
                sends = wide
            else:
                sends = None
            largest = thin if sends is None else sends
            phi, *message = call(
                functools.partial(relax_kernel, thin, sends),
                [f32((rows, count))] if sends is None else [field] + sent(sends),
                [ends(largest), table(largest), halos(thin)],
                rows * count * 60,
                phi, sign, *exchange(*message), send_code, halo_code,
            )
    return phi


def solution(mesh):
    return jax.shard_map(
        per_device,
        mesh=mesh,
        in_specs=(
            P(None, ("group", "dev")),
            P(None, ("group", "dev")),
            P(("group", "dev"), None),
            P(("group", "dev"), None),
            P(None, ("group", "dev")),
        ),
        out_specs=P(None, ("group", "dev")),
        check_vma=False,
    )
```

```python
import functools

import jax
import jax.numpy as jnp
from jax import lax
from jax.experimental import pallas as pl
from jax.experimental.pallas import tpu as pltpu
from jax.sharding import PartitionSpec as P

OFFSET_STEPS = 2
REDIST_PASSES = 2

advect_scale = 0.3
relax_scale = 0.3
weno_floor = 1e-06

LANES = 128


class Plan:
    def __init__(self, count, peers, slots, border, layers):
        self.count = count
        self.peers = peers
        self.slots = slots
        self.border = border
        self.layers = layers
        self.halves = count // LANES
        self.local_tiles = 6 * self.halves
        self.groups = 8 * layers
        self.per_tile = LANES // slots
        self.peer_tiles = -(-peers // self.per_tile)
        used = (peers - (self.peer_tiles - 1) * self.per_tile) * slots
        if used + 2 * border <= LANES:
            self.border_tile = self.peer_tiles - 1
            self.border_lane = used
        else:
            self.border_tile = self.peer_tiles
            self.border_lane = 0
        self.far_tiles = self.border_tile + 1
        self.pieces = min(LANES // slots, self.groups)
        self.piece_groups = -(-self.groups // self.pieces)
        self.border_pieces = min(LANES // border, self.groups)
        self.border_groups = -(-self.groups // self.border_pieces)

    def message(self):
        return (self.peers, 8 * self.piece_groups, LANES)

    def border_message(self):
        return (8 * self.border_groups, LANES)


def lane_ids():
    return lax.broadcasted_iota(jnp.int32, (8, LANES), 1)


def turn(block, shift):
    shift = shift % LANES
    return block if shift == 0 else pltpu.roll(block, shift, 1)


def in_block(lanes, start, size):
    return jnp.logical_and(lanes >= start, lanes < start + size)


def half(h):
    return pl.ds(h * LANES, LANES)


def rows8(start):
    return pl.ds(pl.multiple_of(start, 8), 8)


def bits_of(tile, tiles):
    return [(tile & (1 << b)) != 0 for b in range(max(tiles - 1, 1).bit_length())]


def pick_tile(values, masks):
    def pick(lowest, bit):
        if bit < 0:
            return values(lowest)
        first = pick(lowest, bit - 1)
        if lowest + (1 << bit) >= values.count:
            return first
        return jnp.where(masks[bit], pick(lowest + (1 << bit), bit - 1), first)

    return pick(0, len(masks) - 1)


class Taken:
    def __init__(self, sources, lane):
        self.sources = sources
        self.lane = lane
        self.count = len(sources)

    def __call__(self, tile):
        return jnp.take_along_axis(
            self.sources[tile], self.lane, axis=1, mode="promise_in_bounds"
        )


def gather(sources, code):
    return pick_tile(Taken(sources, code & (LANES - 1)), bits_of(code >> 7, len(sources)))


def local_sources(plan, phi, ends, g):
    w = plan.layers
    if w == 1:
        along_y = g * 64
    else:
        along_y = (g // w) * 64 + lax.rem(g, w) * 8
    starts = [g * 8, (8 - w) * 64 + g * 8, along_y, along_y + (8 - w) * 8]
    found = []
    for start in starts:
        for h in range(plan.halves):
            found.append(phi[h, rows8(start), :])
    for end in range(2):
        for h in range(plan.halves):
            if w == 1:
                found.append(phi[h, pl.ds(g * 64 + 7 * end, 8, stride=8), :])
            else:
                found.append(ends[end, h, rows8(g * 8), :])
    return found


def fill_ends(plan, phi, ends):
    w = plan.layers
    if w == 1:
        return

    @pl.loop(0, 8)
    def _(i):
        for end in range(2):
            for l in range(w):
                k = l + end * (8 - w)
                for h in range(plan.halves):
                    ends[end, h, pl.ds(i * 8 * w + l, 8, stride=w), :] = phi[
                        h, pl.ds(i * 64 + k, 8, stride=8), :
                    ]


def pack_sends(plan, phi, ends, send_code, table, outgoing, borders):
    lanes = lane_ids()
    w = plan.layers

    @pl.loop(0, plan.groups)
    def _(g):
        sources = local_sources(plan, phi, ends, g)
        for t in range(plan.far_tiles):
            code = jnp.broadcast_to(send_code[pl.ds(t, 1), :], (8, LANES))
            table[t, rows8(g * 8), :] = gather(sources, code)

    for e in range(plan.peers):
        t, eq = divmod(e, plan.per_tile)
        for gi in range(plan.piece_groups):
            block = None
            for p in range(plan.pieces):
                g = p * plan.piece_groups + gi
                if g >= plan.groups:
                    continue
                part = turn(table[t, pl.ds(g * 8, 8), :], (p - eq) * plan.slots)
                if block is None:
                    block = part
                else:
                    block = jnp.where(lanes >= p * plan.slots, part, block)
            outgoing[e, pl.ds(gi * 8, 8), :] = block
    for side in range(2):
        for gi in range(plan.border_groups):
            block = None
            for p in range(plan.border_pieces):
                g = p * plan.border_groups + gi
                if g >= plan.groups:
                    continue
                part = turn(
                    table[plan.border_tile, pl.ds(g * 8, 8), :],
                    (p - side) * plan.border - plan.border_lane,
                )
                if block is None:
                    block = part
                else:
                    block = jnp.where(lanes >= p * plan.border, part, block)
            borders[side, pl.ds(gi * 8, 8), :] = block


def unpack_far(plan, region, arrived, beside, table):
    regions = beside.shape[0]
    before = beside.at[lax.rem(region[0] + regions - 1, regions), 1]
    after = beside.at[lax.rem(region[0] + 1, regions), 0]
    lanes = lane_ids()
    for g in range(plan.groups):
        p, gi = divmod(g, plan.piece_groups)
        bp, bgi = divmod(g, plan.border_groups)
        for t in range(plan.far_tiles):
            block = None
            if t < plan.peer_tiles:
                for eq in range(min(plan.per_tile, plan.peers - t * plan.per_tile)):
                    e = t * plan.per_tile + eq
                    part = turn(arrived[e, pl.ds(gi * 8, 8), :], (eq - p) * plan.slots)
                    if block is None:
                        block = part
                    else:
                        block = jnp.where(lanes >= eq * plan.slots, part, block)
            if t == plan.border_tile:
                for q, source in enumerate((before, after)):
                    start = plan.border_lane + q * plan.border
                    part = turn(source[pl.ds(bgi * 8, 8), :], start - bp * plan.border)
                    if block is None:
                        block = part
                    else:
                        block = jnp.where(lanes >= start, part, block)
            table[t, pl.ds(g * 8, 8), :] = block


def pull_halos(plan, phi, ends, table, halo_code, halos):
    @pl.loop(0, plan.groups)
    def _(g):
        sources = local_sources(plan, phi, ends, g)
        sources += [table[t, rows8(g * 8), :] for t in range(plan.far_tiles)]
        for s in range(6):
            for h in range(plan.halves):
                code = jnp.broadcast_to(halo_code[pl.ds(s, 1), half(h)], (8, LANES))
                halos[s, h, rows8(g * 8), :] = gather(sources, code)


def weno_line(q):
    first = [q[m + 1] - q[m] for m in range(13)]
    second = [first[m + 1] - first[m] for m in range(12)]
    third = [second[m + 1] - second[m] for m in range(11)]
    fourth = [(third[m] - third[m + 1]) * (1.0 / 3.0) for m in range(10)]
    bend = [t * t * (4.0 / 3.0) + weno_floor for t in third]
    backward, negated = [], []
    for m in range(9):
        s1, s2 = second[m + 1], second[m + 2]
        a = bend[m] + s1 * (s1 + third[m])
        b = bend[m + 1] + s1 * s2
        c = bend[m + 2] + s2 * (s2 - third[m + 2])
        a, b, c = a * a, b * b, c * c
        x = b * c
        z = a * b
        total = x + z + 6.0 * (a * c)
        xu = x * fourth[m]
        zu = z * fourth[m + 1]
        slope = s1 + s2
        middle = first[m + 2] + third[m + 1] * (1.0 / 12.0)
        if m < 8:
            fix = (xu + 1.5 * zu) * pl.reciprocal(total + 2.0 * z, approx=True)
            backward.append(middle + 0.25 * slope + fix)
        if m > 0:
            fix = (zu + 1.5 * xu) * pl.reciprocal(total + 2.0 * x, approx=True)
            negated.append(fix + 0.25 * slope - middle)
    found = []
    for n in range(8):
        steep = jnp.maximum(jnp.maximum(backward[n], negated[n]), 0.0)
        found.append(steep * steep)
    return found


def advect(plan, phi, speed, halos, squares, moved, sign):
    w = plan.layers
    for h in range(plan.halves):
        at = half(h)

        @pl.loop(0, 8)
        def _(i):
            line = [halos[4, h, pl.ds(i * 8 * w + l, 8, stride=w), :] for l in range(w)]
            line += [phi[h, pl.ds(i * 64 + k, 8, stride=8), :] for k in range(8)]
            line += [halos[5, h, pl.ds(i * 8 * w + l, 8, stride=w), :] for l in range(w)]
            for k, value in enumerate(weno_line(line)):
                squares[pl.ds(i * 64 + k, 8, stride=8), :] = value
            line = [halos[2, h, rows8((i * w + l) * 8), :] for l in range(w)]
            line += [phi[h, rows8(i * 64 + j * 8), :] for j in range(8)]
            line += [halos[3, h, rows8((i * w + l) * 8), :] for l in range(w)]
            for j, value in enumerate(weno_line(line)):
                squares[rows8(i * 64 + j * 8), :] += value

        @pl.loop(0, 8)
        def _(j):
            line = [halos[0, h, rows8((l * 8 + j) * 8), :] for l in range(w)]
            line += [phi[h, rows8(i * 64 + j * 8), :] for i in range(8)]
            line += [halos[1, h, rows8((l * 8 + j) * 8), :] for l in range(w)]
            for i, value in enumerate(weno_line(line)):
                here = rows8(i * 64 + j * 8)
                total = squares[here, :] + value
                value = line[w + i] - advect_scale * speed[here, at] * jnp.sqrt(total)
                moved[h, here, :] = value
                sign[h, here, :] = value * lax.rsqrt(value * value + 1.0)


def relax(plan, phi, sign, halos, moved, joined):
    row = lax.broadcasted_iota(jnp.int32, (8, LANES), 0)
    for h in range(plan.halves):
        at = half(h)

        def plane(i, previous, following):
            centre = [phi[h, rows8(i * 64 + j * 8), :] for j in range(8)]
            along_y = [halos[2, h, rows8(i * 8), :]] + centre + [halos[3, h, rows8(i * 8), :]]
            for j in range(8):
                here = rows8(i * 64 + j * 8)
                value = centre[j]
                sense = sign[h, here, :]
                facing = jnp.where(sense > 0.0, 1.0, -1.0)
                first = jnp.broadcast_to(halos[4, h, pl.ds(i * 8 + j, 1), :], (8, LANES))
                last = jnp.broadcast_to(halos[5, h, pl.ds(i * 8 + j, 1), :], (8, LANES))
                low_z = jnp.where(row == 0, first, pltpu.roll(value, 1, 0))
                high_z = jnp.where(row == 7, last, pltpu.roll(value, 7, 0))
                pairs = (
                    (previous(j), following(j)),
                    (along_y[j], along_y[j + 2]),
                    (low_z, high_z),
                )
                total = None
                for low, high in pairs:
                    steep = jnp.maximum((value - low) * facing, (value - high) * facing)
                    steep = jnp.maximum(steep, 0.0)
                    steep = steep * steep
                    total = steep if total is None else total + steep
                value = value - relax_scale * sense * (jnp.sqrt(total) - 1.0)
                if joined:
                    moved[here, at] = value
                else:
                    moved[h, here, :] = value

        def inner(i, j):
            return phi[h, rows8(i * 64 + j * 8), :]

        plane(0, lambda j: halos[0, h, pl.ds(j * 8, 8), :], lambda j: inner(1, j))

        @pl.loop(1, 7)
        def _(i):
            plane(i, lambda j: inner(i - 1, j), lambda j: inner(i + 1, j))

        plane(7, lambda j: inner(6, j), lambda j: halos[1, h, pl.ds(j * 8, 8), :])


def first_kernel(
    plan, level_set, peer_slabs, region_slabs, halo_source,
    phi, outgoing, borders, send_code, halo_code, ends, table, padded,
):
    lanes = lane_ids()
    for h in range(plan.halves):
        phi[h] = level_set[:, half(h)]
    padded[...] = jnp.zeros_like(padded)
    padded[pl.ds(0, plan.peers), pl.ds(0, plan.slots)] = jnp.maximum(peer_slabs[...], 0)
    padded[pl.ds(plan.peers, 2), pl.ds(0, plan.border)] = region_slabs[...]

    def wide(row):
        return jnp.broadcast_to(padded[pl.ds(row, 1), :], (8, LANES))

    send_code[...] = jnp.zeros_like(send_code)
    for t in range(plan.far_tiles):
        block = jnp.zeros((8, LANES), jnp.int32)
        if t < plan.peer_tiles:
            for eq in range(min(plan.per_tile, plan.peers - t * plan.per_tile)):
                part = turn(wide(t * plan.per_tile + eq), eq * plan.slots)
                block = jnp.where(in_block(lanes, eq * plan.slots, plan.slots), part, block)
        if t == plan.border_tile:
            for side in range(2):
                start = plan.border_lane + side * plan.border
                part = turn(wide(plan.peers + side), start)
                block = jnp.where(in_block(lanes, start, plan.border), part, block)
        send_code[pl.ds(t, 1), :] = block[0:1]

    entry = halo_source[...]
    far = entry - plan.local_tiles * LANES
    tile_span = plan.per_tile * plan.slots
    tile = jnp.zeros_like(entry)
    for k in range(1, plan.peer_tiles):
        tile += (far >= k * tile_span).astype(jnp.int32)
    code = (plan.local_tiles + tile) * LANES + far - tile * tile_span
    edge = far - plan.peers * plan.slots
    edge_code = (plan.local_tiles + plan.border_tile) * LANES + plan.border_lane + edge
    code = jnp.where(edge >= 0, edge_code, code)
    halo_code[...] = jnp.where(far >= 0, code, entry)

    fill_ends(plan, phi, ends)
    pack_sends(plan, phi, ends, send_code, table, outgoing, borders)


def advect_kernel(
    plan, sends, region, phi, speed, arrived, beside, send_code, halo_code,
    moved, sign, outgoing, borders, ends, table, halos, squares,
):
    fill_ends(plan, phi, ends)
    unpack_far(plan, region, arrived, beside, table)
    pull_halos(plan, phi, ends, table, halo_code, halos)
    advect(plan, phi, speed, halos, squares, moved, sign)
    pack_sends(sends, moved, ends, send_code, table, outgoing, borders)


def relax_kernel(plan, sends, region, phi, sign, arrived, beside, send_code, halo_code, *rest):
    if sends is None:
        (moved, ends, table, halos) = rest
    else:
        (moved, outgoing, borders, ends, table, halos) = rest
    unpack_far(plan, region, arrived, beside, table)
    pull_halos(plan, phi, ends, table, halo_code, halos)
    relax(plan, phi, sign, halos, moved, sends is None)
    if sends is not None:
        fill_ends(sends, moved, ends)
        pack_sends(sends, moved, ends, send_code, table, outgoing, borders)


def f32(shape):
    return jax.ShapeDtypeStruct(shape, jnp.float32)


def call(kernel, out_shape, scratch, flops, *operands):
    whole = pl.BlockSpec(memory_space=pltpu.VMEM)
    scalar = pl.BlockSpec(memory_space=pltpu.SMEM)
    size = sum(x.size * 4 for x in operands) + sum(x.size * 4 for x in out_shape)
    return pl.pallas_call(
        kernel,
        out_shape=out_shape,
        in_specs=[scalar if x.ndim == 1 else whole for x in operands],
        out_specs=[whole] * len(out_shape),
        scratch_shapes=scratch,
        cost_estimate=pl.CostEstimate(flops=flops, bytes_accessed=size, transcendentals=0),
        compiler_params=pltpu.CompilerParams(vmem_limit_bytes=24 * 1024 * 1024),
    )(*operands)


def exchange(outgoing, borders):
    beside = lax.all_gather(borders, "group")
    arrived = lax.all_to_all(outgoing, "dev", split_axis=0, concat_axis=0, tiled=True)
    return arrived, beside


def per_device(level_set, speed, peer_slabs, region_slabs, halo_source):
    rows, count = level_set.shape
    peers, slots = peer_slabs.shape
    border = region_slabs.shape[1]
    wide = Plan(count, peers, slots, border, 3)
    thin = Plan(count, peers, slots, border, 1)
    code_rows = -(-wide.far_tiles // 8) * 8

    def ends(plan):
        return pltpu.VMEM((2, wide.halves, 64 * plan.layers, LANES), jnp.float32)

    def table(plan):
        return pltpu.VMEM((plan.far_tiles, 64 * plan.layers, LANES), jnp.float32)

    def halos(plan):
        return pltpu.VMEM((6, wide.halves, 64 * plan.layers, LANES), jnp.float32)

    def sent(plan):
        return [f32(plan.message()), f32((2,) + plan.border_message())]

    region = lax.axis_index("group").reshape(1).astype(jnp.int32)
    field = f32((wide.halves, rows, LANES))
    pad_rows = -(-(peers + 2) // 8) * 8
    phi, *message, send_code, halo_code = call(
        functools.partial(first_kernel, wide),
        [field]
        + sent(wide)
        + [
            jax.ShapeDtypeStruct((code_rows, LANES), jnp.int32),
            jax.ShapeDtypeStruct(halo_source.shape, jnp.int32),
        ],
        [ends(wide), table(wide), pltpu.VMEM((pad_rows, LANES), jnp.int32)],
        1000000,
        level_set, peer_slabs, region_slabs, halo_source,
    )
    for offset_step in range(OFFSET_STEPS):
        phi, sign, *message = call(
            functools.partial(advect_kernel, wide, thin),
            [field, field] + sent(thin),
            [ends(wide), table(wide), halos(wide), pltpu.VMEM((rows, LANES), jnp.float32)],
            rows * count * 300,
            region, phi, speed, *exchange(*message), send_code, halo_code,
        )
        for redist_pass in range(REDIST_PASSES):
            if redist_pass < REDIST_PASSES - 1:
                sends = thin
            elif offset_step < OFFSET_STEPS - 1:
                sends = wide
            else:
                sends = None
            largest = thin if sends is None else sends
            phi, *message = call(
                functools.partial(relax_kernel, thin, sends),
                [f32((rows, count))] if sends is None else [field] + sent(sends),
                [ends(largest), table(largest), halos(thin)],
                rows * count * 60,
                region, phi, sign, *exchange(*message), send_code, halo_code,
            )
    return phi


def solution(mesh):
    return jax.shard_map(
        per_device,
        mesh=mesh,
        in_specs=(
            P(None, ("group", "dev")),
            P(None, ("group", "dev")),
            P(("group", "dev"), None),
            P(("group", "dev"), None),
            P(None, ("group", "dev")),
        ),
        out_specs=P(None, ("group", "dev")),
        check_vma=False,
    )
```

```python
import functools

import jax
import jax.numpy as jnp
from jax import lax
from jax.experimental import pallas as pl
from jax.experimental.pallas import tpu as pltpu
from jax.sharding import PartitionSpec as P

OFFSET_STEPS = 2
REDIST_PASSES = 2

advect_scale = 0.3
relax_scale = 0.3
weno_floor = 1e-06

LANES = 128


class Plan:
    def __init__(self, count, peers, slots, border, layers):
        self.count = count
        self.peers = peers
        self.slots = slots
        self.border = border
        self.layers = layers
        self.halves = count // LANES
        self.local_tiles = 6 * self.halves
        self.groups = 8 * layers
        self.per_tile = LANES // slots
        self.peer_tiles = -(-peers // self.per_tile)
        used = (peers - (self.peer_tiles - 1) * self.per_tile) * slots
        if used + 2 * border <= LANES:
            self.border_tile = self.peer_tiles - 1
            self.border_lane = used
        else:
            self.border_tile = self.peer_tiles
            self.border_lane = 0
        self.far_tiles = self.border_tile + 1
        self.pieces = min(LANES // slots, self.groups)
        self.piece_groups = -(-self.groups // self.pieces)
        self.border_pieces = min(LANES // border, self.groups)
        self.border_groups = -(-self.groups // self.border_pieces)

    def message(self):
        return (self.peers, 8 * self.piece_groups, LANES)

    def border_message(self):
        return (8 * self.border_groups, LANES)


def lane_ids():
    return lax.broadcasted_iota(jnp.int32, (8, LANES), 1)


def turn(block, shift):
    shift = shift % LANES
    return block if shift == 0 else pltpu.roll(block, shift, 1)


def in_block(lanes, start, size):
    return jnp.logical_and(lanes >= start, lanes < start + size)


def half(h):
    return pl.ds(h * LANES, LANES)


def rows8(start):
    return pl.ds(pl.multiple_of(start, 8), 8)


def bits_of(tile, tiles):
    return [(tile & (1 << b)) != 0 for b in range(max(tiles - 1, 1).bit_length())]


def pick_tile(values, masks):
    def pick(lowest, bit):
        if bit < 0:
            return values(lowest)
        first = pick(lowest, bit - 1)
        if lowest + (1 << bit) >= values.count:
            return first
        return jnp.where(masks[bit], pick(lowest + (1 << bit), bit - 1), first)

    return pick(0, len(masks) - 1)


class Taken:
    def __init__(self, sources, lane):
        self.sources = sources
        self.lane = lane
        self.count = len(sources)

    def __call__(self, tile):
        return jnp.take_along_axis(
            self.sources[tile], self.lane, axis=1, mode="promise_in_bounds"
        )


def gather(sources, code):
    return pick_tile(Taken(sources, code & (LANES - 1)), bits_of(code >> 7, len(sources)))


def local_sources(plan, phi, ends, g):
    w = plan.layers
    if w == 1:
        along_y = g * 64
    else:
        along_y = (g // w) * 64 + lax.rem(g, w) * 8
    starts = [g * 8, (8 - w) * 64 + g * 8, along_y, along_y + (8 - w) * 8]
    found = []
    for start in starts:
        for h in range(plan.halves):
            found.append(phi[h, rows8(start), :])
    for end in range(2):
        for h in range(plan.halves):
            if w == 1:
                found.append(phi[h, pl.ds(g * 64 + 7 * end, 8, stride=8), :])
            else:
                found.append(ends[end, h, rows8(g * 8), :])
    return found


def fill_ends(plan, phi, ends):
    w = plan.layers
    if w == 1:
        return

    @pl.loop(0, 8)
    def _(i):
        for end in range(2):
            for l in range(w):
                k = l + end * (8 - w)
                for h in range(plan.halves):
                    ends[end, h, pl.ds(i * 8 * w + l, 8, stride=w), :] = phi[
                        h, pl.ds(i * 64 + k, 8, stride=8), :
                    ]


def pack_sends(plan, phi, ends, send_code, table, outgoing, low, high):
    lanes = lane_ids()
    w = plan.layers

    @pl.loop(0, plan.groups)
    def _(g):
        sources = local_sources(plan, phi, ends, g)
        for t in range(plan.far_tiles):
            code = jnp.broadcast_to(send_code[pl.ds(t, 1), :], (8, LANES))
            table[t, rows8(g * 8), :] = gather(sources, code)

    for e in range(plan.peers):
        t, eq = divmod(e, plan.per_tile)
        for gi in range(plan.piece_groups):
            block = None
            for p in range(plan.pieces):
                g = p * plan.piece_groups + gi
                if g >= plan.groups:
                    continue
                part = turn(table[t, pl.ds(g * 8, 8), :], (p - eq) * plan.slots)
                if block is None:
                    block = part
                else:
                    block = jnp.where(lanes >= p * plan.slots, part, block)
            outgoing[e, pl.ds(gi * 8, 8), :] = block
    for side, target in enumerate((low, high)):
        for gi in range(plan.border_groups):
            block = None
            for p in range(plan.border_pieces):
                g = p * plan.border_groups + gi
                if g >= plan.groups:
                    continue
                part = turn(
                    table[plan.border_tile, pl.ds(g * 8, 8), :],
                    (p - side) * plan.border - plan.border_lane,
                )
                if block is None:
                    block = part
                else:
                    block = jnp.where(lanes >= p * plan.border, part, block)
            target[pl.ds(gi * 8, 8), :] = block


def unpack_far(plan, arrived, before, after, table):
    lanes = lane_ids()
    for g in range(plan.groups):
        p, gi = divmod(g, plan.piece_groups)
        bp, bgi = divmod(g, plan.border_groups)
        for t in range(plan.far_tiles):
            block = None
            if t < plan.peer_tiles:
                for eq in range(min(plan.per_tile, plan.peers - t * plan.per_tile)):
                    e = t * plan.per_tile + eq
                    part = turn(arrived[e, pl.ds(gi * 8, 8), :], (eq - p) * plan.slots)
                    if block is None:
                        block = part
                    else:
                        block = jnp.where(lanes >= eq * plan.slots, part, block)
            if t == plan.border_tile:
                for q, source in enumerate((before, after)):
                    start = plan.border_lane + q * plan.border
                    part = turn(source[pl.ds(bgi * 8, 8), :], start - bp * plan.border)
                    if block is None:
                        block = part
                    else:
                        block = jnp.where(lanes >= start, part, block)
            table[t, pl.ds(g * 8, 8), :] = block


def pull_local(plan, phi, ends, halo_code, halos):
    @pl.loop(0, plan.groups)
    def _(g):
        sources = local_sources(plan, phi, ends, g)
        for s in range(6):
            for h in range(plan.halves):
                code = jnp.broadcast_to(halo_code[pl.ds(s, 1), half(h)], (8, LANES))
                halos[s, h, rows8(g * 8), :] = gather(sources, code)


def pull_far(plan, table, halo_code, near, halos):
    start = plan.local_tiles * LANES

    @pl.loop(0, plan.groups)
    def _(g):
        sources = [table[t, rows8(g * 8), :] for t in range(plan.far_tiles)]
        for s in range(6):
            for h in range(plan.halves):
                code = jnp.broadcast_to(halo_code[pl.ds(s, 1), half(h)], (8, LANES))
                far = gather(sources, code - start)
                here = near[s, h, rows8(g * 8), :]
                halos[s, h, rows8(g * 8), :] = jnp.where(code >= start, far, here)


def weno_line(q):
    first = [q[m + 1] - q[m] for m in range(13)]
    second = [first[m + 1] - first[m] for m in range(12)]
    third = [second[m + 1] - second[m] for m in range(11)]
    fourth = [(third[m] - third[m + 1]) * (1.0 / 3.0) for m in range(10)]
    bend = [t * t * (4.0 / 3.0) + weno_floor for t in third]
    backward, negated = [], []
    for m in range(9):
        s1, s2 = second[m + 1], second[m + 2]
        a = bend[m] + s1 * (s1 + third[m])
        b = bend[m + 1] + s1 * s2
        c = bend[m + 2] + s2 * (s2 - third[m + 2])
        a, b, c = a * a, b * b, c * c
        x = b * c
        z = a * b
        total = x + z + 6.0 * (a * c)
        xu = x * fourth[m]
        zu = z * fourth[m + 1]
        slope = s1 + s2
        middle = first[m + 2] + third[m + 1] * (1.0 / 12.0)
        if m < 8:
            fix = (xu + 1.5 * zu) * pl.reciprocal(total + 2.0 * z, approx=True)
            backward.append(middle + 0.25 * slope + fix)
        if m > 0:
            fix = (zu + 1.5 * xu) * pl.reciprocal(total + 2.0 * x, approx=True)
            negated.append(fix + 0.25 * slope - middle)
    found = []
    for n in range(8):
        steep = jnp.maximum(jnp.maximum(backward[n], negated[n]), 0.0)
        found.append(steep * steep)
    return found


def advect(plan, phi, speed, halos, squares, moved, sign):
    w = plan.layers
    for h in range(plan.halves):
        at = half(h)

        @pl.loop(0, 8)
        def _(i):
            line = [halos[4, h, pl.ds(i * 8 * w + l, 8, stride=w), :] for l in range(w)]
            line += [phi[h, pl.ds(i * 64 + k, 8, stride=8), :] for k in range(8)]
            line += [halos[5, h, pl.ds(i * 8 * w + l, 8, stride=w), :] for l in range(w)]
            for k, value in enumerate(weno_line(line)):
                squares[pl.ds(i * 64 + k, 8, stride=8), :] = value
            line = [halos[2, h, rows8((i * w + l) * 8), :] for l in range(w)]
            line += [phi[h, rows8(i * 64 + j * 8), :] for j in range(8)]
            line += [halos[3, h, rows8((i * w + l) * 8), :] for l in range(w)]
            for j, value in enumerate(weno_line(line)):
                squares[rows8(i * 64 + j * 8), :] += value

        @pl.loop(0, 8)
        def _(j):
            line = [halos[0, h, rows8((l * 8 + j) * 8), :] for l in range(w)]
            line += [phi[h, rows8(i * 64 + j * 8), :] for i in range(8)]
            line += [halos[1, h, rows8((l * 8 + j) * 8), :] for l in range(w)]
            for i, value in enumerate(weno_line(line)):
                here = rows8(i * 64 + j * 8)
                total = squares[here, :] + value
                value = line[w + i] - advect_scale * speed[here, at] * jnp.sqrt(total)
                moved[h, here, :] = value
                sign[h, here, :] = value * lax.rsqrt(value * value + 1.0)


def relax(plan, phi, sign, halos, moved, joined):
    row = lax.broadcasted_iota(jnp.int32, (8, LANES), 0)
    for h in range(plan.halves):
        at = half(h)

        def plane(i, previous, following):
            centre = [phi[h, rows8(i * 64 + j * 8), :] for j in range(8)]
            along_y = [halos[2, h, rows8(i * 8), :]] + centre + [halos[3, h, rows8(i * 8), :]]
            for j in range(8):
                here = rows8(i * 64 + j * 8)
                value = centre[j]
                sense = sign[h, here, :]
                facing = jnp.where(sense > 0.0, 1.0, -1.0)
                first = jnp.broadcast_to(halos[4, h, pl.ds(i * 8 + j, 1), :], (8, LANES))
                last = jnp.broadcast_to(halos[5, h, pl.ds(i * 8 + j, 1), :], (8, LANES))
                low_z = jnp.where(row == 0, first, pltpu.roll(value, 1, 0))
                high_z = jnp.where(row == 7, last, pltpu.roll(value, 7, 0))
                pairs = (
                    (previous(j), following(j)),
                    (along_y[j], along_y[j + 2]),
                    (low_z, high_z),
                )
                total = None
                for low, high in pairs:
                    steep = jnp.maximum((value - low) * facing, (value - high) * facing)
                    steep = jnp.maximum(steep, 0.0)
                    steep = steep * steep
                    total = steep if total is None else total + steep
                value = value - relax_scale * sense * (jnp.sqrt(total) - 1.0)
                if joined:
                    moved[here, at] = value
                else:
                    moved[h, here, :] = value

        def inner(i, j):
            return phi[h, rows8(i * 64 + j * 8), :]

        plane(0, lambda j: halos[0, h, pl.ds(j * 8, 8), :], lambda j: inner(1, j))

        @pl.loop(1, 7)
        def _(i):
            plane(i, lambda j: inner(i - 1, j), lambda j: inner(i + 1, j))

        plane(7, lambda j: inner(6, j), lambda j: halos[1, h, pl.ds(j * 8, 8), :])


def first_kernel(
    plan, level_set, peer_slabs, region_slabs, halo_source,
    phi, outgoing, low, high, send_code, halo_code, ends, table, padded, peer, region, entries, ready,
):
    copies = [
        pltpu.make_async_copy(source, target, ready.at[n])
        for n, (source, target) in enumerate(
            ((peer_slabs, peer), (region_slabs, region), (halo_source, entries))
        )
    ]
    for h in range(plan.halves):
        copies.append(
            pltpu.make_async_copy(level_set.at[:, half(h)], phi.at[h], ready.at[3 + h])
        )
    for copy in copies:
        copy.start()
    for copy in copies:
        copy.wait()
    lanes = lane_ids()
    padded[...] = jnp.zeros_like(padded)
    padded[pl.ds(0, plan.peers), pl.ds(0, plan.slots)] = jnp.maximum(peer[...], 0)
    padded[pl.ds(plan.peers, 2), pl.ds(0, plan.border)] = region[...]

    def wide(row):
        return jnp.broadcast_to(padded[pl.ds(row, 1), :], (8, LANES))

    send_code[...] = jnp.zeros_like(send_code)
    for t in range(plan.far_tiles):
        block = jnp.zeros((8, LANES), jnp.int32)
        if t < plan.peer_tiles:
            for eq in range(min(plan.per_tile, plan.peers - t * plan.per_tile)):
                part = turn(wide(t * plan.per_tile + eq), eq * plan.slots)
                block = jnp.where(in_block(lanes, eq * plan.slots, plan.slots), part, block)
        if t == plan.border_tile:
            for side in range(2):
                start = plan.border_lane + side * plan.border
                part = turn(wide(plan.peers + side), start)
                block = jnp.where(in_block(lanes, start, plan.border), part, block)
        send_code[pl.ds(t, 1), :] = block[0:1]

    entry = entries[...]
    far = entry - plan.local_tiles * LANES
    tile_span = plan.per_tile * plan.slots
    tile = jnp.zeros_like(entry)
    for k in range(1, plan.peer_tiles):
        tile += (far >= k * tile_span).astype(jnp.int32)
    code = (plan.local_tiles + tile) * LANES + far - tile * tile_span
    edge = far - plan.peers * plan.slots
    edge_code = (plan.local_tiles + plan.border_tile) * LANES + plan.border_lane + edge
    code = jnp.where(edge >= 0, edge_code, code)
    halo_code[...] = jnp.where(far >= 0, code, entry)

    fill_ends(plan, phi, ends)
    pack_sends(plan, phi, ends, send_code, table, outgoing, low, high)


def near_kernel(plan, phi, halo_code, near, ends):
    fill_ends(plan, phi, ends)
    pull_local(plan, phi, ends, halo_code, near)


def advect_kernel(
    plan, sends, phi, near, speed, arrived, before, after, send_code, halo_code,
    moved, sign, outgoing, low, high, ends, table, halos, squares,
):
    unpack_far(plan, arrived, before, after, table)
    pull_far(plan, table, halo_code, near, halos)
    advect(plan, phi, speed, halos, squares, moved, sign)
    pack_sends(sends, moved, ends, send_code, table, outgoing, low, high)


def relax_kernel(plan, sends, phi, near, sign, arrived, before, after, send_code, halo_code, *rest):
    if sends is None:
        (moved, ends, table, halos) = rest
    else:
        (moved, outgoing, low, high, ends, table, halos) = rest
    unpack_far(plan, arrived, before, after, table)
    pull_far(plan, table, halo_code, near, halos)
    relax(plan, phi, sign, halos, moved, sends is None)
    if sends is not None:
        fill_ends(sends, moved, ends)
        pack_sends(sends, moved, ends, send_code, table, outgoing, low, high)


def f32(shape):
    return jax.ShapeDtypeStruct(shape, jnp.float32)


def call(kernel, out_shape, scratch, flops, *operands, space=pltpu.VMEM):
    whole = pl.BlockSpec(memory_space=pltpu.VMEM)
    size = sum(x.size * 4 for x in operands) + sum(x.size * 4 for x in out_shape)
    return pl.pallas_call(
        kernel,
        out_shape=out_shape,
        in_specs=[pl.BlockSpec(memory_space=space)] * len(operands),
        out_specs=[whole] * len(out_shape),
        scratch_shapes=scratch,
        cost_estimate=pl.CostEstimate(flops=flops, bytes_accessed=size, transcendentals=0),
        compiler_params=pltpu.CompilerParams(vmem_limit_bytes=24 * 1024 * 1024),
    )(*operands)


def exchange(outgoing, low, high):
    count = lax.axis_size("group")
    up = [(i, (i + 1) % count) for i in range(count)]
    down = [(target, source) for source, target in up]
    arrived = lax.all_to_all(outgoing, "dev", split_axis=0, concat_axis=0, tiled=True)
    before = lax.ppermute(high, "group", up)
    after = lax.ppermute(low, "group", down)
    return arrived, before, after


def per_device(level_set, speed, peer_slabs, region_slabs, halo_source):
    rows, count = level_set.shape
    peers, slots = peer_slabs.shape
    border = region_slabs.shape[1]
    wide = Plan(count, peers, slots, border, 3)
    thin = Plan(count, peers, slots, border, 1)
    code_rows = -(-wide.far_tiles // 8) * 8

    def ends(plan):
        return pltpu.VMEM((2, wide.halves, 64 * plan.layers, LANES), jnp.float32)

    def table(plan):
        return pltpu.VMEM((plan.far_tiles, 64 * plan.layers, LANES), jnp.float32)

    def halos(plan):
        return pltpu.VMEM((6, wide.halves, 64 * plan.layers, LANES), jnp.float32)

    def sent(plan):
        return [f32(plan.message()), f32(plan.border_message()), f32(plan.border_message())]

    field = f32((wide.halves, rows, LANES))
    pad_rows = -(-(peers + 2) // 8) * 8
    phi, *message, send_code, halo_code = call(
        functools.partial(first_kernel, wide),
        [field]
        + sent(wide)
        + [
            jax.ShapeDtypeStruct((code_rows, LANES), jnp.int32),
            jax.ShapeDtypeStruct(halo_source.shape, jnp.int32),
        ],
        [
            ends(wide),
            table(wide),
            pltpu.VMEM((pad_rows, LANES), jnp.int32),
            pltpu.VMEM(peer_slabs.shape, jnp.int32),
            pltpu.VMEM(region_slabs.shape, jnp.int32),
            pltpu.VMEM(halo_source.shape, jnp.int32),
            pltpu.SemaphoreType.DMA((3 + wide.halves,)),
        ],
        1000000,
        *(
            pltpu.with_memory_space_constraint(x, pltpu.HBM)
            for x in (level_set, peer_slabs, region_slabs, halo_source)
        ),
        space=pltpu.HBM,
    )

    def near_halos(plan, phi):
        return call(
            functools.partial(near_kernel, plan),
            [f32((6, plan.halves, 64 * plan.layers, LANES))],
            [ends(plan)],
            rows * count * 100 * plan.layers,
            phi, halo_code,
        )[0]

    for offset_step in range(OFFSET_STEPS):
        phi, sign, *message = call(
            functools.partial(advect_kernel, wide, thin),
            [field, field] + sent(thin),
            [ends(wide), table(wide), halos(wide), pltpu.VMEM((rows, LANES), jnp.float32)],
            rows * count * 300,
            phi, near_halos(wide, phi), speed, *exchange(*message), send_code, halo_code,
        )
        for redist_pass in range(REDIST_PASSES):
            if redist_pass < REDIST_PASSES - 1:
                sends = thin
            elif offset_step < OFFSET_STEPS - 1:
                sends = wide
            else:
                sends = None
            largest = thin if sends is None else sends
            phi, *message = call(
                functools.partial(relax_kernel, thin, sends),
                [f32((rows, count))] if sends is None else [field] + sent(sends),
                [ends(largest), table(largest), halos(thin)],
                rows * count * 60,
                phi, near_halos(thin, phi), sign, *exchange(*message), send_code, halo_code,
            )
    return phi


def solution(mesh):
    return jax.shard_map(
        per_device,
        mesh=mesh,
        in_specs=(
            P(None, ("group", "dev")),
            P(None, ("group", "dev")),
            P(("group", "dev"), None),
            P(("group", "dev"), None),
            P(None, ("group", "dev")),
        ),
        out_specs=P(None, ("group", "dev")),
        check_vma=False,
    )
```

```python
import functools

import jax
import jax.numpy as jnp
from jax import lax
from jax.experimental import pallas as pl
from jax.experimental.pallas import tpu as pltpu
from jax.sharding import PartitionSpec as P

OFFSET_STEPS = 2
REDIST_PASSES = 2

advect_scale = 0.3
relax_scale = 0.3
weno_floor = 1e-06

LANES = 128


class Plan:
    def __init__(self, count, peers, slots, border, layers):
        self.count = count
        self.peers = peers
        self.slots = slots
        self.border = border
        self.layers = layers
        self.halves = count // LANES
        self.local_tiles = 6 * self.halves
        self.groups = 8 * layers
        self.per_tile = LANES // slots
        self.peer_tiles = -(-peers // self.per_tile)
        used = (peers - (self.peer_tiles - 1) * self.per_tile) * slots
        if used + 2 * border <= LANES:
            self.border_tile = self.peer_tiles - 1
            self.border_lane = used
        else:
            self.border_tile = self.peer_tiles
            self.border_lane = 0
        self.far_tiles = self.border_tile + 1
        self.pieces = min(LANES // slots, self.groups)
        self.piece_groups = -(-self.groups // self.pieces)
        self.border_pieces = min(LANES // border, self.groups)
        self.border_groups = -(-self.groups // self.border_pieces)

    def message(self):
        return (self.peers, 8 * self.piece_groups, LANES)

    def border_message(self):
        return (8 * self.border_groups, LANES)


def lane_ids():
    return lax.broadcasted_iota(jnp.int32, (8, LANES), 1)


def turn(block, shift):
    shift = shift % LANES
    return block if shift == 0 else pltpu.roll(block, shift, 1)


def in_block(lanes, start, size):
    return jnp.logical_and(lanes >= start, lanes < start + size)


def half(h):
    return pl.ds(h * LANES, LANES)


def rows8(start):
    return pl.ds(pl.multiple_of(start, 8), 8)


def bits_of(tile, tiles):
    return [(tile & (1 << b)) != 0 for b in range(max(tiles - 1, 1).bit_length())]


def pick_tile(values, masks):
    def pick(lowest, bit):
        if bit < 0:
            return values(lowest)
        first = pick(lowest, bit - 1)
        if lowest + (1 << bit) >= values.count:
            return first
        return jnp.where(masks[bit], pick(lowest + (1 << bit), bit - 1), first)

    return pick(0, len(masks) - 1)


class Taken:
    def __init__(self, sources, lane):
        self.sources = sources
        self.lane = lane
        self.count = len(sources)

    def __call__(self, tile):
        return jnp.take_along_axis(
            self.sources[tile], self.lane, axis=1, mode="promise_in_bounds"
        )


def gather(sources, code):
    return pick_tile(Taken(sources, code & (LANES - 1)), bits_of(code >> 7, len(sources)))


def local_sources(plan, phi, ends, g):
    w = plan.layers
    if w == 1:
        along_y = g * 64
    else:
        along_y = (g // w) * 64 + lax.rem(g, w) * 8
    starts = [g * 8, (8 - w) * 64 + g * 8, along_y, along_y + (8 - w) * 8]
    found = []
    for start in starts:
        for h in range(plan.halves):
            found.append(phi[h, rows8(start), :])
    for end in range(2):
        for h in range(plan.halves):
            if w == 1:
                found.append(phi[h, pl.ds(g * 64 + 7 * end, 8, stride=8), :])
            else:
                found.append(ends[end, h, rows8(g * 8), :])
    return found


def fill_ends(plan, phi, ends):
    w = plan.layers
    if w == 1:
        return

    @pl.loop(0, 8)
    def _(i):
        for end in range(2):
            for l in range(w):
                k = l + end * (8 - w)
                for h in range(plan.halves):
                    ends[end, h, pl.ds(i * 8 * w + l, 8, stride=w), :] = phi[
                        h, pl.ds(i * 64 + k, 8, stride=8), :
                    ]


def pack_sends(plan, phi, ends, send_code, table, outgoing, low, high):
    lanes = lane_ids()
    w = plan.layers

    @pl.loop(0, plan.groups)
    def _(g):
        sources = local_sources(plan, phi, ends, g)
        for t in range(plan.far_tiles):
            code = jnp.broadcast_to(send_code[pl.ds(t, 1), :], (8, LANES))
            table[t, rows8(g * 8), :] = gather(sources, code)

    for e in range(plan.peers):
        t, eq = divmod(e, plan.per_tile)
        for gi in range(plan.piece_groups):
            block = None
            for p in range(plan.pieces):
                g = p * plan.piece_groups + gi
                if g >= plan.groups:
                    continue
                part = turn(table[t, pl.ds(g * 8, 8), :], (p - eq) * plan.slots)
                if block is None:
                    block = part
                else:
                    block = jnp.where(lanes >= p * plan.slots, part, block)
            outgoing[e, pl.ds(gi * 8, 8), :] = block
    for side, target in enumerate((low, high)):
        for gi in range(plan.border_groups):
            block = None
            for p in range(plan.border_pieces):
                g = p * plan.border_groups + gi
                if g >= plan.groups:
                    continue
                part = turn(
                    table[plan.border_tile, pl.ds(g * 8, 8), :],
                    (p - side) * plan.border - plan.border_lane,
                )
                if block is None:
                    block = part
                else:
                    block = jnp.where(lanes >= p * plan.border, part, block)
            target[pl.ds(gi * 8, 8), :] = block


def unpack_far(plan, arrived, before, after, table):
    lanes = lane_ids()
    for g in range(plan.groups):
        p, gi = divmod(g, plan.piece_groups)
        bp, bgi = divmod(g, plan.border_groups)
        for t in range(plan.far_tiles):
            block = None
            if t < plan.peer_tiles:
                for eq in range(min(plan.per_tile, plan.peers - t * plan.per_tile)):
                    e = t * plan.per_tile + eq
                    part = turn(arrived[e, pl.ds(gi * 8, 8), :], (eq - p) * plan.slots)
                    if block is None:
                        block = part
                    else:
                        block = jnp.where(lanes >= eq * plan.slots, part, block)
            if t == plan.border_tile:
                for q, source in enumerate((before, after)):
                    start = plan.border_lane + q * plan.border
                    part = turn(source[pl.ds(bgi * 8, 8), :], start - bp * plan.border)
                    if block is None:
                        block = part
                    else:
                        block = jnp.where(lanes >= start, part, block)
            table[t, pl.ds(g * 8, 8), :] = block


def pull_local(plan, phi, ends, halo_code, halos):
    @pl.loop(0, plan.groups)
    def _(g):
        sources = local_sources(plan, phi, ends, g)
        for s in range(6):
            for h in range(plan.halves):
                code = jnp.broadcast_to(halo_code[pl.ds(s, 1), half(h)], (8, LANES))
                halos[s, h, rows8(g * 8), :] = gather(sources, code)


def pull_far(plan, table, halo_code, near, halos):
    start = plan.local_tiles * LANES

    @pl.loop(0, plan.groups)
    def _(g):
        sources = [table[t, rows8(g * 8), :] for t in range(plan.far_tiles)]
        for s in range(6):
            for h in range(plan.halves):
                code = jnp.broadcast_to(halo_code[pl.ds(s, 1), half(h)], (8, LANES))
                far = gather(sources, code - start)
                here = near[s, h, rows8(g * 8), :]
                halos[s, h, rows8(g * 8), :] = jnp.where(code >= start, far, here)


def weno_line(q):
    first = [q[m + 1] - q[m] for m in range(13)]
    second = [first[m + 1] - first[m] for m in range(12)]
    third = [second[m + 1] - second[m] for m in range(11)]
    fourth = [(third[m] - third[m + 1]) * (1.0 / 3.0) for m in range(10)]
    bend = [t * t * (4.0 / 3.0) + weno_floor for t in third]
    backward, negated = [], []
    for m in range(9):
        s1, s2 = second[m + 1], second[m + 2]
        a = bend[m] + s1 * (s1 + third[m])
        b = bend[m + 1] + s1 * s2
        c = bend[m + 2] + s2 * (s2 - third[m + 2])
        a, b, c = a * a, b * b, c * c
        x = b * c
        z = a * b
        total = x + z + 6.0 * (a * c)
        xu = x * fourth[m]
        zu = z * fourth[m + 1]
        slope = s1 + s2
        middle = first[m + 2] + third[m + 1] * (1.0 / 12.0)
        if m < 8:
            fix = (xu + 1.5 * zu) * pl.reciprocal(total + 2.0 * z, approx=True)
            backward.append(middle + 0.25 * slope + fix)
        if m > 0:
            fix = (zu + 1.5 * xu) * pl.reciprocal(total + 2.0 * x, approx=True)
            negated.append(fix + 0.25 * slope - middle)
    found = []
    for n in range(8):
        steep = jnp.maximum(jnp.maximum(backward[n], negated[n]), 0.0)
        found.append(steep * steep)
    return found


def advect(plan, phi, speed, halos, squares, moved, sign):
    w = plan.layers
    for h in range(plan.halves):
        at = half(h)

        @pl.loop(0, 8)
        def _(i):
            line = [halos[4, h, pl.ds(i * 8 * w + l, 8, stride=w), :] for l in range(w)]
            line += [phi[h, pl.ds(i * 64 + k, 8, stride=8), :] for k in range(8)]
            line += [halos[5, h, pl.ds(i * 8 * w + l, 8, stride=w), :] for l in range(w)]
            for k, value in enumerate(weno_line(line)):
                squares[pl.ds(i * 64 + k, 8, stride=8), :] = value
            line = [halos[2, h, rows8((i * w + l) * 8), :] for l in range(w)]
            line += [phi[h, rows8(i * 64 + j * 8), :] for j in range(8)]
            line += [halos[3, h, rows8((i * w + l) * 8), :] for l in range(w)]
            for j, value in enumerate(weno_line(line)):
                squares[rows8(i * 64 + j * 8), :] += value

        @pl.loop(0, 8)
        def _(j):
            line = [halos[0, h, rows8((l * 8 + j) * 8), :] for l in range(w)]
            line += [phi[h, rows8(i * 64 + j * 8), :] for i in range(8)]
            line += [halos[1, h, rows8((l * 8 + j) * 8), :] for l in range(w)]
            for i, value in enumerate(weno_line(line)):
                here = rows8(i * 64 + j * 8)
                total = squares[here, :] + value
                value = line[w + i] - advect_scale * speed[here, at] * jnp.sqrt(total)
                moved[h, here, :] = value
                sign[h, here, :] = value * lax.rsqrt(value * value + 1.0)


def relax(plan, phi, sign, halos, moved, joined):
    row = lax.broadcasted_iota(jnp.int32, (8, LANES), 0)
    for h in range(plan.halves):
        at = half(h)

        def plane(i, previous, following):
            centre = [phi[h, rows8(i * 64 + j * 8), :] for j in range(8)]
            along_y = [halos[2, h, rows8(i * 8), :]] + centre + [halos[3, h, rows8(i * 8), :]]
            for j in range(8):
                here = rows8(i * 64 + j * 8)
                value = centre[j]
                sense = sign[h, here, :]
                facing = jnp.where(sense > 0.0, 1.0, -1.0)
                first = jnp.broadcast_to(halos[4, h, pl.ds(i * 8 + j, 1), :], (8, LANES))
                last = jnp.broadcast_to(halos[5, h, pl.ds(i * 8 + j, 1), :], (8, LANES))
                low_z = jnp.where(row == 0, first, pltpu.roll(value, 1, 0))
                high_z = jnp.where(row == 7, last, pltpu.roll(value, 7, 0))
                pairs = (
                    (previous(j), following(j)),
                    (along_y[j], along_y[j + 2]),
                    (low_z, high_z),
                )
                total = None
                for low, high in pairs:
                    steep = jnp.maximum((value - low) * facing, (value - high) * facing)
                    steep = jnp.maximum(steep, 0.0)
                    steep = steep * steep
                    total = steep if total is None else total + steep
                value = value - relax_scale * sense * (jnp.sqrt(total) - 1.0)
                if joined:
                    moved[here, at] = value
                else:
                    moved[h, here, :] = value

        def inner(i, j):
            return phi[h, rows8(i * 64 + j * 8), :]

        plane(0, lambda j: halos[0, h, pl.ds(j * 8, 8), :], lambda j: inner(1, j))

        @pl.loop(1, 7)
        def _(i):
            plane(i, lambda j: inner(i - 1, j), lambda j: inner(i + 1, j))

        plane(7, lambda j: inner(6, j), lambda j: halos[1, h, pl.ds(j * 8, 8), :])


def first_kernel(
    plan, level_set, peer_slabs, region_slabs, halo_source,
    phi, outgoing, low, high, send_code, halo_code, ends, table, padded, peer, region, entries, ready,
):
    copies = [
        pltpu.make_async_copy(source, target, ready.at[n])
        for n, (source, target) in enumerate(
            ((peer_slabs, peer), (region_slabs, region), (halo_source, entries))
        )
    ]
    for h in range(plan.halves):
        copies.append(
            pltpu.make_async_copy(level_set.at[:, half(h)], phi.at[h], ready.at[3 + h])
        )
    for copy in copies:
        copy.start()
    for copy in copies:
        copy.wait()
    lanes = lane_ids()
    padded[...] = jnp.zeros_like(padded)
    padded[pl.ds(0, plan.peers), pl.ds(0, plan.slots)] = jnp.maximum(peer[...], 0)
    padded[pl.ds(plan.peers, 2), pl.ds(0, plan.border)] = region[...]

    def wide(row):
        return jnp.broadcast_to(padded[pl.ds(row, 1), :], (8, LANES))

    send_code[...] = jnp.zeros_like(send_code)
    for t in range(plan.far_tiles):
        block = jnp.zeros((8, LANES), jnp.int32)
        if t < plan.peer_tiles:
            for eq in range(min(plan.per_tile, plan.peers - t * plan.per_tile)):
                part = turn(wide(t * plan.per_tile + eq), eq * plan.slots)
                block = jnp.where(in_block(lanes, eq * plan.slots, plan.slots), part, block)
        if t == plan.border_tile:
            for side in range(2):
                start = plan.border_lane + side * plan.border
                part = turn(wide(plan.peers + side), start)
                block = jnp.where(in_block(lanes, start, plan.border), part, block)
        send_code[pl.ds(t, 1), :] = block[0:1]

    entry = entries[...]
    far = entry - plan.local_tiles * LANES
    tile_span = plan.per_tile * plan.slots
    tile = jnp.zeros_like(entry)
    for k in range(1, plan.peer_tiles):
        tile += (far >= k * tile_span).astype(jnp.int32)
    code = (plan.local_tiles + tile) * LANES + far - tile * tile_span
    edge = far - plan.peers * plan.slots
    edge_code = (plan.local_tiles + plan.border_tile) * LANES + plan.border_lane + edge
    code = jnp.where(edge >= 0, edge_code, code)
    halo_code[...] = jnp.where(far >= 0, code, entry)

    fill_ends(plan, phi, ends)
    pack_sends(plan, phi, ends, send_code, table, outgoing, low, high)


def near_kernel(plan, phi, halo_code, near, ends):
    fill_ends(plan, phi, ends)
    pull_local(plan, phi, ends, halo_code, near)


def advect_kernel(
    plan, sends, phi, near, speed, arrived, before, after, send_code, halo_code,
    moved, sign, outgoing, low, high, ends, table, halos, squares,
):
    unpack_far(plan, arrived, before, after, table)
    pull_far(plan, table, halo_code, near, halos)
    advect(plan, phi, speed, halos, squares, moved, sign)
    pack_sends(sends, moved, ends, send_code, table, outgoing, low, high)


def relax_kernel(plan, sends, phi, near, sign, arrived, before, after, send_code, halo_code, *rest):
    if sends is None:
        (moved, ends, table, halos) = rest
    else:
        (moved, outgoing, low, high, ends, table, halos) = rest
    unpack_far(plan, arrived, before, after, table)
    pull_far(plan, table, halo_code, near, halos)
    relax(plan, phi, sign, halos, moved, sends is None)
    if sends is not None:
        fill_ends(sends, moved, ends)
        pack_sends(sends, moved, ends, send_code, table, outgoing, low, high)


def f32(shape):
    return jax.ShapeDtypeStruct(shape, jnp.float32)


def call(kernel, out_shape, scratch, flops, *operands, space=pltpu.VMEM):
    whole = pl.BlockSpec(memory_space=pltpu.VMEM)
    size = sum(x.size * 4 for x in operands) + sum(x.size * 4 for x in out_shape)
    return pl.pallas_call(
        kernel,
        out_shape=out_shape,
        in_specs=[pl.BlockSpec(memory_space=space)] * len(operands),
        out_specs=[whole] * len(out_shape),
        scratch_shapes=scratch,
        cost_estimate=pl.CostEstimate(flops=flops, bytes_accessed=size, transcendentals=0),
        compiler_params=pltpu.CompilerParams(vmem_limit_bytes=8 * 1024 * 1024),
    )(*operands)


def exchange(outgoing, low, high):
    count = lax.axis_size("group")
    up = [(i, (i + 1) % count) for i in range(count)]
    down = [(target, source) for source, target in up]
    arrived = lax.all_to_all(outgoing, "dev", split_axis=0, concat_axis=0, tiled=True)
    before = lax.ppermute(high, "group", up)
    after = lax.ppermute(low, "group", down)
    return arrived, before, after


def per_device(level_set, speed, peer_slabs, region_slabs, halo_source):
    rows, count = level_set.shape
    peers, slots = peer_slabs.shape
    border = region_slabs.shape[1]
    wide = Plan(count, peers, slots, border, 3)
    thin = Plan(count, peers, slots, border, 1)
    code_rows = -(-wide.far_tiles // 8) * 8

    def ends(plan):
        return pltpu.VMEM((2, wide.halves, 64 * plan.layers, LANES), jnp.float32)

    def table(plan):
        return pltpu.VMEM((plan.far_tiles, 64 * plan.layers, LANES), jnp.float32)

    def halos(plan):
        return pltpu.VMEM((6, wide.halves, 64 * plan.layers, LANES), jnp.float32)

    def sent(plan):
        return [f32(plan.message()), f32(plan.border_message()), f32(plan.border_message())]

    field = f32((wide.halves, rows, LANES))
    pad_rows = -(-(peers + 2) // 8) * 8
    phi, *message, send_code, halo_code = call(
        functools.partial(first_kernel, wide),
        [field]
        + sent(wide)
        + [
            jax.ShapeDtypeStruct((code_rows, LANES), jnp.int32),
            jax.ShapeDtypeStruct(halo_source.shape, jnp.int32),
        ],
        [
            ends(wide),
            table(wide),
            pltpu.VMEM((pad_rows, LANES), jnp.int32),
            pltpu.VMEM(peer_slabs.shape, jnp.int32),
            pltpu.VMEM(region_slabs.shape, jnp.int32),
            pltpu.VMEM(halo_source.shape, jnp.int32),
            pltpu.SemaphoreType.DMA((3 + wide.halves,)),
        ],
        1000000,
        *(
            pltpu.with_memory_space_constraint(x, pltpu.HBM)
            for x in (level_set, peer_slabs, region_slabs, halo_source)
        ),
        space=pltpu.HBM,
    )

    def near_halos(plan, phi):
        return call(
            functools.partial(near_kernel, plan),
            [f32((6, plan.halves, 64 * plan.layers, LANES))],
            [ends(plan)],
            rows * count * 100 * plan.layers,
            phi, halo_code,
        )[0]

    for offset_step in range(OFFSET_STEPS):
        phi, sign, *message = call(
            functools.partial(advect_kernel, wide, thin),
            [field, field] + sent(thin),
            [ends(wide), table(wide), halos(wide), pltpu.VMEM((rows, LANES), jnp.float32)],
            rows * count * 300,
            phi, near_halos(wide, phi), speed, *exchange(*message), send_code, halo_code,
        )
        for redist_pass in range(REDIST_PASSES):
            if redist_pass < REDIST_PASSES - 1:
                sends = thin
            elif offset_step < OFFSET_STEPS - 1:
                sends = wide
            else:
                sends = None
            largest = thin if sends is None else sends
            phi, *message = call(
                functools.partial(relax_kernel, thin, sends),
                [f32((rows, count))] if sends is None else [field] + sent(sends),
                [ends(largest), table(largest), halos(thin)],
                rows * count * 60,
                phi, near_halos(thin, phi), sign, *exchange(*message), send_code, halo_code,
            )
    return phi


def solution(mesh):
    return jax.shard_map(
        per_device,
        mesh=mesh,
        in_specs=(
            P(None, ("group", "dev")),
            P(None, ("group", "dev")),
            P(("group", "dev"), None),
            P(("group", "dev"), None),
            P(None, ("group", "dev")),
        ),
        out_specs=P(None, ("group", "dev")),
        check_vma=False,
    )
```

```python
import functools

import jax
import jax.numpy as jnp
from jax import lax
from jax.experimental import pallas as pl
from jax.experimental.pallas import tpu as pltpu
from jax.sharding import PartitionSpec as P

OFFSET_STEPS = 2
REDIST_PASSES = 2

advect_scale = 0.3
relax_scale = 0.3
weno_floor = 1e-06

LANES = 128


class Plan:
    def __init__(self, count, peers, slots, border, layers):
        self.count = count
        self.peers = peers
        self.slots = slots
        self.border = border
        self.layers = layers
        self.halves = count // LANES
        self.local_tiles = 6 * self.halves
        self.groups = 8 * layers
        self.per_tile = LANES // slots
        self.peer_tiles = -(-peers // self.per_tile)
        used = (peers - (self.peer_tiles - 1) * self.per_tile) * slots
        if used + 2 * border <= LANES:
            self.border_tile = self.peer_tiles - 1
            self.border_lane = used
        else:
            self.border_tile = self.peer_tiles
            self.border_lane = 0
        self.far_tiles = self.border_tile + 1
        self.pieces = min(LANES // slots, self.groups)
        self.piece_groups = -(-self.groups // self.pieces)
        self.border_pieces = min(LANES // border, self.groups)
        self.border_groups = -(-self.groups // self.border_pieces)

    def message(self):
        return (self.peers, 8 * self.piece_groups, LANES)

    def border_message(self):
        return (8 * self.border_groups, LANES)


def lane_ids():
    return lax.broadcasted_iota(jnp.int32, (8, LANES), 1)


def turn(block, shift):
    shift = shift % LANES
    return block if shift == 0 else pltpu.roll(block, shift, 1)


def in_block(lanes, start, size):
    return jnp.logical_and(lanes >= start, lanes < start + size)


def half(h):
    return pl.ds(h * LANES, LANES)


def rows8(start):
    return pl.ds(pl.multiple_of(start, 8), 8)


def bits_of(tile, tiles):
    return [(tile & (1 << b)) != 0 for b in range(max(tiles - 1, 1).bit_length())]


def pick_tile(values, masks):
    def pick(lowest, bit):
        if bit < 0:
            return values(lowest)
        first = pick(lowest, bit - 1)
        if lowest + (1 << bit) >= values.count:
            return first
        return jnp.where(masks[bit], pick(lowest + (1 << bit), bit - 1), first)

    return pick(0, len(masks) - 1)


class Taken:
    def __init__(self, sources, lane):
        self.sources = sources
        self.lane = lane
        self.count = len(sources)

    def __call__(self, tile):
        return jnp.take_along_axis(
            self.sources[tile], self.lane, axis=1, mode="promise_in_bounds"
        )


def gather(sources, code):
    return pick_tile(Taken(sources, code & (LANES - 1)), bits_of(code >> 7, len(sources)))


def local_sources(plan, phi, ends, g):
    w = plan.layers
    if w == 1:
        along_y = g * 64
    else:
        along_y = (g // w) * 64 + lax.rem(g, w) * 8
    starts = [g * 8, (8 - w) * 64 + g * 8, along_y, along_y + (8 - w) * 8]
    found = []
    for start in starts:
        for h in range(plan.halves):
            found.append(phi[h, rows8(start), :])
    for end in range(2):
        for h in range(plan.halves):
            if w == 1:
                found.append(phi[h, pl.ds(g * 64 + 7 * end, 8, stride=8), :])
            else:
                found.append(ends[end, h, rows8(g * 8), :])
    return found


def fill_ends(plan, phi, ends):
    w = plan.layers
    if w == 1:
        return

    @pl.loop(0, 8)
    def _(i):
        for end in range(2):
            for l in range(w):
                k = l + end * (8 - w)
                for h in range(plan.halves):
                    ends[end, h, pl.ds(i * 8 * w + l, 8, stride=w), :] = phi[
                        h, pl.ds(i * 64 + k, 8, stride=8), :
                    ]


def pack_sends(plan, phi, ends, send_code, table, outgoing, low, high):
    lanes = lane_ids()
    w = plan.layers

    @pl.loop(0, plan.groups)
    def _(g):
        sources = local_sources(plan, phi, ends, g)
        for t in range(plan.far_tiles):
            code = jnp.broadcast_to(send_code[pl.ds(t, 1), :], (8, LANES))
            table[t, rows8(g * 8), :] = gather(sources, code)

    for e in range(plan.peers):
        t, eq = divmod(e, plan.per_tile)
        for gi in range(plan.piece_groups):
            block = None
            for p in range(plan.pieces):
                g = p * plan.piece_groups + gi
                if g >= plan.groups:
                    continue
                part = turn(table[t, pl.ds(g * 8, 8), :], (p - eq) * plan.slots)
                if block is None:
                    block = part
                else:
                    block = jnp.where(lanes >= p * plan.slots, part, block)
            outgoing[e, pl.ds(gi * 8, 8), :] = block
    for side, target in enumerate((low, high)):
        for gi in range(plan.border_groups):
            block = None
            for p in range(plan.border_pieces):
                g = p * plan.border_groups + gi
                if g >= plan.groups:
                    continue
                part = turn(
                    table[plan.border_tile, pl.ds(g * 8, 8), :],
                    (p - side) * plan.border - plan.border_lane,
                )
                if block is None:
                    block = part
                else:
                    block = jnp.where(lanes >= p * plan.border, part, block)
            target[pl.ds(gi * 8, 8), :] = block


def unpack_far(plan, arrived, before, after, table):
    lanes = lane_ids()
    for g in range(plan.groups):
        p, gi = divmod(g, plan.piece_groups)
        bp, bgi = divmod(g, plan.border_groups)
        for t in range(plan.far_tiles):
            block = None
            if t < plan.peer_tiles:
                for eq in range(min(plan.per_tile, plan.peers - t * plan.per_tile)):
                    e = t * plan.per_tile + eq
                    part = turn(arrived[e, pl.ds(gi * 8, 8), :], (eq - p) * plan.slots)
                    if block is None:
                        block = part
                    else:
                        block = jnp.where(lanes >= eq * plan.slots, part, block)
            if t == plan.border_tile:
                for q, source in enumerate((before, after)):
                    start = plan.border_lane + q * plan.border
                    part = turn(source[pl.ds(bgi * 8, 8), :], start - bp * plan.border)
                    if block is None:
                        block = part
                    else:
                        block = jnp.where(lanes >= start, part, block)
            table[t, pl.ds(g * 8, 8), :] = block


def pull_local(plan, phi, ends, halo_code, halos):
    @pl.loop(0, plan.groups)
    def _(g):
        sources = local_sources(plan, phi, ends, g)
        for s in range(6):
            for h in range(plan.halves):
                code = jnp.broadcast_to(halo_code[pl.ds(s, 1), half(h)], (8, LANES))
                halos[s, h, rows8(g * 8), :] = gather(sources, code)


def pull_far(plan, table, halo_code, near, halos):
    start = plan.local_tiles * LANES

    @pl.loop(0, plan.groups)
    def _(g):
        sources = [table[t, rows8(g * 8), :] for t in range(plan.far_tiles)]
        for s in range(6):
            for h in range(plan.halves):
                code = jnp.broadcast_to(halo_code[pl.ds(s, 1), half(h)], (8, LANES))
                far = gather(sources, code - start)
                here = near[s, h, rows8(g * 8), :]
                halos[s, h, rows8(g * 8), :] = jnp.where(code >= start, far, here)


def weno_line(q):
    first = [q[m + 1] - q[m] for m in range(13)]
    second = [first[m + 1] - first[m] for m in range(12)]
    third = [second[m + 1] - second[m] for m in range(11)]
    fourth = [(third[m] - third[m + 1]) * (1.0 / 3.0) for m in range(10)]
    bend = [t * t * (4.0 / 3.0) + weno_floor for t in third]
    backward, negated = [], []
    for m in range(9):
        s1, s2 = second[m + 1], second[m + 2]
        a = bend[m] + s1 * (s1 + third[m])
        b = bend[m + 1] + s1 * s2
        c = bend[m + 2] + s2 * (s2 - third[m + 2])
        a, b, c = a * a, b * b, c * c
        x = b * c
        z = a * b
        total = x + z + 6.0 * (a * c)
        xu = x * fourth[m]
        zu = z * fourth[m + 1]
        slope = s1 + s2
        middle = first[m + 2] + third[m + 1] * (1.0 / 12.0)
        if m < 8:
            fix = (xu + 1.5 * zu) * pl.reciprocal(total + 2.0 * z, approx=True)
            backward.append(middle + 0.25 * slope + fix)
        if m > 0:
            fix = (zu + 1.5 * xu) * pl.reciprocal(total + 2.0 * x, approx=True)
            negated.append(fix + 0.25 * slope - middle)
    found = []
    for n in range(8):
        steep = jnp.maximum(jnp.maximum(backward[n], negated[n]), 0.0)
        found.append(steep * steep)
    return found


def advect(plan, phi, speed, halos, squares, moved, sign):
    w = plan.layers
    for h in range(plan.halves):
        at = half(h)

        @pl.loop(0, 8)
        def _(i):
            line = [halos[4, h, pl.ds(i * 8 * w + l, 8, stride=w), :] for l in range(w)]
            line += [phi[h, pl.ds(i * 64 + k, 8, stride=8), :] for k in range(8)]
            line += [halos[5, h, pl.ds(i * 8 * w + l, 8, stride=w), :] for l in range(w)]
            for k, value in enumerate(weno_line(line)):
                squares[pl.ds(i * 64 + k, 8, stride=8), :] = value
            line = [halos[2, h, rows8((i * w + l) * 8), :] for l in range(w)]
            line += [phi[h, rows8(i * 64 + j * 8), :] for j in range(8)]
            line += [halos[3, h, rows8((i * w + l) * 8), :] for l in range(w)]
            for j, value in enumerate(weno_line(line)):
                squares[rows8(i * 64 + j * 8), :] += value

        @pl.loop(0, 8)
        def _(j):
            line = [halos[0, h, rows8((l * 8 + j) * 8), :] for l in range(w)]
            line += [phi[h, rows8(i * 64 + j * 8), :] for i in range(8)]
            line += [halos[1, h, rows8((l * 8 + j) * 8), :] for l in range(w)]
            for i, value in enumerate(weno_line(line)):
                here = rows8(i * 64 + j * 8)
                total = squares[here, :] + value
                value = line[w + i] - advect_scale * speed[here, at] * jnp.sqrt(total)
                moved[h, here, :] = value
                sign[h, here, :] = value * lax.rsqrt(value * value + 1.0)


def relax(plan, phi, sign, halos, moved, joined):
    row = lax.broadcasted_iota(jnp.int32, (8, LANES), 0)
    for h in range(plan.halves):
        at = half(h)

        def plane(i, previous, following):
            centre = [phi[h, rows8(i * 64 + j * 8), :] for j in range(8)]
            along_y = [halos[2, h, rows8(i * 8), :]] + centre + [halos[3, h, rows8(i * 8), :]]
            for j in range(8):
                here = rows8(i * 64 + j * 8)
                value = centre[j]
                sense = sign[h, here, :]
                facing = jnp.where(sense > 0.0, 1.0, -1.0)
                first = jnp.broadcast_to(halos[4, h, pl.ds(i * 8 + j, 1), :], (8, LANES))
                last = jnp.broadcast_to(halos[5, h, pl.ds(i * 8 + j, 1), :], (8, LANES))
                low_z = jnp.where(row == 0, first, pltpu.roll(value, 1, 0))
                high_z = jnp.where(row == 7, last, pltpu.roll(value, 7, 0))
                pairs = (
                    (previous(j), following(j)),
                    (along_y[j], along_y[j + 2]),
                    (low_z, high_z),
                )
                total = None
                for low, high in pairs:
                    steep = jnp.maximum((value - low) * facing, (value - high) * facing)
                    steep = jnp.maximum(steep, 0.0)
                    steep = steep * steep
                    total = steep if total is None else total + steep
                value = value - relax_scale * sense * (jnp.sqrt(total) - 1.0)
                if joined:
                    moved[here, at] = value
                else:
                    moved[h, here, :] = value

        def inner(i, j):
            return phi[h, rows8(i * 64 + j * 8), :]

        plane(0, lambda j: halos[0, h, pl.ds(j * 8, 8), :], lambda j: inner(1, j))

        @pl.loop(1, 7)
        def _(i):
            plane(i, lambda j: inner(i - 1, j), lambda j: inner(i + 1, j))

        plane(7, lambda j: inner(6, j), lambda j: halos[1, h, pl.ds(j * 8, 8), :])


def first_kernel(
    plan, level_set, peer_slabs, region_slabs, halo_source,
    phi, outgoing, low, high, send_code, halo_code, ends, table, padded, peer, region, entries, ready,
):
    copies = [
        pltpu.make_async_copy(source, target, ready.at[n])
        for n, (source, target) in enumerate(
            ((peer_slabs, peer), (region_slabs, region), (halo_source, entries))
        )
    ]
    for h in range(plan.halves):
        copies.append(
            pltpu.make_async_copy(level_set.at[:, half(h)], phi.at[h], ready.at[3 + h])
        )
    for copy in copies:
        copy.start()
    for copy in copies:
        copy.wait()
    lanes = lane_ids()
    padded[...] = jnp.zeros_like(padded)
    padded[pl.ds(0, plan.peers), pl.ds(0, plan.slots)] = jnp.maximum(peer[...], 0)
    padded[pl.ds(plan.peers, 2), pl.ds(0, plan.border)] = region[...]

    def wide(row):
        return jnp.broadcast_to(padded[pl.ds(row, 1), :], (8, LANES))

    send_code[...] = jnp.zeros_like(send_code)
    for t in range(plan.far_tiles):
        block = jnp.zeros((8, LANES), jnp.int32)
        if t < plan.peer_tiles:
            for eq in range(min(plan.per_tile, plan.peers - t * plan.per_tile)):
                part = turn(wide(t * plan.per_tile + eq), eq * plan.slots)
                block = jnp.where(in_block(lanes, eq * plan.slots, plan.slots), part, block)
        if t == plan.border_tile:
            for side in range(2):
                start = plan.border_lane + side * plan.border
                part = turn(wide(plan.peers + side), start)
                block = jnp.where(in_block(lanes, start, plan.border), part, block)
        send_code[pl.ds(t, 1), :] = block[0:1]

    entry = entries[...]
    far = entry - plan.local_tiles * LANES
    tile_span = plan.per_tile * plan.slots
    tile = jnp.zeros_like(entry)
    for k in range(1, plan.peer_tiles):
        tile += (far >= k * tile_span).astype(jnp.int32)
    code = (plan.local_tiles + tile) * LANES + far - tile * tile_span
    edge = far - plan.peers * plan.slots
    edge_code = (plan.local_tiles + plan.border_tile) * LANES + plan.border_lane + edge
    code = jnp.where(edge >= 0, edge_code, code)
    halo_code[...] = jnp.where(far >= 0, code, entry)

    fill_ends(plan, phi, ends)
    pack_sends(plan, phi, ends, send_code, table, outgoing, low, high)


def near_kernel(plan, phi, halo_code, near, ends):
    fill_ends(plan, phi, ends)
    pull_local(plan, phi, ends, halo_code, near)


def advect_kernel(
    plan, sends, phi, near, speed, arrived, before, after, send_code, halo_code,
    moved, sign, outgoing, low, high, ends, table, halos, squares,
):
    unpack_far(plan, arrived, before, after, table)
    pull_far(plan, table, halo_code, near, halos)
    advect(plan, phi, speed, halos, squares, moved, sign)
    pack_sends(sends, moved, ends, send_code, table, outgoing, low, high)


def relax_kernel(plan, sends, phi, near, sign, arrived, before, after, send_code, halo_code, *rest):
    if sends is None:
        (moved, ends, table, halos) = rest
    else:
        (moved, outgoing, low, high, ends, table, halos) = rest
    unpack_far(plan, arrived, before, after, table)
    pull_far(plan, table, halo_code, near, halos)
    relax(plan, phi, sign, halos, moved, sends is None)
    if sends is not None:
        fill_ends(sends, moved, ends)
        pack_sends(sends, moved, ends, send_code, table, outgoing, low, high)


def f32(shape):
    return jax.ShapeDtypeStruct(shape, jnp.float32)


def call(kernel, out_shape, scratch, flops, *operands, space=pltpu.VMEM):
    whole = pl.BlockSpec(memory_space=pltpu.VMEM)
    size = sum(x.size * 4 for x in operands) + sum(x.size * 4 for x in out_shape)
    return pl.pallas_call(
        kernel,
        out_shape=out_shape,
        in_specs=[pl.BlockSpec(memory_space=space)] * len(operands),
        out_specs=[whole] * len(out_shape),
        scratch_shapes=scratch,
        cost_estimate=pl.CostEstimate(flops=flops, bytes_accessed=size, transcendentals=0),
        compiler_params=pltpu.CompilerParams(vmem_limit_bytes=8 * 1024 * 1024),
    )(*operands)


def in_vmem(x):
    return pltpu.with_memory_space_constraint(x, pltpu.VMEM)


def exchange(outgoing, low, high):
    count = lax.axis_size("group")
    up = [(i, (i + 1) % count) for i in range(count)]
    down = [(target, source) for source, target in up]
    outgoing, low, high = (in_vmem(x) for x in (outgoing, low, high))
    arrived = lax.all_to_all(outgoing, "dev", split_axis=0, concat_axis=0, tiled=True)
    before = lax.ppermute(high, "group", up)
    after = lax.ppermute(low, "group", down)
    arrived, before, after = (in_vmem(x) for x in (arrived, before, after))
    return arrived, before, after


def per_device(level_set, speed, peer_slabs, region_slabs, halo_source):
    rows, count = level_set.shape
    peers, slots = peer_slabs.shape
    border = region_slabs.shape[1]
    wide = Plan(count, peers, slots, border, 3)
    thin = Plan(count, peers, slots, border, 1)
    code_rows = -(-wide.far_tiles // 8) * 8

    def ends(plan):
        return pltpu.VMEM((2, wide.halves, 64 * plan.layers, LANES), jnp.float32)

    def table(plan):
        return pltpu.VMEM((plan.far_tiles, 64 * plan.layers, LANES), jnp.float32)

    def halos(plan):
        return pltpu.VMEM((6, wide.halves, 64 * plan.layers, LANES), jnp.float32)

    def sent(plan):
        return [f32(plan.message()), f32(plan.border_message()), f32(plan.border_message())]

    field = f32((wide.halves, rows, LANES))
    pad_rows = -(-(peers + 2) // 8) * 8
    phi, *message, send_code, halo_code = call(
        functools.partial(first_kernel, wide),
        [field]
        + sent(wide)
        + [
            jax.ShapeDtypeStruct((code_rows, LANES), jnp.int32),
            jax.ShapeDtypeStruct(halo_source.shape, jnp.int32),
        ],
        [
            ends(wide),
            table(wide),
            pltpu.VMEM((pad_rows, LANES), jnp.int32),
            pltpu.VMEM(peer_slabs.shape, jnp.int32),
            pltpu.VMEM(region_slabs.shape, jnp.int32),
            pltpu.VMEM(halo_source.shape, jnp.int32),
            pltpu.SemaphoreType.DMA((3 + wide.halves,)),
        ],
        1000000,
        *(
            pltpu.with_memory_space_constraint(x, pltpu.HBM)
            for x in (level_set, peer_slabs, region_slabs, halo_source)
        ),
        space=pltpu.HBM,
    )

    def near_halos(plan, phi):
        return call(
            functools.partial(near_kernel, plan),
            [f32((6, plan.halves, 64 * plan.layers, LANES))],
            [ends(plan)],
            rows * count * 100 * plan.layers,
            phi, halo_code,
        )[0]

    for offset_step in range(OFFSET_STEPS):
        phi, sign, *message = call(
            functools.partial(advect_kernel, wide, thin),
            [field, field] + sent(thin),
            [ends(wide), table(wide), halos(wide), pltpu.VMEM((rows, LANES), jnp.float32)],
            rows * count * 300,
            phi, near_halos(wide, phi), speed, *exchange(*message), send_code, halo_code,
        )
        for redist_pass in range(REDIST_PASSES):
            if redist_pass < REDIST_PASSES - 1:
                sends = thin
            elif offset_step < OFFSET_STEPS - 1:
                sends = wide
            else:
                sends = None
            largest = thin if sends is None else sends
            phi, *message = call(
                functools.partial(relax_kernel, thin, sends),
                [f32((rows, count))] if sends is None else [field] + sent(sends),
                [ends(largest), table(largest), halos(thin)],
                rows * count * 60,
                phi, near_halos(thin, phi), sign, *exchange(*message), send_code, halo_code,
            )
    return phi


def solution(mesh):
    return jax.shard_map(
        per_device,
        mesh=mesh,
        in_specs=(
            P(None, ("group", "dev")),
            P(None, ("group", "dev")),
            P(("group", "dev"), None),
            P(("group", "dev"), None),
            P(None, ("group", "dev")),
        ),
        out_specs=P(None, ("group", "dev")),
        check_vma=False,
    )
```

```python
import functools

import jax
import jax.numpy as jnp
from jax import lax
from jax.experimental import pallas as pl
from jax.experimental.pallas import tpu as pltpu
from jax.sharding import PartitionSpec as P

OFFSET_STEPS = 2
REDIST_PASSES = 2

advect_scale = 0.3
relax_scale = 0.3
weno_floor = 1e-06

LANES = 128


class Plan:
    def __init__(self, count, peers, slots, border, layers):
        self.count = count
        self.peers = peers
        self.slots = slots
        self.border = border
        self.layers = layers
        self.halves = count // LANES
        self.local_tiles = 6 * self.halves
        self.groups = 8 * layers
        self.per_tile = LANES // slots
        self.peer_tiles = -(-peers // self.per_tile)
        used = (peers - (self.peer_tiles - 1) * self.per_tile) * slots
        if used + 2 * border <= LANES:
            self.border_tile = self.peer_tiles - 1
            self.border_lane = used
        else:
            self.border_tile = self.peer_tiles
            self.border_lane = 0
        self.far_tiles = self.border_tile + 1
        self.pieces = min(LANES // slots, self.groups)
        self.piece_groups = -(-self.groups // self.pieces)
        self.border_pieces = min(LANES // border, self.groups)
        self.border_groups = -(-self.groups // self.border_pieces)

    def message(self):
        return (self.peers, 8 * self.piece_groups, LANES)

    def border_message(self):
        return (8 * self.border_groups, LANES)


def lane_ids():
    return lax.broadcasted_iota(jnp.int32, (8, LANES), 1)


def turn(block, shift):
    shift = shift % LANES
    return block if shift == 0 else pltpu.roll(block, shift, 1)


def in_block(lanes, start, size):
    return jnp.logical_and(lanes >= start, lanes < start + size)


def half(h):
    return pl.ds(h * LANES, LANES)


def rows8(start):
    return pl.ds(pl.multiple_of(start, 8), 8)


def bits_of(tile, tiles):
    return [(tile & (1 << b)) != 0 for b in range(max(tiles - 1, 1).bit_length())]


def pick_tile(values, masks):
    def pick(lowest, bit):
        if bit < 0:
            return values(lowest)
        first = pick(lowest, bit - 1)
        if lowest + (1 << bit) >= values.count:
            return first
        return jnp.where(masks[bit], pick(lowest + (1 << bit), bit - 1), first)

    return pick(0, len(masks) - 1)


class Taken:
    def __init__(self, sources, lane):
        self.sources = sources
        self.lane = lane
        self.count = len(sources)

    def __call__(self, tile):
        return jnp.take_along_axis(
            self.sources[tile], self.lane, axis=1, mode="promise_in_bounds"
        )


def gather(sources, code):
    return pick_tile(Taken(sources, code & (LANES - 1)), bits_of(code >> 7, len(sources)))


def local_sources(plan, phi, ends, g):
    w = plan.layers
    if w == 1:
        along_y = g * 64
    else:
        along_y = (g // w) * 64 + lax.rem(g, w) * 8
    starts = [g * 8, (8 - w) * 64 + g * 8, along_y, along_y + (8 - w) * 8]
    found = []
    for start in starts:
        for h in range(plan.halves):
            found.append(phi[h, rows8(start), :])
    for end in range(2):
        for h in range(plan.halves):
            if w == 1:
                found.append(phi[h, pl.ds(g * 64 + 7 * end, 8, stride=8), :])
            else:
                found.append(ends[end, h, rows8(g * 8), :])
    return found


def fill_ends(plan, phi, ends):
    w = plan.layers
    if w == 1:
        return

    @pl.loop(0, 8)
    def _(i):
        for end in range(2):
            for l in range(w):
                k = l + end * (8 - w)
                for h in range(plan.halves):
                    ends[end, h, pl.ds(i * 8 * w + l, 8, stride=w), :] = phi[
                        h, pl.ds(i * 64 + k, 8, stride=8), :
                    ]


def pack_sends(plan, phi, ends, send_code, table, outgoing, low, high):
    lanes = lane_ids()
    w = plan.layers

    @pl.loop(0, plan.groups)
    def _(g):
        sources = local_sources(plan, phi, ends, g)
        for t in range(plan.far_tiles):
            code = jnp.broadcast_to(send_code[pl.ds(t, 1), :], (8, LANES))
            table[t, rows8(g * 8), :] = gather(sources, code)

    last = plan.groups - 1

    @pl.loop(0, plan.piece_groups)
    def _(gi):
        for e in range(plan.peers):
            t, eq = divmod(e, plan.per_tile)
            block = None
            for p in range(plan.pieces):
                g = jnp.minimum(p * plan.piece_groups + gi, last)
                part = turn(table[t, rows8(g * 8), :], (p - eq) * plan.slots)
                if block is None:
                    block = part
                else:
                    block = jnp.where(lanes >= p * plan.slots, part, block)
            outgoing[e, rows8(gi * 8), :] = block

    @pl.loop(0, plan.border_groups)
    def _(gi):
        for side, target in enumerate((low, high)):
            block = None
            for p in range(plan.border_pieces):
                g = jnp.minimum(p * plan.border_groups + gi, last)
                part = turn(
                    table[plan.border_tile, rows8(g * 8), :],
                    (p - side) * plan.border - plan.border_lane,
                )
                if block is None:
                    block = part
                else:
                    block = jnp.where(lanes >= p * plan.border, part, block)
            target[rows8(gi * 8), :] = block


def unpack_far(plan, arrived, before, after, table):
    lanes = lane_ids()
    for p in range(plan.pieces):
        first = p * plan.piece_groups

        @pl.loop(0, max(min(plan.piece_groups, plan.groups - first), 0))
        def _(gi):
            for t in range(plan.peer_tiles):
                block = None
                for eq in range(min(plan.per_tile, plan.peers - t * plan.per_tile)):
                    source = arrived[t * plan.per_tile + eq, rows8(gi * 8), :]
                    part = turn(source, (eq - p) * plan.slots)
                    if block is None:
                        block = part
                    else:
                        block = jnp.where(lanes >= eq * plan.slots, part, block)
                table[t, rows8((first + gi) * 8), :] = block

    for p in range(plan.border_pieces):
        first = p * plan.border_groups

        @pl.loop(0, max(min(plan.border_groups, plan.groups - first), 0))
        def _(gi):
            here = rows8((first + gi) * 8)
            if plan.border_tile < plan.peer_tiles:
                block = table[plan.border_tile, here, :]
            else:
                block = jnp.zeros((8, LANES), jnp.float32)
            for q, source in enumerate((before, after)):
                start = plan.border_lane + q * plan.border
                part = turn(source[rows8(gi * 8), :], start - p * plan.border)
                block = jnp.where(lanes >= start, part, block)
            table[plan.border_tile, here, :] = block


def pull_local(plan, phi, ends, halo_code, halos):
    @pl.loop(0, plan.groups)
    def _(g):
        sources = local_sources(plan, phi, ends, g)
        for s in range(6):
            for h in range(plan.halves):
                code = jnp.broadcast_to(halo_code[pl.ds(s, 1), half(h)], (8, LANES))
                halos[s, h, rows8(g * 8), :] = gather(sources, code)


def pull_far(plan, table, halo_code, near, halos):
    start = plan.local_tiles * LANES

    @pl.loop(0, plan.groups)
    def _(g):
        sources = [table[t, rows8(g * 8), :] for t in range(plan.far_tiles)]
        for s in range(6):
            for h in range(plan.halves):
                code = jnp.broadcast_to(halo_code[pl.ds(s, 1), half(h)], (8, LANES))
                far = gather(sources, code - start)
                here = near[s, h, rows8(g * 8), :]
                halos[s, h, rows8(g * 8), :] = jnp.where(code >= start, far, here)


def weno_line(q):
    first = [q[m + 1] - q[m] for m in range(13)]
    second = [first[m + 1] - first[m] for m in range(12)]
    third = [second[m + 1] - second[m] for m in range(11)]
    fourth = [(third[m] - third[m + 1]) * (1.0 / 3.0) for m in range(10)]
    bend = [t * t * (4.0 / 3.0) + weno_floor for t in third]
    backward, negated = [], []
    for m in range(9):
        s1, s2 = second[m + 1], second[m + 2]
        a = bend[m] + s1 * (s1 + third[m])
        b = bend[m + 1] + s1 * s2
        c = bend[m + 2] + s2 * (s2 - third[m + 2])
        a, b, c = a * a, b * b, c * c
        x = b * c
        z = a * b
        total = x + z + 6.0 * (a * c)
        xu = x * fourth[m]
        zu = z * fourth[m + 1]
        slope = s1 + s2
        middle = first[m + 2] + third[m + 1] * (1.0 / 12.0)
        if m < 8:
            fix = (xu + 1.5 * zu) * pl.reciprocal(total + 2.0 * z, approx=True)
            backward.append(middle + 0.25 * slope + fix)
        if m > 0:
            fix = (zu + 1.5 * xu) * pl.reciprocal(total + 2.0 * x, approx=True)
            negated.append(fix + 0.25 * slope - middle)
    found = []
    for n in range(8):
        steep = jnp.maximum(jnp.maximum(backward[n], negated[n]), 0.0)
        found.append(steep * steep)
    return found


def advect(plan, phi, speed, ready, halos, squares, moved):
    w = plan.layers

    @pl.loop(0, 8 * plan.halves)
    def _(q):
        h, i = q >> 3, q & 7
        line = [halos[4, h, pl.ds(i * 8 * w + l, 8, stride=w), :] for l in range(w)]
        line += [phi[h, pl.ds(i * 64 + k, 8, stride=8), :] for k in range(8)]
        line += [halos[5, h, pl.ds(i * 8 * w + l, 8, stride=w), :] for l in range(w)]
        for k, value in enumerate(weno_line(line)):
            squares[h, pl.ds(i * 64 + k, 8, stride=8), :] = value
        line = [halos[2, h, rows8((i * w + l) * 8), :] for l in range(w)]
        line += [phi[h, rows8(i * 64 + j * 8), :] for j in range(8)]
        line += [halos[3, h, rows8((i * w + l) * 8), :] for l in range(w)]
        for j, value in enumerate(weno_line(line)):
            squares[h, rows8(i * 64 + j * 8), :] += value

    ready()

    @pl.loop(0, 8 * plan.halves)
    def _(q):
        h, j = q >> 3, q & 7
        line = [halos[0, h, rows8((l * 8 + j) * 8), :] for l in range(w)]
        line += [phi[h, rows8(i * 64 + j * 8), :] for i in range(8)]
        line += [halos[1, h, rows8((l * 8 + j) * 8), :] for l in range(w)]
        for i, value in enumerate(weno_line(line)):
            here = rows8(i * 64 + j * 8)
            total = squares[h, here, :] + value
            change = advect_scale * speed[h, here, :] * jnp.sqrt(total)
            moved[h, here, :] = line[w + i] - change


def steepness(value, low, high, facing):
    steep = jnp.maximum((value - low) * facing, (value - high) * facing)
    steep = jnp.maximum(steep, 0.0)
    return steep * steep


def relax(plan, phi, origin, halos, squares, moved, joined):
    @pl.loop(0, 8 * plan.halves)
    def _(q):
        h, i = q >> 3, q & 7
        line = [halos[4, h, rows8(i * 8), :]]
        line += [phi[h, pl.ds(i * 64 + k, 8, stride=8), :] for k in range(8)]
        line += [halos[5, h, rows8(i * 8), :]]
        for k in range(8):
            here = pl.ds(i * 64 + k, 8, stride=8)
            facing = jnp.where(origin[h, here, :] > 0.0, 1.0, -1.0)
            squares[h, here, :] = steepness(line[k + 1], line[k], line[k + 2], facing)

    @pl.loop(0, 8 * plan.halves)
    def _(q):
        h, j = q >> 3, q & 7
        line = [halos[0, h, rows8(j * 8), :]]
        line += [phi[h, rows8(i * 64 + j * 8), :] for i in range(8)]
        line += [halos[1, h, rows8(j * 8), :]]
        for i in range(8):
            here = rows8(i * 64 + j * 8)
            facing = jnp.where(origin[h, here, :] > 0.0, 1.0, -1.0)
            squares[h, here, :] += steepness(line[i + 1], line[i], line[i + 2], facing)

    @pl.loop(0, 8 * plan.halves)
    def _(q):
        h, i = q >> 3, q & 7
        line = [halos[2, h, rows8(i * 8), :]]
        line += [phi[h, rows8(i * 64 + j * 8), :] for j in range(8)]
        line += [halos[3, h, rows8(i * 8), :]]
        for j in range(8):
            here = rows8(i * 64 + j * 8)
            start = origin[h, here, :]
            facing = jnp.where(start > 0.0, 1.0, -1.0)
            total = squares[h, here, :] + steepness(line[j + 1], line[j], line[j + 2], facing)
            sign = start * lax.rsqrt(start * start + 1.0)
            value = line[j + 1] - relax_scale * sign * (jnp.sqrt(total) - 1.0)
            if joined:
                moved[here, pl.ds(pl.multiple_of(h * LANES, LANES), LANES)] = value
            else:
                moved[h, here, :] = value


def first_kernel(
    plan, level_set, peer_slabs, region_slabs, halo_source,
    phi, outgoing, low, high, send_code, halo_code, ends, table, padded, peer, region, entries, ready,
):
    copies = [
        pltpu.make_async_copy(source, target, ready.at[n])
        for n, (source, target) in enumerate(
            ((peer_slabs, peer), (region_slabs, region), (halo_source, entries))
        )
    ]
    for h in range(plan.halves):
        copies.append(
            pltpu.make_async_copy(level_set.at[:, half(h)], phi.at[h], ready.at[3 + h])
        )
    for copy in copies:
        copy.start()
    for copy in copies:
        copy.wait()
    lanes = lane_ids()
    padded[...] = jnp.zeros_like(padded)
    padded[pl.ds(0, plan.peers), pl.ds(0, plan.slots)] = jnp.maximum(peer[...], 0)
    padded[pl.ds(plan.peers, 2), pl.ds(0, plan.border)] = region[...]

    def wide(row):
        return jnp.broadcast_to(padded[pl.ds(row, 1), :], (8, LANES))

    send_code[...] = jnp.zeros_like(send_code)
    for t in range(plan.far_tiles):
        block = jnp.zeros((8, LANES), jnp.int32)
        if t < plan.peer_tiles:
            for eq in range(min(plan.per_tile, plan.peers - t * plan.per_tile)):
                part = turn(wide(t * plan.per_tile + eq), eq * plan.slots)
                block = jnp.where(in_block(lanes, eq * plan.slots, plan.slots), part, block)
        if t == plan.border_tile:
            for side in range(2):
                start = plan.border_lane + side * plan.border
                part = turn(wide(plan.peers + side), start)
                block = jnp.where(in_block(lanes, start, plan.border), part, block)
        send_code[pl.ds(t, 1), :] = block[0:1]

    entry = entries[...]
    far = entry - plan.local_tiles * LANES
    tile_span = plan.per_tile * plan.slots
    tile = jnp.zeros_like(entry)
    for k in range(1, plan.peer_tiles):
        tile += (far >= k * tile_span).astype(jnp.int32)
    code = (plan.local_tiles + tile) * LANES + far - tile * tile_span
    edge = far - plan.peers * plan.slots
    edge_code = (plan.local_tiles + plan.border_tile) * LANES + plan.border_lane + edge
    code = jnp.where(edge >= 0, edge_code, code)
    halo_code[...] = jnp.where(far >= 0, code, entry)

    fill_ends(plan, phi, ends)
    pack_sends(plan, phi, ends, send_code, table, outgoing, low, high)


def near_kernel(plan, phi, halo_code, near, ends):
    fill_ends(plan, phi, ends)
    pull_local(plan, phi, ends, halo_code, near)


def advect_kernel(
    plan, sends, phi, near, speed, arrived, before, after, send_code, halo_code,
    moved, outgoing, low, high, ends, table, halos, squares, fast, loaded,
):
    copies = [
        pltpu.make_async_copy(speed.at[:, half(h)], fast.at[h], loaded.at[h])
        for h in range(plan.halves)
    ]
    for copy in copies:
        copy.start()

    def ready():
        for copy in copies:
            copy.wait()

    unpack_far(plan, arrived, before, after, table)
    pull_far(plan, table, halo_code, near, halos)
    advect(plan, phi, fast, ready, halos, squares, moved)
    pack_sends(sends, moved, ends, send_code, table, outgoing, low, high)


def relax_kernel(
    plan, sends, phi, origin, near, arrived, before, after, send_code, halo_code, *rest
):
    if sends is None:
        (moved, table, halos, squares) = rest
    else:
        (moved, outgoing, low, high, ends, table, halos, squares) = rest
    unpack_far(plan, arrived, before, after, table)
    pull_far(plan, table, halo_code, near, halos)
    relax(plan, phi, origin, halos, squares, moved, sends is None)
    if sends is not None:
        fill_ends(sends, moved, ends)
        pack_sends(sends, moved, ends, send_code, table, outgoing, low, high)


def f32(shape):
    return jax.ShapeDtypeStruct(shape, jnp.float32)


def call(kernel, out_shape, scratch, flops, *operands, far=()):
    whole = pl.BlockSpec(memory_space=pltpu.VMEM)
    apart = pl.BlockSpec(memory_space=pltpu.HBM)
    size = sum(x.size * 4 for x in operands) + sum(x.size * 4 for x in out_shape)
    operands = [
        pltpu.with_memory_space_constraint(x, pltpu.HBM) if n in far else x
        for n, x in enumerate(operands)
    ]
    return pl.pallas_call(
        kernel,
        out_shape=out_shape,
        in_specs=[apart if n in far else whole for n in range(len(operands))],
        out_specs=[whole] * len(out_shape),
        scratch_shapes=scratch,
        cost_estimate=pl.CostEstimate(flops=flops, bytes_accessed=size, transcendentals=0),
        compiler_params=pltpu.CompilerParams(vmem_limit_bytes=12 * 1024 * 1024),
    )(*operands)


def exchange(outgoing, low, high):
    count = lax.axis_size("group")
    up = [(i, (i + 1) % count) for i in range(count)]
    down = [(target, source) for source, target in up]
    arrived = lax.all_to_all(outgoing, "dev", split_axis=0, concat_axis=0, tiled=True)
    before = lax.ppermute(high, "group", up)
    after = lax.ppermute(low, "group", down)
    return arrived, before, after


def per_device(level_set, speed, peer_slabs, region_slabs, halo_source):
    rows, count = level_set.shape
    peers, slots = peer_slabs.shape
    border = region_slabs.shape[1]
    wide = Plan(count, peers, slots, border, 3)
    thin = Plan(count, peers, slots, border, 1)
    code_rows = -(-wide.far_tiles // 8) * 8

    def ends(plan):
        return pltpu.VMEM((2, wide.halves, 64 * plan.layers, LANES), jnp.float32)

    def table(plan):
        return pltpu.VMEM((plan.far_tiles, 64 * plan.layers, LANES), jnp.float32)

    def halos(plan):
        return pltpu.VMEM((6, wide.halves, 64 * plan.layers, LANES), jnp.float32)

    def sent(plan):
        return [f32(plan.message()), f32(plan.border_message()), f32(plan.border_message())]

    field = f32((wide.halves, rows, LANES))
    pad_rows = -(-(peers + 2) // 8) * 8
    phi, *message, send_code, halo_code = call(
        functools.partial(first_kernel, wide),
        [field]
        + sent(wide)
        + [
            jax.ShapeDtypeStruct((code_rows, LANES), jnp.int32),
            jax.ShapeDtypeStruct(halo_source.shape, jnp.int32),
        ],
        [
            ends(wide),
            table(wide),
            pltpu.VMEM((pad_rows, LANES), jnp.int32),
            pltpu.VMEM(peer_slabs.shape, jnp.int32),
            pltpu.VMEM(region_slabs.shape, jnp.int32),
            pltpu.VMEM(halo_source.shape, jnp.int32),
            pltpu.SemaphoreType.DMA((3 + wide.halves,)),
        ],
        1000000,
        level_set, peer_slabs, region_slabs, halo_source,
        far=(0, 1, 2, 3),
    )

    def near_halos(plan, phi):
        return call(
            functools.partial(near_kernel, plan),
            [f32((6, plan.halves, 64 * plan.layers, LANES))],
            [ends(plan)],
            rows * count * 100 * plan.layers,
            phi, halo_code,
        )[0]

    block = pltpu.VMEM((wide.halves, rows, LANES), jnp.float32)
    for offset_step in range(OFFSET_STEPS):
        phi, *message = call(
            functools.partial(advect_kernel, wide, thin),
            [field] + sent(thin),
            [ends(wide), table(wide), halos(wide), block, block]
            + [pltpu.SemaphoreType.DMA((wide.halves,))],
            rows * count * 300,
            phi, near_halos(wide, phi), speed, *exchange(*message), send_code, halo_code,
            far=(2,),
        )
        origin = phi
        for redist_pass in range(REDIST_PASSES):
            if redist_pass < REDIST_PASSES - 1:
                sends = thin
            elif offset_step < OFFSET_STEPS - 1:
                sends = wide
            else:
                sends = None
            if sends is None:
                out, scratch = [f32((rows, count))], [table(thin)]
            else:
                out, scratch = [field] + sent(sends), [ends(sends), table(sends)]
            phi, *message = call(
                functools.partial(relax_kernel, thin, sends),
                out,
                scratch + [halos(thin), block],
                rows * count * 60,
                phi, origin, near_halos(thin, phi), *exchange(*message), send_code, halo_code,
            )
    return phi


def solution(mesh):
    return jax.shard_map(
        per_device,
        mesh=mesh,
        in_specs=(
            P(None, ("group", "dev")),
            P(None, ("group", "dev")),
            P(("group", "dev"), None),
            P(("group", "dev"), None),
            P(None, ("group", "dev")),
        ),
        out_specs=P(None, ("group", "dev")),
        check_vma=False,
    )
```

```python
import functools

import jax
import jax.numpy as jnp
from jax import lax
from jax.experimental import pallas as pl
from jax.experimental.pallas import tpu as pltpu
from jax.sharding import PartitionSpec as P

OFFSET_STEPS = 2
REDIST_PASSES = 2

advect_scale = 0.3
relax_scale = 0.3
weno_floor = 1e-06

LANES = 128


class Plan:
    def __init__(self, count, peers, slots, border, layers):
        self.count = count
        self.peers = peers
        self.slots = slots
        self.border = border
        self.layers = layers
        self.halves = count // LANES
        self.local_tiles = 6 * self.halves
        self.groups = 8 * layers
        self.per_tile = LANES // slots
        self.peer_tiles = -(-peers // self.per_tile)
        used = (peers - (self.peer_tiles - 1) * self.per_tile) * slots
        if used + 2 * border <= LANES:
            self.border_tile = self.peer_tiles - 1
            self.border_lane = used
        else:
            self.border_tile = self.peer_tiles
            self.border_lane = 0
        self.far_tiles = self.border_tile + 1
        self.pieces = min(LANES // slots, self.groups)
        self.piece_groups = -(-self.groups // self.pieces)
        self.border_pieces = min(LANES // border, self.groups)
        self.border_groups = -(-self.groups // self.border_pieces)

    def message(self):
        return (self.peers, 8 * self.piece_groups, LANES)

    def border_message(self):
        return (8 * self.border_groups, LANES)


def lane_ids():
    return lax.broadcasted_iota(jnp.int32, (8, LANES), 1)


def turn(block, shift):
    shift = shift % LANES
    return block if shift == 0 else pltpu.roll(block, shift, 1)


def in_block(lanes, start, size):
    return jnp.logical_and(lanes >= start, lanes < start + size)


def half(h):
    return pl.ds(h * LANES, LANES)


def rows8(start):
    return pl.ds(pl.multiple_of(start, 8), 8)


def bits_of(tile, tiles):
    return [(tile & (1 << b)) != 0 for b in range(max(tiles - 1, 1).bit_length())]


def pick_tile(values, masks):
    def pick(lowest, bit):
        if bit < 0:
            return values(lowest)
        first = pick(lowest, bit - 1)
        if lowest + (1 << bit) >= values.count:
            return first
        return jnp.where(masks[bit], pick(lowest + (1 << bit), bit - 1), first)

    return pick(0, len(masks) - 1)


class Taken:
    def __init__(self, sources, lane):
        self.sources = sources
        self.lane = lane
        self.count = len(sources)

    def __call__(self, tile):
        return jnp.take_along_axis(
            self.sources[tile], self.lane, axis=1, mode="promise_in_bounds"
        )


def gather(sources, code):
    return pick_tile(Taken(sources, code & (LANES - 1)), bits_of(code >> 7, len(sources)))


def local_sources(plan, phi, ends, g):
    w = plan.layers
    if w == 1:
        along_y = g * 64
    else:
        along_y = (g // w) * 64 + lax.rem(g, w) * 8
    starts = [g * 8, (8 - w) * 64 + g * 8, along_y, along_y + (8 - w) * 8]
    found = []
    for start in starts:
        for h in range(plan.halves):
            found.append(phi[h, rows8(start), :])
    for end in range(2):
        for h in range(plan.halves):
            if w == 1:
                found.append(phi[h, pl.ds(g * 64 + 7 * end, 8, stride=8), :])
            else:
                found.append(ends[end, h, rows8(g * 8), :])
    return found


def fill_ends(plan, phi, ends):
    w = plan.layers
    if w == 1:
        return

    @pl.loop(0, 8)
    def _(i):
        for end in range(2):
            for l in range(w):
                k = l + end * (8 - w)
                for h in range(plan.halves):
                    ends[end, h, pl.ds(i * 8 * w + l, 8, stride=w), :] = phi[
                        h, pl.ds(i * 64 + k, 8, stride=8), :
                    ]


def pack_sends(plan, phi, ends, send_code, table, outgoing, low, high):
    lanes = lane_ids()
    w = plan.layers

    @pl.loop(0, plan.groups)
    def _(g):
        sources = local_sources(plan, phi, ends, g)
        for t in range(plan.far_tiles):
            code = jnp.broadcast_to(send_code[pl.ds(t, 1), :], (8, LANES))
            table[t, rows8(g * 8), :] = gather(sources, code)

    for e in range(plan.peers):
        t, eq = divmod(e, plan.per_tile)
        for gi in range(plan.piece_groups):
            block = None
            for p in range(plan.pieces):
                g = p * plan.piece_groups + gi
                if g >= plan.groups:
                    continue
                part = turn(table[t, pl.ds(g * 8, 8), :], (p - eq) * plan.slots)
                if block is None:
                    block = part
                else:
                    block = jnp.where(lanes >= p * plan.slots, part, block)
            outgoing[e, pl.ds(gi * 8, 8), :] = block
    for side, target in enumerate((low, high)):
        for gi in range(plan.border_groups):
            block = None
            for p in range(plan.border_pieces):
                g = p * plan.border_groups + gi
                if g >= plan.groups:
                    continue
                part = turn(
                    table[plan.border_tile, pl.ds(g * 8, 8), :],
                    (p - side) * plan.border - plan.border_lane,
                )
                if block is None:
                    block = part
                else:
                    block = jnp.where(lanes >= p * plan.border, part, block)
            target[pl.ds(gi * 8, 8), :] = block


def unpack_far(plan, arrived, before, after, table):
    lanes = lane_ids()
    for g in range(plan.groups):
        p, gi = divmod(g, plan.piece_groups)
        bp, bgi = divmod(g, plan.border_groups)
        for t in range(plan.far_tiles):
            block = None
            if t < plan.peer_tiles:
                for eq in range(min(plan.per_tile, plan.peers - t * plan.per_tile)):
                    e = t * plan.per_tile + eq
                    part = turn(arrived[e, pl.ds(gi * 8, 8), :], (eq - p) * plan.slots)
                    if block is None:
                        block = part
                    else:
                        block = jnp.where(lanes >= eq * plan.slots, part, block)
            if t == plan.border_tile:
                for q, source in enumerate((before, after)):
                    start = plan.border_lane + q * plan.border
                    part = turn(source[pl.ds(bgi * 8, 8), :], start - bp * plan.border)
                    if block is None:
                        block = part
                    else:
                        block = jnp.where(lanes >= start, part, block)
            table[t, pl.ds(g * 8, 8), :] = block


def pull_local(plan, phi, ends, halo_code, halos):
    @pl.loop(0, plan.groups)
    def _(g):
        sources = local_sources(plan, phi, ends, g)
        for s in range(6):
            for h in range(plan.halves):
                code = jnp.broadcast_to(halo_code[pl.ds(s, 1), half(h)], (8, LANES))
                halos[s, h, rows8(g * 8), :] = gather(sources, code)


def pull_far(plan, table, halo_code, near, halos):
    start = plan.local_tiles * LANES

    @pl.loop(0, plan.groups)
    def _(g):
        sources = [table[t, rows8(g * 8), :] for t in range(plan.far_tiles)]
        for s in range(6):
            for h in range(plan.halves):
                code = jnp.broadcast_to(halo_code[pl.ds(s, 1), half(h)], (8, LANES))
                far = gather(sources, code - start)
                here = near[s, h, rows8(g * 8), :]
                halos[s, h, rows8(g * 8), :] = jnp.where(code >= start, far, here)


def weno_line(q):
    first = [q[m + 1] - q[m] for m in range(13)]
    second = [first[m + 1] - first[m] for m in range(12)]
    third = [second[m + 1] - second[m] for m in range(11)]
    fourth = [(third[m] - third[m + 1]) * (1.0 / 3.0) for m in range(10)]
    bend = [t * t * (4.0 / 3.0) + weno_floor for t in third]
    backward, negated = [], []
    for m in range(9):
        s1, s2 = second[m + 1], second[m + 2]
        a = bend[m] + s1 * (s1 + third[m])
        b = bend[m + 1] + s1 * s2
        c = bend[m + 2] + s2 * (s2 - third[m + 2])
        a, b, c = a * a, b * b, c * c
        x = b * c
        z = a * b
        total = x + z + 6.0 * (a * c)
        xu = x * fourth[m]
        zu = z * fourth[m + 1]
        slope = s1 + s2
        middle = first[m + 2] + third[m + 1] * (1.0 / 12.0)
        if m < 8:
            fix = (xu + 1.5 * zu) * pl.reciprocal(total + 2.0 * z, approx=True)
            backward.append(middle + 0.25 * slope + fix)
        if m > 0:
            fix = (zu + 1.5 * xu) * pl.reciprocal(total + 2.0 * x, approx=True)
            negated.append(fix + 0.25 * slope - middle)
    found = []
    for n in range(8):
        steep = jnp.maximum(jnp.maximum(backward[n], negated[n]), 0.0)
        found.append(steep * steep)
    return found


def advect(plan, phi, speed, ready, halos, squares, moved):
    w = plan.layers
    for h in range(plan.halves):
        at = half(h)

        @pl.loop(0, 8)
        def _(i):
            line = [halos[4, h, pl.ds(i * 8 * w + l, 8, stride=w), :] for l in range(w)]
            line += [phi[h, pl.ds(i * 64 + k, 8, stride=8), :] for k in range(8)]
            line += [halos[5, h, pl.ds(i * 8 * w + l, 8, stride=w), :] for l in range(w)]
            for k, value in enumerate(weno_line(line)):
                squares[pl.ds(i * 64 + k, 8, stride=8), :] = value
            line = [halos[2, h, rows8((i * w + l) * 8), :] for l in range(w)]
            line += [phi[h, rows8(i * 64 + j * 8), :] for j in range(8)]
            line += [halos[3, h, rows8((i * w + l) * 8), :] for l in range(w)]
            for j, value in enumerate(weno_line(line)):
                squares[rows8(i * 64 + j * 8), :] += value

        if h == 0:
            ready()

        @pl.loop(0, 8)
        def _(j):
            line = [halos[0, h, rows8((l * 8 + j) * 8), :] for l in range(w)]
            line += [phi[h, rows8(i * 64 + j * 8), :] for i in range(8)]
            line += [halos[1, h, rows8((l * 8 + j) * 8), :] for l in range(w)]
            for i, value in enumerate(weno_line(line)):
                here = rows8(i * 64 + j * 8)
                total = squares[here, :] + value
                value = line[w + i] - advect_scale * speed[h, here, :] * jnp.sqrt(total)
                moved[h, here, :] = value


def relax(plan, phi, origin, halos, moved, joined):
    row = lax.broadcasted_iota(jnp.int32, (8, LANES), 0)
    for h in range(plan.halves):
        at = half(h)

        def plane(i, previous, following):
            centre = [phi[h, rows8(i * 64 + j * 8), :] for j in range(8)]
            along_y = [halos[2, h, rows8(i * 8), :]] + centre + [halos[3, h, rows8(i * 8), :]]
            for j in range(8):
                here = rows8(i * 64 + j * 8)
                value = centre[j]
                start = origin[h, here, :]
                sense = start * lax.rsqrt(start * start + 1.0)
                facing = jnp.where(start > 0.0, 1.0, -1.0)
                first = jnp.broadcast_to(halos[4, h, pl.ds(i * 8 + j, 1), :], (8, LANES))
                last = jnp.broadcast_to(halos[5, h, pl.ds(i * 8 + j, 1), :], (8, LANES))
                low_z = jnp.where(row == 0, first, pltpu.roll(value, 1, 0))
                high_z = jnp.where(row == 7, last, pltpu.roll(value, 7, 0))
                pairs = (
                    (previous(j), following(j)),
                    (along_y[j], along_y[j + 2]),
                    (low_z, high_z),
                )
                total = None
                for low, high in pairs:
                    steep = jnp.maximum((value - low) * facing, (value - high) * facing)
                    steep = jnp.maximum(steep, 0.0)
                    steep = steep * steep
                    total = steep if total is None else total + steep
                value = value - relax_scale * sense * (jnp.sqrt(total) - 1.0)
                if joined:
                    moved[here, at] = value
                else:
                    moved[h, here, :] = value

        def inner(i, j):
            return phi[h, rows8(i * 64 + j * 8), :]

        plane(0, lambda j: halos[0, h, pl.ds(j * 8, 8), :], lambda j: inner(1, j))

        @pl.loop(1, 7)
        def _(i):
            plane(i, lambda j: inner(i - 1, j), lambda j: inner(i + 1, j))

        plane(7, lambda j: inner(6, j), lambda j: halos[1, h, pl.ds(j * 8, 8), :])


def first_kernel(
    plan, level_set, peer_slabs, region_slabs, halo_source,
    phi, outgoing, low, high, send_code, halo_code, ends, table, padded, peer, region, entries, ready,
):
    copies = [
        pltpu.make_async_copy(source, target, ready.at[n])
        for n, (source, target) in enumerate(
            ((peer_slabs, peer), (region_slabs, region), (halo_source, entries))
        )
    ]
    for h in range(plan.halves):
        copies.append(
            pltpu.make_async_copy(level_set.at[:, half(h)], phi.at[h], ready.at[3 + h])
        )
    for copy in copies:
        copy.start()
    for copy in copies:
        copy.wait()
    lanes = lane_ids()
    padded[...] = jnp.zeros_like(padded)
    padded[pl.ds(0, plan.peers), pl.ds(0, plan.slots)] = jnp.maximum(peer[...], 0)
    padded[pl.ds(plan.peers, 2), pl.ds(0, plan.border)] = region[...]

    def wide(row):
        return jnp.broadcast_to(padded[pl.ds(row, 1), :], (8, LANES))

    send_code[...] = jnp.zeros_like(send_code)
    for t in range(plan.far_tiles):
        block = jnp.zeros((8, LANES), jnp.int32)
        if t < plan.peer_tiles:
            for eq in range(min(plan.per_tile, plan.peers - t * plan.per_tile)):
                part = turn(wide(t * plan.per_tile + eq), eq * plan.slots)
                block = jnp.where(in_block(lanes, eq * plan.slots, plan.slots), part, block)
        if t == plan.border_tile:
            for side in range(2):
                start = plan.border_lane + side * plan.border
                part = turn(wide(plan.peers + side), start)
                block = jnp.where(in_block(lanes, start, plan.border), part, block)
        send_code[pl.ds(t, 1), :] = block[0:1]

    entry = entries[...]
    far = entry - plan.local_tiles * LANES
    tile_span = plan.per_tile * plan.slots
    tile = jnp.zeros_like(entry)
    for k in range(1, plan.peer_tiles):
        tile += (far >= k * tile_span).astype(jnp.int32)
    code = (plan.local_tiles + tile) * LANES + far - tile * tile_span
    edge = far - plan.peers * plan.slots
    edge_code = (plan.local_tiles + plan.border_tile) * LANES + plan.border_lane + edge
    code = jnp.where(edge >= 0, edge_code, code)
    halo_code[...] = jnp.where(far >= 0, code, entry)

    fill_ends(plan, phi, ends)
    pack_sends(plan, phi, ends, send_code, table, outgoing, low, high)


def near_kernel(plan, phi, halo_code, near, ends):
    fill_ends(plan, phi, ends)
    pull_local(plan, phi, ends, halo_code, near)


def advect_kernel(
    plan, sends, phi, near, speed, arrived, before, after, send_code, halo_code,
    moved, outgoing, low, high, ends, table, halos, squares, fast, loaded,
):
    copies = [
        pltpu.make_async_copy(speed.at[:, half(h)], fast.at[h], loaded.at[h])
        for h in range(plan.halves)
    ]
    for copy in copies:
        copy.start()

    def ready():
        for copy in copies:
            copy.wait()

    unpack_far(plan, arrived, before, after, table)
    pull_far(plan, table, halo_code, near, halos)
    advect(plan, phi, fast, ready, halos, squares, moved)
    pack_sends(sends, moved, ends, send_code, table, outgoing, low, high)


def relax_kernel(
    plan, sends, phi, origin, near, arrived, before, after, send_code, halo_code, *rest
):
    if sends is None:
        (moved, table, halos) = rest
    else:
        (moved, outgoing, low, high, ends, table, halos) = rest
    unpack_far(plan, arrived, before, after, table)
    pull_far(plan, table, halo_code, near, halos)
    relax(plan, phi, origin, halos, moved, sends is None)
    if sends is not None:
        fill_ends(sends, moved, ends)
        pack_sends(sends, moved, ends, send_code, table, outgoing, low, high)


def f32(shape):
    return jax.ShapeDtypeStruct(shape, jnp.float32)


def call(kernel, out_shape, scratch, flops, *operands, far=()):
    whole = pl.BlockSpec(memory_space=pltpu.VMEM)
    apart = pl.BlockSpec(memory_space=pltpu.HBM)
    size = sum(x.size * 4 for x in operands) + sum(x.size * 4 for x in out_shape)
    operands = [
        pltpu.with_memory_space_constraint(x, pltpu.HBM) if n in far else x
        for n, x in enumerate(operands)
    ]
    return pl.pallas_call(
        kernel,
        out_shape=out_shape,
        in_specs=[apart if n in far else whole for n in range(len(operands))],
        out_specs=[whole] * len(out_shape),
        scratch_shapes=scratch,
        cost_estimate=pl.CostEstimate(flops=flops, bytes_accessed=size, transcendentals=0),
        compiler_params=pltpu.CompilerParams(vmem_limit_bytes=12 * 1024 * 1024),
    )(*operands)


def exchange(outgoing, low, high):
    count = lax.axis_size("group")
    up = [(i, (i + 1) % count) for i in range(count)]
    down = [(target, source) for source, target in up]
    arrived = lax.all_to_all(outgoing, "dev", split_axis=0, concat_axis=0, tiled=True)
    before = lax.ppermute(high, "group", up)
    after = lax.ppermute(low, "group", down)
    return arrived, before, after


def per_device(level_set, speed, peer_slabs, region_slabs, halo_source):
    rows, count = level_set.shape
    peers, slots = peer_slabs.shape
    border = region_slabs.shape[1]
    wide = Plan(count, peers, slots, border, 3)
    thin = Plan(count, peers, slots, border, 1)
    code_rows = -(-wide.far_tiles // 8) * 8

    def ends(plan):
        return pltpu.VMEM((2, wide.halves, 64 * plan.layers, LANES), jnp.float32)

    def table(plan):
        return pltpu.VMEM((plan.far_tiles, 64 * plan.layers, LANES), jnp.float32)

    def halos(plan):
        return pltpu.VMEM((6, wide.halves, 64 * plan.layers, LANES), jnp.float32)

    def sent(plan):
        return [f32(plan.message()), f32(plan.border_message()), f32(plan.border_message())]

    field = f32((wide.halves, rows, LANES))
    pad_rows = -(-(peers + 2) // 8) * 8
    phi, *message, send_code, halo_code = call(
        functools.partial(first_kernel, wide),
        [field]
        + sent(wide)
        + [
            jax.ShapeDtypeStruct((code_rows, LANES), jnp.int32),
            jax.ShapeDtypeStruct(halo_source.shape, jnp.int32),
        ],
        [
            ends(wide),
            table(wide),
            pltpu.VMEM((pad_rows, LANES), jnp.int32),
            pltpu.VMEM(peer_slabs.shape, jnp.int32),
            pltpu.VMEM(region_slabs.shape, jnp.int32),
            pltpu.VMEM(halo_source.shape, jnp.int32),
            pltpu.SemaphoreType.DMA((3 + wide.halves,)),
        ],
        1000000,
        level_set, peer_slabs, region_slabs, halo_source,
        far=(0, 1, 2, 3),
    )

    def near_halos(plan, phi):
        return call(
            functools.partial(near_kernel, plan),
            [f32((6, plan.halves, 64 * plan.layers, LANES))],
            [ends(plan)],
            rows * count * 100 * plan.layers,
            phi, halo_code,
        )[0]

    block = pltpu.VMEM((wide.halves, rows, LANES), jnp.float32)
    for offset_step in range(OFFSET_STEPS):
        phi, *message = call(
            functools.partial(advect_kernel, wide, thin),
            [field] + sent(thin),
            [ends(wide), table(wide), halos(wide)]
            + [pltpu.VMEM((rows, LANES), jnp.float32), block]
            + [pltpu.SemaphoreType.DMA((wide.halves,))],
            rows * count * 300,
            phi, near_halos(wide, phi), speed, *exchange(*message), send_code, halo_code,
            far=(2,),
        )
        origin = phi
        for redist_pass in range(REDIST_PASSES):
            if redist_pass < REDIST_PASSES - 1:
                sends = thin
            elif offset_step < OFFSET_STEPS - 1:
                sends = wide
            else:
                sends = None
            if sends is None:
                out, scratch = [f32((rows, count))], [table(thin)]
            else:
                out, scratch = [field] + sent(sends), [ends(sends), table(sends)]
            phi, *message = call(
                functools.partial(relax_kernel, thin, sends),
                out,
                scratch + [halos(thin)],
                rows * count * 60,
                phi, origin, near_halos(thin, phi), *exchange(*message), send_code, halo_code,
            )
    return phi


def solution(mesh):
    return jax.shard_map(
        per_device,
        mesh=mesh,
        in_specs=(
            P(None, ("group", "dev")),
            P(None, ("group", "dev")),
            P(("group", "dev"), None),
            P(("group", "dev"), None),
            P(None, ("group", "dev")),
        ),
        out_specs=P(None, ("group", "dev")),
        check_vma=False,
    )
```

```python
import functools

import jax
import jax.numpy as jnp
from jax import lax
from jax.experimental import pallas as pl
from jax.experimental.pallas import tpu as pltpu
from jax.sharding import PartitionSpec as P

OFFSET_STEPS = 2
REDIST_PASSES = 2

advect_scale = 0.3
relax_scale = 0.3
weno_floor = 1e-06

LANES = 128


class Plan:
    def __init__(self, count, peers, slots, border, layers):
        self.count = count
        self.peers = peers
        self.slots = slots
        self.border = border
        self.layers = layers
        self.halves = count // LANES
        self.local_tiles = 6 * self.halves
        self.groups = 8 * layers
        self.per_tile = LANES // slots
        self.peer_tiles = -(-peers // self.per_tile)
        used = (peers - (self.peer_tiles - 1) * self.per_tile) * slots
        if used + 2 * border <= LANES:
            self.border_tile = self.peer_tiles - 1
            self.border_lane = used
        else:
            self.border_tile = self.peer_tiles
            self.border_lane = 0
        self.far_tiles = self.border_tile + 1
        self.pieces = min(LANES // slots, self.groups)
        self.piece_groups = -(-self.groups // self.pieces)
        self.border_pieces = min(LANES // border, self.groups)
        self.border_groups = -(-self.groups // self.border_pieces)

    def message(self):
        return (self.peers, 8 * self.piece_groups, LANES)

    def border_message(self):
        return (8 * self.border_groups, LANES)


def lane_ids():
    return lax.broadcasted_iota(jnp.int32, (8, LANES), 1)


def turn(block, shift):
    shift = shift % LANES
    return block if shift == 0 else pltpu.roll(block, shift, 1)


def in_block(lanes, start, size):
    return jnp.logical_and(lanes >= start, lanes < start + size)


def half(h):
    return pl.ds(h * LANES, LANES)


def rows8(start):
    return pl.ds(pl.multiple_of(start, 8), 8)


def bits_of(tile, tiles):
    return [(tile & (1 << b)) != 0 for b in range(max(tiles - 1, 1).bit_length())]


def pick_tile(values, masks):
    def pick(lowest, bit):
        if bit < 0:
            return values(lowest)
        first = pick(lowest, bit - 1)
        if lowest + (1 << bit) >= values.count:
            return first
        return jnp.where(masks[bit], pick(lowest + (1 << bit), bit - 1), first)

    return pick(0, len(masks) - 1)


class Taken:
    def __init__(self, sources, lane):
        self.sources = sources
        self.lane = lane
        self.count = len(sources)

    def __call__(self, tile):
        return jnp.take_along_axis(
            self.sources[tile], self.lane, axis=1, mode="promise_in_bounds"
        )


def gather(sources, code):
    return pick_tile(Taken(sources, code & (LANES - 1)), bits_of(code >> 7, len(sources)))


def local_sources(plan, phi, ends, g):
    w = plan.layers
    if w == 1:
        along_y = g * 64
    else:
        along_y = (g // w) * 64 + lax.rem(g, w) * 8
    starts = [g * 8, (8 - w) * 64 + g * 8, along_y, along_y + (8 - w) * 8]
    found = []
    for start in starts:
        for h in range(plan.halves):
            found.append(phi[h, rows8(start), :])
    for end in range(2):
        for h in range(plan.halves):
            if w == 1:
                found.append(phi[h, pl.ds(g * 64 + 7 * end, 8, stride=8), :])
            else:
                found.append(ends[end, h, rows8(g * 8), :])
    return found


def fill_ends(plan, phi, ends):
    w = plan.layers
    if w == 1:
        return

    @pl.loop(0, 8)
    def _(i):
        for end in range(2):
            for l in range(w):
                k = l + end * (8 - w)
                for h in range(plan.halves):
                    ends[end, h, pl.ds(i * 8 * w + l, 8, stride=w), :] = phi[
                        h, pl.ds(i * 64 + k, 8, stride=8), :
                    ]


def pack_sends(plan, phi, ends, send_code, table, outgoing, low, high):
    lanes = lane_ids()
    w = plan.layers

    @pl.loop(0, plan.groups // 4)
    def _(q):
        for v in range(4):
            g = q * 4 + v
            sources = local_sources(plan, phi, ends, g)
            for t in range(plan.far_tiles):
                code = jnp.broadcast_to(send_code[pl.ds(t, 1), :], (8, LANES))
                table[t, rows8(g * 8), :] = gather(sources, code)

    for e in range(plan.peers):
        t, eq = divmod(e, plan.per_tile)
        for gi in range(plan.piece_groups):
            block = None
            for p in range(plan.pieces):
                g = p * plan.piece_groups + gi
                if g >= plan.groups:
                    continue
                part = turn(table[t, pl.ds(g * 8, 8), :], (p - eq) * plan.slots)
                if block is None:
                    block = part
                else:
                    block = jnp.where(lanes >= p * plan.slots, part, block)
            outgoing[e, pl.ds(gi * 8, 8), :] = block
    for side, target in enumerate((low, high)):
        for gi in range(plan.border_groups):
            block = None
            for p in range(plan.border_pieces):
                g = p * plan.border_groups + gi
                if g >= plan.groups:
                    continue
                part = turn(
                    table[plan.border_tile, pl.ds(g * 8, 8), :],
                    (p - side) * plan.border - plan.border_lane,
                )
                if block is None:
                    block = part
                else:
                    block = jnp.where(lanes >= p * plan.border, part, block)
            target[pl.ds(gi * 8, 8), :] = block


def unpack_far(plan, arrived, before, after, table):
    lanes = lane_ids()
    for g in range(plan.groups):
        p, gi = divmod(g, plan.piece_groups)
        bp, bgi = divmod(g, plan.border_groups)
        for t in range(plan.far_tiles):
            block = None
            if t < plan.peer_tiles:
                for eq in range(min(plan.per_tile, plan.peers - t * plan.per_tile)):
                    e = t * plan.per_tile + eq
                    part = turn(arrived[e, pl.ds(gi * 8, 8), :], (eq - p) * plan.slots)
                    if block is None:
                        block = part
                    else:
                        block = jnp.where(lanes >= eq * plan.slots, part, block)
            if t == plan.border_tile:
                for q, source in enumerate((before, after)):
                    start = plan.border_lane + q * plan.border
                    part = turn(source[pl.ds(bgi * 8, 8), :], start - bp * plan.border)
                    if block is None:
                        block = part
                    else:
                        block = jnp.where(lanes >= start, part, block)
            table[t, pl.ds(g * 8, 8), :] = block


def pull_local(plan, phi, ends, halo_code, halos, g):
    sources = local_sources(plan, phi, ends, g)
    for s in range(6):
        for h in range(plan.halves):
            code = jnp.broadcast_to(halo_code[pl.ds(s, 1), half(h)], (8, LANES))
            halos[s, h, rows8(g * 8), :] = gather(sources, code)


def pull_far(plan, table, halo_code, near, halos, sides, g):
    start = plan.local_tiles * LANES
    sources = [table[t, rows8(g * 8), :] for t in range(plan.far_tiles)]
    for s in sides:
        for h in range(plan.halves):
            code = jnp.broadcast_to(halo_code[pl.ds(s, 1), half(h)], (8, LANES))
            far = gather(sources, code - start)
            here = near[s, h, rows8(g * 8), :]
            halos[s, h, rows8(g * 8), :] = jnp.where(code >= start, far, here)


def weno_windows(q):
    first = [q[m + 1] - q[m] for m in range(7)]
    second = [first[m + 1] - first[m] for m in range(6)]
    third = [second[m + 1] - second[m] for m in range(5)]
    fourth = [(third[m] - third[m + 1]) * (1.0 / 3.0) for m in range(4)]
    bend = [t * t * (4.0 / 3.0) + weno_floor for t in third]
    found = []
    for m in range(3):
        s1, s2 = second[m + 1], second[m + 2]
        a = bend[m] + s1 * (s1 + third[m])
        b = bend[m + 1] + s1 * s2
        c = bend[m + 2] + s2 * (s2 - third[m + 2])
        a, b, c = a * a, b * b, c * c
        x = b * c
        z = a * b
        total = x + z + 6.0 * (a * c)
        xu = x * fourth[m]
        zu = z * fourth[m + 1]
        slope = 0.25 * (s1 + s2)
        middle = first[m + 2] + third[m + 1] * (1.0 / 12.0)
        fix = (xu + 1.5 * zu) * pl.reciprocal(total + 2.0 * z, approx=True)
        backward = middle + slope + fix
        fix = (zu + 1.5 * xu) * pl.reciprocal(total + 2.0 * x, approx=True)
        found.append((backward, fix + slope - middle))
    return found


def inner_values(values):
    three, four, five = weno_windows(values)
    return [three[1], jnp.maximum(three[0], four[1]), jnp.maximum(four[0], five[1]), five[0]]


def line_values(low, values, high, inner):
    zero, one, two = weno_windows(low + values[:5])
    six, seven, last = weno_windows(values[3:] + high)
    steep = [
        jnp.maximum(zero[0], one[1]),
        jnp.maximum(one[0], two[1]),
        jnp.maximum(two[0], inner[0]),
        inner[1],
        inner[2],
        jnp.maximum(inner[3], six[1]),
        jnp.maximum(six[0], seven[1]),
        jnp.maximum(seven[0], last[1]),
    ]
    steep = [jnp.maximum(value, 0.0) for value in steep]
    return [value * value for value in steep]


def line_at(phi, h, axis, q):
    if axis == 0:
        return [phi[h, rows8(m * 64 + q * 8), :] for m in range(8)]
    if axis == 1:
        return [phi[h, rows8(q * 64 + m * 8), :] for m in range(8)]
    return [phi[h, pl.ds(q * 64 + m, 8, stride=8), :] for m in range(8)]


def inner_at(inner, h, axis, q):
    return [inner[axis, h, rows8(q * 32 + m * 8), :] for m in range(4)]


def advect(plan, phi, speed, ready, near, inner, table, halo_code, halos, squares, moved):
    w = plan.layers

    def stage_planes(i):
        for l in range(w):
            pull_far(plan, table, halo_code, near, halos, (2, 3, 4, 5), i * w + l)

    def stage_columns(j):
        for l in range(w):
            pull_far(plan, table, halo_code, near, halos, (0, 1), l * 8 + j)

    stage_planes(0)

    @pl.loop(0, 8)
    def _(i):
        lines = []
        for h in range(plan.halves):
            ends = [
                [halos[s, h, pl.ds(i * 8 * w + l, 8, stride=w), :] for l in range(w)]
                for s in (4, 5)
            ]
            lines.append((ends[0], line_at(phi, h, 2, i), ends[1], inner_at(inner, h, 2, i)))
            ends = [
                [halos[s, h, rows8((i * w + l) * 8), :] for l in range(w)] for s in (2, 3)
            ]
            lines.append((ends[0], line_at(phi, h, 1, i), ends[1], inner_at(inner, h, 1, i)))
        stage_planes(jnp.minimum(i + 1, 7))
        for h in range(plan.halves):
            for k, value in enumerate(line_values(*lines[2 * h])):
                squares[h, pl.ds(i * 64 + k, 8, stride=8), :] = value
            for j, value in enumerate(line_values(*lines[2 * h + 1])):
                squares[h, rows8(i * 64 + j * 8), :] += value

    ready()
    stage_columns(0)

    @pl.loop(0, 8)
    def _(j):
        lines = []
        for h in range(plan.halves):
            ends = [
                [halos[s, h, rows8((l * 8 + j) * 8), :] for l in range(w)] for s in (0, 1)
            ]
            lines.append((ends[0], line_at(phi, h, 0, j), ends[1], inner_at(inner, h, 0, j)))
        stage_columns(jnp.minimum(j + 1, 7))
        for h in range(plan.halves):
            for i, value in enumerate(line_values(*lines[h])):
                here = rows8(i * 64 + j * 8)
                total = squares[h, here, :] + value
                change = advect_scale * speed[h, here, :] * jnp.sqrt(total)
                moved[h, here, :] = lines[h][1][i] - change


def relax(plan, phi, origin, near, table, halo_code, halos, moved, joined):
    row = lax.broadcasted_iota(jnp.int32, (8, LANES), 0)

    @pl.loop(0, 2)
    def _(q):
        for v in range(4):
            pull_far(plan, table, halo_code, near, halos, (0, 1), q * 4 + v)

    def stage(i):
        pull_far(plan, table, halo_code, near, halos, (2, 3, 4, 5), i)

    def plane(i, h, previous, following, sides):
        at = half(h)
        centre = [phi[h, rows8(i * 64 + j * 8), :] for j in range(8)]
        along_y = [sides[0]] + centre + [sides[1]]
        for j in range(8):
            here = rows8(i * 64 + j * 8)
            value = centre[j]
            start = origin[h, here, :]
            sense = start * lax.rsqrt(start * start + 1.0)
            facing = jnp.where(start > 0.0, 1.0, -1.0)
            first = jnp.broadcast_to(sides[2][j : j + 1], (8, LANES))
            last = jnp.broadcast_to(sides[3][j : j + 1], (8, LANES))
            low_z = jnp.where(row == 0, first, pltpu.roll(value, 1, 0))
            high_z = jnp.where(row == 7, last, pltpu.roll(value, 7, 0))
            pairs = (
                (previous(j), following(j)),
                (along_y[j], along_y[j + 2]),
                (low_z, high_z),
            )
            total = None
            for low, high in pairs:
                steep = jnp.maximum((value - low) * facing, (value - high) * facing)
                steep = jnp.maximum(steep, 0.0)
                steep = steep * steep
                total = steep if total is None else total + steep
            value = value - relax_scale * sense * (jnp.sqrt(total) - 1.0)
            if joined:
                moved[here, at] = value
            else:
                moved[h, here, :] = value

    def planes(i, low, high):
        sides = [
            [halos[s, h, rows8(i * 8), :] for s in (2, 3, 4, 5)] for h in range(plan.halves)
        ]
        if not isinstance(i, int) or i < 7:
            stage(i + 1)
        for h in range(plan.halves):

            def previous(j):
                if low is None:
                    return phi[h, rows8((i - 1) * 64 + j * 8), :]
                return halos[low, h, pl.ds(j * 8, 8), :]

            def following(j):
                if high is None:
                    return phi[h, rows8((i + 1) * 64 + j * 8), :]
                return halos[high, h, pl.ds(j * 8, 8), :]

            plane(i, h, previous, following, sides[h])

    stage(0)
    planes(0, 0, None)

    @pl.loop(1, 7)
    def _(i):
        planes(i, None, None)

    planes(7, None, 1)


def first_kernel(
    plan, level_set, peer_slabs, region_slabs, halo_source,
    phi, outgoing, low, high, send_code, halo_code, ends, table, padded, peer, region, entries, ready,
):
    copies = [
        pltpu.make_async_copy(source, target, ready.at[n])
        for n, (source, target) in enumerate(
            ((peer_slabs, peer), (region_slabs, region), (halo_source, entries))
        )
    ]
    for h in range(plan.halves):
        copies.append(
            pltpu.make_async_copy(level_set.at[:, half(h)], phi.at[h], ready.at[3 + h])
        )
    for copy in copies:
        copy.start()
    for copy in copies:
        copy.wait()
    lanes = lane_ids()
    padded[...] = jnp.zeros_like(padded)
    padded[pl.ds(0, plan.peers), pl.ds(0, plan.slots)] = jnp.maximum(peer[...], 0)
    padded[pl.ds(plan.peers, 2), pl.ds(0, plan.border)] = region[...]

    def wide(row):
        return jnp.broadcast_to(padded[pl.ds(row, 1), :], (8, LANES))

    send_code[...] = jnp.zeros_like(send_code)
    for t in range(plan.far_tiles):
        block = jnp.zeros((8, LANES), jnp.int32)
        if t < plan.peer_tiles:
            for eq in range(min(plan.per_tile, plan.peers - t * plan.per_tile)):
                part = turn(wide(t * plan.per_tile + eq), eq * plan.slots)
                block = jnp.where(in_block(lanes, eq * plan.slots, plan.slots), part, block)
        if t == plan.border_tile:
            for side in range(2):
                start = plan.border_lane + side * plan.border
                part = turn(wide(plan.peers + side), start)
                block = jnp.where(in_block(lanes, start, plan.border), part, block)
        send_code[pl.ds(t, 1), :] = block[0:1]

    entry = entries[...]
    far = entry - plan.local_tiles * LANES
    tile_span = plan.per_tile * plan.slots
    tile = jnp.zeros_like(entry)
    for k in range(1, plan.peer_tiles):
        tile += (far >= k * tile_span).astype(jnp.int32)
    code = (plan.local_tiles + tile) * LANES + far - tile * tile_span
    edge = far - plan.peers * plan.slots
    edge_code = (plan.local_tiles + plan.border_tile) * LANES + plan.border_lane + edge
    code = jnp.where(edge >= 0, edge_code, code)
    halo_code[...] = jnp.where(far >= 0, code, entry)

    fill_ends(plan, phi, ends)
    pack_sends(plan, phi, ends, send_code, table, outgoing, low, high)


def near_kernel(plan, phi, halo_code, near, *rest):
    if plan.layers == 1:

        @pl.loop(0, plan.groups // 2)
        def _(q):
            for v in range(2):
                pull_local(plan, phi, None, halo_code, near, q * 2 + v)

        return
    inner, ends = rest
    fill_ends(plan, phi, ends)
    for axis in range(3):

        @pl.loop(0, 8)
        def _(q):
            lines = [line_at(phi, h, axis, q) for h in range(plan.halves)]
            pull_local(plan, phi, ends, halo_code, near, axis * 8 + q)
            for h in range(plan.halves):
                for m, value in enumerate(inner_values(lines[h])):
                    inner[axis, h, rows8(q * 32 + m * 8), :] = value


def advect_kernel(
    plan, sends, phi, near, inner, speed, arrived, before, after, send_code, halo_code,
    moved, outgoing, low, high, ends, table, halos, squares, fast, loaded,
):
    copies = [
        pltpu.make_async_copy(speed.at[:, half(h)], fast.at[h], loaded.at[h])
        for h in range(plan.halves)
    ]
    for copy in copies:
        copy.start()

    def ready():
        for copy in copies:
            copy.wait()

    unpack_far(plan, arrived, before, after, table)
    advect(plan, phi, fast, ready, near, inner, table, halo_code, halos, squares, moved)
    pack_sends(sends, moved, ends, send_code, table, outgoing, low, high)


def relax_kernel(
    plan, sends, phi, origin, near, arrived, before, after, send_code, halo_code, *rest
):
    if sends is None:
        (moved, table, halos) = rest
    else:
        (moved, outgoing, low, high, ends, table, halos) = rest
    unpack_far(plan, arrived, before, after, table)
    relax(plan, phi, origin, near, table, halo_code, halos, moved, sends is None)
    if sends is not None:
        fill_ends(sends, moved, ends)
        pack_sends(sends, moved, ends, send_code, table, outgoing, low, high)


def f32(shape):
    return jax.ShapeDtypeStruct(shape, jnp.float32)


def call(kernel, out_shape, scratch, flops, *operands, far=()):
    whole = pl.BlockSpec(memory_space=pltpu.VMEM)
    apart = pl.BlockSpec(memory_space=pltpu.HBM)
    size = sum(x.size * 4 for x in operands) + sum(x.size * 4 for x in out_shape)
    operands = [
        pltpu.with_memory_space_constraint(x, pltpu.HBM) if n in far else x
        for n, x in enumerate(operands)
    ]
    return pl.pallas_call(
        kernel,
        out_shape=out_shape,
        in_specs=[apart if n in far else whole for n in range(len(operands))],
        out_specs=[whole] * len(out_shape),
        scratch_shapes=scratch,
        cost_estimate=pl.CostEstimate(flops=flops, bytes_accessed=size, transcendentals=0),
        compiler_params=pltpu.CompilerParams(vmem_limit_bytes=12 * 1024 * 1024),
    )(*operands)


def exchange(outgoing, low, high):
    count = lax.axis_size("group")
    up = [(i, (i + 1) % count) for i in range(count)]
    down = [(target, source) for source, target in up]
    arrived = lax.all_to_all(outgoing, "dev", split_axis=0, concat_axis=0, tiled=True)
    before = lax.ppermute(high, "group", up)
    after = lax.ppermute(low, "group", down)
    return arrived, before, after


def per_device(level_set, speed, peer_slabs, region_slabs, halo_source):
    rows, count = level_set.shape
    peers, slots = peer_slabs.shape
    border = region_slabs.shape[1]
    wide = Plan(count, peers, slots, border, 3)
    thin = Plan(count, peers, slots, border, 1)
    code_rows = -(-wide.far_tiles // 8) * 8

    def ends(plan):
        return pltpu.VMEM((2, wide.halves, 64 * plan.layers, LANES), jnp.float32)

    def table(plan):
        return pltpu.VMEM((plan.far_tiles, 64 * plan.layers, LANES), jnp.float32)

    def halos(plan):
        return pltpu.VMEM((6, wide.halves, 64 * plan.layers, LANES), jnp.float32)

    def sent(plan):
        return [f32(plan.message()), f32(plan.border_message()), f32(plan.border_message())]

    field = f32((wide.halves, rows, LANES))
    pad_rows = -(-(peers + 2) // 8) * 8
    phi, *message, send_code, halo_code = call(
        functools.partial(first_kernel, wide),
        [field]
        + sent(wide)
        + [
            jax.ShapeDtypeStruct((code_rows, LANES), jnp.int32),
            jax.ShapeDtypeStruct(halo_source.shape, jnp.int32),
        ],
        [
            ends(wide),
            table(wide),
            pltpu.VMEM((pad_rows, LANES), jnp.int32),
            pltpu.VMEM(peer_slabs.shape, jnp.int32),
            pltpu.VMEM(region_slabs.shape, jnp.int32),
            pltpu.VMEM(halo_source.shape, jnp.int32),
            pltpu.SemaphoreType.DMA((3 + wide.halves,)),
        ],
        1000000,
        level_set, peer_slabs, region_slabs, halo_source,
        far=(0, 1, 2, 3),
    )

    def near_halos(plan, phi):
        out = [f32((6, plan.halves, 64 * plan.layers, LANES))]
        scratch = []
        if plan.layers > 1:
            out.append(f32((3, plan.halves, rows // 2, LANES)))
            scratch.append(ends(plan))
        flops = rows * count * 100 * plan.layers
        return call(functools.partial(near_kernel, plan), out, scratch, flops, phi, halo_code)

    block = pltpu.VMEM((wide.halves, rows, LANES), jnp.float32)
    for offset_step in range(OFFSET_STEPS):
        phi, *message = call(
            functools.partial(advect_kernel, wide, thin),
            [field] + sent(thin),
            [ends(wide), table(wide), halos(wide), block, block]
            + [pltpu.SemaphoreType.DMA((wide.halves,))],
            rows * count * 300,
            phi, *near_halos(wide, phi), speed, *exchange(*message), send_code, halo_code,
            far=(3,),
        )
        origin = phi
        for redist_pass in range(REDIST_PASSES):
            if redist_pass < REDIST_PASSES - 1:
                sends = thin
            elif offset_step < OFFSET_STEPS - 1:
                sends = wide
            else:
                sends = None
            if sends is None:
                out, scratch = [f32((rows, count))], [table(thin)]
            else:
                out, scratch = [field] + sent(sends), [ends(sends), table(sends)]
            phi, *message = call(
                functools.partial(relax_kernel, thin, sends),
                out,
                scratch + [halos(thin)],
                rows * count * 60,
                phi, origin, *near_halos(thin, phi), *exchange(*message), send_code, halo_code,
            )
    return phi


def solution(mesh):
    return jax.shard_map(
        per_device,
        mesh=mesh,
        in_specs=(
            P(None, ("group", "dev")),
            P(None, ("group", "dev")),
            P(("group", "dev"), None),
            P(("group", "dev"), None),
            P(None, ("group", "dev")),
        ),
        out_specs=P(None, ("group", "dev")),
        check_vma=False,
    )
```

```python
import functools

import jax
import jax.numpy as jnp
from jax import lax
from jax.experimental import pallas as pl
from jax.experimental.pallas import tpu as pltpu
from jax.sharding import PartitionSpec as P

OFFSET_STEPS = 2
REDIST_PASSES = 2

advect_scale = 0.3
relax_scale = 0.3
weno_floor = 1e-06

LANES = 128


class Plan:
    def __init__(self, count, peers, slots, border, layers):
        self.count = count
        self.peers = peers
        self.slots = slots
        self.border = border
        self.layers = layers
        self.halves = count // LANES
        self.local_tiles = 6 * self.halves
        self.groups = 8 * layers
        self.per_tile = LANES // slots
        self.peer_tiles = -(-peers // self.per_tile)
        used = (peers - (self.peer_tiles - 1) * self.per_tile) * slots
        if used + 2 * border <= LANES:
            self.border_tile = self.peer_tiles - 1
            self.border_lane = used
        else:
            self.border_tile = self.peer_tiles
            self.border_lane = 0
        self.far_tiles = self.border_tile + 1
        self.pieces = min(LANES // slots, self.groups)
        self.piece_groups = -(-self.groups // self.pieces)
        self.border_pieces = min(LANES // border, self.groups)
        self.border_groups = -(-self.groups // self.border_pieces)

    def message(self):
        return (self.peers, 8 * self.piece_groups, LANES)

    def border_message(self):
        return (8 * self.border_groups, LANES)


def lane_ids():
    return lax.broadcasted_iota(jnp.int32, (8, LANES), 1)


def turn(block, shift):
    shift = shift % LANES
    return block if shift == 0 else pltpu.roll(block, shift, 1)


def in_block(lanes, start, size):
    return jnp.logical_and(lanes >= start, lanes < start + size)


def half(h):
    return pl.ds(h * LANES, LANES)


def rows8(start):
    return pl.ds(pl.multiple_of(start, 8), 8)


def bits_of(tile, tiles):
    return [(tile & (1 << b)) != 0 for b in range(max(tiles - 1, 1).bit_length())]


def pick_tile(values, masks):
    def pick(lowest, bit):
        if bit < 0:
            return values(lowest)
        first = pick(lowest, bit - 1)
        if lowest + (1 << bit) >= values.count:
            return first
        return jnp.where(masks[bit], pick(lowest + (1 << bit), bit - 1), first)

    return pick(0, len(masks) - 1)


class Taken:
    def __init__(self, sources, lane):
        self.sources = sources
        self.lane = lane
        self.count = len(sources)

    def __call__(self, tile):
        return jnp.take_along_axis(
            self.sources[tile], self.lane, axis=1, mode="promise_in_bounds"
        )


def gather(sources, code):
    return pick_tile(Taken(sources, code & (LANES - 1)), bits_of(code >> 7, len(sources)))


def local_sources(plan, phi, ends, g):
    w = plan.layers
    if w == 1:
        along_y = g * 64
    else:
        along_y = (g // w) * 64 + lax.rem(g, w) * 8
    starts = [g * 8, (8 - w) * 64 + g * 8, along_y, along_y + (8 - w) * 8]
    found = []
    for start in starts:
        for h in range(plan.halves):
            found.append(phi[h, rows8(start), :])
    for end in range(2):
        for h in range(plan.halves):
            if w == 1:
                found.append(phi[h, pl.ds(g * 64 + 7 * end, 8, stride=8), :])
            else:
                found.append(ends[end, h, rows8(g * 8), :])
    return found


def fill_ends(plan, phi, ends):
    w = plan.layers
    if w == 1:
        return

    @pl.loop(0, 8)
    def _(i):
        for end in range(2):
            for l in range(w):
                k = l + end * (8 - w)
                for h in range(plan.halves):
                    ends[end, h, pl.ds(i * 8 * w + l, 8, stride=w), :] = phi[
                        h, pl.ds(i * 64 + k, 8, stride=8), :
                    ]


def pick_slabs(plan, phi, ends, send_code, targets, together):
    @pl.loop(0, plan.groups // together)
    def _(q):
        for v in range(together):
            g = q * together + v
            sources = local_sources(plan, phi, ends, g)
            for t, target in targets:
                code = jnp.broadcast_to(send_code[pl.ds(t, 1), :], (8, LANES))
                target[rows8(g * 8), :] = gather(sources, code)


def pack_borders(plan, phi, ends, send_code, shared, low, high):
    lanes = lane_ids()
    pick_slabs(plan, phi, ends, send_code, [(plan.border_tile, shared)], 8)
    for side, target in enumerate((low, high)):
        for gi in range(plan.border_groups):
            block = None
            for p in range(plan.border_pieces):
                g = p * plan.border_groups + gi
                if g >= plan.groups:
                    continue
                part = turn(
                    shared[pl.ds(g * 8, 8), :],
                    (p - side) * plan.border - plan.border_lane,
                )
                if block is None:
                    block = part
                else:
                    block = jnp.where(lanes >= p * plan.border, part, block)
            target[pl.ds(gi * 8, 8), :] = block


def pack_kernel(plan, phi, shared, send_code, outgoing, table, ends):
    lanes = lane_ids()
    fill_ends(plan, phi, ends)
    tiles = [shared if t == plan.border_tile else table.at[t] for t in range(plan.peer_tiles)]
    wanted = [(t, tile) for t, tile in enumerate(tiles) if t != plan.border_tile]
    pick_slabs(plan, phi, ends, send_code, wanted, 4)
    for e in range(plan.peers):
        t, eq = divmod(e, plan.per_tile)
        for gi in range(plan.piece_groups):
            block = None
            for p in range(plan.pieces):
                g = p * plan.piece_groups + gi
                if g >= plan.groups:
                    continue
                part = turn(tiles[t][pl.ds(g * 8, 8), :], (p - eq) * plan.slots)
                if block is None:
                    block = part
                else:
                    block = jnp.where(lanes >= p * plan.slots, part, block)
            outgoing[e, pl.ds(gi * 8, 8), :] = block


def unpack_far(plan, arrived, before, after, table):
    lanes = lane_ids()
    for g in range(plan.groups):
        p, gi = divmod(g, plan.piece_groups)
        bp, bgi = divmod(g, plan.border_groups)
        for t in range(plan.far_tiles):
            block = None
            if t < plan.peer_tiles:
                for eq in range(min(plan.per_tile, plan.peers - t * plan.per_tile)):
                    e = t * plan.per_tile + eq
                    part = turn(arrived[e, pl.ds(gi * 8, 8), :], (eq - p) * plan.slots)
                    if block is None:
                        block = part
                    else:
                        block = jnp.where(lanes >= eq * plan.slots, part, block)
            if t == plan.border_tile:
                for q, source in enumerate((before, after)):
                    start = plan.border_lane + q * plan.border
                    part = turn(source[pl.ds(bgi * 8, 8), :], start - bp * plan.border)
                    if block is None:
                        block = part
                    else:
                        block = jnp.where(lanes >= start, part, block)
            table[t, pl.ds(g * 8, 8), :] = block


def pull_local(plan, phi, ends, halo_code, halos, g):
    sources = local_sources(plan, phi, ends, g)
    for s in range(6):
        for h in range(plan.halves):
            code = jnp.broadcast_to(halo_code[pl.ds(s, 1), half(h)], (8, LANES))
            halos[s, h, rows8(g * 8), :] = gather(sources, code)


def pull_far(plan, table, halo_code, near, halos, sides, g):
    start = plan.local_tiles * LANES
    sources = [table[t, rows8(g * 8), :] for t in range(plan.far_tiles)]
    for s in sides:
        for h in range(plan.halves):
            code = jnp.broadcast_to(halo_code[pl.ds(s, 1), half(h)], (8, LANES))
            far = gather(sources, code - start)
            here = near[s, h, rows8(g * 8), :]
            halos[s, h, rows8(g * 8), :] = jnp.where(code >= start, far, here)


def weno_windows(q):
    first = [q[m + 1] - q[m] for m in range(7)]
    second = [first[m + 1] - first[m] for m in range(6)]
    third = [second[m + 1] - second[m] for m in range(5)]
    fourth = [(third[m] - third[m + 1]) * (1.0 / 3.0) for m in range(4)]
    bend = [t * t * (4.0 / 3.0) + weno_floor for t in third]
    found = []
    for m in range(3):
        s1, s2 = second[m + 1], second[m + 2]
        a = bend[m] + s1 * (s1 + third[m])
        b = bend[m + 1] + s1 * s2
        c = bend[m + 2] + s2 * (s2 - third[m + 2])
        a, b, c = a * a, b * b, c * c
        x = b * c
        z = a * b
        total = x + z + 6.0 * (a * c)
        xu = x * fourth[m]
        zu = z * fourth[m + 1]
        slope = 0.25 * (s1 + s2)
        middle = first[m + 2] + third[m + 1] * (1.0 / 12.0)
        fix = (xu + 1.5 * zu) * pl.reciprocal(total + 2.0 * z, approx=True)
        backward = middle + slope + fix
        fix = (zu + 1.5 * xu) * pl.reciprocal(total + 2.0 * x, approx=True)
        found.append((backward, fix + slope - middle))
    return found


def inner_values(values):
    three, four, five = weno_windows(values)
    return [three[1], jnp.maximum(three[0], four[1]), jnp.maximum(four[0], five[1]), five[0]]


def line_values(low, values, high, inner):
    zero, one, two = weno_windows(low + values[:5])
    six, seven, last = weno_windows(values[3:] + high)
    steep = [
        jnp.maximum(zero[0], one[1]),
        jnp.maximum(one[0], two[1]),
        jnp.maximum(two[0], inner[0]),
        inner[1],
        inner[2],
        jnp.maximum(inner[3], six[1]),
        jnp.maximum(six[0], seven[1]),
        jnp.maximum(seven[0], last[1]),
    ]
    steep = [jnp.maximum(value, 0.0) for value in steep]
    return [value * value for value in steep]


def line_at(phi, h, axis, q):
    if axis == 0:
        return [phi[h, rows8(m * 64 + q * 8), :] for m in range(8)]
    if axis == 1:
        return [phi[h, rows8(q * 64 + m * 8), :] for m in range(8)]
    return [phi[h, pl.ds(q * 64 + m, 8, stride=8), :] for m in range(8)]


def inner_at(inner, h, axis, q):
    return [inner[axis, h, rows8(q * 32 + m * 8), :] for m in range(4)]


def advect(plan, phi, speed, ready, near, inner, table, halo_code, halos, squares, moved):
    w = plan.layers

    def stage_planes(i):
        for l in range(w):
            pull_far(plan, table, halo_code, near, halos, (2, 3, 4, 5), i * w + l)

    def stage_columns(j):
        for l in range(w):
            pull_far(plan, table, halo_code, near, halos, (0, 1), l * 8 + j)

    stage_planes(0)
    ready()

    @pl.loop(0, 8)
    def _(i):
        lines = []
        for h in range(plan.halves):
            ends = [
                [halos[s, h, pl.ds(i * 8 * w + l, 8, stride=w), :] for l in range(w)]
                for s in (4, 5)
            ]
            lines.append((ends[0], line_at(phi, h, 2, i), ends[1], inner_at(inner, h, 2, i)))
            ends = [
                [halos[s, h, rows8((i * w + l) * 8), :] for l in range(w)] for s in (2, 3)
            ]
            lines.append((ends[0], line_at(phi, h, 1, i), ends[1], inner_at(inner, h, 1, i)))
        stage_planes(jnp.minimum(i + 1, 7))
        for h in range(plan.halves):
            for k, value in enumerate(line_values(*lines[2 * h])):
                squares[h, pl.ds(i * 64 + k, 8, stride=8), :] = value
            for j, value in enumerate(line_values(*lines[2 * h + 1])):
                squares[h, rows8(i * 64 + j * 8), :] += value

    stage_columns(0)

    @pl.loop(0, 8)
    def _(j):
        lines = []
        for h in range(plan.halves):
            ends = [
                [halos[s, h, rows8((l * 8 + j) * 8), :] for l in range(w)] for s in (0, 1)
            ]
            lines.append((ends[0], line_at(phi, h, 0, j), ends[1], inner_at(inner, h, 0, j)))
        stage_columns(jnp.minimum(j + 1, 7))
        for h in range(plan.halves):
            for i, value in enumerate(line_values(*lines[h])):
                here = rows8(i * 64 + j * 8)
                total = squares[h, here, :] + value
                change = advect_scale * speed[h, here, :] * jnp.sqrt(total)
                moved[h, here, :] = lines[h][1][i] - change


def relax(plan, phi, origin, near, table, halo_code, halos, moved, joined):
    row = lax.broadcasted_iota(jnp.int32, (8, LANES), 0)

    @pl.loop(0, 2)
    def _(q):
        for v in range(4):
            pull_far(plan, table, halo_code, near, halos, (0, 1), q * 4 + v)

    def stage(i):
        pull_far(plan, table, halo_code, near, halos, (2, 3, 4, 5), i)

    def plane(i, h, previous, following, sides):
        at = half(h)
        centre = [phi[h, rows8(i * 64 + j * 8), :] for j in range(8)]
        along_y = [sides[0]] + centre + [sides[1]]
        for j in range(8):
            here = rows8(i * 64 + j * 8)
            value = centre[j]
            start = origin[h, here, :]
            sense = start * lax.rsqrt(start * start + 1.0)
            facing = jnp.where(start > 0.0, 1.0, -1.0)
            first = jnp.broadcast_to(sides[2][j : j + 1], (8, LANES))
            last = jnp.broadcast_to(sides[3][j : j + 1], (8, LANES))
            low_z = jnp.where(row == 0, first, pltpu.roll(value, 1, 0))
            high_z = jnp.where(row == 7, last, pltpu.roll(value, 7, 0))
            pairs = (
                (previous(j), following(j)),
                (along_y[j], along_y[j + 2]),
                (low_z, high_z),
            )
            total = None
            for low, high in pairs:
                steep = jnp.maximum((value - low) * facing, (value - high) * facing)
                steep = jnp.maximum(steep, 0.0)
                steep = steep * steep
                total = steep if total is None else total + steep
            value = value - relax_scale * sense * (jnp.sqrt(total) - 1.0)
            if joined:
                moved[here, at] = value
            else:
                moved[h, here, :] = value

    def planes(i, low, high):
        sides = [
            [halos[s, h, rows8(i * 8), :] for s in (2, 3, 4, 5)] for h in range(plan.halves)
        ]
        if not isinstance(i, int) or i < 7:
            stage(i + 1)
        for h in range(plan.halves):

            def previous(j):
                if low is None:
                    return phi[h, rows8((i - 1) * 64 + j * 8), :]
                return halos[low, h, pl.ds(j * 8, 8), :]

            def following(j):
                if high is None:
                    return phi[h, rows8((i + 1) * 64 + j * 8), :]
                return halos[high, h, pl.ds(j * 8, 8), :]

            plane(i, h, previous, following, sides[h])

    stage(0)
    planes(0, 0, None)

    @pl.loop(1, 7)
    def _(i):
        planes(i, None, None)

    planes(7, None, 1)


def first_kernel(
    plan, level_set, peer_slabs, region_slabs, halo_source,
    phi, shared, low, high, send_code, halo_code, ends, padded, peer, region, entries, ready,
):
    copies = [
        pltpu.make_async_copy(source, target, ready.at[n])
        for n, (source, target) in enumerate(
            ((peer_slabs, peer), (region_slabs, region), (halo_source, entries))
        )
    ]
    for h in range(plan.halves):
        copies.append(
            pltpu.make_async_copy(level_set.at[:, half(h)], phi.at[h], ready.at[3 + h])
        )
    for copy in copies:
        copy.start()
    for copy in copies:
        copy.wait()
    lanes = lane_ids()
    padded[...] = jnp.zeros_like(padded)
    padded[pl.ds(0, plan.peers), pl.ds(0, plan.slots)] = jnp.maximum(peer[...], 0)
    padded[pl.ds(plan.peers, 2), pl.ds(0, plan.border)] = region[...]

    def wide(row):
        return jnp.broadcast_to(padded[pl.ds(row, 1), :], (8, LANES))

    send_code[...] = jnp.zeros_like(send_code)
    for t in range(plan.far_tiles):
        block = jnp.zeros((8, LANES), jnp.int32)
        if t < plan.peer_tiles:
            for eq in range(min(plan.per_tile, plan.peers - t * plan.per_tile)):
                part = turn(wide(t * plan.per_tile + eq), eq * plan.slots)
                block = jnp.where(in_block(lanes, eq * plan.slots, plan.slots), part, block)
        if t == plan.border_tile:
            for side in range(2):
                start = plan.border_lane + side * plan.border
                part = turn(wide(plan.peers + side), start)
                block = jnp.where(in_block(lanes, start, plan.border), part, block)
        send_code[pl.ds(t, 1), :] = block[0:1]

    entry = entries[...]
    far = entry - plan.local_tiles * LANES
    tile_span = plan.per_tile * plan.slots
    tile = jnp.zeros_like(entry)
    for k in range(1, plan.peer_tiles):
        tile += (far >= k * tile_span).astype(jnp.int32)
    code = (plan.local_tiles + tile) * LANES + far - tile * tile_span
    edge = far - plan.peers * plan.slots
    edge_code = (plan.local_tiles + plan.border_tile) * LANES + plan.border_lane + edge
    code = jnp.where(edge >= 0, edge_code, code)
    halo_code[...] = jnp.where(far >= 0, code, entry)

    fill_ends(plan, phi, ends)
    pack_borders(plan, phi, ends, send_code, shared, low, high)


def near_kernel(plan, phi, halo_code, near, *rest):
    if plan.layers == 1:

        @pl.loop(0, plan.groups // 2)
        def _(q):
            for v in range(2):
                pull_local(plan, phi, None, halo_code, near, q * 2 + v)

        return
    inner, ends, kept, done = rest
    copies = [pltpu.make_async_copy(kept.at[a], inner.at[a], done.at[a]) for a in range(3)]
    fill_ends(plan, phi, ends)
    for axis in range(3):

        @pl.loop(0, 8)
        def _(q):
            lines = [line_at(phi, h, axis, q) for h in range(plan.halves)]
            pull_local(plan, phi, ends, halo_code, near, axis * 8 + q)
            for h in range(plan.halves):
                for m, value in enumerate(inner_values(lines[h])):
                    kept[axis, h, rows8(q * 32 + m * 8), :] = value

        copies[axis].start()
    for copy in copies:
        copy.wait()


def advect_kernel(
    plan, sends, phi, near, inner, speed, arrived, before, after, send_code, halo_code,
    moved, shared, low, high, ends, table, halos, squares, fast, kept, loaded, found,
):
    copies = [pltpu.make_async_copy(inner.at[a], kept.at[a], found.at[a]) for a in range(3)]
    copies += [
        pltpu.make_async_copy(speed.at[:, half(h)], fast.at[h], loaded.at[h])
        for h in range(plan.halves)
    ]
    for copy in copies:
        copy.start()

    def ready():
        for copy in copies:
            copy.wait()

    unpack_far(plan, arrived, before, after, table)
    advect(plan, phi, fast, ready, near, kept, table, halo_code, halos, squares, moved)
    pack_borders(sends, moved, ends, send_code, shared, low, high)


def relax_kernel(
    plan, sends, phi, origin, near, arrived, before, after, send_code, halo_code, *rest
):
    if sends is None:
        (moved, table, halos) = rest
    else:
        (moved, shared, low, high, ends, table, halos) = rest
    unpack_far(plan, arrived, before, after, table)
    relax(plan, phi, origin, near, table, halo_code, halos, moved, sends is None)
    if sends is not None:
        fill_ends(sends, moved, ends)
        pack_borders(sends, moved, ends, send_code, shared, low, high)


def f32(shape):
    return jax.ShapeDtypeStruct(shape, jnp.float32)


def call(kernel, out_shape, scratch, flops, *operands, far=(), far_out=()):
    whole = pl.BlockSpec(memory_space=pltpu.VMEM)
    apart = pl.BlockSpec(memory_space=pltpu.HBM)
    size = sum(x.size * 4 for x in operands) + sum(x.size * 4 for x in out_shape)
    operands = [
        pltpu.with_memory_space_constraint(x, pltpu.HBM) if n in far else x
        for n, x in enumerate(operands)
    ]
    return pl.pallas_call(
        kernel,
        out_shape=[
            pltpu.HBM(x.shape, x.dtype) if n in far_out else x for n, x in enumerate(out_shape)
        ],
        in_specs=[apart if n in far else whole for n in range(len(operands))],
        out_specs=[apart if n in far_out else whole for n in range(len(out_shape))],
        scratch_shapes=scratch,
        cost_estimate=pl.CostEstimate(flops=flops, bytes_accessed=size, transcendentals=0),
        compiler_params=pltpu.CompilerParams(vmem_limit_bytes=12 * 1024 * 1024),
    )(*operands)


def exchange(outgoing, low, high):
    count = lax.axis_size("group")
    up = [(i, (i + 1) % count) for i in range(count)]
    down = [(target, source) for source, target in up]
    arrived = lax.all_to_all(outgoing, "dev", split_axis=0, concat_axis=0, tiled=True)
    before = lax.ppermute(high, "group", up)
    after = lax.ppermute(low, "group", down)
    return arrived, before, after


def per_device(level_set, speed, peer_slabs, region_slabs, halo_source):
    rows, count = level_set.shape
    peers, slots = peer_slabs.shape
    border = region_slabs.shape[1]
    wide = Plan(count, peers, slots, border, 3)
    thin = Plan(count, peers, slots, border, 1)
    code_rows = -(-wide.far_tiles // 8) * 8

    def ends(plan):
        return pltpu.VMEM((2, wide.halves, 64 * plan.layers, LANES), jnp.float32)

    def table(plan):
        return pltpu.VMEM((plan.far_tiles, 64 * plan.layers, LANES), jnp.float32)

    def halos(plan):
        return pltpu.VMEM((6, wide.halves, 64 * plan.layers, LANES), jnp.float32)

    def sent(plan):
        tile = f32((64 * plan.layers, LANES))
        return [tile, f32(plan.border_message()), f32(plan.border_message())]

    def exchanged(plan, phi, shared, low, high):
        outgoing = call(
            functools.partial(pack_kernel, plan),
            [f32(plan.message())],
            [table(plan), ends(plan)],
            rows * count * 20 * plan.layers,
            phi, shared, send_code,
        )[0]
        return exchange(outgoing, low, high)

    field = f32((wide.halves, rows, LANES))
    pad_rows = -(-(peers + 2) // 8) * 8
    phi, *message, send_code, halo_code = call(
        functools.partial(first_kernel, wide),
        [field]
        + sent(wide)
        + [
            jax.ShapeDtypeStruct((code_rows, LANES), jnp.int32),
            jax.ShapeDtypeStruct(halo_source.shape, jnp.int32),
        ],
        [
            ends(wide),
            pltpu.VMEM((pad_rows, LANES), jnp.int32),
            pltpu.VMEM(peer_slabs.shape, jnp.int32),
            pltpu.VMEM(region_slabs.shape, jnp.int32),
            pltpu.VMEM(halo_source.shape, jnp.int32),
            pltpu.SemaphoreType.DMA((3 + wide.halves,)),
        ],
        1000000,
        level_set, peer_slabs, region_slabs, halo_source,
        far=(0, 1, 2, 3),
    )

    def near_halos(plan, phi):
        out = [f32((6, plan.halves, 64 * plan.layers, LANES))]
        scratch = []
        if plan.layers > 1:
            out.append(f32(inner_shape))
            scratch = [ends(plan), pltpu.VMEM(inner_shape, jnp.float32)]
            scratch.append(pltpu.SemaphoreType.DMA((3,)))
        flops = rows * count * 100 * plan.layers
        kernel = functools.partial(near_kernel, plan)
        return call(kernel, out, scratch, flops, phi, halo_code, far_out=(1,))

    inner_shape = (3, wide.halves, rows // 2, LANES)
    block = pltpu.VMEM((wide.halves, rows, LANES), jnp.float32)
    for offset_step in range(OFFSET_STEPS):
        phi, *message = call(
            functools.partial(advect_kernel, wide, thin),
            [field] + sent(thin),
            [ends(wide), table(wide), halos(wide), block, block]
            + [pltpu.VMEM(inner_shape, jnp.float32)]
            + [pltpu.SemaphoreType.DMA((wide.halves,)), pltpu.SemaphoreType.DMA((3,))],
            rows * count * 300,
            phi, *near_halos(wide, phi), speed, *exchanged(wide, phi, *message), send_code, halo_code,
            far=(2, 3),
        )
        origin = phi
        for redist_pass in range(REDIST_PASSES):
            if redist_pass < REDIST_PASSES - 1:
                sends = thin
            elif offset_step < OFFSET_STEPS - 1:
                sends = wide
            else:
                sends = None
            if sends is None:
                out, scratch = [f32((rows, count))], [table(thin)]
            else:
                out, scratch = [field] + sent(sends), [ends(sends), table(sends)]
            phi, *message = call(
                functools.partial(relax_kernel, thin, sends),
                out,
                scratch + [halos(thin)],
                rows * count * 60,
                phi, origin, *near_halos(thin, phi), *exchanged(thin, phi, *message), send_code, halo_code,
            )
    return phi


def solution(mesh):
    return jax.shard_map(
        per_device,
        mesh=mesh,
        in_specs=(
            P(None, ("group", "dev")),
            P(None, ("group", "dev")),
            P(("group", "dev"), None),
            P(("group", "dev"), None),
            P(None, ("group", "dev")),
        ),
        out_specs=P(None, ("group", "dev")),
        check_vma=False,
    )
```

```python
import functools

import jax
import jax.numpy as jnp
from jax import lax
from jax.experimental import pallas as pl
from jax.experimental.pallas import tpu as pltpu
from jax.sharding import PartitionSpec as P

OFFSET_STEPS = 2
REDIST_PASSES = 2

advect_scale = 0.3
relax_scale = 0.3
weno_floor = 1e-06

LANES = 128


class Plan:
    def __init__(self, count, peers, slots, border, layers):
        self.count = count
        self.peers = peers
        self.slots = slots
        self.border = border
        self.layers = layers
        self.halves = count // LANES
        self.local_tiles = 6 * self.halves
        self.groups = 8 * layers
        self.per_tile = LANES // slots
        self.peer_tiles = -(-peers // self.per_tile)
        used = (peers - (self.peer_tiles - 1) * self.per_tile) * slots
        if used + 2 * border <= LANES:
            self.border_tile = self.peer_tiles - 1
            self.border_lane = used
        else:
            self.border_tile = self.peer_tiles
            self.border_lane = 0
        self.far_tiles = self.border_tile + 1
        self.pieces = min(LANES // slots, self.groups)
        self.piece_groups = -(-self.groups // self.pieces)
        self.border_pieces = min(LANES // border, self.groups)
        self.border_groups = -(-self.groups // self.border_pieces)

    def message(self):
        return (self.peers, 8 * self.piece_groups, LANES)

    def border_message(self):
        return (8 * self.border_groups, LANES)


def lane_ids():
    return lax.broadcasted_iota(jnp.int32, (8, LANES), 1)


def turn(block, shift):
    shift = shift % LANES
    return block if shift == 0 else pltpu.roll(block, shift, 1)


def in_block(lanes, start, size):
    return jnp.logical_and(lanes >= start, lanes < start + size)


def half(h):
    return pl.ds(h * LANES, LANES)


def rows8(start):
    return pl.ds(pl.multiple_of(start, 8), 8)


def bits_of(tile, tiles):
    return [(tile & (1 << b)) != 0 for b in range(max(tiles - 1, 1).bit_length())]


def pick_tile(values, masks):
    def pick(lowest, bit):
        if bit < 0:
            return values(lowest)
        first = pick(lowest, bit - 1)
        if lowest + (1 << bit) >= values.count:
            return first
        return jnp.where(masks[bit], pick(lowest + (1 << bit), bit - 1), first)

    return pick(0, len(masks) - 1)


class Taken:
    def __init__(self, sources, lane):
        self.sources = sources
        self.lane = lane
        self.count = len(sources)

    def __call__(self, tile):
        return jnp.take_along_axis(
            self.sources[tile], self.lane, axis=1, mode="promise_in_bounds"
        )


def gather(sources, code):
    return pick_tile(Taken(sources, code & (LANES - 1)), bits_of(code >> 7, len(sources)))


def local_sources(plan, phi, ends, g):
    w = plan.layers
    if w == 1:
        along_y = g * 64
    else:
        along_y = (g // w) * 64 + lax.rem(g, w) * 8
    starts = [g * 8, (8 - w) * 64 + g * 8, along_y, along_y + (8 - w) * 8]
    found = []
    for start in starts:
        for h in range(plan.halves):
            found.append(phi[h, rows8(start), :])
    for end in range(2):
        for h in range(plan.halves):
            if w == 1:
                found.append(phi[h, pl.ds(g * 64 + 7 * end, 8, stride=8), :])
            else:
                found.append(ends[end, h, rows8(g * 8), :])
    return found


def fill_ends(plan, phi, ends):
    w = plan.layers
    if w == 1:
        return

    @pl.loop(0, 8)
    def _(i):
        for end in range(2):
            for l in range(w):
                k = l + end * (8 - w)
                for h in range(plan.halves):
                    ends[end, h, pl.ds(i * 8 * w + l, 8, stride=w), :] = phi[
                        h, pl.ds(i * 64 + k, 8, stride=8), :
                    ]


def pick_slabs(plan, phi, ends, send_code, targets, together):
    @pl.loop(0, plan.groups // together)
    def _(q):
        for v in range(together):
            g = q * together + v
            sources = local_sources(plan, phi, ends, g)
            for t, target in targets:
                code = jnp.broadcast_to(send_code[pl.ds(t, 1), :], (8, LANES))
                target[rows8(g * 8), :] = gather(sources, code)


def pack_borders(plan, phi, ends, send_code, shared, low, high):
    lanes = lane_ids()
    pick_slabs(plan, phi, ends, send_code, [(plan.border_tile, shared)], 8)
    for side, target in enumerate((low, high)):
        for gi in range(plan.border_groups):
            block = None
            for p in range(plan.border_pieces):
                g = p * plan.border_groups + gi
                if g >= plan.groups:
                    continue
                part = turn(
                    shared[pl.ds(g * 8, 8), :],
                    (p - side) * plan.border - plan.border_lane,
                )
                if block is None:
                    block = part
                else:
                    block = jnp.where(lanes >= p * plan.border, part, block)
            target[pl.ds(gi * 8, 8), :] = block


def pack_kernel(plan, phi, shared, send_code, outgoing, table, ends):
    lanes = lane_ids()
    fill_ends(plan, phi, ends)
    tiles = [shared if t == plan.border_tile else table.at[t] for t in range(plan.peer_tiles)]
    wanted = [(t, tile) for t, tile in enumerate(tiles) if t != plan.border_tile]
    pick_slabs(plan, phi, ends, send_code, wanted, 4)
    for e in range(plan.peers):
        t, eq = divmod(e, plan.per_tile)
        for gi in range(plan.piece_groups):
            block = None
            for p in range(plan.pieces):
                g = p * plan.piece_groups + gi
                if g >= plan.groups:
                    continue
                part = turn(tiles[t][pl.ds(g * 8, 8), :], (p - eq) * plan.slots)
                if block is None:
                    block = part
                else:
                    block = jnp.where(lanes >= p * plan.slots, part, block)
            outgoing[e, pl.ds(gi * 8, 8), :] = block


def unpack_far(plan, arrived, before, after, table):
    lanes = lane_ids()
    for g in range(plan.groups):
        p, gi = divmod(g, plan.piece_groups)
        bp, bgi = divmod(g, plan.border_groups)
        for t in range(plan.far_tiles):
            block = None
            if t < plan.peer_tiles:
                for eq in range(min(plan.per_tile, plan.peers - t * plan.per_tile)):
                    e = t * plan.per_tile + eq
                    part = turn(arrived[e, pl.ds(gi * 8, 8), :], (eq - p) * plan.slots)
                    if block is None:
                        block = part
                    else:
                        block = jnp.where(lanes >= eq * plan.slots, part, block)
            if t == plan.border_tile:
                for q, source in enumerate((before, after)):
                    start = plan.border_lane + q * plan.border
                    part = turn(source[pl.ds(bgi * 8, 8), :], start - bp * plan.border)
                    if block is None:
                        block = part
                    else:
                        block = jnp.where(lanes >= start, part, block)
            table[t, pl.ds(g * 8, 8), :] = block


def pull_local(plan, phi, ends, halo_code, halos, g):
    sources = local_sources(plan, phi, ends, g)
    for s in range(6):
        for h in range(plan.halves):
            code = jnp.broadcast_to(halo_code[pl.ds(s, 1), half(h)], (8, LANES))
            halos[s, h, rows8(g * 8), :] = gather(sources, code)


def pull_far(plan, table, halo_code, near, halos, sides, g):
    start = plan.local_tiles * LANES
    sources = [table[t, rows8(g * 8), :] for t in range(plan.far_tiles)]
    for s in sides:
        for h in range(plan.halves):
            code = jnp.broadcast_to(halo_code[pl.ds(s, 1), half(h)], (8, LANES))
            far = gather(sources, code - start)
            here = near[s, h, rows8(g * 8), :]
            halos[s, h, rows8(g * 8), :] = jnp.where(code >= start, far, here)


def weno_windows(q):
    first = [q[m + 1] - q[m] for m in range(7)]
    second = [first[m + 1] - first[m] for m in range(6)]
    third = [second[m + 1] - second[m] for m in range(5)]
    fourth = [(third[m] - third[m + 1]) * (1.0 / 3.0) for m in range(4)]
    bend = [t * t * (4.0 / 3.0) + weno_floor for t in third]
    found = []
    for m in range(3):
        s1, s2 = second[m + 1], second[m + 2]
        a = bend[m] + s1 * (s1 + third[m])
        b = bend[m + 1] + s1 * s2
        c = bend[m + 2] + s2 * (s2 - third[m + 2])
        a, b, c = a * a, b * b, c * c
        x = b * c
        z = a * b
        total = x + z + 6.0 * (a * c)
        xu = x * fourth[m]
        zu = z * fourth[m + 1]
        slope = 0.25 * (s1 + s2)
        middle = first[m + 2] + third[m + 1] * (1.0 / 12.0)
        fix = (xu + 1.5 * zu) * pl.reciprocal(total + 2.0 * z, approx=True)
        backward = middle + slope + fix
        fix = (zu + 1.5 * xu) * pl.reciprocal(total + 2.0 * x, approx=True)
        found.append((backward, fix + slope - middle))
    return found


def inner_values(values):
    three, four, five = weno_windows(values)
    return [three[1], jnp.maximum(three[0], four[1]), jnp.maximum(four[0], five[1]), five[0]]


def line_values(low, values, high, inner):
    zero, one, two = weno_windows(low + values[:5])
    six, seven, last = weno_windows(values[3:] + high)
    steep = [
        jnp.maximum(zero[0], one[1]),
        jnp.maximum(one[0], two[1]),
        jnp.maximum(two[0], inner[0]),
        inner[1],
        inner[2],
        jnp.maximum(inner[3], six[1]),
        jnp.maximum(six[0], seven[1]),
        jnp.maximum(seven[0], last[1]),
    ]
    steep = [jnp.maximum(value, 0.0) for value in steep]
    return [value * value for value in steep]


def line_at(phi, h, axis, q):
    if axis == 0:
        return [phi[h, rows8(m * 64 + q * 8), :] for m in range(8)]
    if axis == 1:
        return [phi[h, rows8(q * 64 + m * 8), :] for m in range(8)]
    return [phi[h, pl.ds(q * 64 + m, 8, stride=8), :] for m in range(8)]


def inner_at(inner, h, axis, q):
    return [inner[axis, h, rows8(q * 32 + m * 8), :] for m in range(4)]


def advect(plan, phi, speed, ready, near, inner, table, halo_code, halos, squares, moved):
    w = plan.layers

    def stage_planes(i):
        for l in range(w):
            pull_far(plan, table, halo_code, near, halos, (2, 3, 4, 5), i * w + l)

    def stage_columns(j):
        for l in range(w):
            pull_far(plan, table, halo_code, near, halos, (0, 1), l * 8 + j)

    stage_planes(0)
    ready()

    @pl.loop(0, 8)
    def _(i):
        lines = []
        for h in range(plan.halves):
            ends = [
                [halos[s, h, pl.ds(i * 8 * w + l, 8, stride=w), :] for l in range(w)]
                for s in (4, 5)
            ]
            lines.append((ends[0], line_at(phi, h, 2, i), ends[1], inner_at(inner, h, 2, i)))
            ends = [
                [halos[s, h, rows8((i * w + l) * 8), :] for l in range(w)] for s in (2, 3)
            ]
            lines.append((ends[0], line_at(phi, h, 1, i), ends[1], inner_at(inner, h, 1, i)))
        stage_planes(jnp.minimum(i + 1, 7))
        for h in range(plan.halves):
            for k, value in enumerate(line_values(*lines[2 * h])):
                squares[h, pl.ds(i * 64 + k, 8, stride=8), :] = value
            for j, value in enumerate(line_values(*lines[2 * h + 1])):
                squares[h, rows8(i * 64 + j * 8), :] += value

    stage_columns(0)

    @pl.loop(0, 8)
    def _(j):
        lines = []
        for h in range(plan.halves):
            ends = [
                [halos[s, h, rows8((l * 8 + j) * 8), :] for l in range(w)] for s in (0, 1)
            ]
            lines.append((ends[0], line_at(phi, h, 0, j), ends[1], inner_at(inner, h, 0, j)))
        stage_columns(jnp.minimum(j + 1, 7))
        for h in range(plan.halves):
            for i, value in enumerate(line_values(*lines[h])):
                here = rows8(i * 64 + j * 8)
                total = squares[h, here, :] + value
                change = advect_scale * speed[h, here, :] * jnp.sqrt(total)
                moved[h, here, :] = lines[h][1][i] - change


def relax(plan, phi, origin, near, table, halo_code, halos, moved, joined):
    row = lax.broadcasted_iota(jnp.int32, (8, LANES), 0)

    @pl.loop(0, 2)
    def _(q):
        for v in range(4):
            pull_far(plan, table, halo_code, near, halos, (0, 1), q * 4 + v)

    def stage(i):
        pull_far(plan, table, halo_code, near, halos, (2, 3, 4, 5), i)

    def plane(i, h, previous, following, sides):
        at = half(h)
        centre = [phi[h, rows8(i * 64 + j * 8), :] for j in range(8)]
        along_y = [sides[0]] + centre + [sides[1]]
        for j in range(8):
            here = rows8(i * 64 + j * 8)
            value = centre[j]
            start = origin[h, here, :]
            sense = start * lax.rsqrt(start * start + 1.0)
            facing = jnp.where(start > 0.0, 1.0, -1.0)
            first = jnp.broadcast_to(sides[2][j : j + 1], (8, LANES))
            last = jnp.broadcast_to(sides[3][j : j + 1], (8, LANES))
            low_z = jnp.where(row == 0, first, pltpu.roll(value, 1, 0))
            high_z = jnp.where(row == 7, last, pltpu.roll(value, 7, 0))
            pairs = (
                (previous(j), following(j)),
                (along_y[j], along_y[j + 2]),
                (low_z, high_z),
            )
            total = None
            for low, high in pairs:
                steep = jnp.maximum((value - low) * facing, (value - high) * facing)
                steep = jnp.maximum(steep, 0.0)
                steep = steep * steep
                total = steep if total is None else total + steep
            value = value - relax_scale * sense * (jnp.sqrt(total) - 1.0)
            if joined:
                moved[here, at] = value
            else:
                moved[h, here, :] = value

    def planes(i, low, high):
        sides = [
            [halos[s, h, rows8(i * 8), :] for s in (2, 3, 4, 5)] for h in range(plan.halves)
        ]
        if not isinstance(i, int) or i < 7:
            stage(i + 1)
        for h in range(plan.halves):

            def previous(j):
                if low is None:
                    return phi[h, rows8((i - 1) * 64 + j * 8), :]
                return halos[low, h, pl.ds(j * 8, 8), :]

            def following(j):
                if high is None:
                    return phi[h, rows8((i + 1) * 64 + j * 8), :]
                return halos[high, h, pl.ds(j * 8, 8), :]

            plane(i, h, previous, following, sides[h])

    stage(0)
    planes(0, 0, None)

    @pl.loop(1, 7)
    def _(i):
        planes(i, None, None)

    planes(7, None, 1)


def first_kernel(
    plan, level_set, peer_slabs, region_slabs, halo_source,
    phi, shared, low, high, send_code, halo_code, ends, padded, peer, region, entries, ready,
):
    copies = [
        pltpu.make_async_copy(source, target, ready.at[n])
        for n, (source, target) in enumerate(
            ((peer_slabs, peer), (region_slabs, region), (halo_source, entries))
        )
    ]
    for h in range(plan.halves):
        copies.append(
            pltpu.make_async_copy(level_set.at[:, half(h)], phi.at[h], ready.at[3 + h])
        )
    for copy in copies:
        copy.start()
    for copy in copies:
        copy.wait()
    lanes = lane_ids()
    padded[...] = jnp.zeros_like(padded)
    padded[pl.ds(0, plan.peers), pl.ds(0, plan.slots)] = jnp.maximum(peer[...], 0)
    padded[pl.ds(plan.peers, 2), pl.ds(0, plan.border)] = region[...]

    def wide(row):
        return jnp.broadcast_to(padded[pl.ds(row, 1), :], (8, LANES))

    send_code[...] = jnp.zeros_like(send_code)
    for t in range(plan.far_tiles):
        block = jnp.zeros((8, LANES), jnp.int32)
        if t < plan.peer_tiles:
            for eq in range(min(plan.per_tile, plan.peers - t * plan.per_tile)):
                part = turn(wide(t * plan.per_tile + eq), eq * plan.slots)
                block = jnp.where(in_block(lanes, eq * plan.slots, plan.slots), part, block)
        if t == plan.border_tile:
            for side in range(2):
                start = plan.border_lane + side * plan.border
                part = turn(wide(plan.peers + side), start)
                block = jnp.where(in_block(lanes, start, plan.border), part, block)
        send_code[pl.ds(t, 1), :] = block[0:1]

    entry = entries[...]
    far = entry - plan.local_tiles * LANES
    tile_span = plan.per_tile * plan.slots
    tile = jnp.zeros_like(entry)
    for k in range(1, plan.peer_tiles):
        tile += (far >= k * tile_span).astype(jnp.int32)
    code = (plan.local_tiles + tile) * LANES + far - tile * tile_span
    edge = far - plan.peers * plan.slots
    edge_code = (plan.local_tiles + plan.border_tile) * LANES + plan.border_lane + edge
    code = jnp.where(edge >= 0, edge_code, code)
    halo_code[...] = jnp.where(far >= 0, code, entry)

    fill_ends(plan, phi, ends)
    pack_borders(plan, phi, ends, send_code, shared, low, high)


def near_kernel(plan, phi, halo_code, near, *rest):
    if plan.layers == 1:

        @pl.loop(0, plan.groups // 2)
        def _(q):
            for v in range(2):
                pull_local(plan, phi, None, halo_code, near, q * 2 + v)

        return
    inner, ends, kept, done = rest
    copies = [pltpu.make_async_copy(kept.at[a], inner.at[a], done.at[a]) for a in range(3)]
    fill_ends(plan, phi, ends)
    for axis in range(3):

        @pl.loop(0, 8)
        def _(q):
            lines = [line_at(phi, h, axis, q) for h in range(plan.halves)]
            pull_local(plan, phi, ends, halo_code, near, axis * 8 + q)
            for h in range(plan.halves):
                for m, value in enumerate(inner_values(lines[h])):
                    kept[axis, h, rows8(q * 32 + m * 8), :] = value

        copies[axis].start()
    for copy in copies:
        copy.wait()


def advect_kernel(
    plan, sends, phi, near, inner, speed, arrived, before, after, send_code, halo_code,
    moved, shared, low, high, ends, table, halos, squares, fast, kept, loaded, found,
):
    copies = [pltpu.make_async_copy(inner.at[a], kept.at[a], found.at[a]) for a in range(3)]
    copies += [
        pltpu.make_async_copy(speed.at[:, half(h)], fast.at[h], loaded.at[h])
        for h in range(plan.halves)
    ]
    for copy in copies:
        copy.start()

    def ready():
        for copy in copies:
            copy.wait()

    unpack_far(plan, arrived, before, after, table)
    advect(plan, phi, fast, ready, near, kept, table, halo_code, halos, squares, moved)
    pack_borders(sends, moved, ends, send_code, shared, low, high)


def relax_kernel(
    plan, sends, phi, origin, near, arrived, before, after, send_code, halo_code, *rest
):
    if sends is None:
        (moved, table, halos) = rest
    else:
        (moved, shared, low, high, ends, table, halos) = rest
    unpack_far(plan, arrived, before, after, table)
    relax(plan, phi, origin, near, table, halo_code, halos, moved, sends is None)
    if sends is not None:
        fill_ends(sends, moved, ends)
        pack_borders(sends, moved, ends, send_code, shared, low, high)


def f32(shape):
    return jax.ShapeDtypeStruct(shape, jnp.float32)


def call(kernel, out_shape, scratch, flops, *operands, far=(), far_out=()):
    whole = pl.BlockSpec(memory_space=pltpu.VMEM)
    apart = pl.BlockSpec(memory_space=pltpu.HBM)
    size = sum(x.size * 4 for x in operands) + sum(x.size * 4 for x in out_shape)
    operands = [
        pltpu.with_memory_space_constraint(x, pltpu.HBM) if n in far else x
        for n, x in enumerate(operands)
    ]
    return pl.pallas_call(
        kernel,
        out_shape=[
            pltpu.HBM(x.shape, x.dtype) if n in far_out else x for n, x in enumerate(out_shape)
        ],
        in_specs=[apart if n in far else whole for n in range(len(operands))],
        out_specs=[apart if n in far_out else whole for n in range(len(out_shape))],
        scratch_shapes=scratch,
        cost_estimate=pl.CostEstimate(flops=flops, bytes_accessed=size, transcendentals=0),
        compiler_params=pltpu.CompilerParams(vmem_limit_bytes=12 * 1024 * 1024),
    )(*operands)


def exchange(outgoing, low, high):
    count = lax.axis_size("group")
    up = [(i, (i + 1) % count) for i in range(count)]
    down = [(target, source) for source, target in up]
    before = lax.ppermute(high, "group", up)
    after = lax.ppermute(low, "group", down)
    outgoing, before, after = lax.optimization_barrier((outgoing, before, after))
    arrived = lax.all_to_all(outgoing, "dev", split_axis=0, concat_axis=0, tiled=True)
    return arrived, before, after


def per_device(level_set, speed, peer_slabs, region_slabs, halo_source):
    rows, count = level_set.shape
    peers, slots = peer_slabs.shape
    border = region_slabs.shape[1]
    wide = Plan(count, peers, slots, border, 3)
    thin = Plan(count, peers, slots, border, 1)
    code_rows = -(-wide.far_tiles // 8) * 8

    def ends(plan):
        return pltpu.VMEM((2, wide.halves, 64 * plan.layers, LANES), jnp.float32)

    def table(plan):
        return pltpu.VMEM((plan.far_tiles, 64 * plan.layers, LANES), jnp.float32)

    def halos(plan):
        return pltpu.VMEM((6, wide.halves, 64 * plan.layers, LANES), jnp.float32)

    def sent(plan):
        tile = f32((64 * plan.layers, LANES))
        return [tile, f32(plan.border_message()), f32(plan.border_message())]

    def exchanged(plan, phi, shared, low, high):
        outgoing = call(
            functools.partial(pack_kernel, plan),
            [f32(plan.message())],
            [table(plan), ends(plan)],
            rows * count * 20 * plan.layers,
            phi, shared, send_code,
        )[0]
        return exchange(outgoing, low, high)

    field = f32((wide.halves, rows, LANES))
    pad_rows = -(-(peers + 2) // 8) * 8
    phi, *message, send_code, halo_code = call(
        functools.partial(first_kernel, wide),
        [field]
        + sent(wide)
        + [
            jax.ShapeDtypeStruct((code_rows, LANES), jnp.int32),
            jax.ShapeDtypeStruct(halo_source.shape, jnp.int32),
        ],
        [
            ends(wide),
            pltpu.VMEM((pad_rows, LANES), jnp.int32),
            pltpu.VMEM(peer_slabs.shape, jnp.int32),
            pltpu.VMEM(region_slabs.shape, jnp.int32),
            pltpu.VMEM(halo_source.shape, jnp.int32),
            pltpu.SemaphoreType.DMA((3 + wide.halves,)),
        ],
        1000000,
        level_set, peer_slabs, region_slabs, halo_source,
        far=(0, 1, 2, 3),
    )

    def near_halos(plan, phi):
        out = [f32((6, plan.halves, 64 * plan.layers, LANES))]
        scratch = []
        if plan.layers > 1:
            out.append(f32(inner_shape))
            scratch = [ends(plan), pltpu.VMEM(inner_shape, jnp.float32)]
            scratch.append(pltpu.SemaphoreType.DMA((3,)))
        flops = rows * count * 100 * plan.layers
        kernel = functools.partial(near_kernel, plan)
        return call(kernel, out, scratch, flops, phi, halo_code, far_out=(1,))

    inner_shape = (3, wide.halves, rows // 2, LANES)
    block = pltpu.VMEM((wide.halves, rows, LANES), jnp.float32)
    for offset_step in range(OFFSET_STEPS):
        phi, *message = call(
            functools.partial(advect_kernel, wide, thin),
            [field] + sent(thin),
            [ends(wide), table(wide), halos(wide), block, block]
            + [pltpu.VMEM(inner_shape, jnp.float32)]
            + [pltpu.SemaphoreType.DMA((wide.halves,)), pltpu.SemaphoreType.DMA((3,))],
            rows * count * 300,
            phi, *near_halos(wide, phi), speed, *exchanged(wide, phi, *message), send_code, halo_code,
            far=(2, 3),
        )
        origin = phi
        for redist_pass in range(REDIST_PASSES):
            if redist_pass < REDIST_PASSES - 1:
                sends = thin
            elif offset_step < OFFSET_STEPS - 1:
                sends = wide
            else:
                sends = None
            if sends is None:
                out, scratch = [f32((rows, count))], [table(thin)]
            else:
                out, scratch = [field] + sent(sends), [ends(sends), table(sends)]
            phi, *message = call(
                functools.partial(relax_kernel, thin, sends),
                out,
                scratch + [halos(thin)],
                rows * count * 60,
                phi, origin, *near_halos(thin, phi), *exchanged(thin, phi, *message), send_code, halo_code,
            )
    return phi


def solution(mesh):
    return jax.shard_map(
        per_device,
        mesh=mesh,
        in_specs=(
            P(None, ("group", "dev")),
            P(None, ("group", "dev")),
            P(("group", "dev"), None),
            P(("group", "dev"), None),
            P(None, ("group", "dev")),
        ),
        out_specs=P(None, ("group", "dev")),
        check_vma=False,
    )
```

```python
import functools

import jax
import jax.numpy as jnp
from jax import lax
from jax.experimental import pallas as pl
from jax.experimental.pallas import tpu as pltpu
from jax.sharding import PartitionSpec as P

OFFSET_STEPS = 2
REDIST_PASSES = 2

advect_scale = 0.3
relax_scale = 0.3
weno_floor = 1e-06

LANES = 128


class Plan:
    def __init__(self, count, peers, slots, border, layers):
        self.count = count
        self.peers = peers
        self.slots = slots
        self.border = border
        self.layers = layers
        self.halves = count // LANES
        self.local_tiles = 6 * self.halves
        self.groups = 8 * layers
        self.per_tile = LANES // slots
        self.peer_tiles = -(-peers // self.per_tile)
        used = (peers - (self.peer_tiles - 1) * self.per_tile) * slots
        if used + 2 * border <= LANES:
            self.border_tile = self.peer_tiles - 1
            self.border_lane = used
        else:
            self.border_tile = self.peer_tiles
            self.border_lane = 0
        self.far_tiles = self.border_tile + 1
        self.pieces = min(LANES // slots, self.groups)
        self.piece_groups = -(-self.groups // self.pieces)
        self.border_pieces = min(LANES // border, self.groups)
        self.border_groups = -(-self.groups // self.border_pieces)

    def message(self):
        return (self.peers, 8 * self.piece_groups, LANES)

    def border_message(self):
        return (8 * self.border_groups, LANES)


def lane_ids():
    return lax.broadcasted_iota(jnp.int32, (8, LANES), 1)


def turn(block, shift):
    shift = shift % LANES
    return block if shift == 0 else pltpu.roll(block, shift, 1)


def in_block(lanes, start, size):
    return jnp.logical_and(lanes >= start, lanes < start + size)


def half(h):
    return pl.ds(h * LANES, LANES)


def rows8(start):
    return pl.ds(pl.multiple_of(start, 8), 8)


def bits_of(tile, tiles):
    return [(tile & (1 << b)) != 0 for b in range(max(tiles - 1, 1).bit_length())]


def pick_tile(values, masks):
    def pick(lowest, bit):
        if bit < 0:
            return values(lowest)
        first = pick(lowest, bit - 1)
        if lowest + (1 << bit) >= values.count:
            return first
        return jnp.where(masks[bit], pick(lowest + (1 << bit), bit - 1), first)

    return pick(0, len(masks) - 1)


class Taken:
    def __init__(self, sources, lane):
        self.sources = sources
        self.lane = lane
        self.count = len(sources)

    def __call__(self, tile):
        return jnp.take_along_axis(
            self.sources[tile], self.lane, axis=1, mode="promise_in_bounds"
        )


def gather(sources, code):
    return pick_tile(Taken(sources, code & (LANES - 1)), bits_of(code >> 7, len(sources)))


def local_sources(plan, phi, ends, g):
    w = plan.layers
    if w == 1:
        along_y = g * 64
    else:
        along_y = (g // w) * 64 + lax.rem(g, w) * 8
    starts = [g * 8, (8 - w) * 64 + g * 8, along_y, along_y + (8 - w) * 8]
    found = []
    for start in starts:
        for h in range(plan.halves):
            found.append(phi[h, rows8(start), :])
    for end in range(2):
        for h in range(plan.halves):
            if w == 1:
                found.append(phi[h, pl.ds(g * 64 + 7 * end, 8, stride=8), :])
            else:
                found.append(ends[end, h, rows8(g * 8), :])
    return found


def fill_ends(plan, phi, ends):
    w = plan.layers
    if w == 1:
        return

    @pl.loop(0, 8)
    def _(i):
        for end in range(2):
            for l in range(w):
                k = l + end * (8 - w)
                for h in range(plan.halves):
                    ends[end, h, pl.ds(i * 8 * w + l, 8, stride=w), :] = phi[
                        h, pl.ds(i * 64 + k, 8, stride=8), :
                    ]


def pack_sends(plan, phi, ends, send_code, table, outgoing, low, high):
    lanes = lane_ids()
    w = plan.layers

    @pl.loop(0, plan.groups // 4)
    def _(q):
        for v in range(4):
            g = q * 4 + v
            sources = local_sources(plan, phi, ends, g)
            for t in range(plan.far_tiles):
                code = jnp.broadcast_to(send_code[pl.ds(t, 1), :], (8, LANES))
                table[t, rows8(g * 8), :] = gather(sources, code)

    for e in range(plan.peers):
        t, eq = divmod(e, plan.per_tile)
        for gi in range(plan.piece_groups):
            block = None
            for p in range(plan.pieces):
                g = p * plan.piece_groups + gi
                if g >= plan.groups:
                    continue
                part = turn(table[t, pl.ds(g * 8, 8), :], (p - eq) * plan.slots)
                if block is None:
                    block = part
                else:
                    block = jnp.where(lanes >= p * plan.slots, part, block)
            outgoing[e, pl.ds(gi * 8, 8), :] = block
    for side, target in enumerate((low, high)):
        for gi in range(plan.border_groups):
            block = None
            for p in range(plan.border_pieces):
                g = p * plan.border_groups + gi
                if g >= plan.groups:
                    continue
                part = turn(
                    table[plan.border_tile, pl.ds(g * 8, 8), :],
                    (p - side) * plan.border - plan.border_lane,
                )
                if block is None:
                    block = part
                else:
                    block = jnp.where(lanes >= p * plan.border, part, block)
            target[pl.ds(gi * 8, 8), :] = block


def unpack_far(plan, arrived, before, after, table):
    lanes = lane_ids()
    for g in range(plan.groups):
        p, gi = divmod(g, plan.piece_groups)
        bp, bgi = divmod(g, plan.border_groups)
        for t in range(plan.far_tiles):
            block = None
            if t < plan.peer_tiles:
                for eq in range(min(plan.per_tile, plan.peers - t * plan.per_tile)):
                    e = t * plan.per_tile + eq
                    part = turn(arrived[e, pl.ds(gi * 8, 8), :], (eq - p) * plan.slots)
                    if block is None:
                        block = part
                    else:
                        block = jnp.where(lanes >= eq * plan.slots, part, block)
            if t == plan.border_tile:
                for q, source in enumerate((before, after)):
                    start = plan.border_lane + q * plan.border
                    part = turn(source[pl.ds(bgi * 8, 8), :], start - bp * plan.border)
                    if block is None:
                        block = part
                    else:
                        block = jnp.where(lanes >= start, part, block)
            table[t, pl.ds(g * 8, 8), :] = block


def pull_local(plan, phi, ends, halo_code, halos, g):
    sources = local_sources(plan, phi, ends, g)
    for s in range(6):
        for h in range(plan.halves):
            code = jnp.broadcast_to(halo_code[pl.ds(s, 1), half(h)], (8, LANES))
            halos[s, h, rows8(g * 8), :] = gather(sources, code)


def pull_far(plan, table, halo_code, near, halos, sides, g):
    start = plan.local_tiles * LANES
    sources = [table[t, rows8(g * 8), :] for t in range(plan.far_tiles)]
    for s in sides:
        for h in range(plan.halves):
            code = jnp.broadcast_to(halo_code[pl.ds(s, 1), half(h)], (8, LANES))
            far = gather(sources, code - start)
            here = near[s, h, rows8(g * 8), :]
            halos[s, h, rows8(g * 8), :] = jnp.where(code >= start, far, here)


def weno_windows(q):
    first = [q[m + 1] - q[m] for m in range(7)]
    second = [first[m + 1] - first[m] for m in range(6)]
    third = [second[m + 1] - second[m] for m in range(5)]
    fourth = [(third[m] - third[m + 1]) * (1.0 / 3.0) for m in range(4)]
    bend = [t * t * (4.0 / 3.0) + weno_floor for t in third]
    found = []
    for m in range(3):
        s1, s2 = second[m + 1], second[m + 2]
        a = bend[m] + s1 * (s1 + third[m])
        b = bend[m + 1] + s1 * s2
        c = bend[m + 2] + s2 * (s2 - third[m + 2])
        a, b, c = a * a, b * b, c * c
        x = b * c
        z = a * b
        total = x + z + 6.0 * (a * c)
        xu = x * fourth[m]
        zu = z * fourth[m + 1]
        slope = 0.25 * (s1 + s2)
        middle = first[m + 2] + third[m + 1] * (1.0 / 12.0)
        fix = (xu + 1.5 * zu) * pl.reciprocal(total + 2.0 * z, approx=True)
        backward = middle + slope + fix
        fix = (zu + 1.5 * xu) * pl.reciprocal(total + 2.0 * x, approx=True)
        found.append((backward, fix + slope - middle))
    return found


def inner_values(values):
    three, four, five = weno_windows(values)
    return [three[1], jnp.maximum(three[0], four[1]), jnp.maximum(four[0], five[1]), five[0]]


def line_values(low, values, high, inner):
    zero, one, two = weno_windows(low + values[:5])
    six, seven, last = weno_windows(values[3:] + high)
    steep = [
        jnp.maximum(zero[0], one[1]),
        jnp.maximum(one[0], two[1]),
        jnp.maximum(two[0], inner[0]),
        inner[1],
        inner[2],
        jnp.maximum(inner[3], six[1]),
        jnp.maximum(six[0], seven[1]),
        jnp.maximum(seven[0], last[1]),
    ]
    steep = [jnp.maximum(value, 0.0) for value in steep]
    return [value * value for value in steep]


def line_at(phi, h, axis, q):
    if axis == 0:
        return [phi[h, rows8(m * 64 + q * 8), :] for m in range(8)]
    if axis == 1:
        return [phi[h, rows8(q * 64 + m * 8), :] for m in range(8)]
    return [phi[h, pl.ds(q * 64 + m, 8, stride=8), :] for m in range(8)]


def inner_at(inner, h, axis, q):
    return [inner[axis, h, rows8(q * 32 + m * 8), :] for m in range(4)]


def advect(plan, phi, speed, ready, near, inner, table, halo_code, halos, squares, moved):
    w = plan.layers

    def stage_planes(i):
        for l in range(w):
            pull_far(plan, table, halo_code, near, halos, (2, 3, 4, 5), i * w + l)

    def stage_columns(j):
        for l in range(w):
            pull_far(plan, table, halo_code, near, halos, (0, 1), l * 8 + j)

    stage_planes(0)
    ready()

    @pl.loop(0, 8)
    def _(i):
        lines = []
        for h in range(plan.halves):
            ends = [
                [halos[s, h, pl.ds(i * 8 * w + l, 8, stride=w), :] for l in range(w)]
                for s in (4, 5)
            ]
            lines.append((ends[0], line_at(phi, h, 2, i), ends[1], inner_at(inner, h, 2, i)))
            ends = [
                [halos[s, h, rows8((i * w + l) * 8), :] for l in range(w)] for s in (2, 3)
            ]
            lines.append((ends[0], line_at(phi, h, 1, i), ends[1], inner_at(inner, h, 1, i)))
        stage_planes(jnp.minimum(i + 1, 7))
        for h in range(plan.halves):
            for k, value in enumerate(line_values(*lines[2 * h])):
                squares[h, pl.ds(i * 64 + k, 8, stride=8), :] = value
            for j, value in enumerate(line_values(*lines[2 * h + 1])):
                squares[h, rows8(i * 64 + j * 8), :] += value

    stage_columns(0)

    @pl.loop(0, 8)
    def _(j):
        lines = []
        for h in range(plan.halves):
            ends = [
                [halos[s, h, rows8((l * 8 + j) * 8), :] for l in range(w)] for s in (0, 1)
            ]
            lines.append((ends[0], line_at(phi, h, 0, j), ends[1], inner_at(inner, h, 0, j)))
        stage_columns(jnp.minimum(j + 1, 7))
        for h in range(plan.halves):
            for i, value in enumerate(line_values(*lines[h])):
                here = rows8(i * 64 + j * 8)
                total = squares[h, here, :] + value
                change = advect_scale * speed[h, here, :] * jnp.sqrt(total)
                moved[h, here, :] = lines[h][1][i] - change


def relax(plan, phi, origin, near, table, halo_code, halos, moved, joined):
    row = lax.broadcasted_iota(jnp.int32, (8, LANES), 0)

    @pl.loop(0, 2)
    def _(q):
        for v in range(4):
            pull_far(plan, table, halo_code, near, halos, (0, 1), q * 4 + v)

    def stage(i):
        pull_far(plan, table, halo_code, near, halos, (2, 3, 4, 5), i)

    def plane(i, h, previous, following, sides):
        at = half(h)
        centre = [phi[h, rows8(i * 64 + j * 8), :] for j in range(8)]
        along_y = [sides[0]] + centre + [sides[1]]
        for j in range(8):
            here = rows8(i * 64 + j * 8)
            value = centre[j]
            start = origin[h, here, :]
            sense = start * lax.rsqrt(start * start + 1.0)
            facing = jnp.where(start > 0.0, 1.0, -1.0)
            first = jnp.broadcast_to(sides[2][j : j + 1], (8, LANES))
            last = jnp.broadcast_to(sides[3][j : j + 1], (8, LANES))
            low_z = jnp.where(row == 0, first, pltpu.roll(value, 1, 0))
            high_z = jnp.where(row == 7, last, pltpu.roll(value, 7, 0))
            pairs = (
                (previous(j), following(j)),
                (along_y[j], along_y[j + 2]),
                (low_z, high_z),
            )
            total = None
            for low, high in pairs:
                steep = jnp.maximum((value - low) * facing, (value - high) * facing)
                steep = jnp.maximum(steep, 0.0)
                steep = steep * steep
                total = steep if total is None else total + steep
            value = value - relax_scale * sense * (jnp.sqrt(total) - 1.0)
            if joined:
                moved[here, at] = value
            else:
                moved[h, here, :] = value

    def planes(i, low, high):
        sides = [
            [halos[s, h, rows8(i * 8), :] for s in (2, 3, 4, 5)] for h in range(plan.halves)
        ]
        if not isinstance(i, int) or i < 7:
            stage(i + 1)
        for h in range(plan.halves):

            def previous(j):
                if low is None:
                    return phi[h, rows8((i - 1) * 64 + j * 8), :]
                return halos[low, h, pl.ds(j * 8, 8), :]

            def following(j):
                if high is None:
                    return phi[h, rows8((i + 1) * 64 + j * 8), :]
                return halos[high, h, pl.ds(j * 8, 8), :]

            plane(i, h, previous, following, sides[h])

    stage(0)
    planes(0, 0, None)

    @pl.loop(1, 7)
    def _(i):
        planes(i, None, None)

    planes(7, None, 1)


def first_kernel(
    plan, level_set, peer_slabs, region_slabs, halo_source,
    phi, outgoing, low, high, send_code, halo_code, ends, table, padded, peer, region, entries, ready,
):
    copies = [
        pltpu.make_async_copy(source, target, ready.at[n])
        for n, (source, target) in enumerate(
            ((peer_slabs, peer), (region_slabs, region), (halo_source, entries))
        )
    ]
    for h in range(plan.halves):
        copies.append(
            pltpu.make_async_copy(level_set.at[:, half(h)], phi.at[h], ready.at[3 + h])
        )
    for copy in copies:
        copy.start()
    for copy in copies:
        copy.wait()
    lanes = lane_ids()
    padded[...] = jnp.zeros_like(padded)
    padded[pl.ds(0, plan.peers), pl.ds(0, plan.slots)] = jnp.maximum(peer[...], 0)
    padded[pl.ds(plan.peers, 2), pl.ds(0, plan.border)] = region[...]

    def wide(row):
        return jnp.broadcast_to(padded[pl.ds(row, 1), :], (8, LANES))

    send_code[...] = jnp.zeros_like(send_code)
    for t in range(plan.far_tiles):
        block = jnp.zeros((8, LANES), jnp.int32)
        if t < plan.peer_tiles:
            for eq in range(min(plan.per_tile, plan.peers - t * plan.per_tile)):
                part = turn(wide(t * plan.per_tile + eq), eq * plan.slots)
                block = jnp.where(in_block(lanes, eq * plan.slots, plan.slots), part, block)
        if t == plan.border_tile:
            for side in range(2):
                start = plan.border_lane + side * plan.border
                part = turn(wide(plan.peers + side), start)
                block = jnp.where(in_block(lanes, start, plan.border), part, block)
        send_code[pl.ds(t, 1), :] = block[0:1]

    entry = entries[...]
    far = entry - plan.local_tiles * LANES
    tile_span = plan.per_tile * plan.slots
    tile = jnp.zeros_like(entry)
    for k in range(1, plan.peer_tiles):
        tile += (far >= k * tile_span).astype(jnp.int32)
    code = (plan.local_tiles + tile) * LANES + far - tile * tile_span
    edge = far - plan.peers * plan.slots
    edge_code = (plan.local_tiles + plan.border_tile) * LANES + plan.border_lane + edge
    code = jnp.where(edge >= 0, edge_code, code)
    halo_code[...] = jnp.where(far >= 0, code, entry)

    fill_ends(plan, phi, ends)
    pack_sends(plan, phi, ends, send_code, table, outgoing, low, high)


def near_kernel(plan, phi, halo_code, near, *rest):
    if plan.layers == 1:

        @pl.loop(0, plan.groups // 2)
        def _(q):
            for v in range(2):
                pull_local(plan, phi, None, halo_code, near, q * 2 + v)

        return
    inner, ends, kept, done = rest
    copies = [pltpu.make_async_copy(kept.at[a], inner.at[a], done.at[a]) for a in range(3)]
    fill_ends(plan, phi, ends)
    for axis in range(3):

        @pl.loop(0, 8)
        def _(q):
            lines = [line_at(phi, h, axis, q) for h in range(plan.halves)]
            pull_local(plan, phi, ends, halo_code, near, axis * 8 + q)
            for h in range(plan.halves):
                for m, value in enumerate(inner_values(lines[h])):
                    kept[axis, h, rows8(q * 32 + m * 8), :] = value

        copies[axis].start()
    for copy in copies:
        copy.wait()


def advect_kernel(
    plan, sends, phi, near, inner, speed, arrived, before, after, send_code, halo_code,
    moved, outgoing, low, high, ends, table, halos, squares, fast, kept, loaded, found,
):
    copies = [pltpu.make_async_copy(inner.at[a], kept.at[a], found.at[a]) for a in range(3)]
    copies += [
        pltpu.make_async_copy(speed.at[:, half(h)], fast.at[h], loaded.at[h])
        for h in range(plan.halves)
    ]
    for copy in copies:
        copy.start()

    def ready():
        for copy in copies:
            copy.wait()

    unpack_far(plan, arrived, before, after, table)
    advect(plan, phi, fast, ready, near, kept, table, halo_code, halos, squares, moved)
    pack_sends(sends, moved, ends, send_code, table, outgoing, low, high)


def relax_kernel(
    plan, sends, phi, origin, near, arrived, before, after, send_code, halo_code, *rest
):
    if sends is None:
        (moved, table, halos) = rest
    else:
        (moved, outgoing, low, high, ends, table, halos) = rest
    unpack_far(plan, arrived, before, after, table)
    relax(plan, phi, origin, near, table, halo_code, halos, moved, sends is None)
    if sends is not None:
        fill_ends(sends, moved, ends)
        pack_sends(sends, moved, ends, send_code, table, outgoing, low, high)


def f32(shape):
    return jax.ShapeDtypeStruct(shape, jnp.float32)


def call(kernel, out_shape, scratch, flops, *operands, far=(), far_out=()):
    whole = pl.BlockSpec(memory_space=pltpu.VMEM)
    apart = pl.BlockSpec(memory_space=pltpu.HBM)
    size = sum(x.size * 4 for x in operands) + sum(x.size * 4 for x in out_shape)
    operands = [
        pltpu.with_memory_space_constraint(x, pltpu.HBM) if n in far else x
        for n, x in enumerate(operands)
    ]
    return pl.pallas_call(
        kernel,
        out_shape=[
            pltpu.HBM(x.shape, x.dtype) if n in far_out else x for n, x in enumerate(out_shape)
        ],
        in_specs=[apart if n in far else whole for n in range(len(operands))],
        out_specs=[apart if n in far_out else whole for n in range(len(out_shape))],
        scratch_shapes=scratch,
        cost_estimate=pl.CostEstimate(flops=flops, bytes_accessed=size, transcendentals=0),
        compiler_params=pltpu.CompilerParams(vmem_limit_bytes=12 * 1024 * 1024),
    )(*operands)


def exchange(outgoing, low, high):
    count = lax.axis_size("group")
    up = [(i, (i + 1) % count) for i in range(count)]
    down = [(target, source) for source, target in up]
    arrived = lax.all_to_all(outgoing, "dev", split_axis=0, concat_axis=0, tiled=True)
    before = lax.ppermute(high, "group", up)
    after = lax.ppermute(low, "group", down)
    return arrived, before, after


def per_device(level_set, speed, peer_slabs, region_slabs, halo_source):
    rows, count = level_set.shape
    peers, slots = peer_slabs.shape
    border = region_slabs.shape[1]
    wide = Plan(count, peers, slots, border, 3)
    thin = Plan(count, peers, slots, border, 1)
    code_rows = -(-wide.far_tiles // 8) * 8

    def ends(plan):
        return pltpu.VMEM((2, wide.halves, 64 * plan.layers, LANES), jnp.float32)

    def table(plan):
        return pltpu.VMEM((plan.far_tiles, 64 * plan.layers, LANES), jnp.float32)

    def halos(plan):
        return pltpu.VMEM((6, wide.halves, 64 * plan.layers, LANES), jnp.float32)

    def sent(plan):
        return [f32(plan.message()), f32(plan.border_message()), f32(plan.border_message())]

    field = f32((wide.halves, rows, LANES))
    pad_rows = -(-(peers + 2) // 8) * 8
    phi, *message, send_code, halo_code = call(
        functools.partial(first_kernel, wide),
        [field]
        + sent(wide)
        + [
            jax.ShapeDtypeStruct((code_rows, LANES), jnp.int32),
            jax.ShapeDtypeStruct(halo_source.shape, jnp.int32),
        ],
        [
            ends(wide),
            table(wide),
            pltpu.VMEM((pad_rows, LANES), jnp.int32),
            pltpu.VMEM(peer_slabs.shape, jnp.int32),
            pltpu.VMEM(region_slabs.shape, jnp.int32),
            pltpu.VMEM(halo_source.shape, jnp.int32),
            pltpu.SemaphoreType.DMA((3 + wide.halves,)),
        ],
        1000000,
        level_set, peer_slabs, region_slabs, halo_source,
        far=(0, 1, 2, 3),
    )

    def near_halos(plan, phi):
        out = [f32((6, plan.halves, 64 * plan.layers, LANES))]
        scratch = []
        if plan.layers > 1:
            out.append(f32(inner_shape))
            scratch = [ends(plan), pltpu.VMEM(inner_shape, jnp.float32)]
            scratch.append(pltpu.SemaphoreType.DMA((3,)))
        flops = rows * count * 100 * plan.layers
        kernel = functools.partial(near_kernel, plan)
        return call(kernel, out, scratch, flops, phi, halo_code, far_out=(1,))

    inner_shape = (3, wide.halves, rows // 2, LANES)
    block = pltpu.VMEM((wide.halves, rows, LANES), jnp.float32)
    for offset_step in range(OFFSET_STEPS):
        phi, *message = call(
            functools.partial(advect_kernel, wide, thin),
            [field] + sent(thin),
            [ends(wide), table(wide), halos(wide), block, block]
            + [pltpu.VMEM(inner_shape, jnp.float32)]
            + [pltpu.SemaphoreType.DMA((wide.halves,)), pltpu.SemaphoreType.DMA((3,))],
            rows * count * 300,
            phi, *near_halos(wide, phi), speed, *exchange(*message), send_code, halo_code,
            far=(2, 3),
        )
        origin = phi
        for redist_pass in range(REDIST_PASSES):
            if redist_pass < REDIST_PASSES - 1:
                sends = thin
            elif offset_step < OFFSET_STEPS - 1:
                sends = wide
            else:
                sends = None
            if sends is None:
                out, scratch = [f32((rows, count))], [table(thin)]
            else:
                out, scratch = [field] + sent(sends), [ends(sends), table(sends)]
            phi, *message = call(
                functools.partial(relax_kernel, thin, sends),
                out,
                scratch + [halos(thin)],
                rows * count * 60,
                phi, origin, *near_halos(thin, phi), *exchange(*message), send_code, halo_code,
            )
    return phi


def solution(mesh):
    return jax.shard_map(
        per_device,
        mesh=mesh,
        in_specs=(
            P(None, ("group", "dev")),
            P(None, ("group", "dev")),
            P(("group", "dev"), None),
            P(("group", "dev"), None),
            P(None, ("group", "dev")),
        ),
        out_specs=P(None, ("group", "dev")),
        check_vma=False,
    )
```

```python
import functools

import jax
import jax.numpy as jnp
from jax import lax
from jax.experimental import pallas as pl
from jax.experimental.pallas import tpu as pltpu
from jax.sharding import PartitionSpec as P

OFFSET_STEPS = 2
REDIST_PASSES = 2

advect_scale = 0.3
relax_scale = 0.3
weno_floor = 1e-06

LANES = 128


class Plan:
    def __init__(self, count, peers, slots, border, layers):
        self.count = count
        self.peers = peers
        self.slots = slots
        self.border = border
        self.layers = layers
        self.halves = count // LANES
        self.local_tiles = 6 * self.halves
        self.groups = 8 * layers
        self.per_tile = LANES // slots
        self.peer_tiles = -(-peers // self.per_tile)
        used = (peers - (self.peer_tiles - 1) * self.per_tile) * slots
        if used + 2 * border <= LANES:
            self.border_tile = self.peer_tiles - 1
            self.border_lane = used
        else:
            self.border_tile = self.peer_tiles
            self.border_lane = 0
        self.far_tiles = self.border_tile + 1
        self.pieces = min(LANES // slots, self.groups)
        self.piece_groups = -(-self.groups // self.pieces)
        self.border_pieces = min(LANES // border, self.groups)
        self.border_groups = -(-self.groups // self.border_pieces)

    def message(self):
        return (self.peers, 8 * self.piece_groups, LANES)

    def border_message(self):
        return (8 * self.border_groups, LANES)


def lane_ids():
    return lax.broadcasted_iota(jnp.int32, (8, LANES), 1)


def turn(block, shift):
    shift = shift % LANES
    return block if shift == 0 else pltpu.roll(block, shift, 1)


def in_block(lanes, start, size):
    return jnp.logical_and(lanes >= start, lanes < start + size)


def half(h):
    return pl.ds(h * LANES, LANES)


def rows8(start):
    return pl.ds(pl.multiple_of(start, 8), 8)


def bits_of(tile, tiles):
    return [(tile & (1 << b)) != 0 for b in range(max(tiles - 1, 1).bit_length())]


def pick_tile(values, masks):
    def pick(lowest, bit):
        if bit < 0:
            return values(lowest)
        first = pick(lowest, bit - 1)
        if lowest + (1 << bit) >= values.count:
            return first
        return jnp.where(masks[bit], pick(lowest + (1 << bit), bit - 1), first)

    return pick(0, len(masks) - 1)


class Taken:
    def __init__(self, sources, lane):
        self.sources = sources
        self.lane = lane
        self.count = len(sources)

    def __call__(self, tile):
        return jnp.take_along_axis(
            self.sources[tile], self.lane, axis=1, mode="promise_in_bounds"
        )


def gather(sources, code):
    return pick_tile(Taken(sources, code & (LANES - 1)), bits_of(code >> 7, len(sources)))


def local_sources(plan, phi, ends, g):
    w = plan.layers
    if w == 1:
        along_y = g * 64
    else:
        along_y = (g // w) * 64 + lax.rem(g, w) * 8
    starts = [g * 8, (8 - w) * 64 + g * 8, along_y, along_y + (8 - w) * 8]
    found = []
    for start in starts:
        for h in range(plan.halves):
            found.append(phi[h, rows8(start), :])
    for end in range(2):
        for h in range(plan.halves):
            if w == 1:
                found.append(phi[h, pl.ds(g * 64 + 7 * end, 8, stride=8), :])
            else:
                found.append(ends[end, h, rows8(g * 8), :])
    return found


def fill_ends(plan, phi, ends):
    w = plan.layers
    if w == 1:
        return

    @pl.loop(0, 8)
    def _(i):
        for end in range(2):
            for l in range(w):
                k = l + end * (8 - w)
                for h in range(plan.halves):
                    ends[end, h, pl.ds(i * 8 * w + l, 8, stride=w), :] = phi[
                        h, pl.ds(i * 64 + k, 8, stride=8), :
                    ]


def pack_sends(plan, phi, ends, send_code, table, outgoing, low, high):
    lanes = lane_ids()
    w = plan.layers

    @pl.loop(0, plan.groups // 4)
    def _(q):
        for v in range(4):
            g = q * 4 + v
            sources = local_sources(plan, phi, ends, g)
            for t in range(plan.far_tiles):
                code = jnp.broadcast_to(send_code[pl.ds(t, 1), :], (8, LANES))
                table[t, rows8(g * 8), :] = gather(sources, code)

    for e in range(plan.peers):
        t, eq = divmod(e, plan.per_tile)
        for gi in range(plan.piece_groups):
            block = None
            for p in range(plan.pieces):
                g = p * plan.piece_groups + gi
                if g >= plan.groups:
                    continue
                part = turn(table[t, pl.ds(g * 8, 8), :], (p - eq) * plan.slots)
                if block is None:
                    block = part
                else:
                    block = jnp.where(lanes >= p * plan.slots, part, block)
            outgoing[e, pl.ds(gi * 8, 8), :] = block
    for side, target in enumerate((low, high)):
        for gi in range(plan.border_groups):
            block = None
            for p in range(plan.border_pieces):
                g = p * plan.border_groups + gi
                if g >= plan.groups:
                    continue
                part = turn(
                    table[plan.border_tile, pl.ds(g * 8, 8), :],
                    (p - side) * plan.border - plan.border_lane,
                )
                if block is None:
                    block = part
                else:
                    block = jnp.where(lanes >= p * plan.border, part, block)
            target[pl.ds(gi * 8, 8), :] = block


def unpack_far(plan, arrived, before, after, table):
    lanes = lane_ids()
    for g in range(plan.groups):
        p, gi = divmod(g, plan.piece_groups)
        bp, bgi = divmod(g, plan.border_groups)
        for t in range(plan.far_tiles):
            block = None
            if t < plan.peer_tiles:
                for eq in range(min(plan.per_tile, plan.peers - t * plan.per_tile)):
                    e = t * plan.per_tile + eq
                    part = turn(arrived[e, pl.ds(gi * 8, 8), :], (eq - p) * plan.slots)
                    if block is None:
                        block = part
                    else:
                        block = jnp.where(lanes >= eq * plan.slots, part, block)
            if t == plan.border_tile:
                for q, source in enumerate((before, after)):
                    start = plan.border_lane + q * plan.border
                    part = turn(source[pl.ds(bgi * 8, 8), :], start - bp * plan.border)
                    if block is None:
                        block = part
                    else:
                        block = jnp.where(lanes >= start, part, block)
            table[t, pl.ds(g * 8, 8), :] = block


def pull_local(plan, phi, ends, halo_code, halos, g):
    sources = local_sources(plan, phi, ends, g)
    for s in range(6):
        for h in range(plan.halves):
            code = jnp.broadcast_to(halo_code[pl.ds(s, 1), half(h)], (8, LANES))
            halos[s, h, rows8(g * 8), :] = gather(sources, code)


def pull_far(plan, table, halo_code, near, halos, sides, g, row=None):
    row = g if row is None else row
    start = plan.local_tiles * LANES
    sources = [table[t, rows8(g * 8), :] for t in range(plan.far_tiles)]
    for s in sides:
        for h in range(plan.halves):
            code = jnp.broadcast_to(halo_code[pl.ds(s, 1), half(h)], (8, LANES))
            far = gather(sources, code - start)
            here = near[s, h, rows8(g * 8), :]
            halos[s - sides[0], h, rows8(row * 8), :] = jnp.where(code >= start, far, here)


def weno_windows(q):
    first = [q[m + 1] - q[m] for m in range(7)]
    second = [first[m + 1] - first[m] for m in range(6)]
    third = [second[m + 1] - second[m] for m in range(5)]
    fourth = [(third[m] - third[m + 1]) * (1.0 / 3.0) for m in range(4)]
    bend = [t * t * (4.0 / 3.0) + weno_floor for t in third]
    found = []
    for m in range(3):
        s1, s2 = second[m + 1], second[m + 2]
        a = bend[m] + s1 * (s1 + third[m])
        b = bend[m + 1] + s1 * s2
        c = bend[m + 2] + s2 * (s2 - third[m + 2])
        a, b, c = (pl.reciprocal(value, approx=True) for value in (a, b, c))
        x, z = a * a, c * c
        total = x + z + (6.0 * b) * b
        xu = x * fourth[m]
        zu = z * fourth[m + 1]
        slope = 0.25 * (s1 + s2)
        middle = first[m + 2] + third[m + 1] * (1.0 / 12.0)
        fix = (xu + 1.5 * zu) * pl.reciprocal(total + 2.0 * z, approx=True)
        backward = middle + slope + fix
        fix = (zu + 1.5 * xu) * pl.reciprocal(total + 2.0 * x, approx=True)
        found.append((backward, fix + slope - middle))
    return found


def inner_values(values):
    three, four, five = weno_windows(values)
    return [three[1], jnp.maximum(three[0], four[1]), jnp.maximum(four[0], five[1]), five[0]]


def line_values(low, values, high, inner):
    zero, one, two = weno_windows(low + values[:5])
    six, seven, last = weno_windows(values[3:] + high)
    steep = [
        jnp.maximum(zero[0], one[1]),
        jnp.maximum(one[0], two[1]),
        jnp.maximum(two[0], inner[0]),
        inner[1],
        inner[2],
        jnp.maximum(inner[3], six[1]),
        jnp.maximum(six[0], seven[1]),
        jnp.maximum(seven[0], last[1]),
    ]
    steep = [jnp.maximum(value, 0.0) for value in steep]
    return [value * value for value in steep]


def line_at(phi, h, axis, q):
    if axis == 0:
        return [phi[h, rows8(m * 64 + q * 8), :] for m in range(8)]
    if axis == 1:
        return [phi[h, rows8(q * 64 + m * 8), :] for m in range(8)]
    return [phi[h, pl.ds(q * 64 + m, 8, stride=8), :] for m in range(8)]


def inner_at(inner, h, axis, q):
    return [inner[axis, h, rows8(q * 32 + m * 8), :] for m in range(4)]


def advect(plan, phi, speed, ready, near, inner, table, halo_code, halos, squares, moved):
    w = plan.layers

    def stage_planes(i, target):
        for l in range(w):
            pull_far(plan, table, halo_code, near, target, (2, 3, 4, 5), i * w + l, l)

    def stage_columns(j, target):
        for l in range(w):
            pull_far(plan, table, halo_code, near, target, (0, 1), l * 8 + j, l)

    def stacked(source, side, h):
        return [source[side, h, pl.ds(l * 8, 8), :] for l in range(w)]

    def spread(source, side, h):
        return [source[side, h, pl.ds(l, 8, stride=w), :] for l in range(w)]

    def plane(i, source):
        for h in range(plan.halves):
            low, high = spread(source, 2, h), spread(source, 3, h)
            values = line_values(low, line_at(phi, h, 2, i), high, inner_at(inner, h, 2, i))
            for k, value in enumerate(values):
                squares[h, pl.ds(i * 64 + k, 8, stride=8), :] = value
        for h in range(plan.halves):
            low, high = stacked(source, 0, h), stacked(source, 1, h)
            values = line_values(low, line_at(phi, h, 1, i), high, inner_at(inner, h, 1, i))
            for j, value in enumerate(values):
                squares[h, rows8(i * 64 + j * 8), :] += value

    def column(j, source):
        for h in range(plan.halves):
            low, high = stacked(source, 0, h), stacked(source, 1, h)
            line = line_at(phi, h, 0, j)
            values = line_values(low, line, high, inner_at(inner, h, 0, j))
            for i, value in enumerate(values):
                here = rows8(i * 64 + j * 8)
                total = squares[h, here, :] + value
                change = advect_scale * speed[h, here, :] * jnp.sqrt(total)
                moved[h, here, :] = line[i] - change

    even, odd = halos
    stage_planes(0, even)
    ready(0)

    @pl.loop(0, 4)
    def _(q):
        i = 2 * q
        stage_planes(i + 1, odd)
        plane(i, even)
        stage_planes(jnp.minimum(i + 2, 7), even)
        plane(i + 1, odd)

    stage_columns(0, even)
    ready(1)

    @pl.loop(0, 4)
    def _(q):
        j = 2 * q
        stage_columns(j + 1, odd)
        column(j, even)
        stage_columns(jnp.minimum(j + 2, 7), even)
        column(j + 1, odd)


def relax(plan, phi, origin, near, table, halo_code, halos, moved, finish):
    row = lax.broadcasted_iota(jnp.int32, (8, LANES), 0)
    columns, faces = halos

    @pl.loop(0, 2)
    def _(q):
        for v in range(4):
            pull_far(plan, table, halo_code, near, columns, (0, 1), q * 4 + v)

    def stage(i):
        pull_far(plan, table, halo_code, near, faces, (2, 3, 4, 5), i)

    def plane(i, h, previous, following, sides):
        at = half(h)
        centre = [phi[h, rows8(i * 64 + j * 8), :] for j in range(8)]
        along_y = [sides[0]] + centre + [sides[1]]
        for j in range(8):
            here = rows8(i * 64 + j * 8)
            value = centre[j]
            start = origin[h, here, :]
            sense = start * lax.rsqrt(start * start + 1.0)
            facing = jnp.where(start > 0.0, 1.0, -1.0)
            first = jnp.broadcast_to(sides[2][j : j + 1], (8, LANES))
            last = jnp.broadcast_to(sides[3][j : j + 1], (8, LANES))
            low_z = jnp.where(row == 0, first, pltpu.roll(value, 1, 0))
            high_z = jnp.where(row == 7, last, pltpu.roll(value, 7, 0))
            pairs = (
                (previous(j), following(j)),
                (along_y[j], along_y[j + 2]),
                (low_z, high_z),
            )
            total = None
            for low, high in pairs:
                steep = jnp.maximum((value - low) * facing, (value - high) * facing)
                steep = jnp.maximum(steep, 0.0)
                steep = steep * steep
                total = steep if total is None else total + steep
            value = value - relax_scale * sense * (jnp.sqrt(total) - 1.0)
            if finish is not None:
                moved[here, at] = value
            else:
                moved[h, here, :] = value

    def planes(i, low, high):
        sides = [
            [faces[s, h, rows8(i * 8), :] for s in range(4)] for h in range(plan.halves)
        ]
        if not isinstance(i, int) or i < 7:
            stage(i + 1)
        for h in range(plan.halves):

            def previous(j):
                if low is None:
                    return phi[h, rows8((i - 1) * 64 + j * 8), :]
                return columns[low, h, pl.ds(j * 8, 8), :]

            def following(j):
                if high is None:
                    return phi[h, rows8((i + 1) * 64 + j * 8), :]
                return columns[high, h, pl.ds(j * 8, 8), :]

            plane(i, h, previous, following, sides[h])
        if finish is not None:
            finish(i)

    stage(0)
    planes(0, 0, None)

    @pl.loop(1, 7)
    def _(i):
        planes(i, None, None)

    planes(7, None, 1)


def first_kernel(
    plan, level_set, peer_slabs, region_slabs, halo_source,
    phi, outgoing, low, high, send_code, halo_code, ends, table, padded, peer, region, entries, ready,
):
    copies = [
        pltpu.make_async_copy(source, target, ready.at[n])
        for n, (source, target) in enumerate(
            ((peer_slabs, peer), (region_slabs, region), (halo_source, entries))
        )
    ]
    for h in range(plan.halves):
        copies.append(
            pltpu.make_async_copy(level_set.at[:, half(h)], phi.at[h], ready.at[3 + h])
        )
    for copy in copies:
        copy.start()
    for copy in copies[:3]:
        copy.wait()
    lanes = lane_ids()
    padded[...] = jnp.zeros_like(padded)
    padded[pl.ds(0, plan.peers), pl.ds(0, plan.slots)] = jnp.maximum(peer[...], 0)
    padded[pl.ds(plan.peers, 2), pl.ds(0, plan.border)] = region[...]

    def wide(row):
        return jnp.broadcast_to(padded[pl.ds(row, 1), :], (8, LANES))

    send_code[...] = jnp.zeros_like(send_code)
    for t in range(plan.far_tiles):
        block = jnp.zeros((8, LANES), jnp.int32)
        if t < plan.peer_tiles:
            for eq in range(min(plan.per_tile, plan.peers - t * plan.per_tile)):
                part = turn(wide(t * plan.per_tile + eq), eq * plan.slots)
                block = jnp.where(in_block(lanes, eq * plan.slots, plan.slots), part, block)
        if t == plan.border_tile:
            for side in range(2):
                start = plan.border_lane + side * plan.border
                part = turn(wide(plan.peers + side), start)
                block = jnp.where(in_block(lanes, start, plan.border), part, block)
        send_code[pl.ds(t, 1), :] = block[0:1]

    entry = entries[...]
    far = entry - plan.local_tiles * LANES
    tile_span = plan.per_tile * plan.slots
    tile = jnp.zeros_like(entry)
    for k in range(1, plan.peer_tiles):
        tile += (far >= k * tile_span).astype(jnp.int32)
    code = (plan.local_tiles + tile) * LANES + far - tile * tile_span
    edge = far - plan.peers * plan.slots
    edge_code = (plan.local_tiles + plan.border_tile) * LANES + plan.border_lane + edge
    code = jnp.where(edge >= 0, edge_code, code)
    halo_code[...] = jnp.where(far >= 0, code, entry)
    for copy in copies[3:]:
        copy.wait()

    fill_ends(plan, phi, ends)
    pack_sends(plan, phi, ends, send_code, table, outgoing, low, high)


def near_kernel(plan, phi, halo_code, near, *rest):
    if plan.layers == 1:

        @pl.loop(0, plan.groups // 2)
        def _(q):
            for v in range(2):
                pull_local(plan, phi, None, halo_code, near, q * 2 + v)

        return
    inner, ends, kept, done = rest
    copies = [pltpu.make_async_copy(kept.at[a], inner.at[a], done.at[a]) for a in range(3)]
    fill_ends(plan, phi, ends)
    for axis in range(3):

        @pl.loop(0, 8)
        def _(q):
            lines = [line_at(phi, h, axis, q) for h in range(plan.halves)]
            pull_local(plan, phi, ends, halo_code, near, axis * 8 + q)
            for h in range(plan.halves):
                for m, value in enumerate(inner_values(lines[h])):
                    kept[axis, h, rows8(q * 32 + m * 8), :] = value

        copies[axis].start()
    for copy in copies:
        copy.wait()


def advect_kernel(
    plan, sends, phi, near, inner, speed, arrived, before, after, send_code, halo_code,
    moved, outgoing, low, high, ends, table, even, odd, squares, fast, kept, loaded, found,
):
    first = [pltpu.make_async_copy(inner.at[a], kept.at[a], found.at[a]) for a in (2, 1)]
    second = [pltpu.make_async_copy(inner.at[0], kept.at[0], found.at[0])]
    for h in range(plan.halves):
        second.append(pltpu.make_async_copy(speed.at[:, half(h)], fast.at[h], loaded.at[h]))
    for copy in first + second:
        copy.start()

    def ready(stage):
        for copy in (first, second)[stage]:
            copy.wait()

    unpack_far(plan, arrived, before, after, table)
    advect(plan, phi, fast, ready, near, kept, table, halo_code, (even, odd), squares, moved)
    pack_sends(sends, moved, ends, send_code, table, outgoing, low, high)


def relax_kernel(
    plan, sends, phi, origin, near, arrived, before, after, send_code, halo_code, *rest
):
    if sends is None:
        (result, table, columns, faces, moved, written) = rest

        def part(i):
            rows = rows8(i * 64)
            rows = pl.ds(rows.start, 64)
            return pltpu.make_async_copy(moved.at[rows], result.at[rows], written.at[i])

        def finish(i):
            part(i).start()

    else:
        (moved, outgoing, low, high, ends, table, columns, faces) = rest
        finish = None
    unpack_far(plan, arrived, before, after, table)
    halos = (columns, faces)
    relax(plan, phi, origin, near, table, halo_code, halos, moved, finish)
    if sends is None:
        for i in range(8):
            part(i).wait()
    else:
        fill_ends(sends, moved, ends)
        pack_sends(sends, moved, ends, send_code, table, outgoing, low, high)


def f32(shape):
    return jax.ShapeDtypeStruct(shape, jnp.float32)


def call(kernel, out_shape, scratch, flops, *operands, far=(), far_out=()):
    whole = pl.BlockSpec(memory_space=pltpu.VMEM)
    apart = pl.BlockSpec(memory_space=pltpu.HBM)
    size = sum(x.size * 4 for x in operands) + sum(x.size * 4 for x in out_shape)
    operands = [
        pltpu.with_memory_space_constraint(x, pltpu.HBM) if n in far else x
        for n, x in enumerate(operands)
    ]
    return pl.pallas_call(
        kernel,
        out_shape=[
            pltpu.HBM(x.shape, x.dtype) if n in far_out else x for n, x in enumerate(out_shape)
        ],
        in_specs=[apart if n in far else whole for n in range(len(operands))],
        out_specs=[apart if n in far_out else whole for n in range(len(out_shape))],
        scratch_shapes=scratch,
        cost_estimate=pl.CostEstimate(flops=flops, bytes_accessed=size, transcendentals=0),
        compiler_params=pltpu.CompilerParams(vmem_limit_bytes=12 * 1024 * 1024),
    )(*operands)


def exchange(outgoing, low, high):
    count = lax.axis_size("group")
    up = [(i, (i + 1) % count) for i in range(count)]
    down = [(target, source) for source, target in up]
    arrived = lax.all_to_all(outgoing, "dev", split_axis=0, concat_axis=0, tiled=True)
    before = lax.ppermute(high, "group", up)
    after = lax.ppermute(low, "group", down)
    return arrived, before, after


def per_device(level_set, speed, peer_slabs, region_slabs, halo_source):
    rows, count = level_set.shape
    peers, slots = peer_slabs.shape
    border = region_slabs.shape[1]
    wide = Plan(count, peers, slots, border, 3)
    thin = Plan(count, peers, slots, border, 1)
    code_rows = -(-wide.far_tiles // 8) * 8

    def ends(plan):
        return pltpu.VMEM((2, wide.halves, 64 * plan.layers, LANES), jnp.float32)

    def table(plan):
        return pltpu.VMEM((plan.far_tiles, 64 * plan.layers, LANES), jnp.float32)

    def halos(sides, groups):
        return pltpu.VMEM((sides, wide.halves, 8 * groups, LANES), jnp.float32)

    def sent(plan):
        return [f32(plan.message()), f32(plan.border_message()), f32(plan.border_message())]

    field = f32((wide.halves, rows, LANES))
    pad_rows = -(-(peers + 2) // 8) * 8
    phi, *message, send_code, halo_code = call(
        functools.partial(first_kernel, wide),
        [field]
        + sent(wide)
        + [
            jax.ShapeDtypeStruct((code_rows, LANES), jnp.int32),
            jax.ShapeDtypeStruct(halo_source.shape, jnp.int32),
        ],
        [
            ends(wide),
            table(wide),
            pltpu.VMEM((pad_rows, LANES), jnp.int32),
            pltpu.VMEM(peer_slabs.shape, jnp.int32),
            pltpu.VMEM(region_slabs.shape, jnp.int32),
            pltpu.VMEM(halo_source.shape, jnp.int32),
            pltpu.SemaphoreType.DMA((3 + wide.halves,)),
        ],
        1000000,
        level_set, peer_slabs, region_slabs, halo_source,
        far=(0, 1, 2, 3),
    )

    def near_halos(plan, phi):
        out = [f32((6, plan.halves, 64 * plan.layers, LANES))]
        scratch = []
        if plan.layers > 1:
            out.append(f32(inner_shape))
            scratch = [ends(plan), pltpu.VMEM(inner_shape, jnp.float32)]
            scratch.append(pltpu.SemaphoreType.DMA((3,)))
        flops = rows * count * 100 * plan.layers
        kernel = functools.partial(near_kernel, plan)
        return call(kernel, out, scratch, flops, phi, halo_code, far_out=(1,))

    inner_shape = (3, wide.halves, rows // 2, LANES)
    block = pltpu.VMEM((wide.halves, rows, LANES), jnp.float32)
    for offset_step in range(OFFSET_STEPS):
        phi, *message = call(
            functools.partial(advect_kernel, wide, thin),
            [field] + sent(thin),
            [ends(wide), table(wide), halos(4, 3), halos(4, 3), block, block]
            + [pltpu.VMEM(inner_shape, jnp.float32)]
            + [pltpu.SemaphoreType.DMA((wide.halves,)), pltpu.SemaphoreType.DMA((3,))],
            rows * count * 300,
            phi, *near_halos(wide, phi), speed, *exchange(*message), send_code, halo_code,
            far=(2, 3),
        )
        origin = phi
        for redist_pass in range(REDIST_PASSES):
            if redist_pass < REDIST_PASSES - 1:
                sends = thin
            elif offset_step < OFFSET_STEPS - 1:
                sends = wide
            else:
                sends = None
            if sends is None:
                out, scratch = [f32((rows, count))], [table(thin)]
                extra = [pltpu.VMEM((rows, count), jnp.float32), pltpu.SemaphoreType.DMA((8,))]
            else:
                out, scratch = [field] + sent(sends), [ends(sends), table(sends)]
                extra = []
            phi, *message = call(
                functools.partial(relax_kernel, thin, sends),
                out,
                scratch + [halos(2, 8), halos(4, 8)] + extra,
                rows * count * 60,
                phi, origin, *near_halos(thin, phi), *exchange(*message), send_code, halo_code,
                far_out=(0,) if sends is None else (),
            )
    return phi


def solution(mesh):
    return jax.shard_map(
        per_device,
        mesh=mesh,
        in_specs=(
            P(None, ("group", "dev")),
            P(None, ("group", "dev")),
            P(("group", "dev"), None),
            P(("group", "dev"), None),
            P(None, ("group", "dev")),
        ),
        out_specs=P(None, ("group", "dev")),
        check_vma=False,
    )
```

```python
import functools

import jax
import jax.numpy as jnp
from jax import lax
from jax.experimental import pallas as pl
from jax.experimental.pallas import tpu as pltpu
from jax.sharding import PartitionSpec as P

OFFSET_STEPS = 2
REDIST_PASSES = 2

advect_scale = 0.3
relax_scale = 0.3
weno_floor = 1e-06

LANES = 128


class Plan:
    def __init__(self, count, peers, slots, border, layers):
        self.count = count
        self.peers = peers
        self.slots = slots
        self.border = border
        self.layers = layers
        self.halves = count // LANES
        self.local_tiles = 6 * self.halves
        self.groups = 8 * layers
        self.per_tile = LANES // slots
        self.peer_tiles = -(-peers // self.per_tile)
        used = (peers - (self.peer_tiles - 1) * self.per_tile) * slots
        if used + 2 * border <= LANES:
            self.border_tile = self.peer_tiles - 1
            self.border_lane = used
        else:
            self.border_tile = self.peer_tiles
            self.border_lane = 0
        self.far_tiles = self.border_tile + 1
        self.pieces = min(LANES // slots, self.groups)
        self.piece_groups = -(-self.groups // self.pieces)
        self.border_pieces = min(LANES // border, self.groups)
        self.border_groups = -(-self.groups // self.border_pieces)

    def message(self):
        return (self.peers, 8 * self.piece_groups, LANES)

    def border_message(self):
        return (8 * self.border_groups, LANES)


def lane_ids():
    return lax.broadcasted_iota(jnp.int32, (8, LANES), 1)


def turn(block, shift):
    shift = shift % LANES
    return block if shift == 0 else pltpu.roll(block, shift, 1)


def in_block(lanes, start, size):
    return jnp.logical_and(lanes >= start, lanes < start + size)


def half(h):
    return pl.ds(h * LANES, LANES)


def rows8(start):
    return pl.ds(pl.multiple_of(start, 8), 8)


def bits_of(tile, tiles):
    return [(tile & (1 << b)) != 0 for b in range(max(tiles - 1, 1).bit_length())]


def pick_tile(values, masks):
    def pick(lowest, bit):
        if bit < 0:
            return values(lowest)
        first = pick(lowest, bit - 1)
        if lowest + (1 << bit) >= values.count:
            return first
        return jnp.where(masks[bit], pick(lowest + (1 << bit), bit - 1), first)

    return pick(0, len(masks) - 1)


class Taken:
    def __init__(self, sources, lane):
        self.sources = sources
        self.lane = lane
        self.count = len(sources)

    def __call__(self, tile):
        return jnp.take_along_axis(
            self.sources[tile], self.lane, axis=1, mode="promise_in_bounds"
        )


def gather(sources, code):
    return pick_tile(Taken(sources, code & (LANES - 1)), bits_of(code >> 7, len(sources)))


def local_sources(plan, phi, ends, g):
    w = plan.layers
    if w == 1:
        along_y = g * 64
    else:
        along_y = (g // w) * 64 + lax.rem(g, w) * 8
    starts = [g * 8, (8 - w) * 64 + g * 8, along_y, along_y + (8 - w) * 8]
    found = []
    for start in starts:
        for h in range(plan.halves):
            found.append(phi[h, rows8(start), :])
    for end in range(2):
        for h in range(plan.halves):
            if w == 1:
                found.append(phi[h, pl.ds(g * 64 + 7 * end, 8, stride=8), :])
            else:
                found.append(ends[end, h, rows8(g * 8), :])
    return found


def fill_ends(plan, phi, ends):
    w = plan.layers
    if w == 1:
        return

    @pl.loop(0, 8)
    def _(i):
        for end in range(2):
            for l in range(w):
                k = l + end * (8 - w)
                for h in range(plan.halves):
                    ends[end, h, pl.ds(i * 8 * w + l, 8, stride=w), :] = phi[
                        h, pl.ds(i * 64 + k, 8, stride=8), :
                    ]


def pack_sends(plan, phi, ends, send_code, table, outgoing, low, high):
    lanes = lane_ids()
    w = plan.layers

    @pl.loop(0, plan.groups // 4)
    def _(q):
        for v in range(4):
            g = q * 4 + v
            sources = local_sources(plan, phi, ends, g)
            for t in range(plan.far_tiles):
                code = jnp.broadcast_to(send_code[pl.ds(t, 1), :], (8, LANES))
                table[t, rows8(g * 8), :] = gather(sources, code)

    for e in range(plan.peers):
        t, eq = divmod(e, plan.per_tile)
        for gi in range(plan.piece_groups):
            block = None
            for p in range(plan.pieces):
                g = p * plan.piece_groups + gi
                if g >= plan.groups:
                    continue
                part = turn(table[t, pl.ds(g * 8, 8), :], (p - eq) * plan.slots)
                if block is None:
                    block = part
                else:
                    block = jnp.where(lanes >= p * plan.slots, part, block)
            outgoing[e, pl.ds(gi * 8, 8), :] = block
    for side, target in enumerate((low, high)):
        for gi in range(plan.border_groups):
            block = None
            for p in range(plan.border_pieces):
                g = p * plan.border_groups + gi
                if g >= plan.groups:
                    continue
                part = turn(
                    table[plan.border_tile, pl.ds(g * 8, 8), :],
                    (p - side) * plan.border - plan.border_lane,
                )
                if block is None:
                    block = part
                else:
                    block = jnp.where(lanes >= p * plan.border, part, block)
            target[pl.ds(gi * 8, 8), :] = block


def unpack_far(plan, arrived, before, after, table):
    lanes = lane_ids()
    for g in range(plan.groups):
        p, gi = divmod(g, plan.piece_groups)
        bp, bgi = divmod(g, plan.border_groups)
        for t in range(plan.far_tiles):
            block = None
            if t < plan.peer_tiles:
                for eq in range(min(plan.per_tile, plan.peers - t * plan.per_tile)):
                    e = t * plan.per_tile + eq
                    part = turn(arrived[e, pl.ds(gi * 8, 8), :], (eq - p) * plan.slots)
                    if block is None:
                        block = part
                    else:
                        block = jnp.where(lanes >= eq * plan.slots, part, block)
            if t == plan.border_tile:
                for q, source in enumerate((before, after)):
                    start = plan.border_lane + q * plan.border
                    part = turn(source[pl.ds(bgi * 8, 8), :], start - bp * plan.border)
                    if block is None:
                        block = part
                    else:
                        block = jnp.where(lanes >= start, part, block)
            table[t, pl.ds(g * 8, 8), :] = block


def pull_local(plan, phi, ends, halo_code, halos, g):
    sources = local_sources(plan, phi, ends, g)
    for s in range(6):
        for h in range(plan.halves):
            code = jnp.broadcast_to(halo_code[pl.ds(s, 1), half(h)], (8, LANES))
            halos[s, h, rows8(g * 8), :] = gather(sources, code)


def far_values(plan, table, halo_code, near, sides, g):
    start = plan.local_tiles * LANES
    sources = [table[t, rows8(g * 8), :] for t in range(plan.far_tiles)]
    found = {}
    for s in sides:
        for h in range(plan.halves):
            code = jnp.broadcast_to(halo_code[pl.ds(s, 1), half(h)], (8, LANES))
            far = gather(sources, code - start)
            found[s, h] = jnp.where(code >= start, far, near[s, h, rows8(g * 8), :])
    return found


def pull_far(plan, table, halo_code, near, halos, sides, g, row):
    for (s, h), value in far_values(plan, table, halo_code, near, sides, g).items():
        halos[s - sides[0], h, rows8(row * 8), :] = value


def weno_windows(q):
    first = [q[m + 1] - q[m] for m in range(7)]
    second = [first[m + 1] - first[m] for m in range(6)]
    third = [second[m + 1] - second[m] for m in range(5)]
    fourth = [(third[m] - third[m + 1]) * (1.0 / 3.0) for m in range(4)]
    bend = [t * t * (4.0 / 3.0) + weno_floor for t in third]
    found = []
    for m in range(3):
        s1, s2 = second[m + 1], second[m + 2]
        a = bend[m] + s1 * (s1 + third[m])
        b = bend[m + 1] + s1 * s2
        c = bend[m + 2] + s2 * (s2 - third[m + 2])
        a, b, c = (pl.reciprocal(value, approx=True) for value in (a, b, c))
        x, z = a * a, c * c
        total = x + z + (6.0 * b) * b
        xu = x * fourth[m]
        zu = z * fourth[m + 1]
        slope = 0.25 * (s1 + s2)
        middle = first[m + 2] + third[m + 1] * (1.0 / 12.0)
        fix = (xu + 1.5 * zu) * pl.reciprocal(total + 2.0 * z, approx=True)
        backward = middle + slope + fix
        fix = (zu + 1.5 * xu) * pl.reciprocal(total + 2.0 * x, approx=True)
        found.append((backward, fix + slope - middle))
    return found


def inner_values(values):
    three, four, five = weno_windows(values)
    return [three[1], jnp.maximum(three[0], four[1]), jnp.maximum(four[0], five[1]), five[0]]


def line_values(low, values, high, inner):
    zero, one, two = weno_windows(low + values[:5])
    six, seven, last = weno_windows(values[3:] + high)
    steep = [
        jnp.maximum(zero[0], one[1]),
        jnp.maximum(one[0], two[1]),
        jnp.maximum(two[0], inner[0]),
        inner[1],
        inner[2],
        jnp.maximum(inner[3], six[1]),
        jnp.maximum(six[0], seven[1]),
        jnp.maximum(seven[0], last[1]),
    ]
    steep = [jnp.maximum(value, 0.0) for value in steep]
    return [value * value for value in steep]


def line_at(phi, h, axis, q):
    if axis == 0:
        return [phi[h, rows8(m * 64 + q * 8), :] for m in range(8)]
    if axis == 1:
        return [phi[h, rows8(q * 64 + m * 8), :] for m in range(8)]
    return [phi[h, pl.ds(q * 64 + m, 8, stride=8), :] for m in range(8)]


def inner_at(inner, h, axis, q):
    return [inner[axis, h, rows8(q * 32 + m * 8), :] for m in range(4)]


def advect(plan, phi, speed, ready, near, inner, table, halo_code, halos, squares, moved):
    w = plan.layers

    def stage_planes(i, target):
        for l in range(w):
            pull_far(plan, table, halo_code, near, target, (2, 3, 4, 5), i * w + l, l)

    def stage_columns(j, target):
        for l in range(w):
            pull_far(plan, table, halo_code, near, target, (0, 1), l * 8 + j, l)

    def stacked(source, side, h):
        return [source[side, h, pl.ds(l * 8, 8), :] for l in range(w)]

    def spread(source, side, h):
        return [source[side, h, pl.ds(l, 8, stride=w), :] for l in range(w)]

    def plane(i, source):
        for h in range(plan.halves):
            low, high = spread(source, 2, h), spread(source, 3, h)
            values = line_values(low, line_at(phi, h, 2, i), high, inner_at(inner, h, 2, i))
            for k, value in enumerate(values):
                squares[h, pl.ds(i * 64 + k, 8, stride=8), :] = value
        for h in range(plan.halves):
            low, high = stacked(source, 0, h), stacked(source, 1, h)
            values = line_values(low, line_at(phi, h, 1, i), high, inner_at(inner, h, 1, i))
            for j, value in enumerate(values):
                squares[h, rows8(i * 64 + j * 8), :] += value

    def column(j, source):
        for h in range(plan.halves):
            low, high = stacked(source, 0, h), stacked(source, 1, h)
            line = line_at(phi, h, 0, j)
            values = line_values(low, line, high, inner_at(inner, h, 0, j))
            for i, value in enumerate(values):
                here = rows8(i * 64 + j * 8)
                total = squares[h, here, :] + value
                change = advect_scale * speed[h, here, :] * jnp.sqrt(total)
                moved[h, here, :] = line[i] - change

    even, odd = halos
    stage_planes(0, even)
    ready(0)

    @pl.loop(0, 4)
    def _(q):
        i = 2 * q
        stage_planes(i + 1, odd)
        plane(i, even)
        stage_planes(jnp.minimum(i + 2, 7), even)
        plane(i + 1, odd)

    stage_columns(0, even)
    ready(1)

    @pl.loop(0, 4)
    def _(q):
        j = 2 * q
        stage_columns(j + 1, odd)
        column(j, even)
        stage_columns(jnp.minimum(j + 2, 7), even)
        column(j + 1, odd)


def steepness(value, low, high, facing):
    steep = jnp.maximum((value - low) * facing, (value - high) * facing)
    steep = jnp.maximum(steep, 0.0)
    return steep * steep


def facing_of(start):
    return jnp.where(start > 0.0, 1.0, -1.0)


def relax_inner(plan, phi, origin, inner, i):
    row = lax.broadcasted_iota(jnp.int32, (8, LANES), 0)
    middle = jnp.logical_and(row > 0, row < 7)
    inside = jnp.where(jnp.logical_and(i > 0, i < 7), 1.0, 0.0)
    below, above = jnp.maximum(i - 1, 0), jnp.minimum(i + 1, 7)
    for h in range(plan.halves):
        line = line_at(phi, h, 1, i)
        for j, value in enumerate(line):
            here = rows8(i * 64 + j * 8)
            facing = facing_of(origin[h, here, :])
            low = phi[h, rows8(below * 64 + j * 8), :]
            high = phi[h, rows8(above * 64 + j * 8), :]
            total = inside * steepness(value, low, high, facing)
            if 0 < j < 7:
                total += steepness(value, line[j - 1], line[j + 1], facing)
            low, high = pltpu.roll(value, 1, 0), pltpu.roll(value, 7, 0)
            total += jnp.where(middle, steepness(value, low, high, facing), 0.0)
            inner[h, here, :] = total


def relax(plan, phi, origin, near, inner, table, halo_code, part, moved, finish):
    @pl.loop(0, 4)
    def _(q):
        for v in range(2):
            i = q * 2 + v
            halo = far_values(plan, table, halo_code, near, (2, 3, 4, 5), i)
            for h in range(plan.halves):
                for j in range(8):
                    here = rows8(i * 64 + j * 8)
                    if 0 < j < 7:
                        part[h, here, :] = jnp.zeros((8, LANES), jnp.float32)
                        continue
                    side, other = (2, 1) if j == 0 else (3, 6)
                    value = phi[h, here, :]
                    beside = phi[h, rows8(i * 64 + other * 8), :]
                    facing = facing_of(origin[h, here, :])
                    part[h, here, :] = steepness(value, halo[side, h], beside, facing)
                for side, k, other in ((4, 0, 1), (5, 7, 6)):
                    here = pl.ds(i * 64 + k, 8, stride=8)
                    value = phi[h, here, :]
                    beside = phi[h, pl.ds(i * 64 + other, 8, stride=8), :]
                    facing = facing_of(origin[h, here, :])
                    part[h, here, :] += steepness(value, halo[side, h], beside, facing)

    @pl.loop(0, 2)
    def _(q):
        for v in range(4):
            j = q * 4 + v
            halo = far_values(plan, table, halo_code, near, (0, 1), j)
            for h in range(plan.halves):
                for side, i, other in ((0, 0, 1), (1, 7, 6)):
                    here = rows8(i * 64 + j * 8)
                    value = phi[h, here, :]
                    beside = phi[h, rows8(other * 64 + j * 8), :]
                    facing = facing_of(origin[h, here, :])
                    part[h, here, :] += steepness(value, halo[side, h], beside, facing)

    @pl.loop(0, 4)
    def _(q):
        for v in range(2):
            i = q * 2 + v
            for h in range(plan.halves):
                for j in range(8):
                    here = rows8(i * 64 + j * 8)
                    start = origin[h, here, :]
                    sense = start * lax.rsqrt(start * start + 1.0)
                    slope = jnp.sqrt(inner[h, here, :] + part[h, here, :])
                    value = phi[h, here, :] - relax_scale * sense * (slope - 1.0)
                    if finish is not None:
                        moved[here, half(h)] = value
                    else:
                        moved[h, here, :] = value
            if finish is not None:
                finish(i)


def first_kernel(
    plan, level_set, peer_slabs, region_slabs, halo_source,
    phi, outgoing, low, high, send_code, halo_code, ends, table, padded, peer, region, entries, ready,
):
    copies = [
        pltpu.make_async_copy(source, target, ready.at[n])
        for n, (source, target) in enumerate(
            ((peer_slabs, peer), (region_slabs, region), (halo_source, entries))
        )
    ]
    for h in range(plan.halves):
        copies.append(
            pltpu.make_async_copy(level_set.at[:, half(h)], phi.at[h], ready.at[3 + h])
        )
    for copy in copies:
        copy.start()
    for copy in copies[:3]:
        copy.wait()
    lanes = lane_ids()
    padded[...] = jnp.zeros_like(padded)
    padded[pl.ds(0, plan.peers), pl.ds(0, plan.slots)] = jnp.maximum(peer[...], 0)
    padded[pl.ds(plan.peers, 2), pl.ds(0, plan.border)] = region[...]

    def wide(row):
        return jnp.broadcast_to(padded[pl.ds(row, 1), :], (8, LANES))

    send_code[...] = jnp.zeros_like(send_code)
    for t in range(plan.far_tiles):
        block = jnp.zeros((8, LANES), jnp.int32)
        if t < plan.peer_tiles:
            for eq in range(min(plan.per_tile, plan.peers - t * plan.per_tile)):
                part = turn(wide(t * plan.per_tile + eq), eq * plan.slots)
                block = jnp.where(in_block(lanes, eq * plan.slots, plan.slots), part, block)
        if t == plan.border_tile:
            for side in range(2):
                start = plan.border_lane + side * plan.border
                part = turn(wide(plan.peers + side), start)
                block = jnp.where(in_block(lanes, start, plan.border), part, block)
        send_code[pl.ds(t, 1), :] = block[0:1]

    entry = entries[...]
    far = entry - plan.local_tiles * LANES
    tile_span = plan.per_tile * plan.slots
    tile = jnp.zeros_like(entry)
    for k in range(1, plan.peer_tiles):
        tile += (far >= k * tile_span).astype(jnp.int32)
    code = (plan.local_tiles + tile) * LANES + far - tile * tile_span
    edge = far - plan.peers * plan.slots
    edge_code = (plan.local_tiles + plan.border_tile) * LANES + plan.border_lane + edge
    code = jnp.where(edge >= 0, edge_code, code)
    halo_code[...] = jnp.where(far >= 0, code, entry)
    for copy in copies[3:]:
        copy.wait()

    fill_ends(plan, phi, ends)
    pack_sends(plan, phi, ends, send_code, table, outgoing, low, high)


def near_thin_kernel(plan, phi, origin, halo_code, near, inner):
    @pl.loop(0, plan.groups // 2)
    def _(q):
        for v in range(2):
            pull_local(plan, phi, None, halo_code, near, q * 2 + v)
            relax_inner(plan, phi, origin, inner, q * 2 + v)


def near_wide_kernel(plan, phi, halo_code, near, *rest):
    inner, ends, kept, done = rest
    copies = [pltpu.make_async_copy(kept.at[a], inner.at[a], done.at[a]) for a in range(3)]
    fill_ends(plan, phi, ends)
    for axis in range(3):

        @pl.loop(0, 8)
        def _(q):
            lines = [line_at(phi, h, axis, q) for h in range(plan.halves)]
            pull_local(plan, phi, ends, halo_code, near, axis * 8 + q)
            for h in range(plan.halves):
                for m, value in enumerate(inner_values(lines[h])):
                    kept[axis, h, rows8(q * 32 + m * 8), :] = value

        copies[axis].start()
    for copy in copies:
        copy.wait()


def advect_kernel(
    plan, sends, phi, near, inner, speed, arrived, before, after, send_code, halo_code,
    moved, outgoing, low, high, ends, table, even, odd, squares, fast, kept, loaded, found,
):
    first = [pltpu.make_async_copy(inner.at[a], kept.at[a], found.at[a]) for a in (2, 1)]
    second = [pltpu.make_async_copy(inner.at[0], kept.at[0], found.at[0])]
    for h in range(plan.halves):
        second.append(pltpu.make_async_copy(speed.at[:, half(h)], fast.at[h], loaded.at[h]))
    for copy in first + second:
        copy.start()

    def ready(stage):
        for copy in (first, second)[stage]:
            copy.wait()

    unpack_far(plan, arrived, before, after, table)
    advect(plan, phi, fast, ready, near, kept, table, halo_code, (even, odd), squares, moved)
    pack_sends(sends, moved, ends, send_code, table, outgoing, low, high)


def relax_kernel(
    plan, sends, phi, origin, near, inner, arrived, before, after, send_code, halo_code, *rest
):
    if sends is None:
        (result, table, part, moved, written) = rest

        def plane_copy(i):
            rows = rows8(i * 64)
            rows = pl.ds(rows.start, 64)
            return pltpu.make_async_copy(moved.at[rows], result.at[rows], written.at[i])

        def finish(i):
            plane_copy(i).start()

    else:
        (moved, outgoing, low, high, ends, table, part) = rest
        finish = None
    unpack_far(plan, arrived, before, after, table)
    relax(plan, phi, origin, near, inner, table, halo_code, part, moved, finish)
    if sends is None:
        for i in range(8):
            plane_copy(i).wait()
    else:
        fill_ends(sends, moved, ends)
        pack_sends(sends, moved, ends, send_code, table, outgoing, low, high)


def f32(shape):
    return jax.ShapeDtypeStruct(shape, jnp.float32)


def call(kernel, out_shape, scratch, flops, *operands, far=(), far_out=()):
    whole = pl.BlockSpec(memory_space=pltpu.VMEM)
    apart = pl.BlockSpec(memory_space=pltpu.HBM)
    size = sum(x.size * 4 for x in operands) + sum(x.size * 4 for x in out_shape)
    operands = [
        pltpu.with_memory_space_constraint(x, pltpu.HBM) if n in far else x
        for n, x in enumerate(operands)
    ]
    return pl.pallas_call(
        kernel,
        out_shape=[
            pltpu.HBM(x.shape, x.dtype) if n in far_out else x for n, x in enumerate(out_shape)
        ],
        in_specs=[apart if n in far else whole for n in range(len(operands))],
        out_specs=[apart if n in far_out else whole for n in range(len(out_shape))],
        scratch_shapes=scratch,
        cost_estimate=pl.CostEstimate(flops=flops, bytes_accessed=size, transcendentals=0),
        compiler_params=pltpu.CompilerParams(vmem_limit_bytes=12 * 1024 * 1024),
    )(*operands)


def exchange(outgoing, low, high):
    count = lax.axis_size("group")
    up = [(i, (i + 1) % count) for i in range(count)]
    down = [(target, source) for source, target in up]
    arrived = lax.all_to_all(outgoing, "dev", split_axis=0, concat_axis=0, tiled=True)
    before = lax.ppermute(high, "group", up)
    after = lax.ppermute(low, "group", down)
    return arrived, before, after


def per_device(level_set, speed, peer_slabs, region_slabs, halo_source):
    rows, count = level_set.shape
    peers, slots = peer_slabs.shape
    border = region_slabs.shape[1]
    wide = Plan(count, peers, slots, border, 3)
    thin = Plan(count, peers, slots, border, 1)
    code_rows = -(-wide.far_tiles // 8) * 8

    def ends(plan):
        return pltpu.VMEM((2, wide.halves, 64 * plan.layers, LANES), jnp.float32)

    def table(plan):
        return pltpu.VMEM((plan.far_tiles, 64 * plan.layers, LANES), jnp.float32)

    def halos(sides, groups):
        return pltpu.VMEM((sides, wide.halves, 8 * groups, LANES), jnp.float32)

    def sent(plan):
        return [f32(plan.message()), f32(plan.border_message()), f32(plan.border_message())]

    field = f32((wide.halves, rows, LANES))
    pad_rows = -(-(peers + 2) // 8) * 8
    phi, *message, send_code, halo_code = call(
        functools.partial(first_kernel, wide),
        [field]
        + sent(wide)
        + [
            jax.ShapeDtypeStruct((code_rows, LANES), jnp.int32),
            jax.ShapeDtypeStruct(halo_source.shape, jnp.int32),
        ],
        [
            ends(wide),
            table(wide),
            pltpu.VMEM((pad_rows, LANES), jnp.int32),
            pltpu.VMEM(peer_slabs.shape, jnp.int32),
            pltpu.VMEM(region_slabs.shape, jnp.int32),
            pltpu.VMEM(halo_source.shape, jnp.int32),
            pltpu.SemaphoreType.DMA((3 + wide.halves,)),
        ],
        1000000,
        level_set, peer_slabs, region_slabs, halo_source,
        far=(0, 1, 2, 3),
    )

    def near_halos(plan, *fields):
        out = [f32((6, plan.halves, 64 * plan.layers, LANES))]
        flops = rows * count * 100 * plan.layers
        if plan.layers == 1:
            kernel = functools.partial(near_thin_kernel, plan)
            return call(kernel, out + [field], [], flops, *fields, halo_code)
        out.append(f32(inner_shape))
        scratch = [ends(plan), pltpu.VMEM(inner_shape, jnp.float32)]
        scratch.append(pltpu.SemaphoreType.DMA((3,)))
        kernel = functools.partial(near_wide_kernel, plan)
        return call(kernel, out, scratch, flops, *fields, halo_code, far_out=(1,))

    inner_shape = (3, wide.halves, rows // 2, LANES)
    block = pltpu.VMEM((wide.halves, rows, LANES), jnp.float32)
    for offset_step in range(OFFSET_STEPS):
        phi, *message = call(
            functools.partial(advect_kernel, wide, thin),
            [field] + sent(thin),
            [ends(wide), table(wide), halos(4, 3), halos(4, 3), block, block]
            + [pltpu.VMEM(inner_shape, jnp.float32)]
            + [pltpu.SemaphoreType.DMA((wide.halves,)), pltpu.SemaphoreType.DMA((3,))],
            rows * count * 300,
            phi, *near_halos(wide, phi), speed, *exchange(*message), send_code, halo_code,
            far=(2, 3),
        )
        origin = phi
        for redist_pass in range(REDIST_PASSES):
            if redist_pass < REDIST_PASSES - 1:
                sends = thin
            elif offset_step < OFFSET_STEPS - 1:
                sends = wide
            else:
                sends = None
            if sends is None:
                out, scratch = [f32((rows, count))], [table(thin)]
                extra = [pltpu.VMEM((rows, count), jnp.float32), pltpu.SemaphoreType.DMA((8,))]
            else:
                out, scratch = [field] + sent(sends), [ends(sends), table(sends)]
                extra = []
            phi, *message = call(
                functools.partial(relax_kernel, thin, sends),
                out,
                scratch + [block] + extra,
                rows * count * 60,
                phi, origin, *near_halos(thin, phi, origin), *exchange(*message), send_code, halo_code,
                far_out=(0,) if sends is None else (),
            )
    return phi


def solution(mesh):
    return jax.shard_map(
        per_device,
        mesh=mesh,
        in_specs=(
            P(None, ("group", "dev")),
            P(None, ("group", "dev")),
            P(("group", "dev"), None),
            P(("group", "dev"), None),
            P(None, ("group", "dev")),
        ),
        out_specs=P(None, ("group", "dev")),
        check_vma=False,
    )
```

```python
import functools

import jax
import jax.numpy as jnp
from jax import lax
from jax.experimental import pallas as pl
from jax.experimental.pallas import tpu as pltpu
from jax.sharding import PartitionSpec as P

OFFSET_STEPS = 2
REDIST_PASSES = 2

advect_scale = 0.3
relax_scale = 0.3
weno_floor = 1e-06

LANES = 128


class Plan:
    def __init__(self, count, peers, slots, border, layers):
        self.count = count
        self.peers = peers
        self.slots = slots
        self.border = border
        self.layers = layers
        self.halves = count // LANES
        self.local_tiles = 6 * self.halves
        self.groups = 8 * layers
        self.per_tile = LANES // slots
        self.peer_tiles = -(-peers // self.per_tile)
        used = (peers - (self.peer_tiles - 1) * self.per_tile) * slots
        if used + 2 * border <= LANES:
            self.border_tile = self.peer_tiles - 1
            self.border_lane = used
        else:
            self.border_tile = self.peer_tiles
            self.border_lane = 0
        self.far_tiles = self.border_tile + 1
        self.pieces = min(LANES // slots, self.groups)
        self.piece_groups = -(-self.groups // self.pieces)
        self.border_pieces = min(LANES // border, self.groups)
        self.border_groups = -(-self.groups // self.border_pieces)

    def message(self):
        return (self.peers, 8 * self.piece_groups, LANES)

    def border_message(self):
        return (8 * self.border_groups, LANES)


def lane_ids():
    return lax.broadcasted_iota(jnp.int32, (8, LANES), 1)


def turn(block, shift):
    shift = shift % LANES
    return block if shift == 0 else pltpu.roll(block, shift, 1)


def in_block(lanes, start, size):
    return jnp.logical_and(lanes >= start, lanes < start + size)


def half(h):
    return pl.ds(h * LANES, LANES)


def rows8(start):
    return pl.ds(pl.multiple_of(start, 8), 8)


def bits_of(tile, tiles):
    return [(tile & (1 << b)) != 0 for b in range(max(tiles - 1, 1).bit_length())]


def pick_tile(values, masks):
    def pick(lowest, bit):
        if bit < 0:
            return values(lowest)
        first = pick(lowest, bit - 1)
        if lowest + (1 << bit) >= values.count:
            return first
        return jnp.where(masks[bit], pick(lowest + (1 << bit), bit - 1), first)

    return pick(0, len(masks) - 1)


class Taken:
    def __init__(self, sources, lane):
        self.sources = sources
        self.lane = lane
        self.count = len(sources)

    def __call__(self, tile):
        return jnp.take_along_axis(
            self.sources[tile], self.lane, axis=1, mode="promise_in_bounds"
        )


def gather(sources, code):
    return pick_tile(Taken(sources, code & (LANES - 1)), bits_of(code >> 7, len(sources)))


def local_sources(plan, phi, ends, g):
    w = plan.layers
    if w == 1:
        along_y = g * 64
    else:
        along_y = (g // w) * 64 + lax.rem(g, w) * 8
    starts = [g * 8, (8 - w) * 64 + g * 8, along_y, along_y + (8 - w) * 8]
    found = []
    for start in starts:
        for h in range(plan.halves):
            found.append(phi[h, rows8(start), :])
    for end in range(2):
        for h in range(plan.halves):
            if w == 1:
                found.append(phi[h, pl.ds(g * 64 + 7 * end, 8, stride=8), :])
            else:
                found.append(ends[end, h, rows8(g * 8), :])
    return found


def fill_ends(plan, phi, ends):
    w = plan.layers
    if w == 1:
        return

    @pl.loop(0, 8)
    def _(i):
        for end in range(2):
            for l in range(w):
                k = l + end * (8 - w)
                for h in range(plan.halves):
                    ends[end, h, pl.ds(i * 8 * w + l, 8, stride=w), :] = phi[
                        h, pl.ds(i * 64 + k, 8, stride=8), :
                    ]


def pack_sends(plan, phi, ends, send_code, table, outgoing, low, high):
    lanes = lane_ids()
    w = plan.layers

    @pl.loop(0, plan.groups // 4)
    def _(q):
        for v in range(4):
            g = q * 4 + v
            sources = local_sources(plan, phi, ends, g)
            for t in range(plan.far_tiles):
                code = jnp.broadcast_to(send_code[pl.ds(t, 1), :], (8, LANES))
                table[t, rows8(g * 8), :] = gather(sources, code)

    for e in range(plan.peers):
        t, eq = divmod(e, plan.per_tile)
        for gi in range(plan.piece_groups):
            block = None
            for p in range(plan.pieces):
                g = p * plan.piece_groups + gi
                if g >= plan.groups:
                    continue
                part = turn(table[t, pl.ds(g * 8, 8), :], (p - eq) * plan.slots)
                if block is None:
                    block = part
                else:
                    block = jnp.where(lanes >= p * plan.slots, part, block)
            outgoing[e, pl.ds(gi * 8, 8), :] = block
    for side, target in enumerate((low, high)):
        for gi in range(plan.border_groups):
            block = None
            for p in range(plan.border_pieces):
                g = p * plan.border_groups + gi
                if g >= plan.groups:
                    continue
                part = turn(
                    table[plan.border_tile, pl.ds(g * 8, 8), :],
                    (p - side) * plan.border - plan.border_lane,
                )
                if block is None:
                    block = part
                else:
                    block = jnp.where(lanes >= p * plan.border, part, block)
            target[pl.ds(gi * 8, 8), :] = block


def unpack_far(plan, arrived, before, after, table):
    lanes = lane_ids()
    for g in range(plan.groups):
        p, gi = divmod(g, plan.piece_groups)
        bp, bgi = divmod(g, plan.border_groups)
        for t in range(plan.far_tiles):
            block = None
            if t < plan.peer_tiles:
                for eq in range(min(plan.per_tile, plan.peers - t * plan.per_tile)):
                    e = t * plan.per_tile + eq
                    part = turn(arrived[e, pl.ds(gi * 8, 8), :], (eq - p) * plan.slots)
                    if block is None:
                        block = part
                    else:
                        block = jnp.where(lanes >= eq * plan.slots, part, block)
            if t == plan.border_tile:
                for q, source in enumerate((before, after)):
                    start = plan.border_lane + q * plan.border
                    part = turn(source[pl.ds(bgi * 8, 8), :], start - bp * plan.border)
                    if block is None:
                        block = part
                    else:
                        block = jnp.where(lanes >= start, part, block)
            table[t, pl.ds(g * 8, 8), :] = block


def pull_local(plan, phi, ends, halo_code, halos, g):
    sources = local_sources(plan, phi, ends, g)
    for s in range(6):
        for h in range(plan.halves):
            code = jnp.broadcast_to(halo_code[pl.ds(s, 1), half(h)], (8, LANES))
            halos[s, h, rows8(g * 8), :] = gather(sources, code)


def far_values(plan, table, halo_code, near, sides, g):
    start = plan.local_tiles * LANES
    sources = [table[t, rows8(g * 8), :] for t in range(plan.far_tiles)]
    found = {}
    for s in sides:
        for h in range(plan.halves):
            code = jnp.broadcast_to(halo_code[pl.ds(s, 1), half(h)], (8, LANES))
            far = gather(sources, code - start)
            found[s, h] = jnp.where(code >= start, far, near[s, h, rows8(g * 8), :])
    return found


def pull_far(plan, table, halo_code, near, halos, sides, g, row):
    for (s, h), value in far_values(plan, table, halo_code, near, sides, g).items():
        halos[s - sides[0], h, rows8(row * 8), :] = value


def weno_windows(q):
    first = [q[m + 1] - q[m] for m in range(7)]
    second = [first[m + 1] - first[m] for m in range(6)]
    third = [second[m + 1] - second[m] for m in range(5)]
    fourth = [(third[m] - third[m + 1]) * (1.0 / 6.0) for m in range(4)]
    bend = [t * t * (4.0 / 3.0) + weno_floor for t in third]
    found = []
    for m in range(3):
        s1, s2 = second[m + 1], second[m + 2]
        a = bend[m] + s1 * (s1 + third[m])
        b = bend[m + 1] + s1 * s2
        c = bend[m + 2] + s2 * (s2 - third[m + 2])
        a, b, c = (pl.reciprocal(value, approx=True) for value in (a, b, c))
        x, z = a * a, c * c
        total = 0.5 * (x + z) + (3.0 * b) * b
        xu = x * fourth[m]
        zu = z * fourth[m + 1]
        slope = 0.25 * (s1 + s2)
        middle = first[m + 2] + third[m + 1] * (1.0 / 12.0)
        fix = (xu + 1.5 * zu) * pl.reciprocal(total + z, approx=True)
        backward = middle + slope + fix
        fix = (zu + 1.5 * xu) * pl.reciprocal(total + x, approx=True)
        found.append((backward, fix + slope - middle))
    return found


def inner_values(values):
    three, four, five = weno_windows(values)
    return [three[1], jnp.maximum(three[0], four[1]), jnp.maximum(four[0], five[1]), five[0]]


def line_values(low, values, high, inner):
    zero, one, two = weno_windows(low + values[:5])
    six, seven, last = weno_windows(values[3:] + high)
    steep = [
        jnp.maximum(zero[0], one[1]),
        jnp.maximum(one[0], two[1]),
        jnp.maximum(two[0], inner[0]),
        inner[1],
        inner[2],
        jnp.maximum(inner[3], six[1]),
        jnp.maximum(six[0], seven[1]),
        jnp.maximum(seven[0], last[1]),
    ]
    steep = [jnp.maximum(value, 0.0) for value in steep]
    return [value * value for value in steep]


def line_at(phi, h, axis, q):
    if axis == 0:
        return [phi[h, rows8(m * 64 + q * 8), :] for m in range(8)]
    if axis == 1:
        return [phi[h, rows8(q * 64 + m * 8), :] for m in range(8)]
    return [phi[h, pl.ds(q * 64 + m, 8, stride=8), :] for m in range(8)]


def inner_at(inner, h, axis, q):
    return [inner[axis, h, rows8(q * 32 + m * 8), :] for m in range(4)]


def advect(plan, phi, speed, ready, near, inner, table, halo_code, halos, squares, moved):
    w = plan.layers

    def stage_planes(i, target):
        for l in range(w):
            pull_far(plan, table, halo_code, near, target, (2, 3, 4, 5), i * w + l, l)

    def stage_columns(j, target):
        for l in range(w):
            pull_far(plan, table, halo_code, near, target, (0, 1), l * 8 + j, l)

    def stacked(source, side, h):
        return [source[side, h, pl.ds(l * 8, 8), :] for l in range(w)]

    def spread(source, side, h):
        return [source[side, h, pl.ds(l, 8, stride=w), :] for l in range(w)]

    def plane(i, source):
        for h in range(plan.halves):
            low, high = spread(source, 2, h), spread(source, 3, h)
            values = line_values(low, line_at(phi, h, 2, i), high, inner_at(inner, h, 2, i))
            for k, value in enumerate(values):
                squares[h, pl.ds(i * 64 + k, 8, stride=8), :] = value
        for h in range(plan.halves):
            low, high = stacked(source, 0, h), stacked(source, 1, h)
            values = line_values(low, line_at(phi, h, 1, i), high, inner_at(inner, h, 1, i))
            for j, value in enumerate(values):
                squares[h, rows8(i * 64 + j * 8), :] += value

    def column(j, source):
        for h in range(plan.halves):
            low, high = stacked(source, 0, h), stacked(source, 1, h)
            line = line_at(phi, h, 0, j)
            values = line_values(low, line, high, inner_at(inner, h, 0, j))
            for i, value in enumerate(values):
                here = rows8(i * 64 + j * 8)
                total = squares[h, here, :] + value
                change = advect_scale * speed[h, here, :] * jnp.sqrt(total)
                moved[h, here, :] = line[i] - change

    even, odd = halos
    stage_planes(0, even)
    ready(0)

    @pl.loop(0, 4)
    def _(q):
        i = 2 * q
        stage_planes(i + 1, odd)
        plane(i, even)
        stage_planes(jnp.minimum(i + 2, 7), even)
        plane(i + 1, odd)

    stage_columns(0, even)
    ready(1)

    @pl.loop(0, 4)
    def _(q):
        j = 2 * q
        stage_columns(j + 1, odd)
        column(j, even)
        stage_columns(jnp.minimum(j + 2, 7), even)
        column(j + 1, odd)


def steepness(value, low, high, facing):
    steep = jnp.maximum((value - low) * facing, (value - high) * facing)
    steep = jnp.maximum(steep, 0.0)
    return steep * steep


def facing_of(start):
    return jnp.where(start > 0.0, 1.0, -1.0)


def relax_inner(plan, phi, origin, inner, i):
    inside = jnp.where(jnp.logical_and(i > 0, i < 7), 1.0, 0.0)
    below, above = jnp.maximum(i - 1, 0), jnp.minimum(i + 1, 7)
    for h in range(plan.halves):
        line = line_at(phi, h, 1, i)
        for j, value in enumerate(line):
            here = rows8(i * 64 + j * 8)
            facing = facing_of(origin[h, here, :])
            low = phi[h, rows8(below * 64 + j * 8), :]
            high = phi[h, rows8(above * 64 + j * 8), :]
            total = inside * steepness(value, low, high, facing)
            if 0 < j < 7:
                total += steepness(value, line[j - 1], line[j + 1], facing)
            inner[h, here, :] = total
        line = line_at(phi, h, 2, i)
        for k in range(1, 7):
            here = pl.ds(i * 64 + k, 8, stride=8)
            facing = facing_of(origin[h, here, :])
            inner[h, here, :] += steepness(line[k], line[k - 1], line[k + 1], facing)


def relax(plan, phi, origin, near, inner, table, halo_code, part, moved, finish):
    @pl.loop(0, 4)
    def _(q):
        for v in range(2):
            i = q * 2 + v
            halo = far_values(plan, table, halo_code, near, (2, 3, 4, 5), i)
            for h in range(plan.halves):
                for j in range(8):
                    here = rows8(i * 64 + j * 8)
                    if 0 < j < 7:
                        part[h, here, :] = jnp.zeros((8, LANES), jnp.float32)
                        continue
                    side, other = (2, 1) if j == 0 else (3, 6)
                    value = phi[h, here, :]
                    beside = phi[h, rows8(i * 64 + other * 8), :]
                    facing = facing_of(origin[h, here, :])
                    part[h, here, :] = steepness(value, halo[side, h], beside, facing)
                for side, k, other in ((4, 0, 1), (5, 7, 6)):
                    here = pl.ds(i * 64 + k, 8, stride=8)
                    value = phi[h, here, :]
                    beside = phi[h, pl.ds(i * 64 + other, 8, stride=8), :]
                    facing = facing_of(origin[h, here, :])
                    part[h, here, :] += steepness(value, halo[side, h], beside, facing)

    @pl.loop(0, 2)
    def _(q):
        for v in range(4):
            j = q * 4 + v
            halo = far_values(plan, table, halo_code, near, (0, 1), j)
            for h in range(plan.halves):
                for side, i, other in ((0, 0, 1), (1, 7, 6)):
                    here = rows8(i * 64 + j * 8)
                    value = phi[h, here, :]
                    beside = phi[h, rows8(other * 64 + j * 8), :]
                    facing = facing_of(origin[h, here, :])
                    part[h, here, :] += steepness(value, halo[side, h], beside, facing)

    @pl.loop(0, 4)
    def _(q):
        for v in range(2):
            i = q * 2 + v
            for h in range(plan.halves):
                for j in range(8):
                    here = rows8(i * 64 + j * 8)
                    start = origin[h, here, :]
                    sense = start * lax.rsqrt(start * start + 1.0)
                    slope = jnp.sqrt(inner[h, here, :] + part[h, here, :])
                    value = phi[h, here, :] - relax_scale * sense * (slope - 1.0)
                    if finish is not None:
                        moved[here, half(h)] = value
                    else:
                        moved[h, here, :] = value
            if finish is not None:
                finish(i)


def first_kernel(
    plan, level_set, peer_slabs, region_slabs, halo_source,
    phi, outgoing, low, high, send_code, halo_code, ends, table, padded, peer, region, entries, ready,
):
    copies = [
        pltpu.make_async_copy(source, target, ready.at[n])
        for n, (source, target) in enumerate(
            ((peer_slabs, peer), (region_slabs, region), (halo_source, entries))
        )
    ]
    for h in range(plan.halves):
        copies.append(
            pltpu.make_async_copy(level_set.at[:, half(h)], phi.at[h], ready.at[3 + h])
        )
    for copy in copies:
        copy.start()
    for copy in copies[:3]:
        copy.wait()
    lanes = lane_ids()
    padded[...] = jnp.zeros_like(padded)
    padded[pl.ds(0, plan.peers), pl.ds(0, plan.slots)] = jnp.maximum(peer[...], 0)
    padded[pl.ds(plan.peers, 2), pl.ds(0, plan.border)] = region[...]

    def wide(row):
        return jnp.broadcast_to(padded[pl.ds(row, 1), :], (8, LANES))

    send_code[...] = jnp.zeros_like(send_code)
    for t in range(plan.far_tiles):
        block = jnp.zeros((8, LANES), jnp.int32)
        if t < plan.peer_tiles:
            for eq in range(min(plan.per_tile, plan.peers - t * plan.per_tile)):
                part = turn(wide(t * plan.per_tile + eq), eq * plan.slots)
                block = jnp.where(in_block(lanes, eq * plan.slots, plan.slots), part, block)
        if t == plan.border_tile:
            for side in range(2):
                start = plan.border_lane + side * plan.border
                part = turn(wide(plan.peers + side), start)
                block = jnp.where(in_block(lanes, start, plan.border), part, block)
        send_code[pl.ds(t, 1), :] = block[0:1]

    entry = entries[...]
    far = entry - plan.local_tiles * LANES
    tile_span = plan.per_tile * plan.slots
    tile = jnp.zeros_like(entry)
    for k in range(1, plan.peer_tiles):
        tile += (far >= k * tile_span).astype(jnp.int32)
    code = (plan.local_tiles + tile) * LANES + far - tile * tile_span
    edge = far - plan.peers * plan.slots
    edge_code = (plan.local_tiles + plan.border_tile) * LANES + plan.border_lane + edge
    code = jnp.where(edge >= 0, edge_code, code)
    halo_code[...] = jnp.where(far >= 0, code, entry)
    for copy in copies[3:]:
        copy.wait()

    fill_ends(plan, phi, ends)
    pack_sends(plan, phi, ends, send_code, table, outgoing, low, high)


def near_thin_kernel(plan, phi, origin, halo_code, near, inner):
    @pl.loop(0, plan.groups // 2)
    def _(q):
        for v in range(2):
            pull_local(plan, phi, None, halo_code, near, q * 2 + v)
            relax_inner(plan, phi, origin, inner, q * 2 + v)


def near_wide_kernel(plan, phi, halo_code, near, *rest):
    inner, ends, kept, done = rest
    copies = [pltpu.make_async_copy(kept.at[a], inner.at[a], done.at[a]) for a in range(3)]
    fill_ends(plan, phi, ends)
    for axis in range(3):

        @pl.loop(0, 8)
        def _(q):
            lines = [line_at(phi, h, axis, q) for h in range(plan.halves)]
            pull_local(plan, phi, ends, halo_code, near, axis * 8 + q)
            for h in range(plan.halves):
                for m, value in enumerate(inner_values(lines[h])):
                    kept[axis, h, rows8(q * 32 + m * 8), :] = value

        copies[axis].start()
    for copy in copies:
        copy.wait()


def advect_kernel(
    plan, sends, phi, near, inner, speed, arrived, before, after, send_code, halo_code,
    moved, outgoing, low, high, ends, table, even, odd, squares, fast, kept, loaded, found,
):
    first = [pltpu.make_async_copy(inner.at[a], kept.at[a], found.at[a]) for a in (2, 1)]
    second = [pltpu.make_async_copy(inner.at[0], kept.at[0], found.at[0])]
    for h in range(plan.halves):
        second.append(pltpu.make_async_copy(speed.at[:, half(h)], fast.at[h], loaded.at[h]))
    for copy in first + second:
        copy.start()

    def ready(stage):
        for copy in (first, second)[stage]:
            copy.wait()

    unpack_far(plan, arrived, before, after, table)
    advect(plan, phi, fast, ready, near, kept, table, halo_code, (even, odd), squares, moved)
    pack_sends(sends, moved, ends, send_code, table, outgoing, low, high)


def relax_kernel(
    plan, sends, phi, origin, near, inner, arrived, before, after, send_code, halo_code, *rest
):
    if sends is None:
        (result, table, part, moved, written) = rest

        def plane_copy(i):
            rows = rows8(i * 64)
            rows = pl.ds(rows.start, 64)
            return pltpu.make_async_copy(moved.at[rows], result.at[rows], written.at[i])

        def finish(i):
            plane_copy(i).start()

    else:
        (moved, outgoing, low, high, ends, table, part) = rest
        finish = None
    unpack_far(plan, arrived, before, after, table)
    relax(plan, phi, origin, near, inner, table, halo_code, part, moved, finish)
    if sends is None:
        for i in range(8):
            plane_copy(i).wait()
    else:
        fill_ends(sends, moved, ends)
        pack_sends(sends, moved, ends, send_code, table, outgoing, low, high)


def f32(shape):
    return jax.ShapeDtypeStruct(shape, jnp.float32)


def call(kernel, out_shape, scratch, flops, *operands, far=(), far_out=()):
    whole = pl.BlockSpec(memory_space=pltpu.VMEM)
    apart = pl.BlockSpec(memory_space=pltpu.HBM)
    size = sum(x.size * 4 for x in operands) + sum(x.size * 4 for x in out_shape)
    operands = [
        pltpu.with_memory_space_constraint(x, pltpu.HBM) if n in far else x
        for n, x in enumerate(operands)
    ]
    return pl.pallas_call(
        kernel,
        out_shape=[
            pltpu.HBM(x.shape, x.dtype) if n in far_out else x for n, x in enumerate(out_shape)
        ],
        in_specs=[apart if n in far else whole for n in range(len(operands))],
        out_specs=[apart if n in far_out else whole for n in range(len(out_shape))],
        scratch_shapes=scratch,
        cost_estimate=pl.CostEstimate(flops=flops, bytes_accessed=size, transcendentals=0),
        compiler_params=pltpu.CompilerParams(vmem_limit_bytes=12 * 1024 * 1024),
    )(*operands)


def exchange(outgoing, low, high):
    count = lax.axis_size("group")
    up = [(i, (i + 1) % count) for i in range(count)]
    down = [(target, source) for source, target in up]
    arrived = lax.all_to_all(outgoing, "dev", split_axis=0, concat_axis=0, tiled=True)
    before = lax.ppermute(high, "group", up)
    after = lax.ppermute(low, "group", down)
    return arrived, before, after


def per_device(level_set, speed, peer_slabs, region_slabs, halo_source):
    rows, count = level_set.shape
    peers, slots = peer_slabs.shape
    border = region_slabs.shape[1]
    wide = Plan(count, peers, slots, border, 3)
    thin = Plan(count, peers, slots, border, 1)
    code_rows = -(-wide.far_tiles // 8) * 8

    def ends(plan):
        return pltpu.VMEM((2, wide.halves, 64 * plan.layers, LANES), jnp.float32)

    def table(plan):
        return pltpu.VMEM((plan.far_tiles, 64 * plan.layers, LANES), jnp.float32)

    def halos(sides, groups):
        return pltpu.VMEM((sides, wide.halves, 8 * groups, LANES), jnp.float32)

    def sent(plan):
        return [f32(plan.message()), f32(plan.border_message()), f32(plan.border_message())]

    field = f32((wide.halves, rows, LANES))
    pad_rows = -(-(peers + 2) // 8) * 8
    phi, *message, send_code, halo_code = call(
        functools.partial(first_kernel, wide),
        [field]
        + sent(wide)
        + [
            jax.ShapeDtypeStruct((code_rows, LANES), jnp.int32),
            jax.ShapeDtypeStruct(halo_source.shape, jnp.int32),
        ],
        [
            ends(wide),
            table(wide),
            pltpu.VMEM((pad_rows, LANES), jnp.int32),
            pltpu.VMEM(peer_slabs.shape, jnp.int32),
            pltpu.VMEM(region_slabs.shape, jnp.int32),
            pltpu.VMEM(halo_source.shape, jnp.int32),
            pltpu.SemaphoreType.DMA((3 + wide.halves,)),
        ],
        1000000,
        level_set, peer_slabs, region_slabs, halo_source,
        far=(0, 1, 2, 3),
    )

    def near_halos(plan, *fields):
        out = [f32((6, plan.halves, 64 * plan.layers, LANES))]
        flops = rows * count * 100 * plan.layers
        if plan.layers == 1:
            kernel = functools.partial(near_thin_kernel, plan)
            return call(kernel, out + [field], [], flops, *fields, halo_code)
        out.append(f32(inner_shape))
        scratch = [ends(plan), pltpu.VMEM(inner_shape, jnp.float32)]
        scratch.append(pltpu.SemaphoreType.DMA((3,)))
        kernel = functools.partial(near_wide_kernel, plan)
        return call(kernel, out, scratch, flops, *fields, halo_code, far_out=(1,))

    inner_shape = (3, wide.halves, rows // 2, LANES)
    block = pltpu.VMEM((wide.halves, rows, LANES), jnp.float32)
    for offset_step in range(OFFSET_STEPS):
        phi, *message = call(
            functools.partial(advect_kernel, wide, thin),
            [field] + sent(thin),
            [ends(wide), table(wide), halos(4, 3), halos(4, 3), block, block]
            + [pltpu.VMEM(inner_shape, jnp.float32)]
            + [pltpu.SemaphoreType.DMA((wide.halves,)), pltpu.SemaphoreType.DMA((3,))],
            rows * count * 300,
            phi, *near_halos(wide, phi), speed, *exchange(*message), send_code, halo_code,
            far=(2, 3),
        )
        origin = phi
        for redist_pass in range(REDIST_PASSES):
            if redist_pass < REDIST_PASSES - 1:
                sends = thin
            elif offset_step < OFFSET_STEPS - 1:
                sends = wide
            else:
                sends = None
            if sends is None:
                out, scratch = [f32((rows, count))], [table(thin)]
                extra = [pltpu.VMEM((rows, count), jnp.float32), pltpu.SemaphoreType.DMA((8,))]
            else:
                out, scratch = [field] + sent(sends), [ends(sends), table(sends)]
                extra = []
            phi, *message = call(
                functools.partial(relax_kernel, thin, sends),
                out,
                scratch + [block] + extra,
                rows * count * 60,
                phi, origin, *near_halos(thin, phi, origin), *exchange(*message), send_code, halo_code,
                far_out=(0,) if sends is None else (),
            )
    return phi


def solution(mesh):
    return jax.shard_map(
        per_device,
        mesh=mesh,
        in_specs=(
            P(None, ("group", "dev")),
            P(None, ("group", "dev")),
            P(("group", "dev"), None),
            P(("group", "dev"), None),
            P(None, ("group", "dev")),
        ),
        out_specs=P(None, ("group", "dev")),
        check_vma=False,
    )
```

```python
import functools

import jax
import jax.numpy as jnp
from jax import lax
from jax.experimental import pallas as pl
from jax.experimental.pallas import tpu as pltpu
from jax.sharding import PartitionSpec as P

OFFSET_STEPS = 2
REDIST_PASSES = 2

advect_scale = 0.3
relax_scale = 0.3
weno_floor = 1e-06

LANES = 128


class Plan:
    def __init__(self, count, peers, slots, border, layers):
        self.count = count
        self.peers = peers
        self.slots = slots
        self.border = border
        self.layers = layers
        self.halves = count // LANES
        self.local_tiles = 6 * self.halves
        self.groups = 8 * layers
        self.per_tile = LANES // slots
        self.peer_tiles = -(-peers // self.per_tile)
        used = (peers - (self.peer_tiles - 1) * self.per_tile) * slots
        if used + 2 * border <= LANES:
            self.border_tile = self.peer_tiles - 1
            self.border_lane = used
        else:
            self.border_tile = self.peer_tiles
            self.border_lane = 0
        self.far_tiles = self.border_tile + 1
        self.pieces = min(LANES // slots, self.groups)
        self.piece_groups = -(-self.groups // self.pieces)
        self.border_pieces = min(LANES // border, self.groups)
        self.border_groups = -(-self.groups // self.border_pieces)

    def message(self):
        return (self.peers, 8 * self.piece_groups, LANES)

    def border_message(self):
        return (8 * self.border_groups, LANES)


def lane_ids():
    return lax.broadcasted_iota(jnp.int32, (8, LANES), 1)


def turn(block, shift):
    shift = shift % LANES
    return block if shift == 0 else pltpu.roll(block, shift, 1)


def in_block(lanes, start, size):
    return jnp.logical_and(lanes >= start, lanes < start + size)


def half(h):
    return pl.ds(h * LANES, LANES)


def rows8(start):
    return pl.ds(pl.multiple_of(start, 8), 8)


def bits_of(tile, tiles):
    return [(tile & (1 << b)) != 0 for b in range(max(tiles - 1, 1).bit_length())]


def pick_tile(values, masks):
    def pick(lowest, bit):
        if bit < 0:
            return values(lowest)
        first = pick(lowest, bit - 1)
        if lowest + (1 << bit) >= values.count:
            return first
        return jnp.where(masks[bit], pick(lowest + (1 << bit), bit - 1), first)

    return pick(0, len(masks) - 1)


class Taken:
    def __init__(self, sources, lane):
        self.sources = sources
        self.lane = lane
        self.count = len(sources)

    def __call__(self, tile):
        return jnp.take_along_axis(
            self.sources[tile], self.lane, axis=1, mode="promise_in_bounds"
        )


def gather(sources, code):
    return pick_tile(Taken(sources, code & (LANES - 1)), bits_of(code >> 7, len(sources)))


def local_sources(plan, phi, ends, g):
    w = plan.layers
    if w == 1:
        along_y = g * 64
    else:
        along_y = (g // w) * 64 + lax.rem(g, w) * 8
    starts = [g * 8, (8 - w) * 64 + g * 8, along_y, along_y + (8 - w) * 8]
    found = []
    for start in starts:
        for h in range(plan.halves):
            found.append(phi[h, rows8(start), :])
    for end in range(2):
        for h in range(plan.halves):
            if w == 1:
                found.append(phi[h, pl.ds(g * 64 + 7 * end, 8, stride=8), :])
            else:
                found.append(ends[end, h, rows8(g * 8), :])
    return found


def fill_ends(plan, phi, ends):
    w = plan.layers
    if w == 1:
        return

    @pl.loop(0, 8)
    def _(i):
        for end in range(2):
            for l in range(w):
                k = l + end * (8 - w)
                for h in range(plan.halves):
                    ends[end, h, pl.ds(i * 8 * w + l, 8, stride=w), :] = phi[
                        h, pl.ds(i * 64 + k, 8, stride=8), :
                    ]


def pack_sends(plan, phi, ends, send_code, table, outgoing, low, high):
    lanes = lane_ids()
    w = plan.layers

    @pl.loop(0, plan.groups // 8)
    def _(q):
        for v in range(8):
            g = q * 8 + v
            sources = local_sources(plan, phi, ends, g)
            for t in range(plan.far_tiles):
                code = jnp.broadcast_to(send_code[pl.ds(t, 1), :], (8, LANES))
                table[t, rows8(g * 8), :] = gather(sources, code)

    for e in range(plan.peers):
        t, eq = divmod(e, plan.per_tile)
        for gi in range(plan.piece_groups):
            block = None
            for p in range(plan.pieces):
                g = p * plan.piece_groups + gi
                if g >= plan.groups:
                    continue
                part = turn(table[t, pl.ds(g * 8, 8), :], (p - eq) * plan.slots)
                if block is None:
                    block = part
                else:
                    block = jnp.where(lanes >= p * plan.slots, part, block)
            outgoing[e, pl.ds(gi * 8, 8), :] = block
    for side, target in enumerate((low, high)):
        for gi in range(plan.border_groups):
            block = None
            for p in range(plan.border_pieces):
                g = p * plan.border_groups + gi
                if g >= plan.groups:
                    continue
                part = turn(
                    table[plan.border_tile, pl.ds(g * 8, 8), :],
                    (p - side) * plan.border - plan.border_lane,
                )
                if block is None:
                    block = part
                else:
                    block = jnp.where(lanes >= p * plan.border, part, block)
            target[pl.ds(gi * 8, 8), :] = block


def unpack_far(plan, arrived, before, after, table):
    lanes = lane_ids()
    for g in range(plan.groups):
        p, gi = divmod(g, plan.piece_groups)
        bp, bgi = divmod(g, plan.border_groups)
        for t in range(plan.far_tiles):
            block = None
            if t < plan.peer_tiles:
                for eq in range(min(plan.per_tile, plan.peers - t * plan.per_tile)):
                    e = t * plan.per_tile + eq
                    part = turn(arrived[e, pl.ds(gi * 8, 8), :], (eq - p) * plan.slots)
                    if block is None:
                        block = part
                    else:
                        block = jnp.where(lanes >= eq * plan.slots, part, block)
            if t == plan.border_tile:
                for q, source in enumerate((before, after)):
                    start = plan.border_lane + q * plan.border
                    part = turn(source[pl.ds(bgi * 8, 8), :], start - bp * plan.border)
                    if block is None:
                        block = part
                    else:
                        block = jnp.where(lanes >= start, part, block)
            table[t, pl.ds(g * 8, 8), :] = block


def pull_local(plan, phi, ends, halo_code, halos, g):
    sources = local_sources(plan, phi, ends, g)
    for s in range(6):
        for h in range(plan.halves):
            code = jnp.broadcast_to(halo_code[pl.ds(s, 1), half(h)], (8, LANES))
            halos[s, h, rows8(g * 8), :] = gather(sources, code)


def far_values(plan, table, halo_code, near, sides, g):
    start = plan.local_tiles * LANES
    sources = [table[t, rows8(g * 8), :] for t in range(plan.far_tiles)]
    found = {}
    for s in sides:
        for h in range(plan.halves):
            code = jnp.broadcast_to(halo_code[pl.ds(s, 1), half(h)], (8, LANES))
            far = gather(sources, code - start)
            found[s, h] = jnp.where(code >= start, far, near[s, h, rows8(g * 8), :])
    return found


def pull_far(plan, table, halo_code, near, halos, sides, g, row):
    for (s, h), value in far_values(plan, table, halo_code, near, sides, g).items():
        halos[s - sides[0], h, rows8(row * 8), :] = value


def weno_windows(q):
    first = [q[m + 1] - q[m] for m in range(7)]
    second = [first[m + 1] - first[m] for m in range(6)]
    third = [second[m + 1] - second[m] for m in range(5)]
    fourth = [(third[m] - third[m + 1]) * (1.0 / 6.0) for m in range(4)]
    bend = [t * t * (4.0 / 3.0) + weno_floor for t in third]
    found = []
    for m in range(3):
        s1, s2 = second[m + 1], second[m + 2]
        a = bend[m] + s1 * (s1 + third[m])
        b = bend[m + 1] + s1 * s2
        c = bend[m + 2] + s2 * (s2 - third[m + 2])
        a, b, c = (pl.reciprocal(value, approx=True) for value in (a, b, c))
        x, z = a * a, c * c
        total = 0.5 * (x + z) + (3.0 * b) * b
        xu = x * fourth[m]
        zu = z * fourth[m + 1]
        slope = 0.25 * (s1 + s2)
        middle = first[m + 2] + third[m + 1] * (1.0 / 12.0)
        fix = (xu + 1.5 * zu) * pl.reciprocal(total + z, approx=True)
        backward = middle + slope + fix
        fix = (zu + 1.5 * xu) * pl.reciprocal(total + x, approx=True)
        found.append((backward, fix + slope - middle))
    return found


def inner_values(values):
    three, four, five = weno_windows(values)
    return [three[1], jnp.maximum(three[0], four[1]), jnp.maximum(four[0], five[1]), five[0]]


def line_values(low, values, high, inner):
    zero, one, two = weno_windows(low + values[:5])
    six, seven, last = weno_windows(values[3:] + high)
    steep = [
        jnp.maximum(zero[0], one[1]),
        jnp.maximum(one[0], two[1]),
        jnp.maximum(two[0], inner[0]),
        inner[1],
        inner[2],
        jnp.maximum(inner[3], six[1]),
        jnp.maximum(six[0], seven[1]),
        jnp.maximum(seven[0], last[1]),
    ]
    steep = [jnp.maximum(value, 0.0) for value in steep]
    return [value * value for value in steep]


def line_at(phi, h, axis, q):
    if axis == 0:
        return [phi[h, rows8(m * 64 + q * 8), :] for m in range(8)]
    if axis == 1:
        return [phi[h, rows8(q * 64 + m * 8), :] for m in range(8)]
    return [phi[h, pl.ds(q * 64 + m, 8, stride=8), :] for m in range(8)]


def inner_at(inner, h, axis, q):
    return [inner[axis, h, rows8(q * 32 + m * 8), :] for m in range(4)]


def advect(plan, phi, speed, ready, near, inner, table, halo_code, halos, squares, moved):
    w = plan.layers

    def stage_planes(i, target):
        for l in range(w):
            pull_far(plan, table, halo_code, near, target, (2, 3, 4, 5), i * w + l, l)

    def stage_columns(j, target):
        for l in range(w):
            pull_far(plan, table, halo_code, near, target, (0, 1), l * 8 + j, l)

    def stacked(source, side, h):
        return [source[side, h, pl.ds(l * 8, 8), :] for l in range(w)]

    def spread(source, side, h):
        return [source[side, h, pl.ds(l, 8, stride=w), :] for l in range(w)]

    def plane(i, source):
        for h in range(plan.halves):
            low, high = spread(source, 2, h), spread(source, 3, h)
            values = line_values(low, line_at(phi, h, 2, i), high, inner_at(inner, h, 2, i))
            for k, value in enumerate(values):
                squares[h, pl.ds(i * 64 + k, 8, stride=8), :] = value
        for h in range(plan.halves):
            low, high = stacked(source, 0, h), stacked(source, 1, h)
            values = line_values(low, line_at(phi, h, 1, i), high, inner_at(inner, h, 1, i))
            for j, value in enumerate(values):
                squares[h, rows8(i * 64 + j * 8), :] += value

    def column(j, source):
        for h in range(plan.halves):
            low, high = stacked(source, 0, h), stacked(source, 1, h)
            line = line_at(phi, h, 0, j)
            values = line_values(low, line, high, inner_at(inner, h, 0, j))
            for i, value in enumerate(values):
                here = rows8(i * 64 + j * 8)
                total = squares[h, here, :] + value
                change = advect_scale * speed[h, here, :] * jnp.sqrt(total)
                moved[h, here, :] = line[i] - change

    even, odd = halos
    stage_planes(0, even)
    ready(0)

    @pl.loop(0, 4)
    def _(q):
        i = 2 * q
        stage_planes(i + 1, odd)
        plane(i, even)
        stage_planes(jnp.minimum(i + 2, 7), even)
        plane(i + 1, odd)

    stage_columns(0, even)
    ready(1)

    @pl.loop(0, 4)
    def _(q):
        j = 2 * q
        stage_columns(j + 1, odd)
        column(j, even)
        stage_columns(jnp.minimum(j + 2, 7), even)
        column(j + 1, odd)


def steepness(value, low, high, facing):
    steep = jnp.maximum((value - low) * facing, (value - high) * facing)
    steep = jnp.maximum(steep, 0.0)
    return steep * steep


def facing_of(start):
    return jnp.where(start > 0.0, 1.0, -1.0)


def relax_inner(plan, phi, origin, inner, i):
    inside = jnp.where(jnp.logical_and(i > 0, i < 7), 1.0, 0.0)
    below, above = jnp.maximum(i - 1, 0), jnp.minimum(i + 1, 7)
    for h in range(plan.halves):
        line = line_at(phi, h, 1, i)
        for j, value in enumerate(line):
            here = rows8(i * 64 + j * 8)
            facing = facing_of(origin[h, here, :])
            low = phi[h, rows8(below * 64 + j * 8), :]
            high = phi[h, rows8(above * 64 + j * 8), :]
            total = inside * steepness(value, low, high, facing)
            if 0 < j < 7:
                total += steepness(value, line[j - 1], line[j + 1], facing)
            inner[h, here, :] = total
        line = line_at(phi, h, 2, i)
        for k in range(1, 7):
            here = pl.ds(i * 64 + k, 8, stride=8)
            facing = facing_of(origin[h, here, :])
            inner[h, here, :] += steepness(line[k], line[k - 1], line[k + 1], facing)


def relax(plan, phi, origin, near, inner, table, halo_code, part, moved, finish):
    @pl.loop(0, 2)
    def _(q):
        for v in range(4):
            i = q * 4 + v
            halo = far_values(plan, table, halo_code, near, (2, 3, 4, 5), i)
            for h in range(plan.halves):
                for j in range(8):
                    here = rows8(i * 64 + j * 8)
                    if 0 < j < 7:
                        part[h, here, :] = jnp.zeros((8, LANES), jnp.float32)
                        continue
                    side, other = (2, 1) if j == 0 else (3, 6)
                    value = phi[h, here, :]
                    beside = phi[h, rows8(i * 64 + other * 8), :]
                    facing = facing_of(origin[h, here, :])
                    part[h, here, :] = steepness(value, halo[side, h], beside, facing)
                for side, k, other in ((4, 0, 1), (5, 7, 6)):
                    here = pl.ds(i * 64 + k, 8, stride=8)
                    value = phi[h, here, :]
                    beside = phi[h, pl.ds(i * 64 + other, 8, stride=8), :]
                    facing = facing_of(origin[h, here, :])
                    part[h, here, :] += steepness(value, halo[side, h], beside, facing)

    for j in range(8):
        halo = far_values(plan, table, halo_code, near, (0, 1), j)
        for h in range(plan.halves):
            for side, i, other in ((0, 0, 1), (1, 7, 6)):
                here = rows8(i * 64 + j * 8)
                value = phi[h, here, :]
                beside = phi[h, rows8(other * 64 + j * 8), :]
                facing = facing_of(origin[h, here, :])
                part[h, here, :] += steepness(value, halo[side, h], beside, facing)

    @pl.loop(0, 2)
    def _(q):
        for v in range(4):
            i = q * 4 + v
            for h in range(plan.halves):
                for j in range(8):
                    here = rows8(i * 64 + j * 8)
                    start = origin[h, here, :]
                    sense = start * lax.rsqrt(start * start + 1.0)
                    slope = jnp.sqrt(inner[h, here, :] + part[h, here, :])
                    value = phi[h, here, :] - relax_scale * sense * (slope - 1.0)
                    if finish is not None:
                        moved[here, half(h)] = value
                    else:
                        moved[h, here, :] = value
            if finish is not None:
                finish(i)


def first_kernel(
    plan, level_set, peer_slabs, region_slabs, halo_source,
    phi, outgoing, low, high, send_code, halo_code, ends, table, padded, peer, region, entries, ready,
):
    copies = [
        pltpu.make_async_copy(source, target, ready.at[n])
        for n, (source, target) in enumerate(
            ((peer_slabs, peer), (region_slabs, region), (halo_source, entries))
        )
    ]
    for h in range(plan.halves):
        copies.append(
            pltpu.make_async_copy(level_set.at[:, half(h)], phi.at[h], ready.at[3 + h])
        )
    for copy in copies:
        copy.start()
    for copy in copies[:3]:
        copy.wait()
    lanes = lane_ids()
    padded[...] = jnp.zeros_like(padded)
    padded[pl.ds(0, plan.peers), pl.ds(0, plan.slots)] = jnp.maximum(peer[...], 0)
    padded[pl.ds(plan.peers, 2), pl.ds(0, plan.border)] = region[...]

    def wide(row):
        return jnp.broadcast_to(padded[pl.ds(row, 1), :], (8, LANES))

    send_code[...] = jnp.zeros_like(send_code)
    for t in range(plan.far_tiles):
        block = jnp.zeros((8, LANES), jnp.int32)
        if t < plan.peer_tiles:
            for eq in range(min(plan.per_tile, plan.peers - t * plan.per_tile)):
                part = turn(wide(t * plan.per_tile + eq), eq * plan.slots)
                block = jnp.where(in_block(lanes, eq * plan.slots, plan.slots), part, block)
        if t == plan.border_tile:
            for side in range(2):
                start = plan.border_lane + side * plan.border
                part = turn(wide(plan.peers + side), start)
                block = jnp.where(in_block(lanes, start, plan.border), part, block)
        send_code[pl.ds(t, 1), :] = block[0:1]

    entry = entries[...]
    far = entry - plan.local_tiles * LANES
    tile_span = plan.per_tile * plan.slots
    tile = jnp.zeros_like(entry)
    for k in range(1, plan.peer_tiles):
        tile += (far >= k * tile_span).astype(jnp.int32)
    code = (plan.local_tiles + tile) * LANES + far - tile * tile_span
    edge = far - plan.peers * plan.slots
    edge_code = (plan.local_tiles + plan.border_tile) * LANES + plan.border_lane + edge
    code = jnp.where(edge >= 0, edge_code, code)
    halo_code[...] = jnp.where(far >= 0, code, entry)
    for copy in copies[3:]:
        copy.wait()

    fill_ends(plan, phi, ends)
    pack_sends(plan, phi, ends, send_code, table, outgoing, low, high)


def near_thin_kernel(plan, phi, origin, halo_code, near, inner):
    @pl.loop(0, plan.groups // 4)
    def _(q):
        for v in range(4):
            pull_local(plan, phi, None, halo_code, near, q * 4 + v)
            relax_inner(plan, phi, origin, inner, q * 4 + v)


def near_wide_kernel(plan, phi, halo_code, near, *rest):
    inner, ends, kept, done = rest
    copies = [pltpu.make_async_copy(kept.at[a], inner.at[a], done.at[a]) for a in range(3)]
    fill_ends(plan, phi, ends)
    for axis in range(3):

        @pl.loop(0, 4)
        def _(pair):
            for v in range(2):
                q = pair * 2 + v
                pull_local(plan, phi, ends, halo_code, near, axis * 8 + q)
                for h in range(plan.halves):
                    for m, value in enumerate(inner_values(line_at(phi, h, axis, q))):
                        kept[axis, h, rows8(q * 32 + m * 8), :] = value

        copies[axis].start()
    for copy in copies:
        copy.wait()


def advect_kernel(
    plan, sends, phi, near, inner, speed, arrived, before, after, send_code, halo_code,
    moved, outgoing, low, high, ends, table, even, odd, squares, fast, kept, loaded, found,
):
    first = [pltpu.make_async_copy(inner.at[a], kept.at[a], found.at[a]) for a in (2, 1)]
    second = [pltpu.make_async_copy(inner.at[0], kept.at[0], found.at[0])]
    for h in range(plan.halves):
        second.append(pltpu.make_async_copy(speed.at[:, half(h)], fast.at[h], loaded.at[h]))
    for copy in first + second:
        copy.start()

    def ready(stage):
        for copy in (first, second)[stage]:
            copy.wait()

    unpack_far(plan, arrived, before, after, table)
    advect(plan, phi, fast, ready, near, kept, table, halo_code, (even, odd), squares, moved)
    pack_sends(sends, moved, ends, send_code, table, outgoing, low, high)


def relax_kernel(
    plan, sends, phi, origin, near, inner, arrived, before, after, send_code, halo_code, *rest
):
    if sends is None:
        (result, table, part, moved, written) = rest

        def plane_copy(i):
            rows = rows8(i * 64)
            rows = pl.ds(rows.start, 64)
            return pltpu.make_async_copy(moved.at[rows], result.at[rows], written.at[i])

        def finish(i):
            plane_copy(i).start()

    else:
        (moved, outgoing, low, high, ends, table, part) = rest
        finish = None
    unpack_far(plan, arrived, before, after, table)
    relax(plan, phi, origin, near, inner, table, halo_code, part, moved, finish)
    if sends is None:
        for i in range(8):
            plane_copy(i).wait()
    else:
        fill_ends(sends, moved, ends)
        pack_sends(sends, moved, ends, send_code, table, outgoing, low, high)


def f32(shape):
    return jax.ShapeDtypeStruct(shape, jnp.float32)


def call(kernel, out_shape, scratch, flops, *operands, far=(), far_out=()):
    whole = pl.BlockSpec(memory_space=pltpu.VMEM)
    apart = pl.BlockSpec(memory_space=pltpu.HBM)
    size = sum(x.size * 4 for x in operands) + sum(x.size * 4 for x in out_shape)
    operands = [
        pltpu.with_memory_space_constraint(x, pltpu.HBM) if n in far else x
        for n, x in enumerate(operands)
    ]
    return pl.pallas_call(
        kernel,
        out_shape=[
            pltpu.HBM(x.shape, x.dtype) if n in far_out else x for n, x in enumerate(out_shape)
        ],
        in_specs=[apart if n in far else whole for n in range(len(operands))],
        out_specs=[apart if n in far_out else whole for n in range(len(out_shape))],
        scratch_shapes=scratch,
        cost_estimate=pl.CostEstimate(flops=flops, bytes_accessed=size, transcendentals=0),
        compiler_params=pltpu.CompilerParams(vmem_limit_bytes=12 * 1024 * 1024),
    )(*operands)


def exchange(outgoing, low, high):
    count = lax.axis_size("group")
    up = [(i, (i + 1) % count) for i in range(count)]
    down = [(target, source) for source, target in up]
    arrived = lax.all_to_all(outgoing, "dev", split_axis=0, concat_axis=0, tiled=True)
    before = lax.ppermute(high, "group", up)
    after = lax.ppermute(low, "group", down)
    return arrived, before, after


def per_device(level_set, speed, peer_slabs, region_slabs, halo_source):
    rows, count = level_set.shape
    peers, slots = peer_slabs.shape
    border = region_slabs.shape[1]
    wide = Plan(count, peers, slots, border, 3)
    thin = Plan(count, peers, slots, border, 1)
    code_rows = -(-wide.far_tiles // 8) * 8

    def ends(plan):
        return pltpu.VMEM((2, wide.halves, 64 * plan.layers, LANES), jnp.float32)

    def table(plan):
        return pltpu.VMEM((plan.far_tiles, 64 * plan.layers, LANES), jnp.float32)

    def halos(sides, groups):
        return pltpu.VMEM((sides, wide.halves, 8 * groups, LANES), jnp.float32)

    def sent(plan):
        return [f32(plan.message()), f32(plan.border_message()), f32(plan.border_message())]

    field = f32((wide.halves, rows, LANES))
    pad_rows = -(-(peers + 2) // 8) * 8
    phi, *message, send_code, halo_code = call(
        functools.partial(first_kernel, wide),
        [field]
        + sent(wide)
        + [
            jax.ShapeDtypeStruct((code_rows, LANES), jnp.int32),
            jax.ShapeDtypeStruct(halo_source.shape, jnp.int32),
        ],
        [
            ends(wide),
            table(wide),
            pltpu.VMEM((pad_rows, LANES), jnp.int32),
            pltpu.VMEM(peer_slabs.shape, jnp.int32),
            pltpu.VMEM(region_slabs.shape, jnp.int32),
            pltpu.VMEM(halo_source.shape, jnp.int32),
            pltpu.SemaphoreType.DMA((3 + wide.halves,)),
        ],
        1000000,
        level_set, peer_slabs, region_slabs, halo_source,
        far=(0, 1, 2, 3),
    )

    def near_halos(plan, *fields):
        out = [f32((6, plan.halves, 64 * plan.layers, LANES))]
        flops = rows * count * 100 * plan.layers
        if plan.layers == 1:
            kernel = functools.partial(near_thin_kernel, plan)
            return call(kernel, out + [field], [], flops, *fields, halo_code)
        out.append(f32(inner_shape))
        scratch = [ends(plan), pltpu.VMEM(inner_shape, jnp.float32)]
        scratch.append(pltpu.SemaphoreType.DMA((3,)))
        kernel = functools.partial(near_wide_kernel, plan)
        return call(kernel, out, scratch, flops, *fields, halo_code, far_out=(1,))

    inner_shape = (3, wide.halves, rows // 2, LANES)
    block = pltpu.VMEM((wide.halves, rows, LANES), jnp.float32)
    for offset_step in range(OFFSET_STEPS):
        phi, *message = call(
            functools.partial(advect_kernel, wide, thin),
            [field] + sent(thin),
            [ends(wide), table(wide), halos(4, 3), halos(4, 3), block, block]
            + [pltpu.VMEM(inner_shape, jnp.float32)]
            + [pltpu.SemaphoreType.DMA((wide.halves,)), pltpu.SemaphoreType.DMA((3,))],
            rows * count * 300,
            phi, *near_halos(wide, phi), speed, *exchange(*message), send_code, halo_code,
            far=(2, 3),
        )
        origin = phi
        for redist_pass in range(REDIST_PASSES):
            if redist_pass < REDIST_PASSES - 1:
                sends = thin
            elif offset_step < OFFSET_STEPS - 1:
                sends = wide
            else:
                sends = None
            if sends is None:
                out, scratch = [f32((rows, count))], [table(thin)]
                extra = [pltpu.VMEM((rows, count), jnp.float32), pltpu.SemaphoreType.DMA((8,))]
            else:
                out, scratch = [field] + sent(sends), [ends(sends), table(sends)]
                extra = []
            phi, *message = call(
                functools.partial(relax_kernel, thin, sends),
                out,
                scratch + [block] + extra,
                rows * count * 60,
                phi, origin, *near_halos(thin, phi, origin), *exchange(*message), send_code, halo_code,
                far_out=(0,) if sends is None else (),
            )
    return phi


def solution(mesh):
    return jax.shard_map(
        per_device,
        mesh=mesh,
        in_specs=(
            P(None, ("group", "dev")),
            P(None, ("group", "dev")),
            P(("group", "dev"), None),
            P(("group", "dev"), None),
            P(None, ("group", "dev")),
        ),
        out_specs=P(None, ("group", "dev")),
        check_vma=False,
    )
```

```python
import functools

import jax
import jax.numpy as jnp
from jax import lax
from jax.experimental import pallas as pl
from jax.experimental.pallas import tpu as pltpu
from jax.sharding import PartitionSpec as P

OFFSET_STEPS = 2
REDIST_PASSES = 2

advect_scale = 0.3
relax_scale = 0.3
weno_floor = 1e-06

LANES = 128


class Plan:
    def __init__(self, count, peers, slots, border, layers):
        self.count = count
        self.peers = peers
        self.slots = slots
        self.border = border
        self.layers = layers
        self.halves = count // LANES
        self.local_tiles = 6 * self.halves
        self.groups = 8 * layers
        self.per_tile = LANES // slots
        self.peer_tiles = -(-peers // self.per_tile)
        used = (peers - (self.peer_tiles - 1) * self.per_tile) * slots
        if used + 2 * border <= LANES:
            self.border_tile = self.peer_tiles - 1
            self.border_lane = used
        else:
            self.border_tile = self.peer_tiles
            self.border_lane = 0
        self.far_tiles = self.border_tile + 1
        self.pieces = min(LANES // slots, self.groups)
        self.piece_groups = -(-self.groups // self.pieces)
        self.border_pieces = min(LANES // border, self.groups)
        self.border_groups = -(-self.groups // self.border_pieces)

    def message(self):
        return (self.peers, 8 * self.piece_groups, LANES)

    def border_message(self):
        return (8 * self.border_groups, LANES)


def lane_ids():
    return lax.broadcasted_iota(jnp.int32, (8, LANES), 1)


def turn(block, shift):
    shift = shift % LANES
    return block if shift == 0 else pltpu.roll(block, shift, 1)


def in_block(lanes, start, size):
    return jnp.logical_and(lanes >= start, lanes < start + size)


def half(h):
    return pl.ds(h * LANES, LANES)


def rows8(start):
    return pl.ds(pl.multiple_of(start, 8), 8)


def bits_of(tile, tiles):
    return [(tile & (1 << b)) != 0 for b in range(max(tiles - 1, 1).bit_length())]


def pick_tile(values, masks):
    def pick(lowest, bit):
        if bit < 0:
            return values(lowest)
        first = pick(lowest, bit - 1)
        if lowest + (1 << bit) >= values.count:
            return first
        return jnp.where(masks[bit], pick(lowest + (1 << bit), bit - 1), first)

    return pick(0, len(masks) - 1)


class Taken:
    def __init__(self, sources, lane):
        self.sources = sources
        self.lane = lane
        self.count = len(sources)

    def __call__(self, tile):
        return jnp.take_along_axis(
            self.sources[tile], self.lane, axis=1, mode="promise_in_bounds"
        )


def gather(sources, code):
    return pick_tile(Taken(sources, code & (LANES - 1)), bits_of(code >> 7, len(sources)))


def local_sources(plan, phi, ends, g):
    w = plan.layers
    if w == 1:
        along_y = g * 64
    else:
        along_y = (g // w) * 64 + lax.rem(g, w) * 8
    starts = [g * 8, (8 - w) * 64 + g * 8, along_y, along_y + (8 - w) * 8]
    found = []
    for start in starts:
        for h in range(plan.halves):
            found.append(phi[h, rows8(start), :])
    for end in range(2):
        for h in range(plan.halves):
            if w == 1:
                found.append(phi[h, pl.ds(g * 64 + 7 * end, 8, stride=8), :])
            else:
                found.append(ends[end, h, rows8(g * 8), :])
    return found


def fill_ends(plan, phi, ends):
    w = plan.layers
    if w == 1:
        return

    @pl.loop(0, 8)
    def _(i):
        for end in range(2):
            for l in range(w):
                k = l + end * (8 - w)
                for h in range(plan.halves):
                    ends[end, h, pl.ds(i * 8 * w + l, 8, stride=w), :] = phi[
                        h, pl.ds(i * 64 + k, 8, stride=8), :
                    ]


def pack_sends(plan, phi, ends, send_code, table, outgoing, low, high):
    lanes = lane_ids()
    w = plan.layers

    together = 8 if plan.layers == 1 else 12

    @pl.loop(0, plan.groups // together)
    def _(q):
        for v in range(together):
            g = q * together + v
            sources = local_sources(plan, phi, ends, g)
            for t in range(plan.far_tiles):
                code = jnp.broadcast_to(send_code[pl.ds(t, 1), :], (8, LANES))
                table[t, rows8(g * 8), :] = gather(sources, code)

    for e in range(plan.peers):
        t, eq = divmod(e, plan.per_tile)
        for gi in range(plan.piece_groups):
            block = None
            for p in range(plan.pieces):
                g = p * plan.piece_groups + gi
                if g >= plan.groups:
                    continue
                part = turn(table[t, pl.ds(g * 8, 8), :], (p - eq) * plan.slots)
                if block is None:
                    block = part
                else:
                    block = jnp.where(lanes >= p * plan.slots, part, block)
            outgoing[e, pl.ds(gi * 8, 8), :] = block
    for side, target in enumerate((low, high)):
        for gi in range(plan.border_groups):
            block = None
            for p in range(plan.border_pieces):
                g = p * plan.border_groups + gi
                if g >= plan.groups:
                    continue
                part = turn(
                    table[plan.border_tile, pl.ds(g * 8, 8), :],
                    (p - side) * plan.border - plan.border_lane,
                )
                if block is None:
                    block = part
                else:
                    block = jnp.where(lanes >= p * plan.border, part, block)
            target[pl.ds(gi * 8, 8), :] = block


def unpack_far(plan, arrived, before, after, table):
    lanes = lane_ids()
    for g in range(plan.groups):
        p, gi = divmod(g, plan.piece_groups)
        bp, bgi = divmod(g, plan.border_groups)
        for t in range(plan.far_tiles):
            block = None
            if t < plan.peer_tiles:
                for eq in range(min(plan.per_tile, plan.peers - t * plan.per_tile)):
                    e = t * plan.per_tile + eq
                    part = turn(arrived[e, pl.ds(gi * 8, 8), :], (eq - p) * plan.slots)
                    if block is None:
                        block = part
                    else:
                        block = jnp.where(lanes >= eq * plan.slots, part, block)
            if t == plan.border_tile:
                for q, source in enumerate((before, after)):
                    start = plan.border_lane + q * plan.border
                    part = turn(source[pl.ds(bgi * 8, 8), :], start - bp * plan.border)
                    if block is None:
                        block = part
                    else:
                        block = jnp.where(lanes >= start, part, block)
            table[t, pl.ds(g * 8, 8), :] = block


def pull_local(plan, phi, ends, halo_code, halos, g):
    sources = local_sources(plan, phi, ends, g)
    for s in range(6):
        for h in range(plan.halves):
            code = jnp.broadcast_to(halo_code[pl.ds(s, 1), half(h)], (8, LANES))
            halos[s, h, rows8(g * 8), :] = gather(sources, code)


def far_values(plan, table, halo_code, near, sides, g):
    start = plan.local_tiles * LANES
    sources = [table[t, rows8(g * 8), :] for t in range(plan.far_tiles)]
    found = {}
    for s in sides:
        for h in range(plan.halves):
            code = jnp.broadcast_to(halo_code[pl.ds(s, 1), half(h)], (8, LANES))
            far = gather(sources, code - start)
            found[s, h] = jnp.where(code >= start, far, near[s, h, rows8(g * 8), :])
    return found


def pull_far(plan, table, halo_code, near, halos, sides, g, row):
    for (s, h), value in far_values(plan, table, halo_code, near, sides, g).items():
        halos[s - sides[0], h, rows8(row * 8), :] = value


def weno_windows(q):
    first = [q[m + 1] - q[m] for m in range(7)]
    second = [first[m + 1] - first[m] for m in range(6)]
    third = [second[m + 1] - second[m] for m in range(5)]
    fourth = [(third[m] - third[m + 1]) * (1.0 / 6.0) for m in range(4)]
    bend = [t * t * (4.0 / 3.0) + weno_floor for t in third]
    found = []
    for m in range(3):
        s1, s2 = second[m + 1], second[m + 2]
        a = bend[m] + s1 * (s1 + third[m])
        b = bend[m + 1] + s1 * s2
        c = bend[m + 2] + s2 * (s2 - third[m + 2])
        a, b, c = (pl.reciprocal(value, approx=True) for value in (a, b, c))
        x, z = a * a, c * c
        total = 0.5 * (x + z) + (3.0 * b) * b
        xu = x * fourth[m]
        zu = z * fourth[m + 1]
        slope = 0.25 * (s1 + s2)
        middle = first[m + 2] + third[m + 1] * (1.0 / 12.0)
        fix = (xu + 1.5 * zu) * pl.reciprocal(total + z, approx=True)
        backward = middle + slope + fix
        fix = (zu + 1.5 * xu) * pl.reciprocal(total + x, approx=True)
        found.append((backward, fix + slope - middle))
    return found


def inner_values(values):
    three, four, five = weno_windows(values)
    return [three[1], jnp.maximum(three[0], four[1]), jnp.maximum(four[0], five[1]), five[0]]


def line_values(low, values, high, inner):
    zero, one, two = weno_windows(low + values[:5])
    six, seven, last = weno_windows(values[3:] + high)
    steep = [
        jnp.maximum(zero[0], one[1]),
        jnp.maximum(one[0], two[1]),
        jnp.maximum(two[0], inner[0]),
        inner[1],
        inner[2],
        jnp.maximum(inner[3], six[1]),
        jnp.maximum(six[0], seven[1]),
        jnp.maximum(seven[0], last[1]),
    ]
    steep = [jnp.maximum(value, 0.0) for value in steep]
    return [value * value for value in steep]


def line_at(phi, h, axis, q):
    if axis == 0:
        return [phi[h, rows8(m * 64 + q * 8), :] for m in range(8)]
    if axis == 1:
        return [phi[h, rows8(q * 64 + m * 8), :] for m in range(8)]
    return [phi[h, pl.ds(q * 64 + m, 8, stride=8), :] for m in range(8)]


def inner_at(inner, h, axis, q):
    return [inner[axis, h, rows8(q * 32 + m * 8), :] for m in range(4)]


def advect(plan, phi, speed, ready, near, inner, table, halo_code, halos, squares, moved):
    w = plan.layers

    def stage_planes(i, target):
        for l in range(w):
            pull_far(plan, table, halo_code, near, target, (2, 3, 4, 5), i * w + l, l)

    def stage_columns(j, target):
        for l in range(w):
            pull_far(plan, table, halo_code, near, target, (0, 1), l * 8 + j, l)

    def stacked(source, side, h):
        return [source[side, h, pl.ds(l * 8, 8), :] for l in range(w)]

    def spread(source, side, h):
        return [source[side, h, pl.ds(l, 8, stride=w), :] for l in range(w)]

    def plane(i, source):
        for h in range(plan.halves):
            low, high = spread(source, 2, h), spread(source, 3, h)
            values = line_values(low, line_at(phi, h, 2, i), high, inner_at(inner, h, 2, i))
            for k, value in enumerate(values):
                squares[h, pl.ds(i * 64 + k, 8, stride=8), :] = value
        for h in range(plan.halves):
            low, high = stacked(source, 0, h), stacked(source, 1, h)
            values = line_values(low, line_at(phi, h, 1, i), high, inner_at(inner, h, 1, i))
            for j, value in enumerate(values):
                squares[h, rows8(i * 64 + j * 8), :] += value

    def column(j, source):
        for h in range(plan.halves):
            low, high = stacked(source, 0, h), stacked(source, 1, h)
            line = line_at(phi, h, 0, j)
            values = line_values(low, line, high, inner_at(inner, h, 0, j))
            for i, value in enumerate(values):
                here = rows8(i * 64 + j * 8)
                total = squares[h, here, :] + value
                change = advect_scale * speed[h, here, :] * jnp.sqrt(total)
                moved[h, here, :] = line[i] - change

    even, odd = halos
    stage_planes(0, even)
    ready(0)

    @pl.loop(0, 4)
    def _(q):
        i = 2 * q
        stage_planes(i + 1, odd)
        plane(i, even)
        stage_planes(jnp.minimum(i + 2, 7), even)
        plane(i + 1, odd)

    stage_columns(0, even)
    ready(1)

    @pl.loop(0, 2)
    def _(q):
        j = 4 * q
        for v in (0, 2):
            stage_columns(j + v + 1, odd)
            column(j + v, even)
            stage_columns(jnp.minimum(j + v + 2, 7), even)
            column(j + v + 1, odd)


def steepness(value, low, high, facing):
    steep = jnp.maximum((value - low) * facing, (value - high) * facing)
    steep = jnp.maximum(steep, 0.0)
    return steep * steep


def facing_of(start):
    return jnp.where(start > 0.0, 1.0, -1.0)


def relax_inner(plan, phi, origin, inner, i):
    inside = jnp.where(jnp.logical_and(i > 0, i < 7), 1.0, 0.0)
    below, above = jnp.maximum(i - 1, 0), jnp.minimum(i + 1, 7)
    for h in range(plan.halves):
        line = line_at(phi, h, 1, i)
        for j, value in enumerate(line):
            here = rows8(i * 64 + j * 8)
            facing = facing_of(origin[h, here, :])
            low = phi[h, rows8(below * 64 + j * 8), :]
            high = phi[h, rows8(above * 64 + j * 8), :]
            total = inside * steepness(value, low, high, facing)
            if 0 < j < 7:
                total += steepness(value, line[j - 1], line[j + 1], facing)
            inner[h, here, :] = total
        line = line_at(phi, h, 2, i)
        for k in range(1, 7):
            here = pl.ds(i * 64 + k, 8, stride=8)
            facing = facing_of(origin[h, here, :])
            inner[h, here, :] += steepness(line[k], line[k - 1], line[k + 1], facing)


def relax(plan, phi, origin, near, inner, table, halo_code, part, moved, finish):
    @pl.loop(0, 1)
    def _(q):
        for v in range(8):
            i = q * 8 + v
            halo = far_values(plan, table, halo_code, near, (2, 3, 4, 5), i)
            for h in range(plan.halves):
                for j in range(8):
                    here = rows8(i * 64 + j * 8)
                    if 0 < j < 7:
                        part[h, here, :] = jnp.zeros((8, LANES), jnp.float32)
                        continue
                    side, other = (2, 1) if j == 0 else (3, 6)
                    value = phi[h, here, :]
                    beside = phi[h, rows8(i * 64 + other * 8), :]
                    facing = facing_of(origin[h, here, :])
                    part[h, here, :] = steepness(value, halo[side, h], beside, facing)
                for side, k, other in ((4, 0, 1), (5, 7, 6)):
                    here = pl.ds(i * 64 + k, 8, stride=8)
                    value = phi[h, here, :]
                    beside = phi[h, pl.ds(i * 64 + other, 8, stride=8), :]
                    facing = facing_of(origin[h, here, :])
                    part[h, here, :] += steepness(value, halo[side, h], beside, facing)

    for j in range(8):
        halo = far_values(plan, table, halo_code, near, (0, 1), j)
        for h in range(plan.halves):
            for side, i, other in ((0, 0, 1), (1, 7, 6)):
                here = rows8(i * 64 + j * 8)
                value = phi[h, here, :]
                beside = phi[h, rows8(other * 64 + j * 8), :]
                facing = facing_of(origin[h, here, :])
                part[h, here, :] += steepness(value, halo[side, h], beside, facing)

    @pl.loop(0, 1)
    def _(q):
        for v in range(8):
            i = q * 8 + v
            for h in range(plan.halves):
                for j in range(8):
                    here = rows8(i * 64 + j * 8)
                    start = origin[h, here, :]
                    sense = start * lax.rsqrt(start * start + 1.0)
                    slope = jnp.sqrt(inner[h, here, :] + part[h, here, :])
                    value = phi[h, here, :] - relax_scale * sense * (slope - 1.0)
                    if finish is not None:
                        moved[here, half(h)] = value
                    else:
                        moved[h, here, :] = value
            if finish is not None:
                finish(i)


def first_kernel(
    plan, level_set, peer_slabs, region_slabs, halo_source,
    phi, outgoing, low, high, send_code, halo_code, ends, table, padded, peer, region, entries, ready,
):
    copies = [
        pltpu.make_async_copy(source, target, ready.at[n])
        for n, (source, target) in enumerate(
            ((peer_slabs, peer), (region_slabs, region), (halo_source, entries))
        )
    ]
    for h in range(plan.halves):
        copies.append(
            pltpu.make_async_copy(level_set.at[:, half(h)], phi.at[h], ready.at[3 + h])
        )
    for copy in copies:
        copy.start()
    for copy in copies[:3]:
        copy.wait()
    lanes = lane_ids()
    padded[...] = jnp.zeros_like(padded)
    padded[pl.ds(0, plan.peers), pl.ds(0, plan.slots)] = jnp.maximum(peer[...], 0)
    padded[pl.ds(plan.peers, 2), pl.ds(0, plan.border)] = region[...]

    def wide(row):
        return jnp.broadcast_to(padded[pl.ds(row, 1), :], (8, LANES))

    send_code[...] = jnp.zeros_like(send_code)
    for t in range(plan.far_tiles):
        block = jnp.zeros((8, LANES), jnp.int32)
        if t < plan.peer_tiles:
            for eq in range(min(plan.per_tile, plan.peers - t * plan.per_tile)):
                part = turn(wide(t * plan.per_tile + eq), eq * plan.slots)
                block = jnp.where(in_block(lanes, eq * plan.slots, plan.slots), part, block)
        if t == plan.border_tile:
            for side in range(2):
                start = plan.border_lane + side * plan.border
                part = turn(wide(plan.peers + side), start)
                block = jnp.where(in_block(lanes, start, plan.border), part, block)
        send_code[pl.ds(t, 1), :] = block[0:1]

    entry = entries[...]
    far = entry - plan.local_tiles * LANES
    tile_span = plan.per_tile * plan.slots
    tile = jnp.zeros_like(entry)
    for k in range(1, plan.peer_tiles):
        tile += (far >= k * tile_span).astype(jnp.int32)
    code = (plan.local_tiles + tile) * LANES + far - tile * tile_span
    edge = far - plan.peers * plan.slots
    edge_code = (plan.local_tiles + plan.border_tile) * LANES + plan.border_lane + edge
    code = jnp.where(edge >= 0, edge_code, code)
    halo_code[...] = jnp.where(far >= 0, code, entry)
    for copy in copies[3:]:
        copy.wait()

    fill_ends(plan, phi, ends)
    pack_sends(plan, phi, ends, send_code, table, outgoing, low, high)


def near_thin_kernel(plan, phi, origin, halo_code, near, inner):
    for g in range(plan.groups):
        pull_local(plan, phi, None, halo_code, near, g)
        relax_inner(plan, phi, origin, inner, g)


def near_wide_kernel(plan, phi, halo_code, near, *rest):
    inner, ends, kept, done = rest
    copies = [pltpu.make_async_copy(kept.at[a], inner.at[a], done.at[a]) for a in range(3)]
    fill_ends(plan, phi, ends)
    for axis in range(3):

        @pl.loop(0, 2)
        def _(four):
            for v in range(4):
                q = four * 4 + v
                pull_local(plan, phi, ends, halo_code, near, axis * 8 + q)
                for h in range(plan.halves):
                    for m, value in enumerate(inner_values(line_at(phi, h, axis, q))):
                        kept[axis, h, rows8(q * 32 + m * 8), :] = value

        copies[axis].start()
    for copy in copies:
        copy.wait()


def advect_kernel(
    plan, sends, phi, near, inner, speed, arrived, before, after, send_code, halo_code,
    moved, outgoing, low, high, ends, table, even, odd, squares, fast, kept, loaded, found,
):
    first = [pltpu.make_async_copy(inner.at[a], kept.at[a], found.at[a]) for a in (2, 1)]
    second = [pltpu.make_async_copy(inner.at[0], kept.at[0], found.at[0])]
    for h in range(plan.halves):
        second.append(pltpu.make_async_copy(speed.at[:, half(h)], fast.at[h], loaded.at[h]))
    for copy in first + second:
        copy.start()

    def ready(stage):
        for copy in (first, second)[stage]:
            copy.wait()

    unpack_far(plan, arrived, before, after, table)
    advect(plan, phi, fast, ready, near, kept, table, halo_code, (even, odd), squares, moved)
    pack_sends(sends, moved, ends, send_code, table, outgoing, low, high)


def relax_kernel(
    plan, sends, phi, origin, near, inner, arrived, before, after, send_code, halo_code, *rest
):
    if sends is None:
        (result, table, part, moved, written) = rest

        def plane_copy(i):
            rows = rows8(i * 64)
            rows = pl.ds(rows.start, 64)
            return pltpu.make_async_copy(moved.at[rows], result.at[rows], written.at[i])

        def finish(i):
            plane_copy(i).start()

    else:
        (moved, outgoing, low, high, ends, table, part) = rest
        finish = None
    unpack_far(plan, arrived, before, after, table)
    relax(plan, phi, origin, near, inner, table, halo_code, part, moved, finish)
    if sends is None:
        for i in range(8):
            plane_copy(i).wait()
    else:
        fill_ends(sends, moved, ends)
        pack_sends(sends, moved, ends, send_code, table, outgoing, low, high)


def f32(shape):
    return jax.ShapeDtypeStruct(shape, jnp.float32)


def call(kernel, out_shape, scratch, flops, *operands, far=(), far_out=()):
    whole = pl.BlockSpec(memory_space=pltpu.VMEM)
    apart = pl.BlockSpec(memory_space=pltpu.HBM)
    size = sum(x.size * 4 for x in operands) + sum(x.size * 4 for x in out_shape)
    operands = [
        pltpu.with_memory_space_constraint(x, pltpu.HBM) if n in far else x
        for n, x in enumerate(operands)
    ]
    return pl.pallas_call(
        kernel,
        out_shape=[
            pltpu.HBM(x.shape, x.dtype) if n in far_out else x for n, x in enumerate(out_shape)
        ],
        in_specs=[apart if n in far else whole for n in range(len(operands))],
        out_specs=[apart if n in far_out else whole for n in range(len(out_shape))],
        scratch_shapes=scratch,
        cost_estimate=pl.CostEstimate(flops=flops, bytes_accessed=size, transcendentals=0),
        compiler_params=pltpu.CompilerParams(vmem_limit_bytes=12 * 1024 * 1024),
    )(*operands)


def exchange(outgoing, low, high):
    count = lax.axis_size("group")
    up = [(i, (i + 1) % count) for i in range(count)]
    down = [(target, source) for source, target in up]
    arrived = lax.all_to_all(outgoing, "dev", split_axis=0, concat_axis=0, tiled=True)
    before = lax.ppermute(high, "group", up)
    after = lax.ppermute(low, "group", down)
    return arrived, before, after


def per_device(level_set, speed, peer_slabs, region_slabs, halo_source):
    rows, count = level_set.shape
    peers, slots = peer_slabs.shape
    border = region_slabs.shape[1]
    wide = Plan(count, peers, slots, border, 3)
    thin = Plan(count, peers, slots, border, 1)
    code_rows = -(-wide.far_tiles // 8) * 8

    def ends(plan):
        return pltpu.VMEM((2, wide.halves, 64 * plan.layers, LANES), jnp.float32)

    def table(plan):
        return pltpu.VMEM((plan.far_tiles, 64 * plan.layers, LANES), jnp.float32)

    def halos(sides, groups):
        return pltpu.VMEM((sides, wide.halves, 8 * groups, LANES), jnp.float32)

    def sent(plan):
        return [f32(plan.message()), f32(plan.border_message()), f32(plan.border_message())]

    field = f32((wide.halves, rows, LANES))
    pad_rows = -(-(peers + 2) // 8) * 8
    phi, *message, send_code, halo_code = call(
        functools.partial(first_kernel, wide),
        [field]
        + sent(wide)
        + [
            jax.ShapeDtypeStruct((code_rows, LANES), jnp.int32),
            jax.ShapeDtypeStruct(halo_source.shape, jnp.int32),
        ],
        [
            ends(wide),
            table(wide),
            pltpu.VMEM((pad_rows, LANES), jnp.int32),
            pltpu.VMEM(peer_slabs.shape, jnp.int32),
            pltpu.VMEM(region_slabs.shape, jnp.int32),
            pltpu.VMEM(halo_source.shape, jnp.int32),
            pltpu.SemaphoreType.DMA((3 + wide.halves,)),
        ],
        1000000,
        level_set, peer_slabs, region_slabs, halo_source,
        far=(0, 1, 2, 3),
    )

    def near_halos(plan, *fields):
        out = [f32((6, plan.halves, 64 * plan.layers, LANES))]
        flops = rows * count * 100 * plan.layers
        if plan.layers == 1:
            kernel = functools.partial(near_thin_kernel, plan)
            return call(kernel, out + [field], [], flops, *fields, halo_code)
        out.append(f32(inner_shape))
        scratch = [ends(plan), pltpu.VMEM(inner_shape, jnp.float32)]
        scratch.append(pltpu.SemaphoreType.DMA((3,)))
        kernel = functools.partial(near_wide_kernel, plan)
        return call(kernel, out, scratch, flops, *fields, halo_code, far_out=(1,))

    inner_shape = (3, wide.halves, rows // 2, LANES)
    block = pltpu.VMEM((wide.halves, rows, LANES), jnp.float32)
    for offset_step in range(OFFSET_STEPS):
        phi, *message = call(
            functools.partial(advect_kernel, wide, thin),
            [field] + sent(thin),
            [ends(wide), table(wide), halos(4, 3), halos(4, 3), block, block]
            + [pltpu.VMEM(inner_shape, jnp.float32)]
            + [pltpu.SemaphoreType.DMA((wide.halves,)), pltpu.SemaphoreType.DMA((3,))],
            rows * count * 300,
            phi, *near_halos(wide, phi), speed, *exchange(*message), send_code, halo_code,
            far=(2, 3),
        )
        origin = phi
        for redist_pass in range(REDIST_PASSES):
            if redist_pass < REDIST_PASSES - 1:
                sends = thin
            elif offset_step < OFFSET_STEPS - 1:
                sends = wide
            else:
                sends = None
            if sends is None:
                out, scratch = [f32((rows, count))], [table(thin)]
                extra = [pltpu.VMEM((rows, count), jnp.float32), pltpu.SemaphoreType.DMA((8,))]
            else:
                out, scratch = [field] + sent(sends), [ends(sends), table(sends)]
                extra = []
            phi, *message = call(
                functools.partial(relax_kernel, thin, sends),
                out,
                scratch + [block] + extra,
                rows * count * 60,
                phi, origin, *near_halos(thin, phi, origin), *exchange(*message), send_code, halo_code,
                far_out=(0,) if sends is None else (),
            )
    return phi


def solution(mesh):
    return jax.shard_map(
        per_device,
        mesh=mesh,
        in_specs=(
            P(None, ("group", "dev")),
            P(None, ("group", "dev")),
            P(("group", "dev"), None),
            P(("group", "dev"), None),
            P(None, ("group", "dev")),
        ),
        out_specs=P(None, ("group", "dev")),
        check_vma=False,
    )
```

```python
import functools

import jax
import jax.numpy as jnp
from jax import lax
from jax.experimental import pallas as pl
from jax.experimental.pallas import tpu as pltpu
from jax.sharding import PartitionSpec as P

OFFSET_STEPS = 2
REDIST_PASSES = 2

advect_scale = 0.3
relax_scale = 0.3
weno_floor = 1e-06

LANES = 128


class Plan:
    def __init__(self, count, peers, slots, border, layers):
        self.count = count
        self.peers = peers
        self.slots = slots
        self.border = border
        self.layers = layers
        self.halves = count // LANES
        self.local_tiles = 6 * self.halves
        self.groups = 8 * layers
        self.per_tile = LANES // slots
        self.peer_tiles = -(-peers // self.per_tile)
        used = (peers - (self.peer_tiles - 1) * self.per_tile) * slots
        if used + 2 * border <= LANES:
            self.border_tile = self.peer_tiles - 1
            self.border_lane = used
        else:
            self.border_tile = self.peer_tiles
            self.border_lane = 0
        self.far_tiles = self.border_tile + 1
        self.pieces = min(LANES // slots, self.groups)
        self.piece_groups = -(-self.groups // self.pieces)
        self.border_pieces = min(LANES // border, self.groups)
        self.border_groups = -(-self.groups // self.border_pieces)

    def message(self):
        return (self.peers, 8 * self.piece_groups, LANES)

    def border_message(self):
        return (8 * self.border_groups, LANES)


def lane_ids():
    return lax.broadcasted_iota(jnp.int32, (8, LANES), 1)


def turn(block, shift):
    shift = shift % LANES
    return block if shift == 0 else pltpu.roll(block, shift, 1)


def in_block(lanes, start, size):
    return jnp.logical_and(lanes >= start, lanes < start + size)


def half(h):
    return pl.ds(h * LANES, LANES)


def rows8(start):
    return pl.ds(pl.multiple_of(start, 8), 8)


def bits_of(tile, tiles):
    return [(tile & (1 << b)) != 0 for b in range(max(tiles - 1, 1).bit_length())]


def pick_tile(values, masks):
    def pick(lowest, bit):
        if bit < 0:
            return values(lowest)
        first = pick(lowest, bit - 1)
        if lowest + (1 << bit) >= values.count:
            return first
        return jnp.where(masks[bit], pick(lowest + (1 << bit), bit - 1), first)

    return pick(0, len(masks) - 1)


class Taken:
    def __init__(self, sources, lane):
        self.sources = sources
        self.lane = lane
        self.count = len(sources)

    def __call__(self, tile):
        return jnp.take_along_axis(
            self.sources[tile], self.lane, axis=1, mode="promise_in_bounds"
        )


def gather(sources, code):
    return pick_tile(Taken(sources, code & (LANES - 1)), bits_of(code >> 7, len(sources)))


def local_sources(plan, phi, ends, g):
    w = plan.layers
    if w == 1:
        along_y = g * 64
    else:
        along_y = (g // w) * 64 + lax.rem(g, w) * 8
    starts = [g * 8, (8 - w) * 64 + g * 8, along_y, along_y + (8 - w) * 8]
    found = []
    for start in starts:
        for h in range(plan.halves):
            found.append(phi[h, rows8(start), :])
    for end in range(2):
        for h in range(plan.halves):
            if w == 1:
                found.append(phi[h, pl.ds(g * 64 + 7 * end, 8, stride=8), :])
            else:
                found.append(ends[end, h, rows8(g * 8), :])
    return found


def fill_ends(plan, phi, ends):
    w = plan.layers
    if w == 1:
        return

    @pl.loop(0, 8)
    def _(i):
        for end in range(2):
            for l in range(w):
                k = l + end * (8 - w)
                for h in range(plan.halves):
                    ends[end, h, pl.ds(i * 8 * w + l, 8, stride=w), :] = phi[
                        h, pl.ds(i * 64 + k, 8, stride=8), :
                    ]


def pack_sends(plan, phi, ends, send_code, table, outgoing, low, high):
    lanes = lane_ids()
    w = plan.layers

    together = 8 if plan.layers == 1 else 12

    @pl.loop(0, plan.groups // together)
    def _(q):
        for v in range(together):
            g = q * together + v
            sources = local_sources(plan, phi, ends, g)
            for t in range(plan.far_tiles):
                code = jnp.broadcast_to(send_code[pl.ds(t, 1), :], (8, LANES))
                table[t, rows8(g * 8), :] = gather(sources, code)

    for e in range(plan.peers):
        t, eq = divmod(e, plan.per_tile)
        for gi in range(plan.piece_groups):
            block = None
            for p in range(plan.pieces):
                g = p * plan.piece_groups + gi
                if g >= plan.groups:
                    continue
                part = turn(table[t, pl.ds(g * 8, 8), :], (p - eq) * plan.slots)
                if block is None:
                    block = part
                else:
                    block = jnp.where(lanes >= p * plan.slots, part, block)
            outgoing[e, pl.ds(gi * 8, 8), :] = block
    for side, target in enumerate((low, high)):
        for gi in range(plan.border_groups):
            block = None
            for p in range(plan.border_pieces):
                g = p * plan.border_groups + gi
                if g >= plan.groups:
                    continue
                part = turn(
                    table[plan.border_tile, pl.ds(g * 8, 8), :],
                    (p - side) * plan.border - plan.border_lane,
                )
                if block is None:
                    block = part
                else:
                    block = jnp.where(lanes >= p * plan.border, part, block)
            target[pl.ds(gi * 8, 8), :] = block


def unpack_far(plan, arrived, before, after, table):
    lanes = lane_ids()
    for g in range(plan.groups):
        p, gi = divmod(g, plan.piece_groups)
        bp, bgi = divmod(g, plan.border_groups)
        for t in range(plan.far_tiles):
            block = None
            if t < plan.peer_tiles:
                for eq in range(min(plan.per_tile, plan.peers - t * plan.per_tile)):
                    e = t * plan.per_tile + eq
                    part = turn(arrived[e, pl.ds(gi * 8, 8), :], (eq - p) * plan.slots)
                    if block is None:
                        block = part
                    else:
                        block = jnp.where(lanes >= eq * plan.slots, part, block)
            if t == plan.border_tile:
                for q, source in enumerate((before, after)):
                    start = plan.border_lane + q * plan.border
                    part = turn(source[pl.ds(bgi * 8, 8), :], start - bp * plan.border)
                    if block is None:
                        block = part
                    else:
                        block = jnp.where(lanes >= start, part, block)
            table[t, pl.ds(g * 8, 8), :] = block


def pull_local(plan, phi, ends, halo_code, halos, g):
    sources = local_sources(plan, phi, ends, g)
    for s in range(6):
        for h in range(plan.halves):
            code = jnp.broadcast_to(halo_code[pl.ds(s, 1), half(h)], (8, LANES))
            halos[s, h, rows8(g * 8), :] = gather(sources, code)


def far_values(plan, table, halo_code, near, sides, g):
    start = plan.local_tiles * LANES
    sources = [table[t, rows8(g * 8), :] for t in range(plan.far_tiles)]
    found = {}
    for s in sides:
        for h in range(plan.halves):
            code = jnp.broadcast_to(halo_code[pl.ds(s, 1), half(h)], (8, LANES))
            far = gather(sources, code - start)
            found[s, h] = jnp.where(code >= start, far, near[s, h, rows8(g * 8), :])
    return found


def pull_far(plan, table, halo_code, near, halos, sides, groups):
    start = plan.local_tiles * LANES
    sources = [
        [table[t, rows8(g * 8), :] for t in range(plan.far_tiles)] for g in groups
    ]
    for s in sides:
        for h in range(plan.halves):
            code = jnp.broadcast_to(halo_code[pl.ds(s, 1), half(h)], (8, LANES))
            local = code < start
            lane = (code - start) & (LANES - 1)
            masks = bits_of((code - start) >> 7, plan.far_tiles)
            for row, g in enumerate(groups):
                far = pick_tile(Taken(sources[row], lane), masks)
                here = near[s, h, rows8(g * 8), :]
                halos[s - sides[0], h, pl.ds(row * 8, 8), :] = jnp.where(local, here, far)


def weno_windows(q):
    first = [q[m + 1] - q[m] for m in range(7)]
    second = [first[m + 1] - first[m] for m in range(6)]
    third = [second[m + 1] - second[m] for m in range(5)]
    fourth = [(third[m] - third[m + 1]) * (1.0 / 6.0) for m in range(4)]
    bend = [t * t * (4.0 / 3.0) + weno_floor for t in third]
    found = []
    for m in range(3):
        s1, s2 = second[m + 1], second[m + 2]
        a = bend[m] + s1 * (s1 + third[m])
        b = bend[m + 1] + s1 * s2
        c = bend[m + 2] + s2 * (s2 - third[m + 2])
        a, b, c = (pl.reciprocal(value, approx=True) for value in (a, b, c))
        x, z = a * a, c * c
        total = 0.5 * (x + z) + (3.0 * b) * b
        xu = x * fourth[m]
        zu = z * fourth[m + 1]
        slope = 0.25 * (s1 + s2)
        middle = first[m + 2] + third[m + 1] * (1.0 / 12.0)
        fix = (xu + 1.5 * zu) * pl.reciprocal(total + z, approx=True)
        backward = middle + slope + fix
        fix = (zu + 1.5 * xu) * pl.reciprocal(total + x, approx=True)
        found.append((backward, fix + slope - middle))
    return found


def inner_values(values):
    three, four, five = weno_windows(values)
    return [three[1], jnp.maximum(three[0], four[1]), jnp.maximum(four[0], five[1]), five[0]]


def line_values(low, values, high, inner):
    zero, one, two = weno_windows(low + values[:5])
    six, seven, last = weno_windows(values[3:] + high)
    steep = [
        jnp.maximum(zero[0], one[1]),
        jnp.maximum(one[0], two[1]),
        jnp.maximum(two[0], inner[0]),
        inner[1],
        inner[2],
        jnp.maximum(inner[3], six[1]),
        jnp.maximum(six[0], seven[1]),
        jnp.maximum(seven[0], last[1]),
    ]
    steep = [jnp.maximum(value, 0.0) for value in steep]
    return [value * value for value in steep]


def line_at(phi, h, axis, q):
    if axis == 0:
        return [phi[h, rows8(m * 64 + q * 8), :] for m in range(8)]
    if axis == 1:
        return [phi[h, rows8(q * 64 + m * 8), :] for m in range(8)]
    return [phi[h, pl.ds(q * 64 + m, 8, stride=8), :] for m in range(8)]


def inner_at(inner, h, axis, q):
    return [inner[axis, h, rows8(q * 32 + m * 8), :] for m in range(4)]


def advect(plan, phi, speed, ready, near, inner, table, halo_code, halos, squares, moved):
    w = plan.layers

    def stage_planes(i, target):
        groups = [i * w + l for l in range(w)]
        pull_far(plan, table, halo_code, near, target, (2, 3, 4, 5), groups)

    def stage_columns(j, target):
        groups = [l * 8 + j for l in range(w)]
        pull_far(plan, table, halo_code, near, target, (0, 1), groups)

    def stacked(source, side, h):
        return [source[side, h, pl.ds(l * 8, 8), :] for l in range(w)]

    def spread(source, side, h):
        return [source[side, h, pl.ds(l, 8, stride=w), :] for l in range(w)]

    def plane(i, source):
        for h in range(plan.halves):
            low, high = spread(source, 2, h), spread(source, 3, h)
            values = line_values(low, line_at(phi, h, 2, i), high, inner_at(inner, h, 2, i))
            for k, value in enumerate(values):
                squares[h, pl.ds(i * 64 + k, 8, stride=8), :] = value
        for h in range(plan.halves):
            low, high = stacked(source, 0, h), stacked(source, 1, h)
            values = line_values(low, line_at(phi, h, 1, i), high, inner_at(inner, h, 1, i))
            for j, value in enumerate(values):
                squares[h, rows8(i * 64 + j * 8), :] += value

    def column(j, source):
        for h in range(plan.halves):
            low, high = stacked(source, 0, h), stacked(source, 1, h)
            line = line_at(phi, h, 0, j)
            values = line_values(low, line, high, inner_at(inner, h, 0, j))
            for i, value in enumerate(values):
                here = rows8(i * 64 + j * 8)
                total = squares[h, here, :] + value
                change = advect_scale * speed[h, here, :] * jnp.sqrt(total)
                moved[h, here, :] = line[i] - change

    even, odd = halos
    stage_planes(0, even)
    ready(0)

    @pl.loop(0, 4)
    def _(q):
        i = 2 * q
        stage_planes(i + 1, odd)
        plane(i, even)
        stage_planes(jnp.minimum(i + 2, 7), even)
        plane(i + 1, odd)

    stage_columns(0, even)
    ready(1)

    @pl.loop(0, 2)
    def _(q):
        j = 4 * q
        for v in (0, 2):
            stage_columns(j + v + 1, odd)
            column(j + v, even)
            stage_columns(jnp.minimum(j + v + 2, 7), even)
            column(j + v + 1, odd)


def steepness(value, low, high, facing):
    steep = jnp.maximum((value - low) * facing, (value - high) * facing)
    steep = jnp.maximum(steep, 0.0)
    return steep * steep


def facing_of(start):
    return jnp.where(start > 0.0, 1.0, -1.0)


def relax_inner(plan, phi, origin, inner, i):
    inside = jnp.where(jnp.logical_and(i > 0, i < 7), 1.0, 0.0)
    below, above = jnp.maximum(i - 1, 0), jnp.minimum(i + 1, 7)
    for h in range(plan.halves):
        line = line_at(phi, h, 1, i)
        for j, value in enumerate(line):
            here = rows8(i * 64 + j * 8)
            facing = facing_of(origin[h, here, :])
            low = phi[h, rows8(below * 64 + j * 8), :]
            high = phi[h, rows8(above * 64 + j * 8), :]
            total = inside * steepness(value, low, high, facing)
            if 0 < j < 7:
                total += steepness(value, line[j - 1], line[j + 1], facing)
            inner[h, here, :] = total
        line = line_at(phi, h, 2, i)
        for k in range(1, 7):
            here = pl.ds(i * 64 + k, 8, stride=8)
            facing = facing_of(origin[h, here, :])
            inner[h, here, :] += steepness(line[k], line[k - 1], line[k + 1], facing)


def relax(plan, phi, origin, near, inner, table, halo_code, part, moved, finish):
    @pl.loop(0, 1)
    def _(q):
        for v in range(8):
            i = q * 8 + v
            halo = far_values(plan, table, halo_code, near, (2, 3, 4, 5), i)
            for h in range(plan.halves):
                for j in range(8):
                    here = rows8(i * 64 + j * 8)
                    if 0 < j < 7:
                        part[h, here, :] = jnp.zeros((8, LANES), jnp.float32)
                        continue
                    side, other = (2, 1) if j == 0 else (3, 6)
                    value = phi[h, here, :]
                    beside = phi[h, rows8(i * 64 + other * 8), :]
                    facing = facing_of(origin[h, here, :])
                    part[h, here, :] = steepness(value, halo[side, h], beside, facing)
                for side, k, other in ((4, 0, 1), (5, 7, 6)):
                    here = pl.ds(i * 64 + k, 8, stride=8)
                    value = phi[h, here, :]
                    beside = phi[h, pl.ds(i * 64 + other, 8, stride=8), :]
                    facing = facing_of(origin[h, here, :])
                    part[h, here, :] += steepness(value, halo[side, h], beside, facing)

    for j in range(8):
        halo = far_values(plan, table, halo_code, near, (0, 1), j)
        for h in range(plan.halves):
            for side, i, other in ((0, 0, 1), (1, 7, 6)):
                here = rows8(i * 64 + j * 8)
                value = phi[h, here, :]
                beside = phi[h, rows8(other * 64 + j * 8), :]
                facing = facing_of(origin[h, here, :])
                part[h, here, :] += steepness(value, halo[side, h], beside, facing)

    @pl.loop(0, 1)
    def _(q):
        for v in range(8):
            i = q * 8 + v
            for h in range(plan.halves):
                for j in range(8):
                    here = rows8(i * 64 + j * 8)
                    start = origin[h, here, :]
                    sense = start * lax.rsqrt(start * start + 1.0)
                    slope = jnp.sqrt(inner[h, here, :] + part[h, here, :])
                    value = phi[h, here, :] - relax_scale * sense * (slope - 1.0)
                    if finish is not None:
                        moved[here, half(h)] = value
                    else:
                        moved[h, here, :] = value
            if finish is not None:
                finish(i)


def first_kernel(
    plan, level_set, peer_slabs, region_slabs, halo_source,
    phi, outgoing, low, high, send_code, halo_code, ends, table, padded, peer, region, entries, ready,
):
    copies = [
        pltpu.make_async_copy(source, target, ready.at[n])
        for n, (source, target) in enumerate(
            ((peer_slabs, peer), (region_slabs, region), (halo_source, entries))
        )
    ]
    for h in range(plan.halves):
        copies.append(
            pltpu.make_async_copy(level_set.at[:, half(h)], phi.at[h], ready.at[3 + h])
        )
    for copy in copies:
        copy.start()
    for copy in copies[:3]:
        copy.wait()
    lanes = lane_ids()
    padded[...] = jnp.zeros_like(padded)
    padded[pl.ds(0, plan.peers), pl.ds(0, plan.slots)] = jnp.maximum(peer[...], 0)
    padded[pl.ds(plan.peers, 2), pl.ds(0, plan.border)] = region[...]

    def wide(row):
        return jnp.broadcast_to(padded[pl.ds(row, 1), :], (8, LANES))

    send_code[...] = jnp.zeros_like(send_code)
    for t in range(plan.far_tiles):
        block = jnp.zeros((8, LANES), jnp.int32)
        if t < plan.peer_tiles:
            for eq in range(min(plan.per_tile, plan.peers - t * plan.per_tile)):
                part = turn(wide(t * plan.per_tile + eq), eq * plan.slots)
                block = jnp.where(in_block(lanes, eq * plan.slots, plan.slots), part, block)
        if t == plan.border_tile:
            for side in range(2):
                start = plan.border_lane + side * plan.border
                part = turn(wide(plan.peers + side), start)
                block = jnp.where(in_block(lanes, start, plan.border), part, block)
        send_code[pl.ds(t, 1), :] = block[0:1]

    entry = entries[...]
    far = entry - plan.local_tiles * LANES
    tile_span = plan.per_tile * plan.slots
    tile = jnp.zeros_like(entry)
    for k in range(1, plan.peer_tiles):
        tile += (far >= k * tile_span).astype(jnp.int32)
    code = (plan.local_tiles + tile) * LANES + far - tile * tile_span
    edge = far - plan.peers * plan.slots
    edge_code = (plan.local_tiles + plan.border_tile) * LANES + plan.border_lane + edge
    code = jnp.where(edge >= 0, edge_code, code)
    halo_code[...] = jnp.where(far >= 0, code, entry)
    for copy in copies[3:]:
        copy.wait()

    fill_ends(plan, phi, ends)
    pack_sends(plan, phi, ends, send_code, table, outgoing, low, high)


def near_thin_kernel(plan, phi, origin, halo_code, near, inner):
    for g in range(plan.groups):
        pull_local(plan, phi, None, halo_code, near, g)
        relax_inner(plan, phi, origin, inner, g)


def near_wide_kernel(plan, phi, halo_code, near, *rest):
    inner, ends, kept, done = rest
    copies = [pltpu.make_async_copy(kept.at[a], inner.at[a], done.at[a]) for a in range(3)]
    fill_ends(plan, phi, ends)
    for axis in range(3):

        @pl.loop(0, 4)
        def _(pair):
            for v in range(2):
                q = pair * 2 + v
                pull_local(plan, phi, ends, halo_code, near, axis * 8 + q)
                for h in range(plan.halves):
                    for m, value in enumerate(inner_values(line_at(phi, h, axis, q))):
                        kept[axis, h, rows8(q * 32 + m * 8), :] = value

        copies[axis].start()
    for copy in copies:
        copy.wait()


def advect_kernel(
    plan, sends, phi, near, inner, speed, arrived, before, after, send_code, halo_code,
    moved, outgoing, low, high, ends, table, even, odd, squares, fast, kept, loaded, found,
):
    first = [pltpu.make_async_copy(inner.at[a], kept.at[a], found.at[a]) for a in (2, 1)]
    second = [pltpu.make_async_copy(inner.at[0], kept.at[0], found.at[0])]
    for h in range(plan.halves):
        second.append(pltpu.make_async_copy(speed.at[:, half(h)], fast.at[h], loaded.at[h]))
    for copy in first + second:
        copy.start()

    def ready(stage):
        for copy in (first, second)[stage]:
            copy.wait()

    unpack_far(plan, arrived, before, after, table)
    advect(plan, phi, fast, ready, near, kept, table, halo_code, (even, odd), squares, moved)
    pack_sends(sends, moved, ends, send_code, table, outgoing, low, high)


def relax_kernel(
    plan, sends, phi, origin, near, inner, arrived, before, after, send_code, halo_code, *rest
):
    if sends is None:
        (result, table, part, moved, written) = rest

        def plane_copy(i):
            rows = rows8(i * 64)
            rows = pl.ds(rows.start, 64)
            return pltpu.make_async_copy(moved.at[rows], result.at[rows], written.at[i])

        def finish(i):
            plane_copy(i).start()

    else:
        (moved, outgoing, low, high, ends, table, part) = rest
        finish = None
    unpack_far(plan, arrived, before, after, table)
    relax(plan, phi, origin, near, inner, table, halo_code, part, moved, finish)
    if sends is None:
        for i in range(8):
            plane_copy(i).wait()
    else:
        fill_ends(sends, moved, ends)
        pack_sends(sends, moved, ends, send_code, table, outgoing, low, high)


def f32(shape):
    return jax.ShapeDtypeStruct(shape, jnp.float32)


def call(kernel, out_shape, scratch, flops, *operands, far=(), far_out=()):
    whole = pl.BlockSpec(memory_space=pltpu.VMEM)
    apart = pl.BlockSpec(memory_space=pltpu.HBM)
    size = sum(x.size * 4 for x in operands) + sum(x.size * 4 for x in out_shape)
    operands = [
        pltpu.with_memory_space_constraint(x, pltpu.HBM) if n in far else x
        for n, x in enumerate(operands)
    ]
    return pl.pallas_call(
        kernel,
        out_shape=[
            pltpu.HBM(x.shape, x.dtype) if n in far_out else x for n, x in enumerate(out_shape)
        ],
        in_specs=[apart if n in far else whole for n in range(len(operands))],
        out_specs=[apart if n in far_out else whole for n in range(len(out_shape))],
        scratch_shapes=scratch,
        cost_estimate=pl.CostEstimate(flops=flops, bytes_accessed=size, transcendentals=0),
        compiler_params=pltpu.CompilerParams(vmem_limit_bytes=12 * 1024 * 1024),
    )(*operands)


def exchange(outgoing, low, high):
    count = lax.axis_size("group")
    up = [(i, (i + 1) % count) for i in range(count)]
    down = [(target, source) for source, target in up]
    arrived = lax.all_to_all(outgoing, "dev", split_axis=0, concat_axis=0, tiled=True)
    before = lax.ppermute(high, "group", up)
    after = lax.ppermute(low, "group", down)
    return arrived, before, after


def per_device(level_set, speed, peer_slabs, region_slabs, halo_source):
    rows, count = level_set.shape
    peers, slots = peer_slabs.shape
    border = region_slabs.shape[1]
    wide = Plan(count, peers, slots, border, 3)
    thin = Plan(count, peers, slots, border, 1)
    code_rows = -(-wide.far_tiles // 8) * 8

    def ends(plan):
        return pltpu.VMEM((2, wide.halves, 64 * plan.layers, LANES), jnp.float32)

    def table(plan):
        return pltpu.VMEM((plan.far_tiles, 64 * plan.layers, LANES), jnp.float32)

    def halos(sides, groups):
        return pltpu.VMEM((sides, wide.halves, 8 * groups, LANES), jnp.float32)

    def sent(plan):
        return [f32(plan.message()), f32(plan.border_message()), f32(plan.border_message())]

    field = f32((wide.halves, rows, LANES))
    pad_rows = -(-(peers + 2) // 8) * 8
    phi, *message, send_code, halo_code = call(
        functools.partial(first_kernel, wide),
        [field]
        + sent(wide)
        + [
            jax.ShapeDtypeStruct((code_rows, LANES), jnp.int32),
            jax.ShapeDtypeStruct(halo_source.shape, jnp.int32),
        ],
        [
            ends(wide),
            table(wide),
            pltpu.VMEM((pad_rows, LANES), jnp.int32),
            pltpu.VMEM(peer_slabs.shape, jnp.int32),
            pltpu.VMEM(region_slabs.shape, jnp.int32),
            pltpu.VMEM(halo_source.shape, jnp.int32),
            pltpu.SemaphoreType.DMA((3 + wide.halves,)),
        ],
        1000000,
        level_set, peer_slabs, region_slabs, halo_source,
        far=(0, 1, 2, 3),
    )

    def near_halos(plan, *fields):
        out = [f32((6, plan.halves, 64 * plan.layers, LANES))]
        flops = rows * count * 100 * plan.layers
        if plan.layers == 1:
            kernel = functools.partial(near_thin_kernel, plan)
            return call(kernel, out + [field], [], flops, *fields, halo_code)
        out.append(f32(inner_shape))
        scratch = [ends(plan), pltpu.VMEM(inner_shape, jnp.float32)]
        scratch.append(pltpu.SemaphoreType.DMA((3,)))
        kernel = functools.partial(near_wide_kernel, plan)
        return call(kernel, out, scratch, flops, *fields, halo_code, far_out=(1,))

    inner_shape = (3, wide.halves, rows // 2, LANES)
    block = pltpu.VMEM((wide.halves, rows, LANES), jnp.float32)
    for offset_step in range(OFFSET_STEPS):
        phi, *message = call(
            functools.partial(advect_kernel, wide, thin),
            [field] + sent(thin),
            [ends(wide), table(wide), halos(4, 3), halos(4, 3), block, block]
            + [pltpu.VMEM(inner_shape, jnp.float32)]
            + [pltpu.SemaphoreType.DMA((wide.halves,)), pltpu.SemaphoreType.DMA((3,))],
            rows * count * 300,
            phi, *near_halos(wide, phi), speed, *exchange(*message), send_code, halo_code,
            far=(2, 3),
        )
        origin = phi
        for redist_pass in range(REDIST_PASSES):
            if redist_pass < REDIST_PASSES - 1:
                sends = thin
            elif offset_step < OFFSET_STEPS - 1:
                sends = wide
            else:
                sends = None
            if sends is None:
                out, scratch = [f32((rows, count))], [table(thin)]
                extra = [pltpu.VMEM((rows, count), jnp.float32), pltpu.SemaphoreType.DMA((8,))]
            else:
                out, scratch = [field] + sent(sends), [ends(sends), table(sends)]
                extra = []
            phi, *message = call(
                functools.partial(relax_kernel, thin, sends),
                out,
                scratch + [block] + extra,
                rows * count * 60,
                phi, origin, *near_halos(thin, phi, origin), *exchange(*message), send_code, halo_code,
                far_out=(0,) if sends is None else (),
            )
    return phi


def solution(mesh):
    return jax.shard_map(
        per_device,
        mesh=mesh,
        in_specs=(
            P(None, ("group", "dev")),
            P(None, ("group", "dev")),
            P(("group", "dev"), None),
            P(("group", "dev"), None),
            P(None, ("group", "dev")),
        ),
        out_specs=P(None, ("group", "dev")),
        check_vma=False,
    )
```
